32 devices in a mesh: lon: 16 (over z, x, core), lat: 2 (over y).
Axes of the slice: x: 2, y: 2, z: 4, core: 2. Of those that a mesh axis runs over, the one named last changes fastest.
Arguments:
- tracers: float32 [3, 10, 128, 2048], P(None, None, 'lat', 'lon'), may hold values from -6 to 6
- offsets: int32 [10, 128, 2048], P(None, 'lat', 'lon'), may hold values from -16 to 15, as said below
- weights: float32 [10, 128, 2048], P(None, 'lat', 'lon'), may hold values from 0 to 1
- diffusion: float32 [9, 128, 2048], P(None, 'lat', 'lon'), may hold values from 0.05 to 5
- send_index: int32 [32, 32, 512], P(('lon', 'lat')), may hold values from 0 to 8191, as said below
- send_count: int32 [32, 32], P(('lon', 'lat')), may hold values from 1 to 512, as said below
Outputs:
- owned_tracers: float32 [3, 10, 262144], P(None, None, ('lon', 'lat'))
The draws below stay inside these ranges and needn't reach their ends.
Inputs may be any that keep to these rules, and one draw needn't show every extreme that they name: `offsets`: the departure interval of a cell starts this many cells east of it on the same row and level; both ends of the range occur. `send_count`: entry [d, e] counts the columns of device d that device e owns. Every row and every column sums to 8192. A device keeps exactly 511 of its own columns and sends exactly one to the device 32 // 2 further on; some list holds exactly 512 columns. `send_index`: entries [d, e, 0 : send_count[d, e]] are local column indices of device d that device e owns, in owner order; each column of d appears in exactly one list once; entries past the count are valid column indices that carry no meaning.
All inputs are finite; a program needn't handle non-finite values.
Results may differ from the reference program's by a relative error of at most 0.0003.
Values sent between devices are 32-bit elements; how exact they have to be, the bound alone decides.
No kernel may reach another device: no remote copies, remote signals or barrier semaphores. Data moves between devices by JAX's collectives and lax.ppermute only.
A program may use at most 128 MiB of HBM per device.

```python
import math
import jax
import jax.numpy as jnp
import numpy as np
from jax import lax

NTR = 3
LEV = 10
HALO = 16
CLAT = 64
CLON = 128
NLAT = 128
NLON = 2048
COLS_DEV = 8192
CAP = 512
N_LON = 16
N_LAT = 2
DEVICES = 32


def draw_offsets(key, part):
    half_reach = HALO // 2
    row_base = jax.random.randint(jax.random.fold_in(key, 21), (LEV, NLAT, 1), -half_reach, half_reach)
    wobble = jax.random.randint(jax.random.fold_in(key, 22), (LEV, NLAT, NLON), -half_reach, half_reach + 1)
    result = (row_base + wobble).astype(jnp.int32)
    result = jnp.clip(result, -HALO, HALO - 1).astype(jnp.int32)
    result = result.at[0, 0, 0].set(-HALO)
    result = result.at[0, 0, NLON - 1].set(HALO - 1)
    return result


def route_counts(key):
    half_count = DEVICES // 2
    base_half = jax.random.randint(jax.random.fold_in(key, 11), (half_count,), 2, CAP - 1)
    base_half = base_half.at[0].set(CAP - 1)
    base_half = base_half.at[2].set(CAP - 2)
    by_offset = jnp.concatenate([base_half, CAP - base_half]).astype(jnp.int32)
    per_device = jnp.broadcast_to(by_offset[None, :], (DEVICES, DEVICES))
    triple_starts = np.concatenate([np.arange(1, half_count, 3), np.arange(half_count + 1, DEVICES, 3)])
    flips = jax.random.randint(jax.random.fold_in(key, 12), (triple_starts.shape[0], DEVICES), 0, 2).astype(jnp.int32)
    flips = flips.at[0, 0].set(1)
    flips = flips.at[0, 1].set(1)
    flips_next = jnp.roll(flips, -1, axis=1)
    delta = jnp.zeros((DEVICES, DEVICES), jnp.int32)
    delta = delta.at[:, triple_starts + 1].add((flips + flips_next).T)
    delta = delta.at[:, triple_starts].add(-flips.T)
    delta = delta.at[:, triple_starts + 2].add(-flips_next.T)
    per_device = per_device + delta
    rank_index = jnp.arange(DEVICES, dtype=jnp.int32)
    offset_table = (rank_index[None, :] - rank_index[:, None]) % DEVICES
    return jnp.take_along_axis(per_device, offset_table, axis=1).astype(jnp.int32)


def draw_send_count(key, part):
    return route_counts(key)


def draw_send_index(key, part):
    counts = route_counts(key)
    device_keys = jax.random.split(jax.random.fold_in(key, 13), DEVICES)
    shuffles = jax.vmap(lambda one_key: jax.random.permutation(one_key, COLS_DEV))(device_keys).astype(jnp.int32)
    starts = jnp.cumsum(counts, axis=1) - counts
    slots = starts[:, :, None] + jnp.arange(CAP, dtype=jnp.int32)[None, None, :]
    slots = jnp.minimum(slots, COLS_DEV - 1)
    return jax.vmap(lambda shuffle, slot_rows: shuffle[slot_rows])(shuffles, slots).astype(jnp.int32)


def steps_of(key, shape, cuts, least, largest):
    level, own = 1.0, jax.random.fold_in(key, 6)
    for axis_at, parts in cuts:
        heights = jnp.exp(jax.random.uniform(jax.random.fold_in(own, axis_at), (parts,), jnp.float32, least / len(cuts), largest / len(cuts)))
        level = level * jnp.repeat(heights, shape[axis_at] // parts).reshape([-1 if axis == axis_at else 1 for axis in range(len(shape))])
    return level


def bell_draw(key, dims, scale, reach, cuts=(), kind=jnp.bfloat16):
    drawn = jax.random.normal(key, dims, jnp.float32) * scale
    if len(cuts) > 0:
        drawn = steps_of(key, dims, cuts, -0.22, 0.18) * drawn
    return jnp.clip(drawn, min=-reach, max=reach).astype(kind)


def setup_inputs(seed: int = 0) -> dict:
    streams_of = jax.random.split(jax.random.key(seed), 7)
    return {
        "tracers": bell_draw(streams_of[0], (NTR, LEV, NLAT, NLON), 1.0, 6.0, ((2, 2), (3, 16)), jnp.float32),
        "offsets": draw_offsets(jax.random.fold_in(streams_of[6], 71), 0),
        "weights": jnp.clip(1.0 * jax.random.uniform(streams_of[2], (LEV, NLAT, NLON), jnp.float32) ** steps_of(streams_of[2], (LEV, NLAT, NLON), ((1, 2), (2, 16)), -0.2, 0.2), 0.0, 1.0),
        "diffusion": jnp.clip(jnp.exp(math.log(5.0) - 4.6051702 * jax.random.uniform(streams_of[3], (LEV - 1, NLAT, NLON), jnp.float32) ** steps_of(streams_of[3], (LEV - 1, NLAT, NLON), ((1, 2), (2, 16)), -0.2, 0.2)), 0.05, 5.0),
        "send_index": draw_send_index(jax.random.fold_in(streams_of[6], 71), 0),
        "send_count": draw_send_count(jax.random.fold_in(streams_of[6], 71), 0),
    }


def solve_columns(values, coef_rows):
    levels = values.shape[1]
    diag = []
    for level in range(levels):
        term = jnp.ones_like(coef_rows[0])
        if level > 0:
            term = term + coef_rows[level - 1]
        if level < levels - 1:
            term = term + coef_rows[level]
        diag.append(term)
    upper = []
    reduced = []
    denom = diag[0]
    upper.append(-coef_rows[0] / denom)
    reduced.append(values[:, 0] / denom)
    for level in range(1, levels):
        denom = diag[level] + coef_rows[level - 1] * upper[level - 1]
        reduced.append((values[:, level] + coef_rows[level - 1] * reduced[level - 1]) / denom)
        if level < levels - 1:
            upper.append(-coef_rows[level] / denom)
    output = [None] * levels
    output[levels - 1] = reduced[levels - 1]
    for level in range(levels - 2, -1, -1):
        output[level] = reduced[level] - upper[level] * output[level + 1]
    return jnp.stack(output, axis=1)


def to_devices(field):
    lead = field.shape[0]
    shaped = field.reshape(lead, N_LAT, CLAT, N_LON, CLON)
    shaped = jnp.transpose(shaped, (0, 3, 1, 2, 4))
    return shaped.reshape(lead, N_LON * N_LAT, CLAT * CLON)


def reference(tracers, offsets, weights, diffusion, send_index, send_count):
    nlon_cells = tracers.shape[3]
    cell_index = jnp.arange(nlon_cells, dtype=jnp.int32)
    left_index = ((offsets + cell_index[None, None, :]) % nlon_cells).astype(jnp.int32)
    right_index = ((left_index + 1) % nlon_cells).astype(jnp.int32)
    full_shape = tracers.shape
    left_value = jnp.take_along_axis(tracers, jnp.broadcast_to(left_index[None], full_shape), axis=3)
    right_value = jnp.take_along_axis(tracers, jnp.broadcast_to(right_index[None], full_shape), axis=3)
    advected = (1.0 - weights)[None] * left_value + weights[None] * right_value
    by_device = to_devices(advected.reshape(NTR * LEV, NLAT, NLON))
    coef_device = to_devices(diffusion)

    def owner_columns(destination):
        offset_rank = jnp.arange(DEVICES, dtype=jnp.int32)
        sources = ((destination - offset_rank) % DEVICES).astype(jnp.int32)
        counts = send_count[sources, destination]
        seg_ends = jnp.cumsum(counts)
        places = jnp.arange(COLS_DEV, dtype=jnp.int32)
        passed = seg_ends[:, None] <= places[None, :]
        segment = jnp.sum(passed.astype(jnp.int32), axis=0).astype(jnp.int32)
        seg_start = jnp.sum(jnp.where(passed, counts[:, None], 0), axis=0).astype(jnp.int32)
        source = ((destination - segment) % DEVICES).astype(jnp.int32)
        column = send_index[source, destination, (places - seg_start).astype(jnp.int32)]
        return source, column.astype(jnp.int32)

    sources, columns = lax.map(owner_columns, jnp.arange(DEVICES, dtype=jnp.int32))
    gathered = by_device[:, sources, columns].reshape(NTR, LEV, DEVICES * COLS_DEV)
    gathered_diffusion = coef_device[:, sources, columns].reshape(LEV - 1, DEVICES * COLS_DEV)
    return solve_columns(gathered, gathered_diffusion)
```

```python
import functools

import jax
import jax.numpy as jnp
from jax import lax
from jax.experimental import pallas as pl
from jax.experimental.pallas import tpu as pltpu
from jax.sharding import PartitionSpec as P

HALO = 16
LANES = 128
SUB = 8
VMEM_LIMIT = 56 * 1024 * 1024


def take_lanes(block, index):
    return jnp.take_along_axis(block, index, axis=1, mode="promise_in_bounds")


def lane_ids(rows):
    return lax.broadcasted_iota(jnp.int32, (rows, LANES), 1)


def pack_halo_kernel(tracers, west_cells, east_cells):
    ntr, levels, lats, _ = tracers.shape
    per_row = LANES // HALO
    group = lane_ids(SUB) // HALO

    def one_level(level, carry):
        for tracer in range(ntr):
            west = jnp.zeros((SUB, LANES), jnp.float32)
            east = jnp.zeros((SUB, LANES), jnp.float32)
            for part in range(lats // SUB):
                cells = tracers[tracer, level, part * SUB : (part + 1) * SUB, :]
                shift = part * HALO
                rolled_west = pltpu.roll(cells, shift, 1) if shift else cells
                shift = (part * HALO + HALO) % LANES
                rolled_east = pltpu.roll(cells, shift, 1) if shift else cells
                west = jnp.where(group == part, rolled_west, west)
                east = jnp.where(group == part, rolled_east, east)
            west_cells[level, tracer] = west
            east_cells[level, tracer] = east
        return carry

    assert lats == SUB * per_row
    lax.fori_loop(0, levels, one_level, 0)


def pack_halo(tracers):
    ntr, levels, _, _ = tracers.shape
    shape = jax.ShapeDtypeStruct((levels, ntr, SUB, LANES), jnp.float32)
    return pl.pallas_call(
        pack_halo_kernel,
        out_shape=(shape, shape),
        in_specs=[pl.BlockSpec(memory_space=pltpu.VMEM)],
        out_specs=[pl.BlockSpec(memory_space=pltpu.VMEM)] * 2,
        compiler_params=pltpu.CompilerParams(vmem_limit_bytes=VMEM_LIMIT),
        name="pack_halo",
    )(tracers)


def merge_halo(west, east, halo, count):
    lane = lane_ids(SUB)
    cell = lane % (2 * HALO)
    for half in range(2):
        source = (half * 4 + lane // (2 * HALO)) * HALO + cell % HALO

        def one_value(value, carry, half=half, source=source):
            merged = jnp.where(cell < HALO, take_lanes(west[value], source), take_lanes(east[value], source))
            halo[value, half] = merged
            return carry

        lax.fori_loop(0, count, one_value, 0)


def advect_and_solve(tracers, offsets, weights, diffusion, halo, solved):
    ntr, levels, lats, _ = tracers.shape
    lane = lane_ids(SUB)

    def one_part(part, carry):
        rows = pl.ds(pl.multiple_of(part * SUB, SUB), SUB)
        half = part // 4
        base = (part % 4) * (2 * HALO)
        coefs = [diffusion[level, rows, :] for level in range(levels - 1)]
        upper = []
        reduced = [[] for _ in range(ntr)]
        for level in range(levels):
            left = lane + offsets[level, rows, :]
            right = left + 1
            weight = weights[level, rows, :]
            left_in = (left >= 0) & (left < LANES)
            right_in = (right >= 0) & (right < LANES)
            left_main = left & (LANES - 1)
            right_main = right & (LANES - 1)
            left_halo = base + ((left + HALO) & (2 * HALO - 1))
            right_halo = base + ((right + HALO) & (2 * HALO - 1))
            denom = 1.0
            if level > 0:
                denom = denom + coefs[level - 1]
            if level < levels - 1:
                denom = denom + coefs[level]
            if level > 0:
                denom = denom - coefs[level - 1] * upper[level - 1]
            inverse = 1.0 / denom
            if level < levels - 1:
                upper.append(coefs[level] * inverse)
            for tracer in range(ntr):
                cells = tracers[tracer, level, rows, :]
                edge = halo[level * ntr + tracer, half]
                left_value = jnp.where(left_in, take_lanes(cells, left_main), take_lanes(edge, left_halo))
                right_value = jnp.where(right_in, take_lanes(cells, right_main), take_lanes(edge, right_halo))
                value = (1.0 - weight) * left_value + weight * right_value
                if level > 0:
                    value = value + coefs[level - 1] * reduced[tracer][level - 1]
                reduced[tracer].append(value * inverse)
        for tracer in range(ntr):
            x = reduced[tracer][levels - 1]
            solved[(levels - 1) * ntr + tracer, rows, :] = x
            for level in range(levels - 2, -1, -1):
                x = reduced[tracer][level] + upper[level] * x
                solved[level * ntr + tracer, rows, :] = x
        return carry

    lax.fori_loop(0, lats // SUB, one_part, 0)


def build_table(solved, table):
    values, lats, _ = solved.shape
    upper_half = lax.broadcasted_iota(jnp.int32, (SUB, LANES), 0) < 4

    def one_row(row, carry):
        tiles = []
        for pair in range(values // 2):
            first = jnp.broadcast_to(solved[2 * pair, pl.ds(row, 1), :], (SUB, LANES))
            second = jnp.broadcast_to(solved[2 * pair + 1, pl.ds(row, 1), :], (SUB, LANES))
            tiles.append(jnp.where(upper_half, first, second))
        while len(tiles) < LANES // SUB:
            tiles.append(jnp.zeros((SUB, LANES), jnp.float32))
        block = jnp.concatenate(tiles, axis=0)
        table[pl.ds(pl.multiple_of(row * LANES, LANES), LANES), :] = block.T
        return carry

    lax.fori_loop(0, lats, one_row, 0)


def pick_rows(table, index, count, packed, sent):
    blocks, height, _ = sent.shape
    parts = index.shape[2] // LANES
    lists = 4 // parts
    stream = lax.broadcasted_iota(jnp.int32, (1, LANES), 1) % 4

    def one_block(block, carry):
        owners = [block * lists + item for item in range(lists)]
        rows = [(count[0, owner] + (parts - 1)) // parts for owner in owners]
        longest = functools.reduce(jnp.maximum, rows)
        places = [(owners[g // parts], (g % parts) * rows[g // parts]) for g in range(4)]

        def eight_rows(step, inner):
            start = pl.multiple_of(step * SUB, SUB)
            for line in range(SUB):
                picked = [
                    table[pl.ds(index[0, owner, place + start + line], 1), :] for owner, place in places
                ]
                low = jnp.where(stream == 0, picked[0], picked[1])
                high = jnp.where(stream == 2, picked[2], picked[3])
                packed[pl.ds(start + line, 1), :] = jnp.where(stream < 2, low, high)
            return inner

        lax.fori_loop(0, (longest + (SUB - 1)) // SUB, eight_rows, 0)
        sent[block] = packed[...].T[:height, :]
        return carry

    lax.fori_loop(0, blocks, one_block, 0)


def send_kernel(tracers, offsets, weights, diffusion, west, east, index, count, sent, halo, solved, table, packed):
    merge_halo(west, east, halo, solved.shape[0])
    advect_and_solve(tracers, offsets, weights, diffusion, halo, solved)
    build_table(solved, table)
    packed[...] = jnp.zeros_like(packed)
    pick_rows(table, index, count, packed, sent)


def make_sent(tracers, offsets, weights, diffusion, west, east, index, count):
    ntr, levels, lats, lons = tracers.shape
    values = ntr * levels
    lists, cap = index.shape[1:]
    blocks = lists * (cap // LANES) // 4
    vmem = pl.BlockSpec(memory_space=pltpu.VMEM)
    smem = pl.BlockSpec(memory_space=pltpu.SMEM)
    return pl.pallas_call(
        send_kernel,
        out_shape=jax.ShapeDtypeStruct((blocks, 4 * values, LANES), jnp.float32),
        in_specs=[vmem] * 6 + [smem] * 2,
        out_specs=vmem,
        scratch_shapes=[
            pltpu.VMEM((values, 2, SUB, LANES), jnp.float32),
            pltpu.VMEM((values, lats, LANES), jnp.float32),
            pltpu.VMEM((lats * lons, LANES), jnp.float32),
            pltpu.VMEM((LANES, LANES), jnp.float32),
        ],
        compiler_params=pltpu.CompilerParams(vmem_limit_bytes=VMEM_LIMIT),
        name="advect_solve_pick",
    )(
        tracers,
        offsets,
        weights,
        diffusion,
        west.reshape(values, SUB, LANES),
        east.reshape(values, SUB, LANES),
        index,
        count,
    )


def place_kernel(arrived, counts, own, owned, row):
    sources, height, _ = arrived.shape
    levels, ntr, columns = owned.shape
    values = levels * ntr
    parts = height // values
    lane = lane_ids(1)

    def one_source(turn, start):
        source = lax.rem(own[0] - turn + sources, sources)
        total = counts[source, own[0]]
        rows = (total + (parts - 1)) // parts
        for part in range(parts):
            place = start + jnp.minimum(part * rows, total)
            tile = place // LANES
            shift = place % LANES
            piece = arrived[source, pl.ds(part, values, stride=parts), :]
            rolled = pltpu.roll(piece, shift, 1)
            here = pl.ds(pl.multiple_of(tile * LANES, LANES), LANES)
            after = pl.ds(pl.multiple_of(tile * LANES + LANES, LANES), LANES)
            row[:, here] = jnp.where(lane >= shift, rolled, row[:, here])
            row[:, after] = rolled
        return start + total

    lax.fori_loop(0, sources, one_source, 0)
    for level in range(levels):
        owned[level] = row[level * ntr : (level + 1) * ntr, :columns]


def place_owned(arrived, counts, own, levels, ntr, columns):
    vmem = pl.BlockSpec(memory_space=pltpu.VMEM)
    smem = pl.BlockSpec(memory_space=pltpu.SMEM)
    return pl.pallas_call(
        place_kernel,
        out_shape=jax.ShapeDtypeStruct((levels, ntr, columns), jnp.float32),
        in_specs=[vmem, smem, smem],
        out_specs=vmem,
        scratch_shapes=[pltpu.VMEM((levels * ntr, columns + 2 * LANES), jnp.float32)],
        compiler_params=pltpu.CompilerParams(vmem_limit_bytes=VMEM_LIMIT),
        name="place_owned",
    )(arrived, counts, own)


def ring(axis, distance):
    size = lax.axis_size(axis)
    return [(i, (i + distance) % size) for i in range(size)]


def body(tracers, offsets, weights, diffusion, send_index, send_count):
    ntr, levels, lats, lons = tracers.shape
    columns = lats * lons
    lists, cap = send_index.shape[1:]
    parts = cap // LANES
    values = ntr * levels
    west_cells, east_cells = pack_halo(tracers)
    from_west = lax.ppermute(east_cells, "lon", ring("lon", 1))
    from_east = lax.ppermute(west_cells, "lon", ring("lon", -1))
    counts = lax.all_gather(send_count, ("lon", "lat"), axis=0, tiled=True)
    sent = make_sent(tracers, offsets, weights, diffusion, from_west, from_east, send_index, send_count)
    if parts < 4:
        sent = sent.reshape(-1, values, 4 // parts, parts, LANES)
        sent = jnp.transpose(sent, (0, 2, 1, 3, 4)).reshape(lists, values * parts, LANES)
    arrived = lax.all_to_all(sent, ("lon", "lat"), split_axis=0, concat_axis=0, tiled=True)
    own = lax.axis_index(("lon", "lat")).astype(jnp.int32).reshape(1)
    owned = place_owned(arrived, counts, own, levels, ntr, columns)
    return jnp.transpose(owned, (1, 0, 2))


def solution(mesh):
    return jax.shard_map(
        body,
        mesh=mesh,
        in_specs=(
            P(None, None, "lat", "lon"),
            P(None, "lat", "lon"),
            P(None, "lat", "lon"),
            P(None, "lat", "lon"),
            P(("lon", "lat"), None, None),
            P(("lon", "lat"), None),
        ),
        out_specs=P(None, None, ("lon", "lat")),
        check_vma=False,
    )
```

```python
import functools

import jax
import jax.numpy as jnp
from jax import lax
from jax.experimental import pallas as pl
from jax.experimental.pallas import tpu as pltpu
from jax.sharding import PartitionSpec as P

HALO = 16
LANES = 128
SUB = 8
SLOT = 32
MIB = 1024 * 1024


def take_lanes(block, index):
    return jnp.take_along_axis(block, index, axis=1, mode="promise_in_bounds")


def lane_ids(rows):
    return lax.broadcasted_iota(jnp.int32, (rows, LANES), 1)


def pack_halo_kernel(tracers, west_cells, east_cells):
    ntr, levels, lats, _ = tracers.shape
    per_row = LANES // HALO
    group = lane_ids(SUB) // HALO

    def one_level(level, carry):
        for tracer in range(ntr):
            west = jnp.zeros((SUB, LANES), jnp.float32)
            east = jnp.zeros((SUB, LANES), jnp.float32)
            for part in range(lats // SUB):
                cells = tracers[tracer, level, part * SUB : (part + 1) * SUB, :]
                shift = part * HALO
                rolled_west = pltpu.roll(cells, shift, 1) if shift else cells
                shift = (part * HALO + HALO) % LANES
                rolled_east = pltpu.roll(cells, shift, 1) if shift else cells
                west = jnp.where(group == part, rolled_west, west)
                east = jnp.where(group == part, rolled_east, east)
            west_cells[level, tracer] = west
            east_cells[level, tracer] = east
        return carry

    assert lats == SUB * per_row
    lax.fori_loop(0, levels, one_level, 0)


def pack_halo(tracers):
    ntr, levels, _, _ = tracers.shape
    shape = jax.ShapeDtypeStruct((levels, ntr, SUB, LANES), jnp.float32)
    return pl.pallas_call(
        pack_halo_kernel,
        out_shape=(shape, shape),
        in_specs=[pl.BlockSpec(memory_space=pltpu.VMEM)],
        out_specs=[pl.BlockSpec(memory_space=pltpu.VMEM)] * 2,
        compiler_params=pltpu.CompilerParams(vmem_limit_bytes=16 * MIB),
        name="pack_halo",
    )(tracers)


def merge_halo(west, east, halo, count):
    lane = lane_ids(SUB)
    cell = lane % (2 * HALO)
    for half in range(2):
        source = (half * 4 + lane // (2 * HALO)) * HALO + cell % HALO

        def one_value(value, carry, half=half, source=source):
            merged = jnp.where(cell < HALO, take_lanes(west[value], source), take_lanes(east[value], source))
            halo[value, half] = merged
            return carry

        lax.fori_loop(0, count, one_value, 0)


def advect_and_solve(tracers, offsets, weights, diffusion, halo, solved):
    ntr, levels, lats, _ = tracers.shape
    lane = lane_ids(SUB)

    def one_part(part, carry):
        rows = pl.ds(pl.multiple_of(part * SUB, SUB), SUB)
        half = part // 4
        base = (part % 4) * (2 * HALO)
        coefs = [diffusion[level, rows, :] for level in range(levels - 1)]
        upper = []
        reduced = [[] for _ in range(ntr)]
        for level in range(levels):
            left = lane + offsets[level, rows, :]
            right = left + 1
            weight = weights[level, rows, :]
            left_in = (left >= 0) & (left < LANES)
            right_in = (right >= 0) & (right < LANES)
            left_main = left & (LANES - 1)
            right_main = right & (LANES - 1)
            left_halo = base + ((left + HALO) & (2 * HALO - 1))
            right_halo = base + ((right + HALO) & (2 * HALO - 1))
            denom = 1.0
            if level > 0:
                denom = denom + coefs[level - 1]
            if level < levels - 1:
                denom = denom + coefs[level]
            if level > 0:
                denom = denom - coefs[level - 1] * upper[level - 1]
            inverse = 1.0 / denom
            if level < levels - 1:
                upper.append(coefs[level] * inverse)
            for tracer in range(ntr):
                cells = tracers[tracer, level, rows, :]
                edge = halo[level * ntr + tracer, half]
                left_value = jnp.where(left_in, take_lanes(cells, left_main), take_lanes(edge, left_halo))
                right_value = jnp.where(right_in, take_lanes(cells, right_main), take_lanes(edge, right_halo))
                value = (1.0 - weight) * left_value + weight * right_value
                if level > 0:
                    value = value + coefs[level - 1] * reduced[tracer][level - 1]
                reduced[tracer].append(value * inverse)
        for tracer in range(ntr):
            x = reduced[tracer][levels - 1]
            for level in range(levels - 1, -1, -1):
                if level < levels - 1:
                    x = reduced[tracer][level] + upper[level] * x
                solved[pl.ds(part * SUB * SLOT + level * ntr + tracer, SUB, stride=SLOT), :] = x
        return carry

    lax.fori_loop(0, lats // SUB, one_part, 0)


def build_table(solved, table):
    rows_per = LANES // SLOT
    spread = lane_ids(LANES) // 4

    def four_rows(step, carry):
        block = solved[pl.ds(pl.multiple_of(step * LANES, LANES), LANES), :].T
        for item in range(rows_per):
            start = pl.multiple_of((step * rows_per + item) * LANES, LANES)
            table[pl.ds(start, LANES), :] = take_lanes(block, spread + item * SLOT)
        return carry

    lax.fori_loop(0, solved.shape[0] // LANES, four_rows, 0)


def pick_rows(table, index, count, packed, sent):
    blocks, height, _ = sent.shape
    parts = index.shape[2] // LANES
    lists = 4 // parts
    stream = lax.broadcasted_iota(jnp.int32, (1, LANES), 1) % 4

    def one_block(block, carry):
        owners = [block * lists + item for item in range(lists)]
        rows = [(count[0, owner] + (parts - 1)) // parts for owner in owners]
        longest = functools.reduce(jnp.maximum, rows)
        places = [(owners[g // parts], (g % parts) * rows[g // parts]) for g in range(4)]

        def eight_rows(step, inner):
            start = pl.multiple_of(step * SUB, SUB)
            for line in range(SUB):
                picked = [
                    table[index[0, owner, place + start + line]] for owner, place in places
                ]
                low = jnp.where(stream == 0, picked[0], picked[1])
                high = jnp.where(stream == 2, picked[2], picked[3])
                packed[pl.ds(start + line, 1), :] = jnp.where(stream < 2, low, high)
            return inner

        lax.fori_loop(0, (longest + (SUB - 1)) // SUB, eight_rows, 0)
        sent[block] = packed[...].T[:height, :]
        return carry

    lax.fori_loop(0, blocks, one_block, 0)


def solve_kernel(tracers, offsets, weights, diffusion, west, east, table, halo, solved):
    values = west.shape[0]
    merge_halo(west, east, halo, values)
    for value in range(values, SLOT):
        solved[pl.ds(value, tracers.shape[2], stride=SLOT), :] = jnp.zeros((tracers.shape[2], LANES), jnp.float32)
    advect_and_solve(tracers, offsets, weights, diffusion, halo, solved)
    build_table(solved, table)


def make_table(tracers, offsets, weights, diffusion, west, east):
    ntr, levels, lats, lons = tracers.shape
    values = ntr * levels
    vmem = pl.BlockSpec(memory_space=pltpu.VMEM)
    return pl.pallas_call(
        solve_kernel,
        out_shape=jax.ShapeDtypeStruct((lats * lons, LANES), jnp.float32),
        in_specs=[vmem] * 6,
        out_specs=vmem,
        scratch_shapes=[
            pltpu.VMEM((values, 2, SUB, LANES), jnp.float32),
            pltpu.VMEM((lats * SLOT, LANES), jnp.float32),
        ],
        compiler_params=pltpu.CompilerParams(vmem_limit_bytes=16 * MIB),
        name="advect_solve",
    )(
        tracers,
        offsets,
        weights,
        diffusion,
        west.reshape(values, SUB, LANES),
        east.reshape(values, SUB, LANES),
    )


def pick_kernel(table, index, count, sent, packed):
    packed[...] = jnp.zeros_like(packed)
    pick_rows(table, index, count, packed, sent)


def pick_columns(table, index, count, values):
    lists, cap = index.shape[1:]
    blocks = lists * (cap // LANES) // 4
    vmem = pl.BlockSpec(memory_space=pltpu.VMEM)
    smem = pl.BlockSpec(memory_space=pltpu.SMEM)
    return pl.pallas_call(
        pick_kernel,
        out_shape=jax.ShapeDtypeStruct((blocks, 4 * values, LANES), jnp.float32),
        in_specs=[vmem, smem, smem],
        out_specs=vmem,
        scratch_shapes=[pltpu.VMEM((LANES, LANES), jnp.float32)],
        compiler_params=pltpu.CompilerParams(vmem_limit_bytes=16 * MIB),
        name="pick_columns",
    )(table.reshape(-1, 1, LANES), index, count)


def place_kernel(arrived, counts, own, owned, held, row, ready):
    sources, height, _ = arrived.shape
    levels, ntr, columns = owned.shape
    values = levels * ntr
    parts = height // values
    lane = lane_ids(1)

    def fetch(turn):
        source = lax.rem(own[0] - turn + sources, sources)
        return pltpu.make_async_copy(arrived.at[source], held.at[turn], ready.at[turn])

    def start_fetch(turn, carry):
        fetch(turn).start()
        return carry

    def one_source(turn, start):
        fetch(turn).wait()
        total = counts[0, lax.rem(own[0] - turn + sources, sources)]
        rows = (total + (parts - 1)) // parts
        for part in range(parts):
            place = start + jnp.minimum(part * rows, total)
            tile = place // LANES
            shift = place % LANES
            piece = held[turn, pl.ds(part, values, stride=parts), :]
            rolled = pltpu.roll(piece, shift, 1)
            here = pl.ds(pl.multiple_of(tile * LANES, LANES), LANES)
            after = pl.ds(pl.multiple_of(tile * LANES + LANES, LANES), LANES)
            row[:, here] = jnp.where(lane >= shift, rolled, row[:, here])
            row[:, after] = rolled
        return start + total

    lax.fori_loop(0, sources, start_fetch, 0)
    lax.fori_loop(0, sources, one_source, 0)
    for level in range(levels):
        owned[level] = row[level * ntr : (level + 1) * ntr, :columns]


def place_owned(arrived, counts, own, levels, ntr, columns):
    sources = arrived.shape[0]
    vmem = pl.BlockSpec(memory_space=pltpu.VMEM)
    smem = pl.BlockSpec(memory_space=pltpu.SMEM)
    return pl.pallas_call(
        place_kernel,
        out_shape=jax.ShapeDtypeStruct((levels, ntr, columns), jnp.float32),
        in_specs=[pl.BlockSpec(memory_space=pl.ANY), smem, smem],
        out_specs=vmem,
        scratch_shapes=[
            pltpu.VMEM(arrived.shape, jnp.float32),
            pltpu.VMEM((levels * ntr, columns + 2 * LANES), jnp.float32),
            pltpu.SemaphoreType.DMA((sources,)),
        ],
        compiler_params=pltpu.CompilerParams(vmem_limit_bytes=16 * MIB),
        name="place_owned",
    )(arrived, counts, own)


def ring(axis, distance):
    size = lax.axis_size(axis)
    return [(i, (i + distance) % size) for i in range(size)]


def body(tracers, offsets, weights, diffusion, send_index, send_count):
    ntr, levels, lats, lons = tracers.shape
    columns = lats * lons
    lists, cap = send_index.shape[1:]
    parts = cap // LANES
    values = ntr * levels
    west_cells, east_cells = pack_halo(tracers)
    from_west = lax.ppermute(east_cells, "lon", ring("lon", 1))
    from_east = lax.ppermute(west_cells, "lon", ring("lon", -1))
    counts = lax.all_to_all(send_count, ("lon", "lat"), split_axis=1, concat_axis=1, tiled=True)
    table = make_table(tracers, offsets, weights, diffusion, from_west, from_east)
    sent = pick_columns(table, send_index, send_count, values)
    if parts < 4:
        sent = sent.reshape(-1, values, 4 // parts, parts, LANES)
        sent = jnp.transpose(sent, (0, 2, 1, 3, 4)).reshape(lists, values * parts, LANES)
    arrived = lax.all_to_all(sent, ("lon", "lat"), split_axis=0, concat_axis=0, tiled=True)
    own = lax.axis_index(("lon", "lat")).astype(jnp.int32).reshape(1)
    owned = place_owned(arrived, counts, own, levels, ntr, columns)
    return jnp.transpose(owned, (1, 0, 2))


def solution(mesh):
    return jax.shard_map(
        body,
        mesh=mesh,
        in_specs=(
            P(None, None, "lat", "lon"),
            P(None, "lat", "lon"),
            P(None, "lat", "lon"),
            P(None, "lat", "lon"),
            P(("lon", "lat"), None, None),
            P(("lon", "lat"), None),
        ),
        out_specs=P(None, None, ("lon", "lat")),
        check_vma=False,
    )
```

```python
import functools

import jax
import jax.numpy as jnp
from jax import lax
from jax.experimental import pallas as pl
from jax.experimental.pallas import tpu as pltpu
from jax.sharding import PartitionSpec as P

HALO = 16
LANES = 128
SUB = 8
SLOT = 32
LINES = 16
MIB = 1024 * 1024


def take_lanes(block, index):
    return jnp.take_along_axis(block, index, axis=1, mode="promise_in_bounds")


def lane_ids(rows):
    return lax.broadcasted_iota(jnp.int32, (rows, LANES), 1)


def pack_halo_kernel(tracers, west_cells, east_cells):
    ntr, levels, lats, _ = tracers.shape
    per_row = LANES // HALO
    group = lane_ids(SUB) // HALO

    def one_level(level, carry):
        for tracer in range(ntr):
            west = jnp.zeros((SUB, LANES), jnp.float32)
            east = jnp.zeros((SUB, LANES), jnp.float32)
            for part in range(lats // SUB):
                cells = tracers[tracer, level, part * SUB : (part + 1) * SUB, :]
                shift = part * HALO
                rolled_west = pltpu.roll(cells, shift, 1) if shift else cells
                shift = (part * HALO + HALO) % LANES
                rolled_east = pltpu.roll(cells, shift, 1) if shift else cells
                west = jnp.where(group == part, rolled_west, west)
                east = jnp.where(group == part, rolled_east, east)
            west_cells[level, tracer] = west
            east_cells[level, tracer] = east
        return carry

    assert lats == SUB * per_row
    lax.fori_loop(0, levels, one_level, 0)


def pack_halo(tracers):
    ntr, levels, _, _ = tracers.shape
    shape = jax.ShapeDtypeStruct((levels, ntr, SUB, LANES), jnp.float32)
    return pl.pallas_call(
        pack_halo_kernel,
        out_shape=(shape, shape),
        in_specs=[pl.BlockSpec(memory_space=pltpu.VMEM)],
        out_specs=[pl.BlockSpec(memory_space=pltpu.VMEM)] * 2,
        compiler_params=pltpu.CompilerParams(vmem_limit_bytes=16 * MIB),
        name="pack_halo",
    )(tracers)


def merge_halo(west, east, halo, count):
    lane = lane_ids(SUB)
    cell = lane % (2 * HALO)
    sources = [(half * 4 + lane // (2 * HALO)) * HALO + cell % HALO for half in range(2)]
    chunk = 5 if count % 5 == 0 else 1

    def some_values(step, carry):
        merged = []
        for item in range(chunk):
            value = step * chunk + item
            for half in range(2):
                both = take_lanes(west[value], sources[half]), take_lanes(east[value], sources[half])
                merged.append((value, half, jnp.where(cell < HALO, *both)))
        for value, half, cells in merged:
            halo[value, half] = cells
        return carry

    lax.fori_loop(0, count // chunk, some_values, 0)


def advect_and_solve(tracers, offsets, weights, diffusion, halo, solved):
    ntr, levels, lats, _ = tracers.shape
    lane = lane_ids(SUB)

    def one_part(part, carry):
        rows = pl.ds(pl.multiple_of(part * SUB, SUB), SUB)
        half = part // 4
        base = (part % 4) * (2 * HALO)
        coefs = [diffusion[level, rows, :] for level in range(levels - 1)]
        upper = []
        reduced = [[] for _ in range(ntr)]
        for level in range(levels):
            left = lane + offsets[level, rows, :]
            right = left + 1
            weight = weights[level, rows, :]
            left_in = (left >= 0) & (left < LANES)
            right_in = (right >= 0) & (right < LANES)
            left_main = left & (LANES - 1)
            right_main = right & (LANES - 1)
            left_halo = base + ((left + HALO) & (2 * HALO - 1))
            right_halo = base + ((right + HALO) & (2 * HALO - 1))
            denom = 1.0
            if level > 0:
                denom = denom + coefs[level - 1]
            if level < levels - 1:
                denom = denom + coefs[level]
            if level > 0:
                denom = denom - coefs[level - 1] * upper[level - 1]
            inverse = 1.0 / denom
            if level < levels - 1:
                upper.append(coefs[level] * inverse)
            for tracer in range(ntr):
                cells = tracers[tracer, level, rows, :]
                edge = halo[level * ntr + tracer, half]
                left_value = jnp.where(left_in, take_lanes(cells, left_main), take_lanes(edge, left_halo))
                right_value = jnp.where(right_in, take_lanes(cells, right_main), take_lanes(edge, right_halo))
                value = (1.0 - weight) * left_value + weight * right_value
                if level > 0:
                    value = value + coefs[level - 1] * reduced[tracer][level - 1]
                reduced[tracer].append(value * inverse)
        for tracer in range(ntr):
            x = reduced[tracer][levels - 1]
            for level in range(levels - 1, -1, -1):
                if level < levels - 1:
                    x = reduced[tracer][level] + upper[level] * x
                solved[pl.ds(part * SUB * SLOT + level * ntr + tracer, SUB, stride=SLOT), :] = x
        return carry

    lax.fori_loop(0, lats // SUB, one_part, 0)


def build_table(solved, table):
    rows_per = LANES // SLOT
    spread = lane_ids(LANES) // 4
    together = 2

    def some_rows(step, carry):
        blocks = []
        for item in range(together):
            start = pl.multiple_of((step * together + item) * LANES, LANES)
            blocks.append(solved[pl.ds(start, LANES), :].T)
        for item, block in enumerate(blocks):
            for row in range(rows_per):
                start = pl.multiple_of(((step * together + item) * rows_per + row) * LANES, LANES)
                table[pl.ds(start, LANES), :] = take_lanes(block, spread + row * SLOT)
        return carry

    lax.fori_loop(0, solved.shape[0] // (LANES * together), some_rows, 0)


def pick_rows(table, index, count, packed, sent):
    blocks, height, _ = sent.shape
    parts = index.shape[2] // LANES
    lists = 4 // parts
    stream = lax.broadcasted_iota(jnp.int32, (1, LANES), 1) % 4
    together = 2 if blocks % 2 == 0 else 1

    def one_block(block, carry):
        owners = [block * lists + item for item in range(lists)]
        rows = [lax.div(count[0, owner] + (parts - 1), parts) for owner in owners]
        longest = functools.reduce(jnp.maximum, rows)
        places = [(owners[g // parts], (g % parts) * rows[g // parts]) for g in range(4)]

        def some_lines(step, inner):
            start = pl.multiple_of(step * LINES, LINES)
            lines = []
            for line in range(LINES):
                picked = [table[index[0, owner, place + start + line]] for owner, place in places]
                low = jnp.where(stream == 0, picked[0], picked[1])
                high = jnp.where(stream == 2, picked[2], picked[3])
                lines.append(jnp.where(stream < 2, low, high))
            first = pl.multiple_of(block * LANES + start, LINES)
            for line in range(LINES):
                packed[pl.ds(first + line, 1), :] = lines[line]
            return inner

        lax.fori_loop(0, lax.div(longest + (LINES - 1), LINES), some_lines, 0)
        return carry

    def turn_blocks(step, carry):
        turned = []
        for item in range(together):
            start = pl.multiple_of((step * together + item) * LANES, LANES)
            turned.append(packed[pl.ds(start, LANES), :].T)
        for item in range(together):
            sent[step * together + item] = turned[item][:height, :]
        return carry

    lax.fori_loop(0, blocks, one_block, 0)
    lax.fori_loop(0, blocks // together, turn_blocks, 0)


def solve_kernel(tracers, offsets, weights, diffusion, west, east, table, halo, solved):
    values = west.shape[0]
    merge_halo(west, east, halo, values)
    for value in range(values, SLOT):
        solved[pl.ds(value, tracers.shape[2], stride=SLOT), :] = jnp.zeros((tracers.shape[2], LANES), jnp.float32)
    advect_and_solve(tracers, offsets, weights, diffusion, halo, solved)
    build_table(solved, table)


def make_table(tracers, offsets, weights, diffusion, west, east):
    ntr, levels, lats, lons = tracers.shape
    values = ntr * levels
    vmem = pl.BlockSpec(memory_space=pltpu.VMEM)
    return pl.pallas_call(
        solve_kernel,
        out_shape=jax.ShapeDtypeStruct((lats * lons, LANES), jnp.float32),
        in_specs=[vmem] * 6,
        out_specs=vmem,
        scratch_shapes=[
            pltpu.VMEM((values, 2, SUB, LANES), jnp.float32),
            pltpu.VMEM((lats * SLOT, LANES), jnp.float32),
        ],
        compiler_params=pltpu.CompilerParams(vmem_limit_bytes=16 * MIB),
        name="advect_solve",
    )(
        tracers,
        offsets,
        weights,
        diffusion,
        west.reshape(values, SUB, LANES),
        east.reshape(values, SUB, LANES),
    )


def pick_kernel(table, index, count, sent, packed):
    pick_rows(table, index, count, packed, sent)


def pick_columns(table, index, count, values):
    lists, cap = index.shape[1:]
    blocks = lists * (cap // LANES) // 4
    vmem = pl.BlockSpec(memory_space=pltpu.VMEM)
    smem = pl.BlockSpec(memory_space=pltpu.SMEM)
    return pl.pallas_call(
        pick_kernel,
        out_shape=jax.ShapeDtypeStruct((blocks, 4 * values, LANES), jnp.float32),
        in_specs=[vmem, smem, smem],
        out_specs=vmem,
        scratch_shapes=[pltpu.VMEM((blocks * LANES, LANES), jnp.float32)],
        compiler_params=pltpu.CompilerParams(vmem_limit_bytes=16 * MIB),
        name="pick_columns",
    )(table.reshape(-1, 1, LANES), index, count)


def place_kernel(arrived, counts, own, owned, row):
    sources, height, _ = arrived.shape
    levels, ntr, columns = owned.shape
    values = levels * ntr
    parts = height // values
    lane = lax.broadcasted_iota(jnp.int32, (values, LANES), 1)
    together = 2 if sources % 2 == 0 else 1

    def some_sources(step, start):
        pieces = []
        for item in range(together):
            source = lax.rem(own[0] - (step * together + item) + sources, sources)
            total = counts[0, source]
            rows = lax.div(total + (parts - 1), parts)
            for part in range(parts):
                place = start + jnp.minimum(part * rows, total)
                shift = lax.rem(place, LANES)
                piece = arrived[source, pl.ds(part, values, stride=parts), :]
                pieces.append((place - shift, shift, pltpu.roll(piece, shift, 1)))
            start = start + total
        for tile, shift, rolled in pieces:
            here = pl.ds(pl.multiple_of(tile, LANES), LANES)
            after = pl.ds(pl.multiple_of(tile + LANES, LANES), LANES)
            pltpu.store(row.at[:, here], rolled, mask=lane >= shift)
            row[:, after] = rolled
        return start

    lax.fori_loop(0, sources // together, some_sources, 0)
    for level in range(levels):
        owned[level] = row[level * ntr : (level + 1) * ntr, :columns]


def place_owned(arrived, counts, own, levels, ntr, columns):
    vmem = pl.BlockSpec(memory_space=pltpu.VMEM)
    smem = pl.BlockSpec(memory_space=pltpu.SMEM)
    return pl.pallas_call(
        place_kernel,
        out_shape=jax.ShapeDtypeStruct((levels, ntr, columns), jnp.float32),
        in_specs=[vmem, smem, smem],
        out_specs=vmem,
        scratch_shapes=[pltpu.VMEM((levels * ntr, columns + 2 * LANES), jnp.float32)],
        compiler_params=pltpu.CompilerParams(vmem_limit_bytes=16 * MIB),
        name="place_owned",
    )(arrived, counts, own)


def ring(axis, distance):
    size = lax.axis_size(axis)
    return [(i, (i + distance) % size) for i in range(size)]


def body(tracers, offsets, weights, diffusion, send_index, send_count):
    ntr, levels, lats, lons = tracers.shape
    columns = lats * lons
    lists, cap = send_index.shape[1:]
    parts = cap // LANES
    values = ntr * levels
    west_cells, east_cells = pack_halo(tracers)
    from_west = lax.ppermute(east_cells, "lon", ring("lon", 1))
    from_east = lax.ppermute(west_cells, "lon", ring("lon", -1))
    counts = lax.all_to_all(send_count, ("lon", "lat"), split_axis=1, concat_axis=1, tiled=True)
    table = make_table(tracers, offsets, weights, diffusion, from_west, from_east)
    sent = pick_columns(table, send_index, send_count, values)
    if parts < 4:
        sent = sent.reshape(-1, values, 4 // parts, parts, LANES)
        sent = jnp.transpose(sent, (0, 2, 1, 3, 4)).reshape(lists, values * parts, LANES)
    arrived = lax.all_to_all(sent, ("lon", "lat"), split_axis=0, concat_axis=0, tiled=True)
    own = lax.axis_index(("lon", "lat")).astype(jnp.int32).reshape(1)
    owned = place_owned(arrived, counts, own, levels, ntr, columns)
    return jnp.transpose(owned, (1, 0, 2))


def solution(mesh):
    return jax.shard_map(
        body,
        mesh=mesh,
        in_specs=(
            P(None, None, "lat", "lon"),
            P(None, "lat", "lon"),
            P(None, "lat", "lon"),
            P(None, "lat", "lon"),
            P(("lon", "lat"), None, None),
            P(("lon", "lat"), None),
        ),
        out_specs=P(None, None, ("lon", "lat")),
        check_vma=False,
    )
```

```python
import functools

import jax
import jax.numpy as jnp
from jax import lax
from jax.experimental import pallas as pl
from jax.experimental.pallas import tpu as pltpu
from jax.sharding import PartitionSpec as P

HALO = 16
LANES = 128
SUB = 8
SLOT = 32
LINES = 16
MIB = 1024 * 1024


def take_lanes(block, index):
    return jnp.take_along_axis(block, index, axis=1, mode="promise_in_bounds")


def lane_ids(rows):
    return lax.broadcasted_iota(jnp.int32, (rows, LANES), 1)


def pack_halo_kernel(tracers, west_cells, east_cells):
    ntr, levels, lats, _ = tracers.shape
    per_row = LANES // HALO
    group = lane_ids(SUB) // HALO

    def one_level(level, carry):
        for tracer in range(ntr):
            west = jnp.zeros((SUB, LANES), jnp.float32)
            east = jnp.zeros((SUB, LANES), jnp.float32)
            for part in range(lats // SUB):
                cells = tracers[tracer, level, part * SUB : (part + 1) * SUB, :]
                shift = part * HALO
                rolled_west = pltpu.roll(cells, shift, 1) if shift else cells
                shift = (part * HALO + HALO) % LANES
                rolled_east = pltpu.roll(cells, shift, 1) if shift else cells
                west = jnp.where(group == part, rolled_west, west)
                east = jnp.where(group == part, rolled_east, east)
            west_cells[level, tracer] = west
            east_cells[level, tracer] = east
        return carry

    assert lats == SUB * per_row
    lax.fori_loop(0, levels, one_level, 0)


def pack_halo(tracers):
    ntr, levels, _, _ = tracers.shape
    shape = jax.ShapeDtypeStruct((levels, ntr, SUB, LANES), jnp.float32)
    return pl.pallas_call(
        pack_halo_kernel,
        out_shape=(shape, shape),
        in_specs=[pl.BlockSpec(memory_space=pltpu.VMEM)],
        out_specs=[pl.BlockSpec(memory_space=pltpu.VMEM)] * 2,
        compiler_params=pltpu.CompilerParams(vmem_limit_bytes=16 * MIB),
        name="pack_halo",
    )(tracers)


def merge_halo(west, east, halo, count):
    lane = lane_ids(SUB)
    cell = lane % (2 * HALO)
    sources = [(half * 4 + lane // (2 * HALO)) * HALO + cell % HALO for half in range(2)]
    chunk = 5 if count % 5 == 0 else 1

    def some_values(step, carry):
        merged = []
        for item in range(chunk):
            value = step * chunk + item
            for half in range(2):
                both = take_lanes(west[value], sources[half]), take_lanes(east[value], sources[half])
                merged.append((value, half, jnp.where(cell < HALO, *both)))
        for value, half, cells in merged:
            halo[value, half] = cells
        return carry

    lax.fori_loop(0, count // chunk, some_values, 0)


def advect_and_solve(tracers, offsets, weights, diffusion, halo, solved):
    ntr, levels, lats, _ = tracers.shape
    lane = lane_ids(SUB)

    def one_part(part, carry):
        rows = pl.ds(pl.multiple_of(part * SUB, SUB), SUB)
        half = part // 4
        base = (part % 4) * (2 * HALO)
        coefs = [diffusion[level, rows, :] for level in range(levels - 1)]
        upper = []
        reduced = [[] for _ in range(ntr)]
        for level in range(levels):
            left = lane + offsets[level, rows, :]
            right = left + 1
            weight = weights[level, rows, :]
            left_in = (left >= 0) & (left < LANES)
            right_in = (right >= 0) & (right < LANES)
            left_main = left & (LANES - 1)
            right_main = right & (LANES - 1)
            left_halo = base + ((left + HALO) & (2 * HALO - 1))
            right_halo = base + ((right + HALO) & (2 * HALO - 1))
            denom = 1.0
            if level > 0:
                denom = denom + coefs[level - 1]
            if level < levels - 1:
                denom = denom + coefs[level]
            if level > 0:
                denom = denom - coefs[level - 1] * upper[level - 1]
            inverse = 1.0 / denom
            if level < levels - 1:
                upper.append(coefs[level] * inverse)
            for tracer in range(ntr):
                cells = tracers[tracer, level, rows, :]
                edge = halo[level * ntr + tracer, half]
                left_value = jnp.where(left_in, take_lanes(cells, left_main), take_lanes(edge, left_halo))
                right_value = jnp.where(right_in, take_lanes(cells, right_main), take_lanes(edge, right_halo))
                value = (1.0 - weight) * left_value + weight * right_value
                if level > 0:
                    value = value + coefs[level - 1] * reduced[tracer][level - 1]
                reduced[tracer].append(value * inverse)
        for tracer in range(ntr):
            x = reduced[tracer][levels - 1]
            for level in range(levels - 1, -1, -1):
                if level < levels - 1:
                    x = reduced[tracer][level] + upper[level] * x
                solved[pl.ds(part * SUB * SLOT + level * ntr + tracer, SUB, stride=SLOT), :] = x
        return carry

    lax.fori_loop(0, lats // SUB, one_part, 0)


def build_table(solved, table):
    rows_per = LANES // SLOT
    spread = lane_ids(LANES) // 4
    together = 2

    def some_rows(step, carry):
        blocks = []
        for item in range(together):
            start = pl.multiple_of((step * together + item) * LANES, LANES)
            blocks.append(solved[pl.ds(start, LANES), :].T)
        for item, block in enumerate(blocks):
            for row in range(rows_per):
                start = pl.multiple_of(((step * together + item) * rows_per + row) * LANES, LANES)
                table[pl.ds(start, LANES), :] = take_lanes(block, spread + row * SLOT)
        return carry

    lax.fori_loop(0, solved.shape[0] // (LANES * together), some_rows, 0)


def pick_rows(table, index, count, packed, sent, wait_list):
    blocks, height, _ = sent.shape
    parts = index.shape[1] // LANES
    lists = 4 // parts
    stream = lax.broadcasted_iota(jnp.int32, (1, LANES), 1) % 4
    together = 2 if blocks % 2 == 0 else 1

    def one_block(block, carry):
        owners = [block * lists + item for item in range(lists)]
        rows = [lax.div(count[0, owner] + (parts - 1), parts) for owner in owners]
        for owner in owners:
            wait_list(owner)
        longest = functools.reduce(jnp.maximum, rows)
        places = [(owners[g // parts], (g % parts) * rows[g // parts]) for g in range(4)]

        def some_lines(step, inner):
            start = pl.multiple_of(step * LINES, LINES)
            lines = []
            for line in range(LINES):
                picked = [table[index[owner, place + start + line]] for owner, place in places]
                low = jnp.where(stream == 0, picked[0], picked[1])
                high = jnp.where(stream == 2, picked[2], picked[3])
                lines.append(jnp.where(stream < 2, low, high))
            first = pl.multiple_of(block * LANES + start, LINES)
            for line in range(LINES):
                packed[pl.ds(first + line, 1), :] = lines[line]
            return inner

        lax.fori_loop(0, lax.div(longest + (LINES - 1), LINES), some_lines, 0)
        return carry

    def turn_blocks(step, carry):
        turned = []
        for item in range(together):
            start = pl.multiple_of((step * together + item) * LANES, LANES)
            turned.append(packed[pl.ds(start, LANES), :].T)
        for item in range(together):
            sent[step * together + item] = turned[item][:height, :]
        return carry

    lax.fori_loop(0, blocks, one_block, 0)
    lax.fori_loop(0, blocks // together, turn_blocks, 0)


def send_kernel(
    tracers_in, offsets_in, weights_in, diffusion_in, west_in, east_in, index_in, count, sent,
    tracers, offsets, weights, diffusion, west, east, halo, solved, table, packed, index, ready, listed,
):
    lists = index_in.shape[1]

    def list_copy(item):
        return pltpu.make_async_copy(index_in.at[0, item], index.at[item], listed.at[item])

    def start_list(item, carry):
        list_copy(item).start()
        return carry

    sources = (west_in, east_in, offsets_in, weights_in, diffusion_in, tracers_in)
    targets = (west, east, offsets, weights, diffusion, tracers)
    copies = [
        pltpu.make_async_copy(source, target, ready.at[item])
        for item, (source, target) in enumerate(zip(sources, targets))
    ]
    for copy in copies:
        copy.start()
    lax.fori_loop(0, lists, start_list, 0)
    copies[0].wait()
    copies[1].wait()
    merge_halo(west, east, halo, west.shape[0])
    for value in range(west.shape[0], SLOT):
        solved[pl.ds(value, tracers.shape[2], stride=SLOT), :] = jnp.zeros((tracers.shape[2], LANES), jnp.float32)
    for copy in copies[2:]:
        copy.wait()
    advect_and_solve(tracers, offsets, weights, diffusion, halo, solved)
    build_table(solved, table.reshape(table.shape[0], LANES))
    pick_rows(table, index, count, packed, sent, lambda item: list_copy(item).wait())


def make_sent(tracers, offsets, weights, diffusion, west, east, index, count):
    ntr, levels, lats, lons = tracers.shape
    values = ntr * levels
    lists, cap = index.shape[1:]
    blocks = lists * (cap // LANES) // 4
    hbm = pl.BlockSpec(memory_space=pl.ANY)
    smem = pl.BlockSpec(memory_space=pltpu.SMEM)
    west = west.reshape(values, SUB, LANES)
    east = east.reshape(values, SUB, LANES)
    inputs = (tracers, offsets, weights, diffusion, west, east)
    return pl.pallas_call(
        send_kernel,
        out_shape=jax.ShapeDtypeStruct((blocks, 4 * values, LANES), jnp.float32),
        in_specs=[hbm] * 7 + [smem],
        out_specs=pl.BlockSpec(memory_space=pltpu.VMEM),
        scratch_shapes=[pltpu.VMEM(array.shape, array.dtype) for array in inputs]
        + [
            pltpu.VMEM((values, 2, SUB, LANES), jnp.float32),
            pltpu.VMEM((lats * SLOT, LANES), jnp.float32),
            pltpu.VMEM((lats * lons, 1, LANES), jnp.float32),
            pltpu.VMEM((blocks * LANES, LANES), jnp.float32),
            pltpu.SMEM((lists, cap), jnp.int32),
            pltpu.SemaphoreType.DMA((len(inputs),)),
            pltpu.SemaphoreType.DMA((lists,)),
        ],
        compiler_params=pltpu.CompilerParams(vmem_limit_bytes=56 * MIB),
        name="advect_solve_pick",
    )(*inputs, index, count)


def place_kernel(arrived, counts, own, owned, row):
    sources, height, _ = arrived.shape
    levels, ntr, columns = owned.shape
    values = levels * ntr
    parts = height // values
    lane = lax.broadcasted_iota(jnp.int32, (values, LANES), 1)
    together = 2 if sources % 2 == 0 else 1

    def some_sources(step, start):
        pieces = []
        for item in range(together):
            source = lax.rem(own[0] - (step * together + item) + sources, sources)
            total = counts[0, source]
            rows = lax.div(total + (parts - 1), parts)
            for part in range(parts):
                place = start + jnp.minimum(part * rows, total)
                shift = lax.rem(place, LANES)
                piece = arrived[source, pl.ds(part, values, stride=parts), :]
                pieces.append((place - shift, shift, pltpu.roll(piece, shift, 1)))
            start = start + total
        for tile, shift, rolled in pieces:
            here = pl.ds(pl.multiple_of(tile, LANES), LANES)
            after = pl.ds(pl.multiple_of(tile + LANES, LANES), LANES)
            pltpu.store(row.at[:, here], rolled, mask=lane >= shift)
            row[:, after] = rolled
        return start

    lax.fori_loop(0, sources // together, some_sources, 0)
    for level in range(levels):
        owned[level] = row[level * ntr : (level + 1) * ntr, :columns]


def place_owned(arrived, counts, own, levels, ntr, columns):
    vmem = pl.BlockSpec(memory_space=pltpu.VMEM)
    smem = pl.BlockSpec(memory_space=pltpu.SMEM)
    return pl.pallas_call(
        place_kernel,
        out_shape=jax.ShapeDtypeStruct((levels, ntr, columns), jnp.float32),
        in_specs=[vmem, smem, smem],
        out_specs=vmem,
        scratch_shapes=[pltpu.VMEM((levels * ntr, columns + 2 * LANES), jnp.float32)],
        compiler_params=pltpu.CompilerParams(vmem_limit_bytes=16 * MIB),
        name="place_owned",
    )(arrived, counts, own)


def ring(axis, distance):
    size = lax.axis_size(axis)
    return [(i, (i + distance) % size) for i in range(size)]


def body(tracers, offsets, weights, diffusion, send_index, send_count):
    ntr, levels, lats, lons = tracers.shape
    columns = lats * lons
    lists, cap = send_index.shape[1:]
    parts = cap // LANES
    values = ntr * levels
    west_cells, east_cells = pack_halo(tracers)
    from_west = lax.ppermute(east_cells, "lon", ring("lon", 1))
    from_east = lax.ppermute(west_cells, "lon", ring("lon", -1))
    counts = lax.all_to_all(send_count, ("lon", "lat"), split_axis=1, concat_axis=1, tiled=True)
    sent = make_sent(tracers, offsets, weights, diffusion, from_west, from_east, send_index, send_count)
    if parts < 4:
        sent = sent.reshape(-1, values, 4 // parts, parts, LANES)
        sent = jnp.transpose(sent, (0, 2, 1, 3, 4)).reshape(lists, values * parts, LANES)
    arrived = lax.all_to_all(sent, ("lon", "lat"), split_axis=0, concat_axis=0, tiled=True)
    own = lax.axis_index(("lon", "lat")).astype(jnp.int32).reshape(1)
    owned = place_owned(arrived, counts, own, levels, ntr, columns)
    return jnp.transpose(owned, (1, 0, 2))


def solution(mesh):
    return jax.shard_map(
        body,
        mesh=mesh,
        in_specs=(
            P(None, None, "lat", "lon"),
            P(None, "lat", "lon"),
            P(None, "lat", "lon"),
            P(None, "lat", "lon"),
            P(("lon", "lat"), None, None),
            P(("lon", "lat"), None),
        ),
        out_specs=P(None, None, ("lon", "lat")),
        check_vma=False,
    )
```

```python
import jax
import jax.numpy as jnp
from jax import lax
from jax.experimental import pallas as pl
from jax.experimental.pallas import tpu as pltpu
from jax.sharding import PartitionSpec as P

HALO = 16
LANES = 128
SUB = 8
SLOT = 32
MIB = 1024 * 1024


def take_lanes(block, index):
    return jnp.take_along_axis(block, index, axis=1, mode="promise_in_bounds")


def lane_ids(rows):
    return lax.broadcasted_iota(jnp.int32, (rows, LANES), 1)


def pack_halo_kernel(tracers, west_cells, east_cells):
    ntr, levels, lats, _ = tracers.shape
    per_row = LANES // HALO
    group = lane_ids(SUB) // HALO

    def one_level(level, carry):
        for tracer in range(ntr):
            west = jnp.zeros((SUB, LANES), jnp.float32)
            east = jnp.zeros((SUB, LANES), jnp.float32)
            for part in range(lats // SUB):
                cells = tracers[tracer, level, part * SUB : (part + 1) * SUB, :]
                shift = part * HALO
                rolled_west = pltpu.roll(cells, shift, 1) if shift else cells
                shift = (part * HALO + HALO) % LANES
                rolled_east = pltpu.roll(cells, shift, 1) if shift else cells
                west = jnp.where(group == part, rolled_west, west)
                east = jnp.where(group == part, rolled_east, east)
            west_cells[level, tracer] = west
            east_cells[level, tracer] = east
        return carry

    assert lats == SUB * per_row
    lax.fori_loop(0, levels, one_level, 0)


def pack_halo(tracers):
    ntr, levels, _, _ = tracers.shape
    shape = jax.ShapeDtypeStruct((levels, ntr, SUB, LANES), jnp.float32)
    return pl.pallas_call(
        pack_halo_kernel,
        out_shape=(shape, shape),
        in_specs=[pl.BlockSpec(memory_space=pltpu.VMEM)],
        out_specs=[pl.BlockSpec(memory_space=pltpu.VMEM)] * 2,
        compiler_params=pltpu.CompilerParams(vmem_limit_bytes=16 * MIB),
        name="pack_halo",
    )(tracers)


def merge_halo(west, east, halo, count):
    lane = lane_ids(SUB)
    cell = lane % (2 * HALO)
    sources = [(half * 4 + lane // (2 * HALO)) * HALO + cell % HALO for half in range(2)]
    chunk = 5 if count % 5 == 0 else 1

    def some_values(step, carry):
        merged = []
        for item in range(chunk):
            value = step * chunk + item
            for half in range(2):
                both = take_lanes(west[value], sources[half]), take_lanes(east[value], sources[half])
                merged.append((value, half, jnp.where(cell < HALO, *both)))
        for value, half, cells in merged:
            halo[value, half] = cells
        return carry

    lax.fori_loop(0, count // chunk, some_values, 0)


def advect_and_solve(tracers, offsets, weights, diffusion, halo, solved):
    ntr, levels, lats, _ = tracers.shape
    lane = lane_ids(SUB)

    def one_part(part, carry):
        rows = pl.ds(pl.multiple_of(part * SUB, SUB), SUB)
        half = part // 4
        base = (part % 4) * (2 * HALO)
        coefs = [diffusion[level, rows, :] for level in range(levels - 1)]
        upper = []
        reduced = [[] for _ in range(ntr)]
        for level in range(levels):
            left = lane + offsets[level, rows, :]
            right = left + 1
            weight = weights[level, rows, :]
            left_in = (left >= 0) & (left < LANES)
            right_in = (right >= 0) & (right < LANES)
            left_main = left & (LANES - 1)
            right_main = right & (LANES - 1)
            left_halo = base + ((left + HALO) & (2 * HALO - 1))
            right_halo = base + ((right + HALO) & (2 * HALO - 1))
            denom = 1.0
            if level > 0:
                denom = denom + coefs[level - 1]
            if level < levels - 1:
                denom = denom + coefs[level]
            if level > 0:
                denom = denom - coefs[level - 1] * upper[level - 1]
            inverse = 1.0 / denom
            if level < levels - 1:
                upper.append(coefs[level] * inverse)
            for tracer in range(ntr):
                cells = tracers[tracer, level, rows, :]
                edge = halo[level * ntr + tracer, half]
                left_value = jnp.where(left_in, take_lanes(cells, left_main), take_lanes(edge, left_halo))
                right_value = jnp.where(right_in, take_lanes(cells, right_main), take_lanes(edge, right_halo))
                value = (1.0 - weight) * left_value + weight * right_value
                if level > 0:
                    value = value + coefs[level - 1] * reduced[tracer][level - 1]
                reduced[tracer].append(value * inverse)
        for tracer in range(ntr):
            x = reduced[tracer][levels - 1]
            for level in range(levels - 1, -1, -1):
                if level < levels - 1:
                    x = reduced[tracer][level] + upper[level] * x
                solved[pl.ds(part * SUB * SLOT + level * ntr + tracer, SUB, stride=SLOT), :] = x
        return carry

    lax.fori_loop(0, lats // SUB, one_part, 0)


def pick_tiles(solved, index, count, sent, values):
    parts, lists, _ = index.shape
    rows = solved.shape[0] // SLOT
    groups = [(first, min(SUB, values - first)) for first in range(0, values, SUB)]

    def one_list(item, carry):
        def one_tile(part, inner):
            columns = jnp.broadcast_to(index[part, pl.ds(item, 1), :], (SUB, LANES))
            row_of = lax.shift_right_logical(columns, 7)
            lane_of = columns & (LANES - 1)
            picked = [jnp.zeros((SUB, LANES), jnp.float32) for _ in groups]
            for row in range(rows):
                here = row_of == row
                for place, (first, _) in enumerate(groups):
                    cells = solved[row * SLOT + first : row * SLOT + first + SUB, :]
                    picked[place] = jnp.where(here, take_lanes(cells, lane_of), picked[place])
            for place, (first, size) in enumerate(groups):
                sent[item, pl.ds(part + first * parts, size, stride=parts), :] = picked[place][:size]
            return inner

        lax.fori_loop(0, lax.div(count[0, item] + (LANES - 1), LANES), one_tile, 0)
        return carry

    lax.fori_loop(0, lists, one_list, 0)


def send_kernel(
    tracers_in, offsets_in, weights_in, diffusion_in, west_in, east_in, index_in, count, sent,
    tracers, offsets, weights, diffusion, west, east, index, halo, solved, ready,
):
    values = west.shape[0]
    parts = index.shape[0]
    sources = [west_in, east_in, offsets_in, weights_in, diffusion_in, tracers_in]
    targets = [west, east, offsets, weights, diffusion, tracers]
    sources += [index_in.at[0, :, part * LANES : (part + 1) * LANES] for part in range(parts)]
    targets += [index.at[part] for part in range(parts)]
    copies = [
        pltpu.make_async_copy(source, target, ready.at[item])
        for item, (source, target) in enumerate(zip(sources, targets))
    ]
    for copy in copies:
        copy.start()
    copies[0].wait()
    copies[1].wait()
    merge_halo(west, east, halo, values)
    for value in range(values, SLOT):
        solved[pl.ds(value, tracers.shape[2], stride=SLOT), :] = jnp.zeros((tracers.shape[2], LANES), jnp.float32)
    for copy in copies[2:]:
        copy.wait()
    advect_and_solve(tracers, offsets, weights, diffusion, halo, solved)
    pick_tiles(solved, index, count, sent, values)


def make_sent(tracers, offsets, weights, diffusion, west, east, index, count):
    ntr, levels, lats, _ = tracers.shape
    values = ntr * levels
    lists, cap = index.shape[1:]
    parts = cap // LANES
    hbm = pl.BlockSpec(memory_space=pl.ANY)
    smem = pl.BlockSpec(memory_space=pltpu.SMEM)
    west = west.reshape(values, SUB, LANES)
    east = east.reshape(values, SUB, LANES)
    inputs = (tracers, offsets, weights, diffusion, west, east)
    return pl.pallas_call(
        send_kernel,
        out_shape=jax.ShapeDtypeStruct((lists, values * parts, LANES), jnp.float32),
        in_specs=[hbm] * 7 + [smem],
        out_specs=pl.BlockSpec(memory_space=pltpu.VMEM),
        scratch_shapes=[pltpu.VMEM(array.shape, array.dtype) for array in inputs]
        + [
            pltpu.VMEM((parts, lists, LANES), jnp.int32),
            pltpu.VMEM((values, 2, SUB, LANES), jnp.float32),
            pltpu.VMEM((lats * SLOT, LANES), jnp.float32),
            pltpu.SemaphoreType.DMA((len(inputs) + parts,)),
        ],
        compiler_params=pltpu.CompilerParams(vmem_limit_bytes=56 * MIB),
        name="advect_solve_pick",
    )(*inputs, index, count)


def place_kernel(arrived, counts, own, owned, row):
    sources, height, _ = arrived.shape
    levels, ntr, columns = owned.shape
    values = levels * ntr
    parts = height // values
    lane = lax.broadcasted_iota(jnp.int32, (values, LANES), 1)
    together = 2 if sources % 2 == 0 else 1

    def some_sources(step, start):
        pieces = []
        for item in range(together):
            source = lax.rem(own[0] - (step * together + item) + sources, sources)
            total = counts[0, source]
            for part in range(parts):
                place = start + jnp.minimum(part * LANES, total)
                shift = lax.rem(place, LANES)
                piece = arrived[source, pl.ds(part, values, stride=parts), :]
                pieces.append((place - shift, shift, pltpu.roll(piece, shift, 1)))
            start = start + total
        for tile, shift, rolled in pieces:
            here = pl.ds(pl.multiple_of(tile, LANES), LANES)
            after = pl.ds(pl.multiple_of(tile + LANES, LANES), LANES)
            pltpu.store(row.at[:, here], rolled, mask=lane >= shift)
            row[:, after] = rolled
        return start

    lax.fori_loop(0, sources // together, some_sources, 0)
    for level in range(levels):
        owned[level] = row[level * ntr : (level + 1) * ntr, :columns]


def place_owned(arrived, counts, own, levels, ntr, columns):
    vmem = pl.BlockSpec(memory_space=pltpu.VMEM)
    smem = pl.BlockSpec(memory_space=pltpu.SMEM)
    return pl.pallas_call(
        place_kernel,
        out_shape=jax.ShapeDtypeStruct((levels, ntr, columns), jnp.float32),
        in_specs=[vmem, smem, smem],
        out_specs=vmem,
        scratch_shapes=[pltpu.VMEM((levels * ntr, columns + 2 * LANES), jnp.float32)],
        compiler_params=pltpu.CompilerParams(vmem_limit_bytes=16 * MIB),
        name="place_owned",
    )(arrived, counts, own)


def ring(axis, distance):
    size = lax.axis_size(axis)
    return [(i, (i + distance) % size) for i in range(size)]


def body(tracers, offsets, weights, diffusion, send_index, send_count):
    ntr, levels, lats, lons = tracers.shape
    columns = lats * lons
    west_cells, east_cells = pack_halo(tracers)
    from_west = lax.ppermute(east_cells, "lon", ring("lon", 1))
    from_east = lax.ppermute(west_cells, "lon", ring("lon", -1))
    counts = lax.all_to_all(send_count, ("lon", "lat"), split_axis=1, concat_axis=1, tiled=True)
    sent = make_sent(tracers, offsets, weights, diffusion, from_west, from_east, send_index, send_count)
    arrived = lax.all_to_all(sent, ("lon", "lat"), split_axis=0, concat_axis=0, tiled=True)
    own = lax.axis_index(("lon", "lat")).astype(jnp.int32).reshape(1)
    owned = place_owned(arrived, counts, own, levels, ntr, columns)
    return jnp.transpose(owned, (1, 0, 2))


def solution(mesh):
    return jax.shard_map(
        body,
        mesh=mesh,
        in_specs=(
            P(None, None, "lat", "lon"),
            P(None, "lat", "lon"),
            P(None, "lat", "lon"),
            P(None, "lat", "lon"),
            P(("lon", "lat"), None, None),
            P(("lon", "lat"), None),
        ),
        out_specs=P(None, None, ("lon", "lat")),
        check_vma=False,
    )
```

```python
import functools

import jax
import jax.numpy as jnp
from jax import lax
from jax.experimental import pallas as pl
from jax.experimental.pallas import tpu as pltpu
from jax.sharding import PartitionSpec as P

HALO = 16
LANES = 128
SUB = 8
SLOT = 32
LINES = 16
MIB = 1024 * 1024


def take_lanes(block, index):
    return jnp.take_along_axis(block, index, axis=1, mode="promise_in_bounds")


def lane_ids(rows):
    return lax.broadcasted_iota(jnp.int32, (rows, LANES), 1)


def pack_halo_kernel(tracers, west_cells, east_cells):
    ntr, levels, lats, _ = tracers.shape
    per_row = LANES // HALO
    group = lane_ids(SUB) // HALO

    def one_level(level, carry):
        for tracer in range(ntr):
            west = jnp.zeros((SUB, LANES), jnp.float32)
            east = jnp.zeros((SUB, LANES), jnp.float32)
            for part in range(lats // SUB):
                cells = tracers[tracer, level, part * SUB : (part + 1) * SUB, :]
                shift = part * HALO
                rolled_west = pltpu.roll(cells, shift, 1) if shift else cells
                shift = (part * HALO + HALO) % LANES
                rolled_east = pltpu.roll(cells, shift, 1) if shift else cells
                west = jnp.where(group == part, rolled_west, west)
                east = jnp.where(group == part, rolled_east, east)
            west_cells[level, tracer] = west
            east_cells[level, tracer] = east
        return carry

    assert lats == SUB * per_row
    lax.fori_loop(0, levels, one_level, 0)


def pack_halo(tracers):
    ntr, levels, _, _ = tracers.shape
    shape = jax.ShapeDtypeStruct((levels, ntr, SUB, LANES), jnp.float32)
    return pl.pallas_call(
        pack_halo_kernel,
        out_shape=(shape, shape),
        in_specs=[pl.BlockSpec(memory_space=pltpu.VMEM)],
        out_specs=[pl.BlockSpec(memory_space=pltpu.VMEM)] * 2,
        compiler_params=pltpu.CompilerParams(vmem_limit_bytes=16 * MIB),
        name="pack_halo",
    )(tracers)


def merge_halo(west, east, halo, count):
    lane = lane_ids(SUB)
    cell = lane % (2 * HALO)
    sources = [(half * 4 + lane // (2 * HALO)) * HALO + cell % HALO for half in range(2)]
    chunk = 5 if count % 5 == 0 else 1

    def some_values(step, carry):
        merged = []
        for item in range(chunk):
            value = step * chunk + item
            for half in range(2):
                both = take_lanes(west[value], sources[half]), take_lanes(east[value], sources[half])
                merged.append((value, half, jnp.where(cell < HALO, *both)))
        for value, half, cells in merged:
            halo[value, half] = cells
        return carry

    lax.fori_loop(0, count // chunk, some_values, 0)


def advect_and_solve(tracers, offsets, weights, diffusion, halo, solved):
    ntr, levels, lats, _ = tracers.shape
    lane = lane_ids(SUB)

    def one_part(part, carry):
        rows = pl.ds(pl.multiple_of(part * SUB, SUB), SUB)
        half = part // 4
        base = (part % 4) * (2 * HALO)
        coefs = [diffusion[level, rows, :] for level in range(levels - 1)]
        upper = []
        reduced = [[] for _ in range(ntr)]
        for level in range(levels):
            left = lane + offsets[level, rows, :]
            right = left + 1
            weight = weights[level, rows, :]
            left_in = (left >= 0) & (left < LANES)
            right_in = (right >= 0) & (right < LANES)
            left_main = left & (LANES - 1)
            right_main = right & (LANES - 1)
            left_halo = base + ((left + HALO) & (2 * HALO - 1))
            right_halo = base + ((right + HALO) & (2 * HALO - 1))
            denom = 1.0
            if level > 0:
                denom = denom + coefs[level - 1]
            if level < levels - 1:
                denom = denom + coefs[level]
            if level > 0:
                denom = denom - coefs[level - 1] * upper[level - 1]
            inverse = 1.0 / denom
            if level < levels - 1:
                upper.append(coefs[level] * inverse)
            for tracer in range(ntr):
                cells = tracers[tracer, level, rows, :]
                edge = halo[level * ntr + tracer, half]
                left_value = jnp.where(left_in, take_lanes(cells, left_main), take_lanes(edge, left_halo))
                right_value = jnp.where(right_in, take_lanes(cells, right_main), take_lanes(edge, right_halo))
                value = (1.0 - weight) * left_value + weight * right_value
                if level > 0:
                    value = value + coefs[level - 1] * reduced[tracer][level - 1]
                reduced[tracer].append(value * inverse)
        for tracer in range(ntr):
            x = reduced[tracer][levels - 1]
            for level in range(levels - 1, -1, -1):
                if level < levels - 1:
                    x = reduced[tracer][level] + upper[level] * x
                solved[pl.ds(part * SUB * SLOT + level * ntr + tracer, SUB, stride=SLOT), :] = x
        return carry

    lax.fori_loop(0, lats // SUB, one_part, 0)


def build_table(solved, table):
    rows_per = LANES // SLOT
    spread = lane_ids(LANES) // 4
    together = 2

    def some_rows(step, carry):
        blocks = []
        for item in range(together):
            start = pl.multiple_of((step * together + item) * LANES, LANES)
            blocks.append(solved[pl.ds(start, LANES), :].T)
        for item, block in enumerate(blocks):
            for row in range(rows_per):
                start = pl.multiple_of(((step * together + item) * rows_per + row) * LANES, LANES)
                table[pl.ds(start, LANES), :] = take_lanes(block, spread + row * SLOT)
        return carry

    lax.fori_loop(0, solved.shape[0] // (LANES * together), some_rows, 0)


def pick_rows(table, index, count, cap, packed, sent, wait_list):
    blocks, height, _ = sent.shape
    parts = cap // LANES
    lists = 4 // parts
    stream = lax.broadcasted_iota(jnp.int32, (1, LANES), 1) % 4
    together = 2 if blocks % 2 == 0 else 1

    def one_block(block, carry):
        owners = [block * lists + item for item in range(lists)]
        rows = [lax.div(count[0, owner] + (parts - 1), parts) for owner in owners]
        for owner in owners:
            wait_list(owner)
        longest = functools.reduce(jnp.maximum, rows)
        places = [owners[g // parts] * cap + (g % parts) * rows[g // parts] for g in range(4)]

        def some_lines(step, inner):
            start = pl.multiple_of(step * LINES, LINES)
            bases = [place + start for place in places]
            lines = []
            for line in range(LINES):
                picked = [table[index[base + line]] for base in bases]
                low = jnp.where(stream == 0, picked[0], picked[1])
                high = jnp.where(stream == 2, picked[2], picked[3])
                lines.append(jnp.where(stream < 2, low, high))
            first = pl.multiple_of(block * LANES + start, LINES)
            for line in range(LINES):
                packed[pl.ds(first + line, 1), :] = lines[line]
            return inner

        lax.fori_loop(0, lax.div(longest + (LINES - 1), LINES), some_lines, 0)
        return carry

    def turn_blocks(step, carry):
        turned = []
        for item in range(together):
            start = pl.multiple_of((step * together + item) * LANES, LANES)
            turned.append(packed[pl.ds(start, LANES), :].T)
        for item in range(together):
            sent[step * together + item] = turned[item][:height, :]
        return carry

    lax.fori_loop(0, blocks, one_block, 0)
    lax.fori_loop(0, blocks // together, turn_blocks, 0)


def send_kernel(
    tracers_in, offsets_in, weights_in, diffusion_in, west_in, east_in, index_in, count, sent,
    tracers, offsets, weights, diffusion, west, east, halo, solved, table, packed, index, ready, listed,
):
    lists, cap = index_in.shape[1:]

    def list_copy(item):
        place = pl.ds(pl.multiple_of(item * cap, LANES), cap)
        return pltpu.make_async_copy(index_in.at[0, item], index.at[place], listed.at[item])

    def start_list(item, carry):
        list_copy(item).start()
        return carry

    sources = (west_in, east_in, offsets_in, weights_in, diffusion_in, tracers_in)
    targets = (west, east, offsets, weights, diffusion, tracers)
    copies = [
        pltpu.make_async_copy(source, target, ready.at[item])
        for item, (source, target) in enumerate(zip(sources, targets))
    ]
    for copy in copies:
        copy.start()
    lax.fori_loop(0, lists, start_list, 0)
    copies[0].wait()
    copies[1].wait()
    merge_halo(west, east, halo, west.shape[0])
    for value in range(west.shape[0], SLOT):
        solved[pl.ds(value, tracers.shape[2], stride=SLOT), :] = jnp.zeros((tracers.shape[2], LANES), jnp.float32)
    for copy in copies[2:]:
        copy.wait()
    advect_and_solve(tracers, offsets, weights, diffusion, halo, solved)
    build_table(solved, table.reshape(table.shape[0], LANES))
    pick_rows(table, index, count, cap, packed, sent, lambda item: list_copy(item).wait())


def make_sent(tracers, offsets, weights, diffusion, west, east, index, count):
    ntr, levels, lats, lons = tracers.shape
    values = ntr * levels
    lists, cap = index.shape[1:]
    blocks = lists * (cap // LANES) // 4
    hbm = pl.BlockSpec(memory_space=pl.ANY)
    smem = pl.BlockSpec(memory_space=pltpu.SMEM)
    west = west.reshape(values, SUB, LANES)
    east = east.reshape(values, SUB, LANES)
    inputs = (tracers, offsets, weights, diffusion, west, east)
    return pl.pallas_call(
        send_kernel,
        out_shape=jax.ShapeDtypeStruct((blocks, 4 * values, LANES), jnp.float32),
        in_specs=[hbm] * 7 + [smem],
        out_specs=pl.BlockSpec(memory_space=pltpu.VMEM),
        scratch_shapes=[pltpu.VMEM(array.shape, array.dtype) for array in inputs]
        + [
            pltpu.VMEM((values, 2, SUB, LANES), jnp.float32),
            pltpu.VMEM((lats * SLOT, LANES), jnp.float32),
            pltpu.VMEM((lats * lons, 1, LANES), jnp.float32),
            pltpu.VMEM((blocks * LANES, LANES), jnp.float32),
            pltpu.SMEM((lists * cap,), jnp.int32),
            pltpu.SemaphoreType.DMA((len(inputs),)),
            pltpu.SemaphoreType.DMA((lists,)),
        ],
        compiler_params=pltpu.CompilerParams(vmem_limit_bytes=56 * MIB),
        name="advect_solve_pick",
    )(*inputs, index, count)


def place_kernel(arrived, counts, own, owned, row):
    sources, height, _ = arrived.shape
    levels, ntr, columns = owned.shape
    values = levels * ntr
    parts = height // values
    lane = lax.broadcasted_iota(jnp.int32, (values, LANES), 1)
    together = 2 if sources % 2 == 0 else 1

    def some_sources(step, start):
        pieces = []
        for item in range(together):
            source = lax.rem(own[0] - (step * together + item) + sources, sources)
            total = counts[0, source]
            rows = lax.div(total + (parts - 1), parts)
            for part in range(parts):
                place = start + jnp.minimum(part * rows, total)
                shift = lax.rem(place, LANES)
                piece = arrived[source, pl.ds(part, values, stride=parts), :]
                pieces.append((place - shift, shift, pltpu.roll(piece, shift, 1)))
            start = start + total
        for tile, shift, rolled in pieces:
            here = pl.ds(pl.multiple_of(tile, LANES), LANES)
            after = pl.ds(pl.multiple_of(tile + LANES, LANES), LANES)
            pltpu.store(row.at[:, here], rolled, mask=lane >= shift)
            row[:, after] = rolled
        return start

    lax.fori_loop(0, sources // together, some_sources, 0)
    for level in range(levels):
        owned[level] = row[level * ntr : (level + 1) * ntr, :columns]


def place_owned(arrived, counts, own, levels, ntr, columns):
    vmem = pl.BlockSpec(memory_space=pltpu.VMEM)
    smem = pl.BlockSpec(memory_space=pltpu.SMEM)
    return pl.pallas_call(
        place_kernel,
        out_shape=jax.ShapeDtypeStruct((levels, ntr, columns), jnp.float32),
        in_specs=[vmem, smem, smem],
        out_specs=vmem,
        scratch_shapes=[pltpu.VMEM((levels * ntr, columns + 2 * LANES), jnp.float32)],
        compiler_params=pltpu.CompilerParams(vmem_limit_bytes=16 * MIB),
        name="place_owned",
    )(arrived, counts, own)


def ring(axis, distance):
    size = lax.axis_size(axis)
    return [(i, (i + distance) % size) for i in range(size)]


def body(tracers, offsets, weights, diffusion, send_index, send_count):
    ntr, levels, lats, lons = tracers.shape
    columns = lats * lons
    lists, cap = send_index.shape[1:]
    parts = cap // LANES
    values = ntr * levels
    west_cells, east_cells = pack_halo(tracers)
    from_west = lax.ppermute(east_cells, "lon", ring("lon", 1))
    from_east = lax.ppermute(west_cells, "lon", ring("lon", -1))
    counts = lax.all_to_all(send_count, ("lon", "lat"), split_axis=1, concat_axis=1, tiled=True)
    sent = make_sent(tracers, offsets, weights, diffusion, from_west, from_east, send_index, send_count)
    if parts < 4:
        sent = sent.reshape(-1, values, 4 // parts, parts, LANES)
        sent = jnp.transpose(sent, (0, 2, 1, 3, 4)).reshape(lists, values * parts, LANES)
    arrived = lax.all_to_all(sent, ("lon", "lat"), split_axis=0, concat_axis=0, tiled=True)
    own = lax.axis_index(("lon", "lat")).astype(jnp.int32).reshape(1)
    owned = place_owned(arrived, counts, own, levels, ntr, columns)
    return jnp.transpose(owned, (1, 0, 2))


def solution(mesh):
    return jax.shard_map(
        body,
        mesh=mesh,
        in_specs=(
            P(None, None, "lat", "lon"),
            P(None, "lat", "lon"),
            P(None, "lat", "lon"),
            P(None, "lat", "lon"),
            P(("lon", "lat"), None, None),
            P(("lon", "lat"), None),
        ),
        out_specs=P(None, None, ("lon", "lat")),
        check_vma=False,
    )
```

```python
import functools

import jax
import jax.numpy as jnp
from jax import lax
from jax.experimental import pallas as pl
from jax.experimental.pallas import tpu as pltpu
from jax.sharding import PartitionSpec as P

HALO = 16
LANES = 128
SUB = 8
SLOT = 32
LINES = 16
MIB = 1024 * 1024


def take_lanes(block, index):
    return jnp.take_along_axis(block, index, axis=1, mode="promise_in_bounds")


def lane_ids(rows):
    return lax.broadcasted_iota(jnp.int32, (rows, LANES), 1)


def pack_halo_kernel(tracers, west_cells, east_cells):
    ntr, levels, lats, _ = tracers.shape
    per_row = LANES // HALO
    group = lane_ids(SUB) // HALO

    def one_level(level, carry):
        for tracer in range(ntr):
            west = jnp.zeros((SUB, LANES), jnp.float32)
            east = jnp.zeros((SUB, LANES), jnp.float32)
            for part in range(lats // SUB):
                cells = tracers[tracer, level, part * SUB : (part + 1) * SUB, :]
                shift = part * HALO
                rolled_west = pltpu.roll(cells, shift, 1) if shift else cells
                shift = (part * HALO + HALO) % LANES
                rolled_east = pltpu.roll(cells, shift, 1) if shift else cells
                west = jnp.where(group == part, rolled_west, west)
                east = jnp.where(group == part, rolled_east, east)
            west_cells[level, tracer] = west
            east_cells[level, tracer] = east
        return carry

    assert lats == SUB * per_row
    lax.fori_loop(0, levels, one_level, 0)


def pack_halo(tracers):
    ntr, levels, _, _ = tracers.shape
    shape = jax.ShapeDtypeStruct((levels, ntr, SUB, LANES), jnp.float32)
    return pl.pallas_call(
        pack_halo_kernel,
        out_shape=(shape, shape),
        in_specs=[pl.BlockSpec(memory_space=pltpu.VMEM)],
        out_specs=[pl.BlockSpec(memory_space=pltpu.VMEM)] * 2,
        compiler_params=pltpu.CompilerParams(vmem_limit_bytes=16 * MIB),
        name="pack_halo",
    )(tracers)


def merge_halo(west, east, halo, count):
    lane = lane_ids(SUB)
    cell = lane % (2 * HALO)
    sources = [(half * 4 + lane // (2 * HALO)) * HALO + cell % HALO for half in range(2)]
    chunk = 5 if count % 5 == 0 else 1

    def some_values(step, carry):
        merged = []
        for item in range(chunk):
            value = step * chunk + item
            for half in range(2):
                both = take_lanes(west[value], sources[half]), take_lanes(east[value], sources[half])
                merged.append((value, half, jnp.where(cell < HALO, *both)))
        for value, half, cells in merged:
            halo[value, half] = cells
        return carry

    lax.fori_loop(0, count // chunk, some_values, 0)


def advect_and_solve(tracers, offsets, weights, diffusion, halo, solved):
    ntr, levels, lats, _ = tracers.shape
    lane = lane_ids(SUB)

    def one_part(part, carry):
        rows = pl.ds(pl.multiple_of(part * SUB, SUB), SUB)
        half = part // 4
        base = (part % 4) * (2 * HALO)
        coefs = [diffusion[level, rows, :] for level in range(levels - 1)]
        upper = []
        reduced = [[] for _ in range(ntr)]
        for level in range(levels):
            left = lane + offsets[level, rows, :]
            right = left + 1
            weight = weights[level, rows, :]
            left_in = (left >= 0) & (left < LANES)
            right_in = (right >= 0) & (right < LANES)
            left_main = left & (LANES - 1)
            right_main = right & (LANES - 1)
            left_halo = base + ((left + HALO) & (2 * HALO - 1))
            right_halo = base + ((right + HALO) & (2 * HALO - 1))
            denom = 1.0
            if level > 0:
                denom = denom + coefs[level - 1]
            if level < levels - 1:
                denom = denom + coefs[level]
            if level > 0:
                denom = denom - coefs[level - 1] * upper[level - 1]
            inverse = 1.0 / denom
            if level < levels - 1:
                upper.append(coefs[level] * inverse)
            for tracer in range(ntr):
                cells = tracers[tracer, level, rows, :]
                edge = halo[level * ntr + tracer, half]
                left_value = jnp.where(left_in, take_lanes(cells, left_main), take_lanes(edge, left_halo))
                right_value = jnp.where(right_in, take_lanes(cells, right_main), take_lanes(edge, right_halo))
                value = (1.0 - weight) * left_value + weight * right_value
                if level > 0:
                    value = value + coefs[level - 1] * reduced[tracer][level - 1]
                reduced[tracer].append(value * inverse)
        for tracer in range(ntr):
            x = reduced[tracer][levels - 1]
            for level in range(levels - 1, -1, -1):
                if level < levels - 1:
                    x = reduced[tracer][level] + upper[level] * x
                solved[pl.ds(part * SUB * SLOT + level * ntr + tracer, SUB, stride=SLOT), :] = x
        return carry

    lax.fori_loop(0, lats // SUB, one_part, 0)


def streams_of(rows, values, parts):
    lane = lane_ids(rows)
    width = values * parts
    item = sum((lane >= width * step).astype(jnp.int32) for step in range(1, 4 // parts))
    held = lane - item * width
    part = held & (parts - 1)
    return jnp.minimum(lax.shift_right_logical(held, parts.bit_length() - 1), values - 1), item * parts + part


def build_table(solved, table, values, parts):
    rows_per = LANES // SLOT
    spread = streams_of(LANES, values, parts)[0]
    together = 2

    def some_rows(step, carry):
        blocks = []
        for item in range(together):
            start = pl.multiple_of((step * together + item) * LANES, LANES)
            blocks.append(solved[pl.ds(start, LANES), :].T)
        for item, block in enumerate(blocks):
            for row in range(rows_per):
                start = pl.multiple_of(((step * together + item) * rows_per + row) * LANES, LANES)
                table[pl.ds(start, LANES), :] = take_lanes(block, spread + row * SLOT)
        return carry

    lax.fori_loop(0, solved.shape[0] // (LANES * together), some_rows, 0)


def pick_rows(table, index, count, cap, chunk, parts, values, packed, sent, wait_list):
    blocks, height, _ = sent.shape
    all_parts = cap // LANES
    lists = 4 // parts
    stream = streams_of(1, values, parts)[1]
    together = 2 if blocks % 2 == 0 else 1

    def one_block(block, carry):
        owners = [block * lists + item for item in range(lists)]
        rows = [lax.div(count[0, owner] + (all_parts - 1), all_parts) for owner in owners]
        for owner in owners:
            wait_list(owner)
        longest = functools.reduce(jnp.maximum, rows)
        places = [owners[g // parts] * cap + (chunk * parts + g % parts) * rows[g // parts] for g in range(4)]

        def some_lines(step, inner):
            start = pl.multiple_of(step * LINES, LINES)
            bases = [place + start for place in places]
            lines = []
            for line in range(LINES):
                picked = [table[index[base + line]] for base in bases]
                low = jnp.where(stream == 0, picked[0], picked[1])
                high = jnp.where(stream == 2, picked[2], picked[3])
                lines.append(jnp.where(stream < 2, low, high))
            first = pl.multiple_of(block * LANES + start, LINES)
            for line in range(LINES):
                packed[pl.ds(first + line, 1), :] = lines[line]
            return inner

        lax.fori_loop(0, lax.div(longest + (LINES - 1), LINES), some_lines, 0)
        return carry

    def turn_blocks(step, carry):
        turned = []
        for item in range(together):
            start = pl.multiple_of((step * together + item) * LANES, LANES)
            turned.append(packed[pl.ds(start, LANES), :].T)
        for item in range(together):
            sent[step * together + item] = turned[item][:height, :]
        return carry

    lax.fori_loop(0, blocks, one_block, 0)
    lax.fori_loop(0, blocks // together, turn_blocks, 0)


def list_copies(index_in, index, listed):
    lists, cap = index_in.shape[1:]

    def list_copy(item):
        place = pl.ds(pl.multiple_of(item * cap, LANES), cap)
        return pltpu.make_async_copy(index_in.at[0, item], index.at[place], listed.at[item])

    def start_list(item, carry):
        list_copy(item).start()
        return carry

    lax.fori_loop(0, lists, start_list, 0)
    return lambda item: list_copy(item).wait()


def solve_kernel(
    parts, tracers_in, offsets_in, weights_in, diffusion_in, west_in, east_in, index_in, count, table, sent,
    tracers, offsets, weights, diffusion, west, east, halo, solved, packed, index, ready, listed,
):
    values = west.shape[0]
    sources = (west_in, east_in, offsets_in, weights_in, diffusion_in, tracers_in)
    targets = (west, east, offsets, weights, diffusion, tracers)
    copies = [
        pltpu.make_async_copy(source, target, ready.at[item])
        for item, (source, target) in enumerate(zip(sources, targets))
    ]
    for copy in copies:
        copy.start()
    wait_list = list_copies(index_in, index, listed)
    copies[0].wait()
    copies[1].wait()
    merge_halo(west, east, halo, values)
    for value in range(values, SLOT):
        solved[pl.ds(value, tracers.shape[2], stride=SLOT), :] = jnp.zeros((tracers.shape[2], LANES), jnp.float32)
    for copy in copies[2:]:
        copy.wait()
    advect_and_solve(tracers, offsets, weights, diffusion, halo, solved)
    build_table(solved, table.reshape(table.shape[0], LANES), values, parts)
    pick_rows(table, index, count, index_in.shape[2], 0, parts, values, packed, sent, wait_list)


def more_kernel(chunk, parts, values, table, index_in, count, sent, packed, index, listed):
    wait_list = list_copies(index_in, index, listed)
    pick_rows(table, index, count, index_in.shape[2], chunk, parts, values, packed, sent, wait_list)


def make_sent(tracers, offsets, weights, diffusion, west, east, index, count):
    ntr, levels, lats, lons = tracers.shape
    values = ntr * levels
    lists, cap = index.shape[1:]
    chunks = 2 if cap // LANES % 2 == 0 else 1
    parts = cap // LANES // chunks
    blocks = lists * parts // 4
    hbm = pl.BlockSpec(memory_space=pl.ANY)
    vmem = pl.BlockSpec(memory_space=pltpu.VMEM)
    smem = pl.BlockSpec(memory_space=pltpu.SMEM)
    west = west.reshape(values, SUB, LANES)
    east = east.reshape(values, SUB, LANES)
    inputs = (tracers, offsets, weights, diffusion, west, east)
    sent_shape = jax.ShapeDtypeStruct((blocks, 4 * values, LANES), jnp.float32)
    pick_scratch = [
        pltpu.VMEM((blocks * LANES, LANES), jnp.float32),
        pltpu.SMEM((lists * cap,), jnp.int32),
    ]
    table, first = pl.pallas_call(
        functools.partial(solve_kernel, parts),
        out_shape=(jax.ShapeDtypeStruct((lats * lons, 1, LANES), jnp.float32), sent_shape),
        in_specs=[hbm] * 7 + [smem],
        out_specs=(vmem, vmem),
        scratch_shapes=[pltpu.VMEM(array.shape, array.dtype) for array in inputs]
        + [
            pltpu.VMEM((values, 2, SUB, LANES), jnp.float32),
            pltpu.VMEM((lats * SLOT, LANES), jnp.float32),
            *pick_scratch,
            pltpu.SemaphoreType.DMA((len(inputs),)),
            pltpu.SemaphoreType.DMA((lists,)),
        ],
        compiler_params=pltpu.CompilerParams(vmem_limit_bytes=20 * MIB),
        name="advect_solve_pick",
    )(*inputs, index, count)
    sent = [first]
    for chunk in range(1, chunks):
        sent.append(
            pl.pallas_call(
                functools.partial(more_kernel, chunk, parts, values),
                out_shape=sent_shape,
                in_specs=[vmem, hbm, smem],
                out_specs=vmem,
                scratch_shapes=[*pick_scratch, pltpu.SemaphoreType.DMA((lists,))],
                compiler_params=pltpu.CompilerParams(vmem_limit_bytes=16 * MIB),
                name="pick_more",
            )(table, index, count)
        )
    rows = values * parts
    tile = max(size for size in (1, 2, 4, 8) if rows % size == 0)
    return [array.reshape(lists, rows // tile, tile, LANES) for array in sent]


def place_kernel(counts, own, *refs):
    *arrived, owned, row, starts = refs
    levels, ntr, columns = owned.shape
    values = levels * ntr
    sources = counts.shape[1]
    blocks, height, _ = arrived[0].shape
    lists = sources // blocks
    parts = height // values // lists
    all_parts = parts * len(arrived)
    lane = lax.broadcasted_iota(jnp.int32, (values, LANES), 1)

    def one_start(turn, start):
        source = lax.rem(own[0] - turn + sources, sources)
        starts[source] = start
        return start + counts[0, source]

    def one_block(block, carry):
        pieces = []
        for item in range(lists):
            source = block * lists + item
            total = counts[0, source]
            rows = lax.div(total + (all_parts - 1), all_parts)
            for part in range(all_parts):
                place = starts[source] + jnp.minimum(part * rows, total)
                shift = lax.rem(place, LANES)
                end = shift + jnp.clip(total - part * rows, 0, rows)
                first = item * values * parts + part % parts
                piece = arrived[part // parts][block, pl.ds(first, values, stride=parts), :]
                pieces.append((place - shift, shift, end, pltpu.roll(piece, shift, 1)))
        for tile, shift, end, rolled in pieces:
            here = pl.ds(pl.multiple_of(tile, LANES), LANES)
            after = pl.ds(pl.multiple_of(tile + LANES, LANES), LANES)
            pltpu.store(row.at[:, here], rolled, mask=(lane >= shift) & (lane < end))
            pltpu.store(row.at[:, after], rolled, mask=lane < end - LANES)
        return carry

    lax.fori_loop(0, sources, one_start, 0)
    lax.fori_loop(0, blocks, one_block, 0)
    for level in range(levels):
        owned[level] = row[level * ntr : (level + 1) * ntr, :columns]


def place_owned(arrived, counts, own, levels, ntr, columns):
    vmem = pl.BlockSpec(memory_space=pltpu.VMEM)
    smem = pl.BlockSpec(memory_space=pltpu.SMEM)
    values = levels * ntr
    arrived = [array.reshape(-1, 4 * values, LANES) for array in arrived]
    return pl.pallas_call(
        place_kernel,
        out_shape=jax.ShapeDtypeStruct((levels, ntr, columns), jnp.float32),
        in_specs=[smem, smem] + [vmem] * len(arrived),
        out_specs=vmem,
        scratch_shapes=[
            pltpu.VMEM((values, columns + 2 * LANES), jnp.float32),
            pltpu.SMEM((counts.shape[1],), jnp.int32),
        ],
        compiler_params=pltpu.CompilerParams(vmem_limit_bytes=16 * MIB),
        name="place_owned",
    )(counts, own, *arrived)


def ring(axis, distance):
    size = lax.axis_size(axis)
    return [(i, (i + distance) % size) for i in range(size)]


def body(tracers, offsets, weights, diffusion, send_index, send_count):
    ntr, levels, lats, lons = tracers.shape
    columns = lats * lons
    west_cells, east_cells = pack_halo(tracers)
    from_west = lax.ppermute(east_cells, "lon", ring("lon", 1))
    from_east = lax.ppermute(west_cells, "lon", ring("lon", -1))
    counts = lax.all_to_all(send_count, ("lon", "lat"), split_axis=1, concat_axis=1, tiled=True)
    sent = make_sent(tracers, offsets, weights, diffusion, from_west, from_east, send_index, send_count)
    arrived = [
        lax.all_to_all(array, ("lon", "lat"), split_axis=0, concat_axis=0, tiled=True) for array in sent
    ]
    own = lax.axis_index(("lon", "lat")).astype(jnp.int32).reshape(1)
    owned = place_owned(arrived, counts, own, levels, ntr, columns)
    return jnp.transpose(owned, (1, 0, 2))


def solution(mesh):
    return jax.shard_map(
        body,
        mesh=mesh,
        in_specs=(
            P(None, None, "lat", "lon"),
            P(None, "lat", "lon"),
            P(None, "lat", "lon"),
            P(None, "lat", "lon"),
            P(("lon", "lat"), None, None),
            P(("lon", "lat"), None),
        ),
        out_specs=P(None, None, ("lon", "lat")),
        check_vma=False,
    )
```

```python
import functools

import jax
import jax.numpy as jnp
from jax import lax
from jax.experimental import pallas as pl
from jax.experimental.pallas import tpu as pltpu
from jax.sharding import PartitionSpec as P

HALO = 16
LANES = 128
SUB = 8
SLOT = 32
LINES = 16
MIB = 1024 * 1024
LENGTH_BASE = 1000.0
BIG = 60 * MIB


def take_lanes(block, index):
    return jnp.take_along_axis(block, index, axis=1, mode="promise_in_bounds")


def lane_ids(rows):
    return lax.broadcasted_iota(jnp.int32, (rows, LANES), 1)


def pack_halo_kernel(tracers, west_cells, east_cells):
    ntr, levels, lats, _ = tracers.shape
    per_row = LANES // HALO
    group = lane_ids(SUB) // HALO

    def one_level(level, carry):
        for tracer in range(ntr):
            west = jnp.zeros((SUB, LANES), jnp.float32)
            east = jnp.zeros((SUB, LANES), jnp.float32)
            for part in range(lats // SUB):
                cells = tracers[tracer, level, part * SUB : (part + 1) * SUB, :]
                shift = part * HALO
                rolled_west = pltpu.roll(cells, shift, 1) if shift else cells
                shift = (part * HALO + HALO) % LANES
                rolled_east = pltpu.roll(cells, shift, 1) if shift else cells
                west = jnp.where(group == part, rolled_west, west)
                east = jnp.where(group == part, rolled_east, east)
            west_cells[level, tracer] = west
            east_cells[level, tracer] = east
        return carry

    assert lats == SUB * per_row
    lax.fori_loop(0, levels, one_level, 0)


def pack_halo(tracers):
    ntr, levels, _, _ = tracers.shape
    shape = jax.ShapeDtypeStruct((levels, ntr, SUB, LANES), jnp.float32)
    return pl.pallas_call(
        pack_halo_kernel,
        out_shape=(shape, shape),
        in_specs=[pl.BlockSpec(memory_space=pltpu.VMEM)],
        out_specs=[pl.BlockSpec(memory_space=pltpu.VMEM)] * 2,
        compiler_params=pltpu.CompilerParams(vmem_limit_bytes=16 * MIB),
        name="pack_halo",
    )(tracers)


def merge_halo(west, east, halo, count):
    lane = lane_ids(SUB)
    cell = lane % (2 * HALO)
    sources = [(half * 4 + lane // (2 * HALO)) * HALO + cell % HALO for half in range(2)]
    chunk = 5 if count % 5 == 0 else 1

    def some_values(step, carry):
        merged = []
        for item in range(chunk):
            value = step * chunk + item
            for half in range(2):
                both = take_lanes(west[value], sources[half]), take_lanes(east[value], sources[half])
                merged.append((value, half, jnp.where(cell < HALO, *both)))
        for value, half, cells in merged:
            halo[value, half] = cells
        return carry

    lax.fori_loop(0, count // chunk, some_values, 0)


def fetch(sources, targets, ready):
    copies = [
        pltpu.make_async_copy(source, target, ready.at[item])
        for item, (source, target) in enumerate(zip(sources, targets))
    ]
    for copy in copies:
        copy.start()
    return copies


def inside_kernel(
    tracers_in, offsets_in, weights_in, diffusion_in, index_in, count,
    inside, left_cell, west_edge, east_edge, lower, upper, lists,
    tracers, offsets, weights, diffusion, ready,
):
    ntr, levels, lats, _ = tracers.shape
    lane = lane_ids(SUB)
    owners = count.shape[1]
    copies = fetch(
        (diffusion_in, offsets_in, weights_in, tracers_in, index_in.at[0]),
        (diffusion, offsets, weights, tracers, lists.at[pl.ds(0, owners)]),
        ready,
    )
    lists[owners : owners + 1, :owners] = count[...]
    for copy in copies:
        copy.wait()

    def one_part(part, carry):
        rows = pl.ds(pl.multiple_of(part * SUB, SUB), SUB)
        coefs = [diffusion[level, rows, :] for level in range(levels - 1)]
        lowers, uppers, edges, results = [], [], [], []
        for level in range(levels):
            denom = 1.0
            if level > 0:
                denom = denom + coefs[level - 1]
            if level < levels - 1:
                denom = denom + coefs[level]
            if level > 0:
                denom = denom - coefs[level - 1] * uppers[level - 1]
            inverse = 1.0 / denom
            if level > 0:
                lowers.append(coefs[level - 1] * inverse)
            if level < levels - 1:
                uppers.append(coefs[level] * inverse)
            left = lane + offsets[level, rows, :]
            right = left + 1
            weight = weights[level, rows, :]
            west_weight = (1.0 - weight) * inverse
            east_weight = weight * inverse
            left_in = (left >= 0) & (left < LANES)
            right_in = (right >= 0) & (right < LANES)
            edges.append((left, jnp.where(left_in, 0.0, west_weight), jnp.where(right_in, 0.0, east_weight)))
            west_weight = jnp.where(left_in, west_weight, 0.0)
            east_weight = jnp.where(right_in, east_weight, 0.0)
            left = left & (LANES - 1)
            right = right & (LANES - 1)
            for tracer in range(ntr):
                cells = tracers[tracer, level, rows, :]
                results.append(west_weight * take_lanes(cells, left) + east_weight * take_lanes(cells, right))
        for value, result in enumerate(results):
            inside[value, rows, :] = result
        for level, (left, west_weight, east_weight) in enumerate(edges):
            left_cell[level, rows, :] = left
            west_edge[level, rows, :] = west_weight
            east_edge[level, rows, :] = east_weight
        for level in range(levels - 1):
            lower[level, rows, :] = lowers[level]
            upper[level, rows, :] = uppers[level]
        return carry

    lax.fori_loop(0, lats // SUB, one_part, 0)


def advect_inside(tracers, offsets, weights, diffusion, index, count):
    ntr, levels, lats, lons = tracers.shape
    lists, cap = index.shape[1:]
    vmem = pl.BlockSpec(memory_space=pltpu.VMEM)
    field = lambda count, kind=jnp.float32: jax.ShapeDtypeStruct((count, lats, lons), kind)
    outputs = (
        field(ntr * levels),
        field(levels, jnp.int32),
        field(levels),
        field(levels),
        field(levels - 1),
        field(levels - 1),
        jax.ShapeDtypeStruct((lists + SUB, cap), jnp.int32),
    )
    return pl.pallas_call(
        inside_kernel,
        out_shape=outputs,
        in_specs=[pl.BlockSpec(memory_space=pl.ANY)] * 5 + [vmem],
        out_specs=(vmem,) * len(outputs),
        scratch_shapes=[pltpu.VMEM(array.shape, array.dtype) for array in (tracers, offsets, weights, diffusion)]
        + [pltpu.SemaphoreType.DMA((5,))],
        compiler_params=pltpu.CompilerParams(vmem_limit_bytes=BIG),
        cost_estimate=pl.CostEstimate(flops=0, bytes_accessed=20 * MIB, transcendentals=0),
        name="advect_inside",
    )(tracers, offsets, weights, diffusion, index, count)


def add_edges_and_solve(inside, left_cell, west_edge, east_edge, lower, upper, halo, solved):
    levels, lats, _ = left_cell.shape
    ntr = inside.shape[0] // levels

    def one_part(part, carry):
        rows = pl.ds(pl.multiple_of(part * SUB, SUB), SUB)
        half = part // 4
        base = (part % 4) * (2 * HALO)
        reduced = [[] for _ in range(ntr)]
        for level in range(levels):
            left = left_cell[level, rows, :]
            right = base + ((left + (HALO + 1)) & (2 * HALO - 1))
            left = base + ((left + HALO) & (2 * HALO - 1))
            west_weight = west_edge[level, rows, :]
            east_weight = east_edge[level, rows, :]
            for tracer in range(ntr):
                value = level * ntr + tracer
                cells = halo[value, half]
                edges = west_weight * take_lanes(cells, left) + east_weight * take_lanes(cells, right)
                total = inside[value, rows, :] + edges
                if level > 0:
                    total = total + lower[level - 1, rows, :] * reduced[tracer][level - 1]
                reduced[tracer].append(total)
        results = []
        for tracer in range(ntr):
            x = reduced[tracer][levels - 1]
            for level in range(levels - 1, -1, -1):
                if level < levels - 1:
                    x = reduced[tracer][level] + upper[level, rows, :] * x
                results.append((level * ntr + tracer, x))
        for value, x in results:
            solved[pl.ds(part * SUB * SLOT + value, SUB, stride=SLOT), :] = x
        return carry

    lax.fori_loop(0, lats // SUB, one_part, 0)


def streams_of(rows, values, parts):
    lane = lane_ids(rows)
    width = values * parts
    item = sum((lane >= width * step).astype(jnp.int32) for step in range(1, 4 // parts))
    held = lane - item * width
    part = held & (parts - 1)
    return jnp.minimum(lax.shift_right_logical(held, parts.bit_length() - 1), values - 1), item * parts + part


def build_table(solved, table, values, parts):
    rows_per = LANES // SLOT
    spread = streams_of(LANES, values, parts)[0]
    together = 2

    def some_rows(step, carry):
        blocks = []
        for item in range(together):
            start = pl.multiple_of((step * together + item) * LANES, LANES)
            blocks.append(solved[pl.ds(start, LANES), :].T)
        for item, block in enumerate(blocks):
            for row in range(rows_per):
                start = pl.multiple_of(((step * together + item) * rows_per + row) * LANES, LANES)
                table[pl.ds(start, LANES), :] = take_lanes(block, spread + row * SLOT)
        return carry

    lax.fori_loop(0, solved.shape[0] // (LANES * together), some_rows, 0)


def pick_rows(table, index, count, cap, chunk, parts, values, packed, sent, wait_list):
    blocks, height, _ = sent.shape
    all_parts = cap // LANES
    lists = 4 // parts
    stream = streams_of(1, values, parts)[1]
    together = 2 if blocks % 2 == 0 else 1

    def one_block(block, carry):
        owners = [block * lists + item for item in range(lists)]
        rows = [lax.div(count[owner] + (all_parts - 1), all_parts) for owner in owners]
        for owner in owners:
            wait_list(owner)
        longest = functools.reduce(jnp.maximum, rows)
        places = [owners[g // parts] * cap + (chunk * parts + g % parts) * rows[g // parts] for g in range(4)]

        def some_lines(step, inner):
            start = pl.multiple_of(step * LINES, LINES)
            bases = [place + start for place in places]
            lines = []
            for line in range(LINES):
                picked = [table[index[base + line]] for base in bases]
                low = jnp.where(stream == 0, picked[0], picked[1])
                high = jnp.where(stream == 2, picked[2], picked[3])
                lines.append(jnp.where(stream < 2, low, high))
            first = pl.multiple_of(block * LANES + start, LINES)
            for line in range(LINES):
                packed[pl.ds(first + line, 1), :] = lines[line]
            return inner

        lax.fori_loop(0, lax.div(longest + (LINES - 1), LINES), some_lines, 0)
        return carry

    def turn_blocks(step, carry):
        turned = []
        for item in range(together):
            start = pl.multiple_of((step * together + item) * LANES, LANES)
            turned.append(packed[pl.ds(start, LANES), :].T)
        for item in range(together):
            block = step * together + item
            sent[block] = turned[item][:height, :]
            for owner in range(lists if last else 0):
                total = count[block * lists + owner]
                row = sent.at[block, pl.ds((owner * values + 1) * parts - 1, 1), :]
                note = jnp.full((1, LANES), LENGTH_BASE + total.astype(jnp.float32))
                pltpu.store(row, note, mask=(lane_ids(1) == LANES - 1) & (total < cap))
        return carry

    last = (chunk + 1) * parts == all_parts
    lax.fori_loop(0, blocks, one_block, 0)
    lax.fori_loop(0, blocks // together, turn_blocks, 0)


def list_copies(lists_in, index, count, listed):
    owners = lists_in.shape[0] - SUB
    cap = lists_in.shape[1]
    lengths = pltpu.make_async_copy(lists_in.at[owners], count, listed.at[owners])

    def list_copy(item):
        place = pl.ds(pl.multiple_of(item * cap, LANES), cap)
        return pltpu.make_async_copy(lists_in.at[item], index.at[place], listed.at[item])

    def start_list(item, carry):
        list_copy(item).start()
        return carry

    lengths.start()
    lax.fori_loop(0, owners, start_list, 0)
    return lengths.wait, lambda item: list_copy(item).wait()


def solve_kernel(
    chunk, parts, west_in, east_in, inside_in, left_cell_in, west_edge_in, east_edge_in, lower_in, upper_in, lists_in,
    sent, west, east, inside, left_cell, west_edge, east_edge, lower, upper, ready,
    halo, solved, table, packed, index, count, listed,
):
    values, lats, _ = inside.shape
    sources = (west_in, east_in, left_cell_in, west_edge_in, east_edge_in, lower_in, upper_in, inside_in)
    copies = fetch(sources, (west, east, left_cell, west_edge, east_edge, lower, upper, inside), ready)
    wait_lengths, wait_list = list_copies(lists_in, index, count, listed)
    for value in range(values, SLOT):
        solved[pl.ds(value, lats, stride=SLOT), :] = jnp.zeros((lats, LANES), jnp.float32)
    for copy in copies[:2]:
        copy.wait()
    merge_halo(west, east, halo, values)
    for copy in copies[2:]:
        copy.wait()
    add_edges_and_solve(inside, left_cell, west_edge, east_edge, lower, upper, halo, solved)
    build_table(solved, table.reshape(table.shape[0], LANES), values, parts)
    wait_lengths()
    pick_rows(table, index, count, lists_in.shape[1], chunk, parts, values, packed, sent, wait_list)


def make_sent(west, east, fields, lists_in):
    values, lats, lons = fields[0].shape
    lists, cap = lists_in.shape[0] - SUB, lists_in.shape[1]
    parts = cap // LANES
    blocks = lists * parts // 4
    inputs = (west.reshape(values, SUB, LANES), east.reshape(values, SUB, LANES), *fields)
    sent = pl.pallas_call(
        functools.partial(solve_kernel, 0, parts),
        out_shape=jax.ShapeDtypeStruct((blocks, 4 * values, LANES), jnp.float32),
        in_specs=[pl.BlockSpec(memory_space=pl.ANY)] * (len(inputs) + 1),
        out_specs=pl.BlockSpec(memory_space=pltpu.VMEM),
        scratch_shapes=[pltpu.VMEM(array.shape, array.dtype) for array in inputs]
        + [
            pltpu.SemaphoreType.DMA((len(inputs),)),
            pltpu.VMEM((values, 2, SUB, LANES), jnp.float32),
            pltpu.VMEM((lats * SLOT, LANES), jnp.float32),
            pltpu.VMEM((lats * lons, 1, LANES), jnp.float32),
            pltpu.VMEM((blocks * LANES, LANES), jnp.float32),
            pltpu.SMEM((lists * cap,), jnp.int32),
            pltpu.SMEM((cap,), jnp.int32),
            pltpu.SemaphoreType.DMA((lists + 1,)),
        ],
        compiler_params=pltpu.CompilerParams(vmem_limit_bytes=BIG),
        cost_estimate=pl.CostEstimate(flops=0, bytes_accessed=40 * MIB, transcendentals=0),
        name="solve_pick",
    )(*inputs, lists_in)
    rows = values * parts
    tile = max(size for size in (1, 2, 4, 8) if rows % size == 0)
    return sent.reshape(lists, rows // tile, tile, LANES)


def place_kernel(own, *refs):
    *arrived, owned, row, totals, starts = refs
    levels, ntr, columns = owned.shape
    values = levels * ntr
    sources = totals.shape[0]
    blocks, height, _ = arrived[0].shape
    lists = sources // blocks
    parts = height // values // lists
    all_parts = parts * len(arrived)
    lane = lax.broadcasted_iota(jnp.int32, (values, LANES), 1)

    for source in range(sources):
        note_row = (source % lists * values + 1) * parts - 1
        note = arrived[0][source // lists, note_row : note_row + 1, :]
        total = jnp.where(note > 0.5 * LENGTH_BASE, note - LENGTH_BASE, 1.0 * all_parts * LANES)
        totals[source] = total.astype(jnp.int32)[0, LANES - 1]

    def one_start(turn, start):
        source = lax.rem(own[0] - turn + sources, sources)
        starts[source] = start
        return start + totals[source]

    def one_block(block, carry):
        pieces = []
        for item in range(lists):
            source = block * lists + item
            total = totals[source]
            rows = lax.div(total + (all_parts - 1), all_parts)
            for part in range(all_parts):
                place = starts[source] + jnp.minimum(part * rows, total)
                shift = lax.rem(place, LANES)
                end = shift + jnp.clip(total - part * rows, 0, rows)
                first = item * values * parts + part % parts
                piece = arrived[-1 - part // parts][block, pl.ds(first, values, stride=parts), :]
                pieces.append((place - shift, shift, end, pltpu.roll(piece, shift, 1)))
        for tile, shift, end, rolled in pieces:
            here = pl.ds(pl.multiple_of(tile, LANES), LANES)
            after = pl.ds(pl.multiple_of(tile + LANES, LANES), LANES)
            pltpu.store(row.at[:, here], rolled, mask=(lane >= shift) & (lane < end))
            pltpu.store(row.at[:, after], rolled, mask=lane < end - LANES)
        return carry

    lax.fori_loop(0, sources, one_start, 0)
    lax.fori_loop(0, blocks, one_block, 0)
    for level in range(levels):
        owned[level] = row[level * ntr : (level + 1) * ntr, :columns]


def place_owned(arrived, own, levels, ntr, columns):
    vmem = pl.BlockSpec(memory_space=pltpu.VMEM)
    smem = pl.BlockSpec(memory_space=pltpu.SMEM)
    values = levels * ntr
    sources = arrived[0].shape[0]
    arrived = [array.reshape(-1, 4 * values, LANES) for array in arrived]
    return pl.pallas_call(
        place_kernel,
        out_shape=jax.ShapeDtypeStruct((levels, ntr, columns), jnp.float32),
        in_specs=[smem] + [vmem] * len(arrived),
        out_specs=vmem,
        scratch_shapes=[
            pltpu.VMEM((values, columns + 2 * LANES), jnp.float32),
            pltpu.SMEM((sources,), jnp.int32),
            pltpu.SMEM((sources,), jnp.int32),
        ],
        compiler_params=pltpu.CompilerParams(vmem_limit_bytes=16 * MIB),
        name="place_owned",
    )(own, *arrived)


def ring(axis, distance):
    size = lax.axis_size(axis)
    return [(i, (i + distance) % size) for i in range(size)]


def body(tracers, offsets, weights, diffusion, send_index, send_count):
    ntr, levels, lats, lons = tracers.shape
    columns = lats * lons
    west_cells, east_cells = pack_halo(tracers)
    from_west = lax.ppermute(east_cells, "lon", ring("lon", 1))
    from_east = lax.ppermute(west_cells, "lon", ring("lon", -1))
    *fields, lists = advect_inside(tracers, offsets, weights, diffusion, send_index, send_count)
    sent = make_sent(from_west, from_east, fields, lists)
    arrived = lax.all_to_all(sent, ("lon", "lat"), split_axis=0, concat_axis=0, tiled=True)
    own = lax.axis_index(("lon", "lat")).astype(jnp.int32).reshape(1)
    owned = place_owned([arrived], own, levels, ntr, columns)
    return jnp.transpose(owned, (1, 0, 2))


def solution(mesh):
    return jax.shard_map(
        body,
        mesh=mesh,
        in_specs=(
            P(None, None, "lat", "lon"),
            P(None, "lat", "lon"),
            P(None, "lat", "lon"),
            P(None, "lat", "lon"),
            P(("lon", "lat"), None, None),
            P(("lon", "lat"), None),
        ),
        out_specs=P(None, None, ("lon", "lat")),
        check_vma=False,
    )
```

```python
import functools

import jax
import jax.numpy as jnp
from jax import lax
from jax.experimental import pallas as pl
from jax.experimental.pallas import tpu as pltpu
from jax.sharding import PartitionSpec as P

HALO = 16
LANES = 128
SUB = 8
SLOT = 32
LINES = 16
MIB = 1024 * 1024
LENGTH_BASE = 1000.0
BIG = 60 * MIB


def take_lanes(block, index):
    return jnp.take_along_axis(block, index, axis=1, mode="promise_in_bounds")


def lane_ids(rows):
    return lax.broadcasted_iota(jnp.int32, (rows, LANES), 1)


def pack_halo_kernel(tracers, west_cells, east_cells):
    ntr, levels, lats, _ = tracers.shape
    per_row = LANES // HALO
    group = lane_ids(SUB) // HALO

    def one_level(level, carry):
        for tracer in range(ntr):
            west = jnp.zeros((SUB, LANES), jnp.float32)
            east = jnp.zeros((SUB, LANES), jnp.float32)
            for part in range(lats // SUB):
                cells = tracers[tracer, level, part * SUB : (part + 1) * SUB, :]
                shift = part * HALO
                rolled_west = pltpu.roll(cells, shift, 1) if shift else cells
                shift = (part * HALO + HALO) % LANES
                rolled_east = pltpu.roll(cells, shift, 1) if shift else cells
                west = jnp.where(group == part, rolled_west, west)
                east = jnp.where(group == part, rolled_east, east)
            west_cells[level, tracer] = west
            east_cells[level, tracer] = east
        return carry

    assert lats == SUB * per_row
    lax.fori_loop(0, levels, one_level, 0)


def pack_halo(tracers):
    ntr, levels, _, _ = tracers.shape
    shape = jax.ShapeDtypeStruct((levels, ntr, SUB, LANES), jnp.float32)
    return pl.pallas_call(
        pack_halo_kernel,
        out_shape=(shape, shape),
        in_specs=[pl.BlockSpec(memory_space=pltpu.VMEM)],
        out_specs=[pl.BlockSpec(memory_space=pltpu.VMEM)] * 2,
        compiler_params=pltpu.CompilerParams(vmem_limit_bytes=16 * MIB),
        name="pack_halo",
    )(tracers)


def merge_halo(west, east, halo, count):
    lane = lane_ids(SUB)
    cell = lane % (2 * HALO)
    sources = [(half * 4 + lane // (2 * HALO)) * HALO + cell % HALO for half in range(2)]
    chunk = 5 if count % 5 == 0 else 1

    def some_values(step, carry):
        merged = []
        for item in range(chunk):
            value = step * chunk + item
            for half in range(2):
                both = take_lanes(west[value], sources[half]), take_lanes(east[value], sources[half])
                merged.append((value, half, jnp.where(cell < HALO, *both)))
        for value, half, cells in merged:
            halo[value, half] = cells
        return carry

    lax.fori_loop(0, count // chunk, some_values, 0)


def fetch(sources, targets, ready):
    copies = [
        pltpu.make_async_copy(source, target, ready.at[item])
        for item, (source, target) in enumerate(zip(sources, targets))
    ]
    for copy in copies:
        copy.start()
    return copies


def inside_kernel(
    tracers_in, offsets_in, weights_in, diffusion_in, index_in, count,
    inside, left_cell, west_edge, east_edge, lower, upper, lists,
    tracers, offsets, weights, diffusion, ready,
):
    ntr, levels, lats, _ = tracers.shape
    lane = lane_ids(SUB)
    owners = count.shape[1]
    copies = fetch(
        (diffusion_in, offsets_in, weights_in, tracers_in, index_in.at[0]),
        (diffusion, offsets, weights, tracers, lists.at[pl.ds(0, owners)]),
        ready,
    )
    lists[owners : owners + 1, :owners] = count[...]
    for copy in copies:
        copy.wait()

    def one_part(part, carry):
        rows = pl.ds(pl.multiple_of(part * SUB, SUB), SUB)
        coefs = [diffusion[level, rows, :] for level in range(levels - 1)]
        lowers, uppers, edges, results = [], [], [], []
        for level in range(levels):
            denom = 1.0
            if level > 0:
                denom = denom + coefs[level - 1]
            if level < levels - 1:
                denom = denom + coefs[level]
            if level > 0:
                denom = denom - coefs[level - 1] * uppers[level - 1]
            inverse = 1.0 / denom
            if level > 0:
                lowers.append(coefs[level - 1] * inverse)
            if level < levels - 1:
                uppers.append(coefs[level] * inverse)
            left = lane + offsets[level, rows, :]
            right = left + 1
            weight = weights[level, rows, :]
            west_weight = (1.0 - weight) * inverse
            east_weight = weight * inverse
            left_in = (left >= 0) & (left < LANES)
            right_in = (right >= 0) & (right < LANES)
            edges.append((left, jnp.where(left_in, 0.0, west_weight), jnp.where(right_in, 0.0, east_weight)))
            west_weight = jnp.where(left_in, west_weight, 0.0)
            east_weight = jnp.where(right_in, east_weight, 0.0)
            left = left & (LANES - 1)
            right = right & (LANES - 1)
            for tracer in range(ntr):
                cells = tracers[tracer, level, rows, :]
                results.append(west_weight * take_lanes(cells, left) + east_weight * take_lanes(cells, right))
        for value, result in enumerate(results):
            inside[value, rows, :] = result
        for level, (left, west_weight, east_weight) in enumerate(edges):
            left_cell[level, rows, :] = left
            west_edge[level, rows, :] = west_weight
            east_edge[level, rows, :] = east_weight
        for level in range(levels - 1):
            lower[level, rows, :] = lowers[level]
            upper[level, rows, :] = uppers[level]
        return carry

    lax.fori_loop(0, lats // SUB, one_part, 0)


def advect_inside(tracers, offsets, weights, diffusion, index, count):
    ntr, levels, lats, lons = tracers.shape
    lists, cap = index.shape[1:]
    vmem = pl.BlockSpec(memory_space=pltpu.VMEM)
    field = lambda count, kind=jnp.float32: jax.ShapeDtypeStruct((count, lats, lons), kind)
    outputs = (
        field(ntr * levels),
        field(levels, jnp.int32),
        field(levels),
        field(levels),
        field(levels - 1),
        field(levels - 1),
        jax.ShapeDtypeStruct((lists + SUB, cap), jnp.int32),
    )
    return pl.pallas_call(
        inside_kernel,
        out_shape=outputs,
        in_specs=[pl.BlockSpec(memory_space=pl.ANY)] * 5 + [vmem],
        out_specs=(vmem,) * len(outputs),
        scratch_shapes=[pltpu.VMEM(array.shape, array.dtype) for array in (tracers, offsets, weights, diffusion)]
        + [pltpu.SemaphoreType.DMA((5,))],
        compiler_params=pltpu.CompilerParams(vmem_limit_bytes=BIG),
        cost_estimate=pl.CostEstimate(flops=0, bytes_accessed=20 * MIB, transcendentals=0),
        name="advect_inside",
    )(tracers, offsets, weights, diffusion, index, count)


def add_edges_and_solve(inside, left_cell, west_edge, east_edge, lower, upper, halo, solved):
    levels, lats, _ = left_cell.shape
    ntr = inside.shape[0] // levels

    def one_part(part, carry):
        rows = pl.ds(pl.multiple_of(part * SUB, SUB), SUB)
        half = part // 4
        base = (part % 4) * (2 * HALO)
        reduced = [[] for _ in range(ntr)]
        for level in range(levels):
            left = left_cell[level, rows, :]
            right = base + ((left + (HALO + 1)) & (2 * HALO - 1))
            left = base + ((left + HALO) & (2 * HALO - 1))
            west_weight = west_edge[level, rows, :]
            east_weight = east_edge[level, rows, :]
            for tracer in range(ntr):
                value = level * ntr + tracer
                cells = halo[value, half]
                edges = west_weight * take_lanes(cells, left) + east_weight * take_lanes(cells, right)
                total = inside[value, rows, :] + edges
                if level > 0:
                    total = total + lower[level - 1, rows, :] * reduced[tracer][level - 1]
                reduced[tracer].append(total)
        results = []
        for tracer in range(ntr):
            x = reduced[tracer][levels - 1]
            for level in range(levels - 1, -1, -1):
                if level < levels - 1:
                    x = reduced[tracer][level] + upper[level, rows, :] * x
                results.append((level * ntr + tracer, x))
        for value, x in results:
            solved[pl.ds(part * SUB * SLOT + value, SUB, stride=SLOT), :] = x
        return carry

    lax.fori_loop(0, lats // SUB, one_part, 0)


def streams_of(rows, values, parts):
    lane = lane_ids(rows)
    width = values * parts
    item = sum((lane >= width * step).astype(jnp.int32) for step in range(1, 4 // parts))
    held = lane - item * width
    part = held & (parts - 1)
    return jnp.minimum(lax.shift_right_logical(held, parts.bit_length() - 1), values - 1), item * parts + part


def build_table(solved, table, values, parts):
    rows_per = LANES // SLOT
    spread = streams_of(LANES, values, parts)[0]
    together = 2

    def some_rows(step, carry):
        blocks = []
        for item in range(together):
            start = pl.multiple_of((step * together + item) * LANES, LANES)
            blocks.append(solved[pl.ds(start, LANES), :].T)
        for item, block in enumerate(blocks):
            for row in range(rows_per):
                start = pl.multiple_of(((step * together + item) * rows_per + row) * LANES, LANES)
                table[pl.ds(start, LANES), :] = take_lanes(block, spread + row * SLOT)
        return carry

    lax.fori_loop(0, solved.shape[0] // (LANES * together), some_rows, 0)


def device_index():
    return lax.axis_index("lon") * lax.axis_size("lat") + lax.axis_index("lat")


def pick_rows(table, index, count, cap, values, packed, sent, wait_list):
    parts = cap // LANES
    turns = len(sent)
    stream = streams_of(1, values, parts)[1] & (parts - 1)
    own = device_index()

    def one_turn(turn, carry):
        owner = lax.rem(own + turn, turns)
        rows = lax.div(count[owner] + (parts - 1), parts)
        wait_list(owner)
        places = [owner * cap + part * rows for part in range(parts)]

        def some_lines(step, inner):
            start = pl.multiple_of(step * LINES, LINES)
            bases = [place + start for place in places]
            lines = []
            for line in range(LINES):
                picked = [table[index[base + line]] for base in bases]
                merged = picked[0]
                for part in range(1, parts):
                    merged = jnp.where(stream == part, picked[part], merged)
                lines.append(merged)
            first = pl.multiple_of(turn * LANES + start, LINES)
            for line in range(LINES):
                packed[pl.ds(first + line, 1), :] = lines[line]
            return inner

        lax.fori_loop(0, lax.div(rows + (LINES - 1), LINES), some_lines, 0)
        return carry

    lax.fori_loop(0, turns, one_turn, 0)
    for first in range(0, turns, 2):
        turned = [packed[turn * LANES : (turn + 1) * LANES, :].T for turn in range(first, min(first + 2, turns))]
        for turn, block in enumerate(turned, first):
            sent[turn][...] = block[: values * parts, :]
            total = count[lax.rem(own + turn, turns)]
            note = jnp.full((1, LANES), LENGTH_BASE + total.astype(jnp.float32))
            mask = (lane_ids(1) == LANES - 1) & (total < cap)
            pltpu.store(sent[turn].at[pl.ds(parts - 1, 1), :], note, mask=mask)


def list_copies(lists_in, index, count, listed):
    owners = lists_in.shape[0] - SUB
    cap = lists_in.shape[1]
    lengths = pltpu.make_async_copy(lists_in.at[owners], count, listed.at[owners])

    def list_copy(item):
        place = pl.ds(pl.multiple_of(item * cap, LANES), cap)
        return pltpu.make_async_copy(lists_in.at[item], index.at[place], listed.at[item])

    def start_list(item, carry):
        list_copy(item).start()
        return carry

    lengths.start()
    lax.fori_loop(0, owners, start_list, 0)
    return lengths.wait, lambda item: list_copy(item).wait()


def solve_kernel(
    parts, west_in, east_in, inside_in, left_cell_in, west_edge_in, east_edge_in, lower_in, upper_in, lists_in, *refs
):
    turns = lists_in.shape[0] - SUB
    sent = refs[:turns]
    (
        west, east, inside, left_cell, west_edge, east_edge, lower, upper, ready,
        halo, solved, table, packed, index, count, listed,
    ) = refs[turns:]
    values, lats, _ = inside.shape
    sources = (west_in, east_in, left_cell_in, west_edge_in, east_edge_in, lower_in, upper_in, inside_in)
    copies = fetch(sources, (west, east, left_cell, west_edge, east_edge, lower, upper, inside), ready)
    wait_lengths, wait_list = list_copies(lists_in, index, count, listed)
    for value in range(values, SLOT):
        solved[pl.ds(value, lats, stride=SLOT), :] = jnp.zeros((lats, LANES), jnp.float32)
    for copy in copies[:2]:
        copy.wait()
    merge_halo(west, east, halo, values)
    for copy in copies[2:]:
        copy.wait()
    add_edges_and_solve(inside, left_cell, west_edge, east_edge, lower, upper, halo, solved)
    build_table(solved, table.reshape(table.shape[0], LANES), values, parts)
    wait_lengths()
    pick_rows(table, index, count, lists_in.shape[1], values, packed, sent, wait_list)


def make_sent(west, east, fields, lists_in):
    values, lats, lons = fields[0].shape
    lists, cap = lists_in.shape[0] - SUB, lists_in.shape[1]
    parts = cap // LANES
    inputs = (west.reshape(values, SUB, LANES), east.reshape(values, SUB, LANES), *fields)
    return pl.pallas_call(
        functools.partial(solve_kernel, parts),
        out_shape=(jax.ShapeDtypeStruct((parts * values, LANES), jnp.float32),) * lists,
        in_specs=[pl.BlockSpec(memory_space=pl.ANY)] * (len(inputs) + 1),
        out_specs=(pl.BlockSpec(memory_space=pltpu.VMEM),) * lists,
        scratch_shapes=[pltpu.VMEM(array.shape, array.dtype) for array in inputs]
        + [
            pltpu.SemaphoreType.DMA((len(inputs),)),
            pltpu.VMEM((values, 2, SUB, LANES), jnp.float32),
            pltpu.VMEM((lats * SLOT, LANES), jnp.float32),
            pltpu.VMEM((lats * lons, 1, LANES), jnp.float32),
            pltpu.VMEM((lists * LANES, LANES), jnp.float32),
            pltpu.SMEM((lists * cap,), jnp.int32),
            pltpu.SMEM((cap,), jnp.int32),
            pltpu.SemaphoreType.DMA((lists + 1,)),
        ],
        compiler_params=pltpu.CompilerParams(vmem_limit_bytes=BIG),
        cost_estimate=pl.CostEstimate(flops=0, bytes_accessed=40 * MIB, transcendentals=0),
        name="solve_pick",
    )(*inputs, lists_in)


def place_kernel(parts, *refs):
    *arrived, owned, row = refs
    levels, ntr, columns = owned.shape
    values = levels * ntr
    lane = lax.broadcasted_iota(jnp.int32, (values, LANES), 1)
    totals = []
    for held in arrived:
        note = held[parts - 1 : parts, :]
        total = jnp.where(note > 0.5 * LENGTH_BASE, note - LENGTH_BASE, 1.0 * parts * LANES)
        totals.append(total.astype(jnp.int32)[0, LANES - 1])
    start = 0
    for held, total in zip(arrived, totals):
        rows = lax.div(total + (parts - 1), parts)
        pieces = []
        for part in range(parts):
            place = start + jnp.minimum(part * rows, total)
            shift = lax.rem(place, LANES)
            piece = held[pl.ds(part, values, stride=parts), :]
            pieces.append((place - shift, shift, pltpu.roll(piece, shift, 1)))
        for tile, shift, rolled in pieces:
            here = pl.ds(pl.multiple_of(tile, LANES), LANES)
            after = pl.ds(pl.multiple_of(tile + LANES, LANES), LANES)
            pltpu.store(row.at[:, here], rolled, mask=lane >= shift)
            row[:, after] = rolled
        start = start + total
    for level in range(levels):
        owned[level] = row[level * ntr : (level + 1) * ntr, :columns]


def place_owned(arrived, levels, ntr, columns):
    vmem = pl.BlockSpec(memory_space=pltpu.VMEM)
    values = levels * ntr
    return pl.pallas_call(
        functools.partial(place_kernel, arrived[0].shape[0] // values),
        out_shape=jax.ShapeDtypeStruct((levels, ntr, columns), jnp.float32),
        in_specs=[vmem] * len(arrived),
        out_specs=vmem,
        scratch_shapes=[pltpu.VMEM((values, columns + 2 * LANES), jnp.float32)],
        compiler_params=pltpu.CompilerParams(vmem_limit_bytes=16 * MIB),
        name="place_owned",
    )(*arrived)


def exchange_order(devices):
    half = devices // 2
    order = [half]
    for step in range(1, half):
        distance = half - step if step % 2 else step
        order += [distance, devices - distance]
    seen = list(dict.fromkeys(order))
    return seen + [d for d in range(1, devices) if d not in seen]


def ring(axis, distance):
    size = lax.axis_size(axis)
    return [(i, (i + distance) % size) for i in range(size)]


def body(tracers, offsets, weights, diffusion, send_index, send_count):
    ntr, levels, lats, lons = tracers.shape
    columns = lats * lons
    west_cells, east_cells = pack_halo(tracers)
    from_west = lax.ppermute(east_cells, "lon", ring("lon", 1))
    from_east = lax.ppermute(west_cells, "lon", ring("lon", -1))
    *fields, lists = advect_inside(tracers, offsets, weights, diffusion, send_index, send_count)
    sent = make_sent(from_west, from_east, fields, lists)
    axes = ("lon", "lat")
    arrived = {0: sent[0]}
    for turn in exchange_order(len(sent)):
        arrived[turn] = lax.ppermute(sent[turn], axes, ring(axes, turn))
    owned = place_owned([arrived[turn] for turn in range(len(sent))], levels, ntr, columns)
    return jnp.transpose(owned, (1, 0, 2))


def solution(mesh):
    return jax.shard_map(
        body,
        mesh=mesh,
        in_specs=(
            P(None, None, "lat", "lon"),
            P(None, "lat", "lon"),
            P(None, "lat", "lon"),
            P(None, "lat", "lon"),
            P(("lon", "lat"), None, None),
            P(("lon", "lat"), None),
        ),
        out_specs=P(None, None, ("lon", "lat")),
        check_vma=False,
    )
```

```python
import functools

import jax
import jax.numpy as jnp
from jax import lax
from jax.experimental import pallas as pl
from jax.experimental.pallas import tpu as pltpu
from jax.sharding import PartitionSpec as P

HALO = 16
LANES = 128
SUB = 8
SLOT = 32
MIB = 1024 * 1024
LENGTH_BASE = 1000.0
BIG = 60 * MIB


def take_lanes(block, index):
    return jnp.take_along_axis(block, index, axis=1, mode="promise_in_bounds")


def lane_ids(rows):
    return lax.broadcasted_iota(jnp.int32, (rows, LANES), 1)


def pack_halo_kernel(tracers, west_cells, east_cells):
    ntr, levels, lats, _ = tracers.shape
    per_row = LANES // HALO
    group = lane_ids(SUB) // HALO

    def one_level(level, carry):
        for tracer in range(ntr):
            west = jnp.zeros((SUB, LANES), jnp.float32)
            east = jnp.zeros((SUB, LANES), jnp.float32)
            for part in range(lats // SUB):
                cells = tracers[tracer, level, part * SUB : (part + 1) * SUB, :]
                shift = part * HALO
                rolled_west = pltpu.roll(cells, shift, 1) if shift else cells
                shift = (part * HALO + HALO) % LANES
                rolled_east = pltpu.roll(cells, shift, 1) if shift else cells
                west = jnp.where(group == part, rolled_west, west)
                east = jnp.where(group == part, rolled_east, east)
            west_cells[level, tracer] = west
            east_cells[level, tracer] = east
        return carry

    assert lats == SUB * per_row
    lax.fori_loop(0, levels, one_level, 0)


def pack_halo(tracers):
    ntr, levels, _, _ = tracers.shape
    shape = jax.ShapeDtypeStruct((levels, ntr, SUB, LANES), jnp.float32)
    return pl.pallas_call(
        pack_halo_kernel,
        out_shape=(shape, shape),
        in_specs=[pl.BlockSpec(memory_space=pltpu.VMEM)],
        out_specs=[pl.BlockSpec(memory_space=pltpu.VMEM)] * 2,
        compiler_params=pltpu.CompilerParams(vmem_limit_bytes=16 * MIB),
        name="pack_halo",
    )(tracers)


def merge_halo(west, east, halo, count):
    lane = lane_ids(SUB)
    cell = lane % (2 * HALO)
    sources = [(half * 4 + lane // (2 * HALO)) * HALO + cell % HALO for half in range(2)]
    chunk = 5 if count % 5 == 0 else 1

    def some_values(step, carry):
        merged = []
        for item in range(chunk):
            value = step * chunk + item
            for half in range(2):
                both = take_lanes(west[value], sources[half]), take_lanes(east[value], sources[half])
                merged.append((value, half, jnp.where(cell < HALO, *both)))
        for value, half, cells in merged:
            halo[value, half] = cells
        return carry

    lax.fori_loop(0, count // chunk, some_values, 0)


def fetch(sources, targets, ready):
    copies = [
        pltpu.make_async_copy(source, target, ready.at[item])
        for item, (source, target) in enumerate(zip(sources, targets))
    ]
    for copy in copies:
        copy.start()
    return copies


def inside_kernel(
    tracers_in, offsets_in, weights_in, diffusion_in, index_in, count,
    inside, left_cell, west_edge, east_edge, lower, upper, lists,
    tracers, offsets, weights, diffusion, ready,
):
    ntr, levels, lats, _ = tracers.shape
    lane = lane_ids(SUB)
    owners = count.shape[1]
    copies = fetch(
        (diffusion_in, offsets_in, weights_in, tracers_in, index_in.at[0]),
        (diffusion, offsets, weights, tracers, lists.at[pl.ds(0, owners)]),
        ready,
    )
    lists[owners : owners + 1, :owners] = count[...]
    for copy in copies:
        copy.wait()

    def one_part(part, carry):
        rows = pl.ds(pl.multiple_of(part * SUB, SUB), SUB)
        coefs = [diffusion[level, rows, :] for level in range(levels - 1)]
        lowers, uppers, edges, results = [], [], [], []
        for level in range(levels):
            denom = 1.0
            if level > 0:
                denom = denom + coefs[level - 1]
            if level < levels - 1:
                denom = denom + coefs[level]
            if level > 0:
                denom = denom - coefs[level - 1] * uppers[level - 1]
            inverse = 1.0 / denom
            if level > 0:
                lowers.append(coefs[level - 1] * inverse)
            if level < levels - 1:
                uppers.append(coefs[level] * inverse)
            left = lane + offsets[level, rows, :]
            right = left + 1
            weight = weights[level, rows, :]
            west_weight = (1.0 - weight) * inverse
            east_weight = weight * inverse
            left_in = (left >= 0) & (left < LANES)
            right_in = (right >= 0) & (right < LANES)
            edges.append((left, jnp.where(left_in, 0.0, west_weight), jnp.where(right_in, 0.0, east_weight)))
            west_weight = jnp.where(left_in, west_weight, 0.0)
            east_weight = jnp.where(right_in, east_weight, 0.0)
            left = left & (LANES - 1)
            right = right & (LANES - 1)
            for tracer in range(ntr):
                cells = tracers[tracer, level, rows, :]
                results.append(west_weight * take_lanes(cells, left) + east_weight * take_lanes(cells, right))
        for value, result in enumerate(results):
            inside[value, rows, :] = result
        for level, (left, west_weight, east_weight) in enumerate(edges):
            left_cell[level, rows, :] = left
            west_edge[level, rows, :] = west_weight
            east_edge[level, rows, :] = east_weight
        for level in range(levels - 1):
            lower[level, rows, :] = lowers[level]
            upper[level, rows, :] = uppers[level]
        return carry

    lax.fori_loop(0, lats // SUB, one_part, 0)


def advect_inside(tracers, offsets, weights, diffusion, index, count):
    ntr, levels, lats, lons = tracers.shape
    lists, cap = index.shape[1:]
    vmem = pl.BlockSpec(memory_space=pltpu.VMEM)
    field = lambda count, kind=jnp.float32: jax.ShapeDtypeStruct((count, lats, lons), kind)
    outputs = (
        field(ntr * levels),
        field(levels, jnp.int32),
        field(levels),
        field(levels),
        field(levels - 1),
        field(levels - 1),
        jax.ShapeDtypeStruct((lists + SUB, cap), jnp.int32),
    )
    return pl.pallas_call(
        inside_kernel,
        out_shape=outputs,
        in_specs=[pl.BlockSpec(memory_space=pl.ANY)] * 5 + [vmem],
        out_specs=(vmem,) * len(outputs),
        scratch_shapes=[pltpu.VMEM(array.shape, array.dtype) for array in (tracers, offsets, weights, diffusion)]
        + [pltpu.SemaphoreType.DMA((5,))],
        compiler_params=pltpu.CompilerParams(vmem_limit_bytes=BIG),
        cost_estimate=pl.CostEstimate(flops=0, bytes_accessed=20 * MIB, transcendentals=0),
        name="advect_inside",
    )(tracers, offsets, weights, diffusion, index, count)


def add_edges_and_solve(inside, left_cell, west_edge, east_edge, lower, upper, halo, solved):
    levels, lats, _ = left_cell.shape
    ntr = inside.shape[0] // levels

    def one_part(part, carry):
        rows = pl.ds(pl.multiple_of(part * SUB, SUB), SUB)
        half = part // 4
        base = (part % 4) * (2 * HALO)
        reduced = [[] for _ in range(ntr)]
        for level in range(levels):
            left = left_cell[level, rows, :]
            right = base + ((left + (HALO + 1)) & (2 * HALO - 1))
            left = base + ((left + HALO) & (2 * HALO - 1))
            west_weight = west_edge[level, rows, :]
            east_weight = east_edge[level, rows, :]
            for tracer in range(ntr):
                value = level * ntr + tracer
                cells = halo[value, half]
                edges = west_weight * take_lanes(cells, left) + east_weight * take_lanes(cells, right)
                total = inside[value, rows, :] + edges
                if level > 0:
                    total = total + lower[level - 1, rows, :] * reduced[tracer][level - 1]
                reduced[tracer].append(total)
        results = []
        for tracer in range(ntr):
            x = reduced[tracer][levels - 1]
            for level in range(levels - 1, -1, -1):
                if level < levels - 1:
                    x = reduced[tracer][level] + upper[level, rows, :] * x
                results.append((level * ntr + tracer, x))
        for value, x in results:
            solved[pl.ds(part * SUB * SLOT + value, SUB, stride=SLOT), :] = x
        return carry

    lax.fori_loop(0, lats // SUB, one_part, 0)


def streams_of(rows, values, parts):
    lane = lane_ids(rows)
    width = values * parts
    item = sum((lane >= width * step).astype(jnp.int32) for step in range(1, 4 // parts))
    held = lane - item * width
    part = held & (parts - 1)
    return jnp.minimum(lax.shift_right_logical(held, parts.bit_length() - 1), values - 1), item * parts + part


def build_table(solved, table, values, parts):
    rows_per = LANES // SLOT
    spread = streams_of(LANES, values, parts)[0]
    together = 2

    def some_rows(step, carry):
        blocks = []
        for item in range(together):
            start = pl.multiple_of((step * together + item) * LANES, LANES)
            blocks.append(solved[pl.ds(start, LANES), :].T)
        for item, block in enumerate(blocks):
            for row in range(rows_per):
                start = pl.multiple_of(((step * together + item) * rows_per + row) * LANES, LANES)
                table[pl.ds(start, LANES), :] = take_lanes(block, spread + row * SLOT)
        return carry

    lax.fori_loop(0, solved.shape[0] // (LANES * together), some_rows, 0)


def pick_rows(table, index, count, cap, values, packed, turned, sent, copied, wait_list):
    blocks, height, _ = sent.shape
    parts = cap // LANES
    lists = 4 // parts
    stream = streams_of(1, values, parts)[1]
    together = 2 if blocks % 2 == 0 else 1

    def copy_out(block):
        return pltpu.make_async_copy(turned.at[block], sent.at[block], copied.at[block])

    def pick_block(block, item):
        owners = [block * lists + member for member in range(lists)]
        rows = [lax.div(count[owner] + (parts - 1), parts) for owner in owners]
        for owner in owners:
            wait_list(owner)
        longest = functools.reduce(jnp.maximum, rows)
        places = [owners[g // parts] * cap + (g % parts) * rows[g // parts] for g in range(4)]

        def pick_lines(start, lines):
            bases = [place + start for place in places]
            merged = []
            for line in range(lines):
                picked = [table[index[base + line]] for base in bases]
                low = jnp.where(stream == 0, picked[0], picked[1])
                high = jnp.where(stream == 2, picked[2], picked[3])
                merged.append(jnp.where(stream < 2, low, high))
            first = pl.multiple_of(item * LANES + start, SUB)
            for line in range(lines):
                packed[pl.ds(first + line, 1), :] = merged[line]

        def steps(begin, trips, lines):
            def one_step(step, carry):
                pick_lines(pl.multiple_of(begin + step * lines, SUB), lines)
                return carry

            lax.fori_loop(0, trips, one_step, 0)
            return begin + trips * lines

        eights = lax.div(longest + (SUB - 1), SUB)
        done = steps(0, lax.div(eights, 4), 4 * SUB)
        done = steps(done, lax.div(lax.rem(eights, 4), 2), 2 * SUB)
        steps(done, lax.rem(eights, 2), SUB)

    def some_blocks(step, carry):
        for item in range(together):
            pick_block(step * together + item, item)
        results = [packed[item * LANES : (item + 1) * LANES, :].T for item in range(together)]
        for item in range(together):
            block = step * together + item
            turned[block] = results[item][:height, :]
            for member in range(lists):
                total = count[block * lists + member]
                row = turned.at[block, pl.ds((member * values + 1) * parts - 1, 1), :]
                note = jnp.full((1, LANES), LENGTH_BASE + total.astype(jnp.float32))
                pltpu.store(row, note, mask=(lane_ids(1) == LANES - 1) & (total < cap))
            copy_out(block).start()
        return carry

    def finish(block, carry):
        copy_out(block).wait()
        return carry

    lax.fori_loop(0, blocks // together, some_blocks, 0)
    lax.fori_loop(0, blocks, finish, 0)


def list_copies(lists_in, index, count, listed):
    owners = lists_in.shape[0] - SUB
    cap = lists_in.shape[1]
    lengths = pltpu.make_async_copy(lists_in.at[owners], count, listed.at[owners])

    def list_copy(item):
        place = pl.ds(pl.multiple_of(item * cap, LANES), cap)
        return pltpu.make_async_copy(lists_in.at[item], index.at[place], listed.at[item])

    def start_list(item, carry):
        list_copy(item).start()
        return carry

    lengths.start()
    lax.fori_loop(0, owners, start_list, 0)
    return lengths.wait, lambda item: list_copy(item).wait()


def solve_kernel(
    parts, west_in, east_in, inside_in, left_cell_in, west_edge_in, east_edge_in, lower_in, upper_in, lists_in,
    sent, west, east, inside, left_cell, west_edge, east_edge, lower, upper, ready,
    halo, solved, table, packed, turned, index, count, listed, copied,
):
    values, lats, _ = inside.shape
    sources = (west_in, east_in, left_cell_in, west_edge_in, east_edge_in, lower_in, upper_in, inside_in)
    copies = fetch(sources, (west, east, left_cell, west_edge, east_edge, lower, upper, inside), ready)
    wait_lengths, wait_list = list_copies(lists_in, index, count, listed)
    for value in range(values, SLOT):
        solved[pl.ds(value, lats, stride=SLOT), :] = jnp.zeros((lats, LANES), jnp.float32)
    for copy in copies[:2]:
        copy.wait()
    merge_halo(west, east, halo, values)
    for copy in copies[2:]:
        copy.wait()
    add_edges_and_solve(inside, left_cell, west_edge, east_edge, lower, upper, halo, solved)
    build_table(solved, table.reshape(table.shape[0], LANES), values, parts)
    wait_lengths()
    pick_rows(table, index, count, lists_in.shape[1], values, packed, turned, sent, copied, wait_list)


def make_sent(west, east, fields, lists_in):
    values, lats, lons = fields[0].shape
    lists, cap = lists_in.shape[0] - SUB, lists_in.shape[1]
    parts = cap // LANES
    blocks = lists * parts // 4
    inputs = (west.reshape(values, SUB, LANES), east.reshape(values, SUB, LANES), *fields)
    sent = pl.pallas_call(
        functools.partial(solve_kernel, parts),
        out_shape=jax.ShapeDtypeStruct((blocks, 4 * values, LANES), jnp.float32),
        in_specs=[pl.BlockSpec(memory_space=pl.ANY)] * (len(inputs) + 1),
        out_specs=pl.BlockSpec(memory_space=pl.ANY),
        scratch_shapes=[pltpu.VMEM(array.shape, array.dtype) for array in inputs]
        + [
            pltpu.SemaphoreType.DMA((len(inputs),)),
            pltpu.VMEM((values, 2, SUB, LANES), jnp.float32),
            pltpu.VMEM((lats * SLOT, LANES), jnp.float32),
            pltpu.VMEM((lats * lons, 1, LANES), jnp.float32),
            pltpu.VMEM((2 * LANES, LANES), jnp.float32),
            pltpu.VMEM((blocks, 4 * values, LANES), jnp.float32),
            pltpu.SMEM((lists * cap,), jnp.int32),
            pltpu.SMEM((cap,), jnp.int32),
            pltpu.SemaphoreType.DMA((lists + 1,)),
            pltpu.SemaphoreType.DMA((blocks,)),
        ],
        compiler_params=pltpu.CompilerParams(vmem_limit_bytes=BIG),
        cost_estimate=pl.CostEstimate(flops=0, bytes_accessed=40 * MIB, transcendentals=0),
        name="solve_pick",
    )(*inputs, lists_in)
    rows = values * parts
    tile = max(size for size in (1, 2, 4, 8) if rows % size == 0)
    return sent.reshape(lists, rows // tile, tile, LANES)


def place_kernel(own, arrived, owned, row):
    sources, height, _ = arrived.shape
    levels, ntr, columns = owned.shape
    values = levels * ntr
    parts = height // values
    lane = lax.broadcasted_iota(jnp.int32, (values, LANES), 1)
    order = [lax.rem(own[0] - turn + sources, sources) for turn in range(sources)]
    totals = []
    for source in order:
        note = arrived[source, parts - 1 : parts, :]
        total = jnp.where(note > 0.5 * LENGTH_BASE, note - LENGTH_BASE, 1.0 * parts * LANES)
        totals.append(total.astype(jnp.int32)[0, LANES - 1])
    start = 0
    for source, total in zip(order, totals):
        rows = lax.div(total + (parts - 1), parts)
        pieces = []
        for part in range(parts):
            place = start + jnp.minimum(part * rows, total)
            shift = lax.rem(place, LANES)
            piece = arrived[source, pl.ds(part, values, stride=parts), :]
            pieces.append((place - shift, shift, pltpu.roll(piece, shift, 1)))
        for tile, shift, rolled in pieces:
            here = pl.ds(pl.multiple_of(tile, LANES), LANES)
            after = pl.ds(pl.multiple_of(tile + LANES, LANES), LANES)
            pltpu.store(row.at[:, here], rolled, mask=lane >= shift)
            row[:, after] = rolled
        start = start + total
    for level in range(levels):
        owned[level] = row[level * ntr : (level + 1) * ntr, :columns]


def place_owned(arrived, own, levels, ntr, columns):
    vmem = pl.BlockSpec(memory_space=pltpu.VMEM)
    smem = pl.BlockSpec(memory_space=pltpu.SMEM)
    values = levels * ntr
    return pl.pallas_call(
        place_kernel,
        out_shape=jax.ShapeDtypeStruct((levels, ntr, columns), jnp.float32),
        in_specs=[smem, vmem],
        out_specs=vmem,
        scratch_shapes=[pltpu.VMEM((values, columns + 2 * LANES), jnp.float32)],
        compiler_params=pltpu.CompilerParams(vmem_limit_bytes=16 * MIB),
        name="place_owned",
    )(own, arrived.reshape(arrived.shape[0], -1, LANES))


def ring(axis, distance):
    size = lax.axis_size(axis)
    return [(i, (i + distance) % size) for i in range(size)]


def body(tracers, offsets, weights, diffusion, send_index, send_count):
    ntr, levels, lats, lons = tracers.shape
    columns = lats * lons
    west_cells, east_cells = pack_halo(tracers)
    from_west = lax.ppermute(east_cells, "lon", ring("lon", 1))
    from_east = lax.ppermute(west_cells, "lon", ring("lon", -1))
    *fields, lists = advect_inside(tracers, offsets, weights, diffusion, send_index, send_count)
    sent = make_sent(from_west, from_east, fields, lists)
    arrived = lax.all_to_all(sent, ("lon", "lat"), split_axis=0, concat_axis=0, tiled=True)
    own = lax.axis_index(("lon", "lat")).astype(jnp.int32).reshape(1)
    owned = place_owned(arrived, own, levels, ntr, columns)
    return jnp.transpose(owned, (1, 0, 2))


def solution(mesh):
    return jax.shard_map(
        body,
        mesh=mesh,
        in_specs=(
            P(None, None, "lat", "lon"),
            P(None, "lat", "lon"),
            P(None, "lat", "lon"),
            P(None, "lat", "lon"),
            P(("lon", "lat"), None, None),
            P(("lon", "lat"), None),
        ),
        out_specs=P(None, None, ("lon", "lat")),
        check_vma=False,
    )
```

```python
import functools

import jax
import jax.numpy as jnp
from jax import lax
from jax.experimental import pallas as pl
from jax.experimental.pallas import tpu as pltpu
from jax.sharding import PartitionSpec as P

HALO = 16
LANES = 128
SUB = 8
SLOT = 32
MIB = 1024 * 1024
LENGTH_BASE = 1000.0
BIG = 60 * MIB


def take_lanes(block, index):
    return jnp.take_along_axis(block, index, axis=1, mode="promise_in_bounds")


def lane_ids(rows):
    return lax.broadcasted_iota(jnp.int32, (rows, LANES), 1)


def pack_halo_kernel(tracers, west_cells, east_cells):
    ntr, levels, lats, _ = tracers.shape
    per_row = LANES // HALO
    group = lane_ids(SUB) // HALO

    def one_level(level, carry):
        for tracer in range(ntr):
            west = jnp.zeros((SUB, LANES), jnp.float32)
            east = jnp.zeros((SUB, LANES), jnp.float32)
            for part in range(lats // SUB):
                cells = tracers[tracer, level, part * SUB : (part + 1) * SUB, :]
                shift = part * HALO
                rolled_west = pltpu.roll(cells, shift, 1) if shift else cells
                shift = (part * HALO + HALO) % LANES
                rolled_east = pltpu.roll(cells, shift, 1) if shift else cells
                west = jnp.where(group == part, rolled_west, west)
                east = jnp.where(group == part, rolled_east, east)
            west_cells[level, tracer] = west
            east_cells[level, tracer] = east
        return carry

    assert lats == SUB * per_row
    lax.fori_loop(0, levels, one_level, 0)


def pack_halo(tracers):
    ntr, levels, _, _ = tracers.shape
    shape = jax.ShapeDtypeStruct((levels, ntr, SUB, LANES), jnp.float32)
    return pl.pallas_call(
        pack_halo_kernel,
        out_shape=(shape, shape),
        in_specs=[pl.BlockSpec(memory_space=pltpu.VMEM)],
        out_specs=[pl.BlockSpec(memory_space=pltpu.VMEM)] * 2,
        compiler_params=pltpu.CompilerParams(vmem_limit_bytes=16 * MIB),
        name="pack_halo",
    )(tracers)


def merge_halo(west, east, halo, count):
    lane = lane_ids(SUB)
    cell = lane % (2 * HALO)
    sources = [(half * 4 + lane // (2 * HALO)) * HALO + cell % HALO for half in range(2)]
    chunk = 5 if count % 5 == 0 else 1

    def some_values(step, carry):
        merged = []
        for item in range(chunk):
            value = step * chunk + item
            for half in range(2):
                both = take_lanes(west[value], sources[half]), take_lanes(east[value], sources[half])
                merged.append((value, half, jnp.where(cell < HALO, *both)))
        for value, half, cells in merged:
            halo[value, half] = cells
        return carry

    lax.fori_loop(0, count // chunk, some_values, 0)


def fetch(sources, targets, ready):
    copies = [
        pltpu.make_async_copy(source, target, ready.at[item])
        for item, (source, target) in enumerate(zip(sources, targets))
    ]
    for copy in copies:
        copy.start()
    return copies


def inside_kernel(
    tracers_in, offsets_in, weights_in, diffusion_in, index_in, count,
    inside, left_cell, west_edge, east_edge, lower, upper, lists,
    tracers, offsets, weights, diffusion, ready,
):
    ntr, levels, lats, _ = tracers.shape
    lane = lane_ids(SUB)
    owners = count.shape[1]
    copies = fetch(
        (diffusion_in, offsets_in, weights_in, tracers_in, index_in.at[0]),
        (diffusion, offsets, weights, tracers, lists.at[pl.ds(0, owners)]),
        ready,
    )
    lists[owners : owners + 1, :owners] = count[...]
    for copy in copies:
        copy.wait()

    def one_part(part, carry):
        rows = pl.ds(pl.multiple_of(part * SUB, SUB), SUB)
        coefs = [diffusion[level, rows, :] for level in range(levels - 1)]
        lowers, uppers, edges, results = [], [], [], []
        for level in range(levels):
            denom = 1.0
            if level > 0:
                denom = denom + coefs[level - 1]
            if level < levels - 1:
                denom = denom + coefs[level]
            if level > 0:
                denom = denom - coefs[level - 1] * uppers[level - 1]
            inverse = 1.0 / denom
            if level > 0:
                lowers.append(coefs[level - 1] * inverse)
            if level < levels - 1:
                uppers.append(coefs[level] * inverse)
            left = lane + offsets[level, rows, :]
            right = left + 1
            weight = weights[level, rows, :]
            west_weight = (1.0 - weight) * inverse
            east_weight = weight * inverse
            left_in = (left >= 0) & (left < LANES)
            right_in = (right >= 0) & (right < LANES)
            edges.append((left, jnp.where(left_in, 0.0, west_weight), jnp.where(right_in, 0.0, east_weight)))
            west_weight = jnp.where(left_in, west_weight, 0.0)
            east_weight = jnp.where(right_in, east_weight, 0.0)
            left = left & (LANES - 1)
            right = right & (LANES - 1)
            for tracer in range(ntr):
                cells = tracers[tracer, level, rows, :]
                results.append(west_weight * take_lanes(cells, left) + east_weight * take_lanes(cells, right))
        for value, result in enumerate(results):
            inside[value, rows, :] = result
        for level, (left, west_weight, east_weight) in enumerate(edges):
            left_cell[level, rows, :] = left
            west_edge[level, rows, :] = west_weight
            east_edge[level, rows, :] = east_weight
        for level in range(levels - 1):
            lower[level, rows, :] = lowers[level]
            upper[level, rows, :] = uppers[level]
        return carry

    lax.fori_loop(0, lats // SUB, one_part, 0)


def advect_inside(tracers, offsets, weights, diffusion, index, count):
    ntr, levels, lats, lons = tracers.shape
    lists, cap = index.shape[1:]
    vmem = pl.BlockSpec(memory_space=pltpu.VMEM)
    field = lambda count, kind=jnp.float32: jax.ShapeDtypeStruct((count, lats, lons), kind)
    outputs = (
        field(ntr * levels),
        field(levels, jnp.int32),
        field(levels),
        field(levels),
        field(levels - 1),
        field(levels - 1),
        jax.ShapeDtypeStruct((lists + SUB, cap), jnp.int32),
    )
    return pl.pallas_call(
        inside_kernel,
        out_shape=outputs,
        in_specs=[pl.BlockSpec(memory_space=pl.ANY)] * 5 + [vmem],
        out_specs=(vmem,) * len(outputs),
        scratch_shapes=[pltpu.VMEM(array.shape, array.dtype) for array in (tracers, offsets, weights, diffusion)]
        + [pltpu.SemaphoreType.DMA((5,))],
        compiler_params=pltpu.CompilerParams(vmem_limit_bytes=BIG),
        cost_estimate=pl.CostEstimate(flops=0, bytes_accessed=20 * MIB, transcendentals=0),
        name="advect_inside",
    )(tracers, offsets, weights, diffusion, index, count)


def add_edges_and_solve(inside, left_cell, west_edge, east_edge, lower, upper, halo, solved):
    levels, lats, _ = left_cell.shape
    ntr = inside.shape[0] // levels

    def one_part(part, carry):
        rows = pl.ds(pl.multiple_of(part * SUB, SUB), SUB)
        half = part // 4
        base = (part % 4) * (2 * HALO)
        reduced = [[] for _ in range(ntr)]
        for level in range(levels):
            left = left_cell[level, rows, :]
            right = base + ((left + (HALO + 1)) & (2 * HALO - 1))
            left = base + ((left + HALO) & (2 * HALO - 1))
            west_weight = west_edge[level, rows, :]
            east_weight = east_edge[level, rows, :]
            for tracer in range(ntr):
                value = level * ntr + tracer
                cells = halo[value, half]
                edges = west_weight * take_lanes(cells, left) + east_weight * take_lanes(cells, right)
                total = inside[value, rows, :] + edges
                if level > 0:
                    total = total + lower[level - 1, rows, :] * reduced[tracer][level - 1]
                reduced[tracer].append(total)
        results = []
        for tracer in range(ntr):
            x = reduced[tracer][levels - 1]
            for level in range(levels - 1, -1, -1):
                if level < levels - 1:
                    x = reduced[tracer][level] + upper[level, rows, :] * x
                results.append((level * ntr + tracer, x))
        for value, x in results:
            solved[pl.ds(part * SUB * SLOT + value, SUB, stride=SLOT), :] = x
        return carry

    lax.fori_loop(0, lats // SUB, one_part, 0)


def streams_of(rows, values, parts):
    lane = lane_ids(rows)
    width = values * parts
    item = sum((lane >= width * step).astype(jnp.int32) for step in range(1, 4 // parts))
    held = lane - item * width
    part = held & (parts - 1)
    return jnp.minimum(lax.shift_right_logical(held, parts.bit_length() - 1), values - 1), item * parts + part


def build_table(solved, table, values, parts):
    rows_per = LANES // SLOT
    spread = streams_of(LANES, values, parts)[0]
    together = 2

    def some_rows(step, carry):
        blocks = []
        for item in range(together):
            start = pl.multiple_of((step * together + item) * LANES, LANES)
            blocks.append(solved[pl.ds(start, LANES), :].T)
        for item, block in enumerate(blocks):
            for row in range(rows_per):
                start = pl.multiple_of(((step * together + item) * rows_per + row) * LANES, LANES)
                table[pl.ds(start, LANES), :] = take_lanes(block, spread + row * SLOT)
        return carry

    lax.fori_loop(0, solved.shape[0] // (LANES * together), some_rows, 0)


def pick_rows(table, index, count, cap, values, packed, turned, sent, copied, wait_list):
    blocks, height, _ = sent.shape
    parts = cap // LANES
    lists = 4 // parts
    stream = streams_of(1, values, parts)[1]
    together = 2 if blocks % 2 == 0 else 1

    def copy_out(block):
        return pltpu.make_async_copy(turned.at[block], sent.at[block], copied.at[block])

    def pick_block(block, item):
        owners = [block * lists + member for member in range(lists)]
        rows = [lax.div(count[owner] + (parts - 1), parts) for owner in owners]
        for owner in owners:
            wait_list(owner)
        longest = functools.reduce(jnp.maximum, rows)
        places = [owners[g // parts] * cap + (g % parts) * rows[g // parts] for g in range(4)]

        def pick_lines(start, lines):
            views = [index.at[pl.ds(place + start, lines)] for place in places]
            merged = []
            for line in range(lines):
                picked = [table[view[line]] for view in views]
                low = jnp.where(stream == 0, picked[0], picked[1])
                high = jnp.where(stream == 2, picked[2], picked[3])
                merged.append(jnp.where(stream < 2, low, high))
            first = pl.multiple_of(item * LANES + start, SUB)
            for line in range(lines):
                packed[pl.ds(first + line, 1), :] = merged[line]

        def steps(begin, trips, lines):
            def one_step(step, carry):
                pick_lines(pl.multiple_of(begin + step * lines, SUB), lines)
                return carry

            lax.fori_loop(0, trips, one_step, 0)
            return begin + trips * lines

        eights = lax.div(longest + (SUB - 1), SUB)
        done = steps(0, lax.div(eights, 4), 4 * SUB)
        done = steps(done, lax.div(lax.rem(eights, 4), 2), 2 * SUB)
        steps(done, lax.rem(eights, 2), SUB)

    def some_blocks(step, carry):
        for item in range(together):
            pick_block(step * together + item, item)
        results = [packed[item * LANES : (item + 1) * LANES, :].T for item in range(together)]
        for item in range(together):
            block = step * together + item
            turned[block] = results[item][:height, :]
            for member in range(lists):
                total = count[block * lists + member]
                row = turned.at[block, pl.ds((member * values + 1) * parts - 1, 1), :]
                note = jnp.full((1, LANES), LENGTH_BASE + total.astype(jnp.float32))
                pltpu.store(row, note, mask=(lane_ids(1) == LANES - 1) & (total < cap))
            copy_out(block).start()
        return carry

    def finish(block, carry):
        copy_out(block).wait()
        return carry

    lax.fori_loop(0, blocks // together, some_blocks, 0)
    lax.fori_loop(0, blocks, finish, 0)


def list_copies(lists_in, index, count, listed):
    owners = lists_in.shape[0] - SUB
    cap = lists_in.shape[1]
    lengths = pltpu.make_async_copy(lists_in.at[owners], count, listed.at[owners])

    def list_copy(item):
        place = pl.ds(pl.multiple_of(item * cap, LANES), cap)
        return pltpu.make_async_copy(lists_in.at[item], index.at[place], listed.at[item])

    def start_list(item, carry):
        list_copy(item).start()
        return carry

    lengths.start()
    lax.fori_loop(0, owners, start_list, 0)
    return lengths.wait, lambda item: list_copy(item).wait()


def solve_kernel(
    parts, west_in, east_in, inside_in, left_cell_in, west_edge_in, east_edge_in, lower_in, upper_in, lists_in,
    sent, west, east, inside, left_cell, west_edge, east_edge, lower, upper, ready,
    halo, solved, table, packed, turned, index, count, listed, copied,
):
    values, lats, _ = inside.shape
    sources = (west_in, east_in, left_cell_in, west_edge_in, east_edge_in, lower_in, upper_in, inside_in)
    copies = fetch(sources, (west, east, left_cell, west_edge, east_edge, lower, upper, inside), ready)
    wait_lengths, wait_list = list_copies(lists_in, index, count, listed)
    for value in range(values, SLOT):
        solved[pl.ds(value, lats, stride=SLOT), :] = jnp.zeros((lats, LANES), jnp.float32)
    for copy in copies[:2]:
        copy.wait()
    merge_halo(west, east, halo, values)
    for copy in copies[2:]:
        copy.wait()
    add_edges_and_solve(inside, left_cell, west_edge, east_edge, lower, upper, halo, solved)
    build_table(solved, table.reshape(table.shape[0], LANES), values, parts)
    wait_lengths()
    pick_rows(table, index, count, lists_in.shape[1], values, packed, turned, sent, copied, wait_list)


def make_sent(west, east, fields, lists_in):
    values, lats, lons = fields[0].shape
    lists, cap = lists_in.shape[0] - SUB, lists_in.shape[1]
    parts = cap // LANES
    blocks = lists * parts // 4
    inputs = (west.reshape(values, SUB, LANES), east.reshape(values, SUB, LANES), *fields)
    sent = pl.pallas_call(
        functools.partial(solve_kernel, parts),
        out_shape=jax.ShapeDtypeStruct((blocks, 4 * values, LANES), jnp.float32),
        in_specs=[pl.BlockSpec(memory_space=pl.ANY)] * (len(inputs) + 1),
        out_specs=pl.BlockSpec(memory_space=pl.ANY),
        scratch_shapes=[pltpu.VMEM(array.shape, array.dtype) for array in inputs]
        + [
            pltpu.SemaphoreType.DMA((len(inputs),)),
            pltpu.VMEM((values, 2, SUB, LANES), jnp.float32),
            pltpu.VMEM((lats * SLOT, LANES), jnp.float32),
            pltpu.VMEM((lats * lons, 1, LANES), jnp.float32),
            pltpu.VMEM((2 * LANES, LANES), jnp.float32),
            pltpu.VMEM((blocks, 4 * values, LANES), jnp.float32),
            pltpu.SMEM((lists * cap,), jnp.int32),
            pltpu.SMEM((cap,), jnp.int32),
            pltpu.SemaphoreType.DMA((lists + 1,)),
            pltpu.SemaphoreType.DMA((blocks,)),
        ],
        compiler_params=pltpu.CompilerParams(vmem_limit_bytes=BIG),
        cost_estimate=pl.CostEstimate(flops=0, bytes_accessed=40 * MIB, transcendentals=0),
        name="solve_pick",
    )(*inputs, lists_in)
    rows = values * parts
    tile = max(size for size in (1, 2, 4, 8) if rows % size == 0)
    return sent.reshape(lists, rows // tile, tile, LANES)


def place_kernel(own, arrived, owned, row):
    sources, height, _ = arrived.shape
    levels, ntr, columns = owned.shape
    values = levels * ntr
    parts = height // values
    lane = lax.broadcasted_iota(jnp.int32, (values, LANES), 1)
    order = [lax.rem(own[0] - turn + sources, sources) for turn in range(sources)]
    totals = []
    for source in order:
        note = arrived[source, parts - 1 : parts, :]
        total = jnp.where(note > 0.5 * LENGTH_BASE, note - LENGTH_BASE, 1.0 * parts * LANES)
        totals.append(total.astype(jnp.int32)[0, LANES - 1])
    start = 0
    for source, total in zip(order, totals):
        rows = lax.div(total + (parts - 1), parts)
        pieces = []
        for part in range(parts):
            place = start + jnp.minimum(part * rows, total)
            shift = lax.rem(place, LANES)
            piece = arrived[source, pl.ds(part, values, stride=parts), :]
            pieces.append((place - shift, shift, pltpu.roll(piece, shift, 1)))
        for tile, shift, rolled in pieces:
            here = pl.ds(pl.multiple_of(tile, LANES), LANES)
            after = pl.ds(pl.multiple_of(tile + LANES, LANES), LANES)
            pltpu.store(row.at[:, here], rolled, mask=lane >= shift)
            row[:, after] = rolled
        start = start + total
    for level in range(levels):
        owned[level] = row[level * ntr : (level + 1) * ntr, :columns]


def place_owned(arrived, own, levels, ntr, columns):
    vmem = pl.BlockSpec(memory_space=pltpu.VMEM)
    smem = pl.BlockSpec(memory_space=pltpu.SMEM)
    values = levels * ntr
    return pl.pallas_call(
        place_kernel,
        out_shape=jax.ShapeDtypeStruct((levels, ntr, columns), jnp.float32),
        in_specs=[smem, vmem],
        out_specs=vmem,
        scratch_shapes=[pltpu.VMEM((values, columns + 2 * LANES), jnp.float32)],
        compiler_params=pltpu.CompilerParams(vmem_limit_bytes=16 * MIB),
        name="place_owned",
    )(own, arrived.reshape(arrived.shape[0], -1, LANES))


def ring(axis, distance):
    size = lax.axis_size(axis)
    return [(i, (i + distance) % size) for i in range(size)]


def body(tracers, offsets, weights, diffusion, send_index, send_count):
    ntr, levels, lats, lons = tracers.shape
    columns = lats * lons
    west_cells, east_cells = pack_halo(tracers)
    from_west = lax.ppermute(east_cells, "lon", ring("lon", 1))
    from_east = lax.ppermute(west_cells, "lon", ring("lon", -1))
    *fields, lists = advect_inside(tracers, offsets, weights, diffusion, send_index, send_count)
    sent = make_sent(from_west, from_east, fields, lists)
    arrived = lax.all_to_all(sent, ("lon", "lat"), split_axis=0, concat_axis=0, tiled=True)
    own = lax.axis_index(("lon", "lat")).astype(jnp.int32).reshape(1)
    owned = place_owned(arrived, own, levels, ntr, columns)
    return jnp.transpose(owned, (1, 0, 2))


def solution(mesh):
    return jax.shard_map(
        body,
        mesh=mesh,
        in_specs=(
            P(None, None, "lat", "lon"),
            P(None, "lat", "lon"),
            P(None, "lat", "lon"),
            P(None, "lat", "lon"),
            P(("lon", "lat"), None, None),
            P(("lon", "lat"), None),
        ),
        out_specs=P(None, None, ("lon", "lat")),
        check_vma=False,
    )
```

```python
import functools

import jax
import jax.numpy as jnp
from jax import lax
from jax.experimental import pallas as pl
from jax.experimental.pallas import tpu as pltpu
from jax.sharding import PartitionSpec as P

HALO = 16
LANES = 128
SUB = 8
SLOT = 32
MIB = 1024 * 1024
LENGTH_BASE = 1000.0
BIG = 60 * MIB


def take_lanes(block, index):
    return jnp.take_along_axis(block, index, axis=1, mode="promise_in_bounds")


def lane_ids(rows):
    return lax.broadcasted_iota(jnp.int32, (rows, LANES), 1)


def pack_halo_kernel(tracers, west_cells, east_cells):
    ntr, levels, lats, _ = tracers.shape
    per_row = LANES // HALO
    group = lane_ids(SUB) // HALO

    def one_level(level, carry):
        for tracer in range(ntr):
            west = jnp.zeros((SUB, LANES), jnp.float32)
            east = jnp.zeros((SUB, LANES), jnp.float32)
            for part in range(lats // SUB):
                cells = tracers[tracer, level, part * SUB : (part + 1) * SUB, :]
                shift = part * HALO
                rolled_west = pltpu.roll(cells, shift, 1) if shift else cells
                shift = (part * HALO + HALO) % LANES
                rolled_east = pltpu.roll(cells, shift, 1) if shift else cells
                west = jnp.where(group == part, rolled_west, west)
                east = jnp.where(group == part, rolled_east, east)
            west_cells[level, tracer] = west
            east_cells[level, tracer] = east
        return carry

    assert lats == SUB * per_row
    lax.fori_loop(0, levels, one_level, 0)


def pack_halo(tracers):
    ntr, levels, _, _ = tracers.shape
    shape = jax.ShapeDtypeStruct((levels, ntr, SUB, LANES), jnp.float32)
    return pl.pallas_call(
        pack_halo_kernel,
        out_shape=(shape, shape),
        in_specs=[pl.BlockSpec(memory_space=pltpu.VMEM)],
        out_specs=[pl.BlockSpec(memory_space=pltpu.VMEM)] * 2,
        compiler_params=pltpu.CompilerParams(vmem_limit_bytes=16 * MIB),
        name="pack_halo",
    )(tracers)


def merge_halo(west, east, halo, count):
    lane = lane_ids(SUB)
    cell = lane % (2 * HALO)
    sources = [(half * 4 + lane // (2 * HALO)) * HALO + cell % HALO for half in range(2)]
    chunk = 5 if count % 5 == 0 else 1

    def some_values(step, carry):
        merged = []
        for item in range(chunk):
            value = step * chunk + item
            for half in range(2):
                both = take_lanes(west[value], sources[half]), take_lanes(east[value], sources[half])
                merged.append((value, half, jnp.where(cell < HALO, *both)))
        for value, half, cells in merged:
            halo[value, half] = cells
        return carry

    lax.fori_loop(0, count // chunk, some_values, 0)


def fetch(sources, targets, ready):
    copies = [
        pltpu.make_async_copy(source, target, ready.at[item])
        for item, (source, target) in enumerate(zip(sources, targets))
    ]
    for copy in copies:
        copy.start()
    return copies


def inside_kernel(
    tracers_in, offsets_in, weights_in, diffusion_in, index_in, count,
    inside, left_cell, west_edge, east_edge, lower, upper, lists,
    tracers, offsets, weights, diffusion, ready,
):
    ntr, levels, lats, _ = tracers.shape
    lane = lane_ids(SUB)
    owners = count.shape[1]
    copies = fetch(
        (diffusion_in, offsets_in, weights_in, tracers_in, index_in.at[0]),
        (diffusion, offsets, weights, tracers, lists.at[pl.ds(0, owners)]),
        ready,
    )
    lists[owners : owners + 1, :owners] = count[...]
    for copy in copies:
        copy.wait()

    def one_part(part, carry):
        rows = pl.ds(pl.multiple_of(part * SUB, SUB), SUB)
        coefs = [diffusion[level, rows, :] for level in range(levels - 1)]
        lowers, uppers, edges, results = [], [], [], []
        for level in range(levels):
            denom = 1.0
            if level > 0:
                denom = denom + coefs[level - 1]
            if level < levels - 1:
                denom = denom + coefs[level]
            if level > 0:
                denom = denom - coefs[level - 1] * uppers[level - 1]
            inverse = 1.0 / denom
            if level > 0:
                lowers.append(coefs[level - 1] * inverse)
            if level < levels - 1:
                uppers.append(coefs[level] * inverse)
            left = lane + offsets[level, rows, :]
            right = left + 1
            weight = weights[level, rows, :]
            west_weight = (1.0 - weight) * inverse
            east_weight = weight * inverse
            left_in = (left >= 0) & (left < LANES)
            right_in = (right >= 0) & (right < LANES)
            edges.append((left, jnp.where(left_in, 0.0, west_weight), jnp.where(right_in, 0.0, east_weight)))
            west_weight = jnp.where(left_in, west_weight, 0.0)
            east_weight = jnp.where(right_in, east_weight, 0.0)
            left = left & (LANES - 1)
            right = right & (LANES - 1)
            for tracer in range(ntr):
                cells = tracers[tracer, level, rows, :]
                results.append(west_weight * take_lanes(cells, left) + east_weight * take_lanes(cells, right))
        for value, result in enumerate(results):
            inside[value, rows, :] = result
        for level, (left, west_weight, east_weight) in enumerate(edges):
            left_cell[level, rows, :] = left
            west_edge[level, rows, :] = west_weight
            east_edge[level, rows, :] = east_weight
        for level in range(levels - 1):
            lower[level, rows, :] = lowers[level]
            upper[level, rows, :] = uppers[level]
        return carry

    lax.fori_loop(0, lats // SUB, one_part, 0)


def advect_inside(tracers, offsets, weights, diffusion, index, count):
    ntr, levels, lats, lons = tracers.shape
    lists, cap = index.shape[1:]
    vmem = pl.BlockSpec(memory_space=pltpu.VMEM)
    field = lambda count, kind=jnp.float32: jax.ShapeDtypeStruct((count, lats, lons), kind)
    outputs = (
        field(ntr * levels),
        field(levels, jnp.int32),
        field(levels),
        field(levels),
        field(levels - 1),
        field(levels - 1),
        jax.ShapeDtypeStruct((lists + SUB, cap), jnp.int32),
    )
    return pl.pallas_call(
        inside_kernel,
        out_shape=outputs,
        in_specs=[pl.BlockSpec(memory_space=pl.ANY)] * 5 + [vmem],
        out_specs=(vmem,) * len(outputs),
        scratch_shapes=[pltpu.VMEM(array.shape, array.dtype) for array in (tracers, offsets, weights, diffusion)]
        + [pltpu.SemaphoreType.DMA((5,))],
        compiler_params=pltpu.CompilerParams(vmem_limit_bytes=BIG),
        cost_estimate=pl.CostEstimate(flops=0, bytes_accessed=20 * MIB, transcendentals=0),
        name="advect_inside",
    )(tracers, offsets, weights, diffusion, index, count)


def add_edges_and_solve(inside, left_cell, west_edge, east_edge, lower, upper, halo, solved):
    levels, lats, _ = left_cell.shape
    ntr = inside.shape[0] // levels

    def one_part(part, carry):
        rows = pl.ds(pl.multiple_of(part * SUB, SUB), SUB)
        half = part // 4
        base = (part % 4) * (2 * HALO)
        reduced = [[] for _ in range(ntr)]
        for level in range(levels):
            left = left_cell[level, rows, :]
            right = base + ((left + (HALO + 1)) & (2 * HALO - 1))
            left = base + ((left + HALO) & (2 * HALO - 1))
            west_weight = west_edge[level, rows, :]
            east_weight = east_edge[level, rows, :]
            for tracer in range(ntr):
                value = level * ntr + tracer
                cells = halo[value, half]
                edges = west_weight * take_lanes(cells, left) + east_weight * take_lanes(cells, right)
                total = inside[value, rows, :] + edges
                if level > 0:
                    total = total + lower[level - 1, rows, :] * reduced[tracer][level - 1]
                reduced[tracer].append(total)
        results = []
        for tracer in range(ntr):
            x = reduced[tracer][levels - 1]
            for level in range(levels - 1, -1, -1):
                if level < levels - 1:
                    x = reduced[tracer][level] + upper[level, rows, :] * x
                results.append((level * ntr + tracer, x))
        target = solved.at[pl.ds(pl.multiple_of(part * (SUB * SLOT), SUB * SLOT), SUB * SLOT), :]
        for value, x in results:
            target[pl.ds(value, SUB, stride=SLOT), :] = x
        return carry

    lax.fori_loop(0, lats // SUB, one_part, 0)


def streams_of(rows, values, parts):
    lane = lane_ids(rows)
    width = values * parts
    item = sum((lane >= width * step).astype(jnp.int32) for step in range(1, 4 // parts))
    held = lane - item * width
    part = held & (parts - 1)
    return jnp.minimum(lax.shift_right_logical(held, parts.bit_length() - 1), values - 1), item * parts + part


def build_table(solved, table, values, parts):
    rows_per = LANES // SLOT
    spread = streams_of(LANES, values, parts)[0]
    together = 2

    def some_rows(step, carry):
        blocks = []
        for item in range(together):
            start = pl.multiple_of((step * together + item) * LANES, LANES)
            blocks.append(solved[pl.ds(start, LANES), :].T)
        for item, block in enumerate(blocks):
            for row in range(rows_per):
                start = pl.multiple_of(((step * together + item) * rows_per + row) * LANES, LANES)
                table[pl.ds(start, LANES), :] = take_lanes(block, spread + row * SLOT)
        return carry

    lax.fori_loop(0, solved.shape[0] // (LANES * together), some_rows, 0)


def pick_rows(table, index, count, cap, values, packed, turned, sent, copied, wait_list):
    blocks, height, _ = sent.shape
    parts = cap // LANES
    lists = 4 // parts
    stream = streams_of(1, values, parts)[1]
    together = 2 if blocks % 2 == 0 else 1

    def copy_out(block):
        return pltpu.make_async_copy(turned.at[block], sent.at[block], copied.at[block])

    def pick_block(block, item):
        owners = [block * lists + member for member in range(lists)]
        rows = [lax.div(count[owner] + (parts - 1), parts) for owner in owners]
        for owner in owners:
            wait_list(owner)
        longest = functools.reduce(jnp.maximum, rows)
        places = [owners[g // parts] * cap + (g % parts) * rows[g // parts] for g in range(4)]

        def pick_lines(start, lines):
            views = [index.at[pl.ds(place + start, lines)] for place in places]
            merged = []
            for line in range(lines):
                picked = [table[view[line]] for view in views]
                low = jnp.where(stream == 0, picked[0], picked[1])
                high = jnp.where(stream == 2, picked[2], picked[3])
                merged.append(jnp.where(stream < 2, low, high))
            target = packed.at[pl.ds(pl.multiple_of(item * LANES + start, SUB), lines), :]
            for line in range(lines):
                target[line : line + 1, :] = merged[line]

        def steps(begin, trips, lines):
            def one_step(step, carry):
                pick_lines(pl.multiple_of(begin + step * lines, SUB), lines)
                return carry

            lax.fori_loop(0, trips, one_step, 0)
            return begin + trips * lines

        eights = lax.div(longest + (SUB - 1), SUB)
        done = steps(0, lax.div(eights, 4), 4 * SUB)
        done = steps(done, lax.div(lax.rem(eights, 4), 2), 2 * SUB)
        steps(done, lax.rem(eights, 2), SUB)

    def some_blocks(step, carry):
        for item in range(together):
            pick_block(step * together + item, item)
        results = [packed[item * LANES : (item + 1) * LANES, :].T for item in range(together)]
        for item in range(together):
            block = step * together + item
            turned[block] = results[item][:height, :]
            for member in range(lists):
                total = count[block * lists + member]
                row = turned.at[block, pl.ds((member * values + 1) * parts - 1, 1), :]
                note = jnp.full((1, LANES), LENGTH_BASE + total.astype(jnp.float32))
                pltpu.store(row, note, mask=(lane_ids(1) == LANES - 1) & (total < cap))
            copy_out(block).start()
        return carry

    def finish(block, carry):
        copy_out(block).wait()
        return carry

    lax.fori_loop(0, blocks // together, some_blocks, 0)
    lax.fori_loop(0, blocks, finish, 0)


def list_copies(lists_in, index, count, listed):
    owners = lists_in.shape[0] - SUB
    cap = lists_in.shape[1]
    lengths = pltpu.make_async_copy(lists_in.at[owners], count, listed.at[owners])

    def list_copy(item):
        place = pl.ds(pl.multiple_of(item * cap, LANES), cap)
        return pltpu.make_async_copy(lists_in.at[item], index.at[place], listed.at[item])

    def start_list(item, carry):
        list_copy(item).start()
        return carry

    lengths.start()
    lax.fori_loop(0, owners, start_list, 0)
    return lengths.wait, lambda item: list_copy(item).wait()


def solve_kernel(
    parts, west_in, east_in, inside_in, left_cell_in, west_edge_in, east_edge_in, lower_in, upper_in, lists_in,
    sent, west, east, inside, left_cell, west_edge, east_edge, lower, upper, ready,
    halo, solved, table, packed, turned, index, count, listed, copied,
):
    values, lats, _ = inside.shape
    sources = (west_in, east_in, left_cell_in, west_edge_in, east_edge_in, lower_in, upper_in, inside_in)
    copies = fetch(sources, (west, east, left_cell, west_edge, east_edge, lower, upper, inside), ready)
    wait_lengths, wait_list = list_copies(lists_in, index, count, listed)
    for value in range(values, SLOT):
        solved[pl.ds(value, lats, stride=SLOT), :] = jnp.zeros((lats, LANES), jnp.float32)
    for copy in copies[:2]:
        copy.wait()
    merge_halo(west, east, halo, values)
    for copy in copies[2:]:
        copy.wait()
    add_edges_and_solve(inside, left_cell, west_edge, east_edge, lower, upper, halo, solved)
    build_table(solved, table.reshape(table.shape[0], LANES), values, parts)
    wait_lengths()
    pick_rows(table, index, count, lists_in.shape[1], values, packed, turned, sent, copied, wait_list)


def make_sent(west, east, fields, lists_in):
    values, lats, lons = fields[0].shape
    lists, cap = lists_in.shape[0] - SUB, lists_in.shape[1]
    parts = cap // LANES
    blocks = lists * parts // 4
    inputs = (west.reshape(values, SUB, LANES), east.reshape(values, SUB, LANES), *fields)
    sent = pl.pallas_call(
        functools.partial(solve_kernel, parts),
        out_shape=jax.ShapeDtypeStruct((blocks, 4 * values, LANES), jnp.float32),
        in_specs=[pl.BlockSpec(memory_space=pl.ANY)] * (len(inputs) + 1),
        out_specs=pl.BlockSpec(memory_space=pl.ANY),
        scratch_shapes=[pltpu.VMEM(array.shape, array.dtype) for array in inputs]
        + [
            pltpu.SemaphoreType.DMA((len(inputs),)),
            pltpu.VMEM((values, 2, SUB, LANES), jnp.float32),
            pltpu.VMEM((lats * SLOT, LANES), jnp.float32),
            pltpu.VMEM((lats * lons, 1, LANES), jnp.float32),
            pltpu.VMEM((2 * LANES, LANES), jnp.float32),
            pltpu.VMEM((blocks, 4 * values, LANES), jnp.float32),
            pltpu.SMEM((lists * cap,), jnp.int32),
            pltpu.SMEM((cap,), jnp.int32),
            pltpu.SemaphoreType.DMA((lists + 1,)),
            pltpu.SemaphoreType.DMA((blocks,)),
        ],
        compiler_params=pltpu.CompilerParams(vmem_limit_bytes=BIG),
        cost_estimate=pl.CostEstimate(flops=0, bytes_accessed=40 * MIB, transcendentals=0),
        name="solve_pick",
    )(*inputs, lists_in)
    rows = values * parts
    tile = max(size for size in (1, 2, 4, 8) if rows % size == 0)
    return sent.reshape(lists, rows // tile, tile, LANES)


def place_kernel(own, arrived, owned, row):
    sources, height, _ = arrived.shape
    levels, ntr, columns = owned.shape
    values = levels * ntr
    parts = height // values
    lane = lax.broadcasted_iota(jnp.int32, (values, LANES), 1)
    order = [lax.rem(own[0] - turn + sources, sources) for turn in range(sources)]
    totals = []
    for source in order:
        note = arrived[source, parts - 1 : parts, :]
        total = jnp.where(note > 0.5 * LENGTH_BASE, note - LENGTH_BASE, 1.0 * parts * LANES)
        totals.append(total.astype(jnp.int32)[0, LANES - 1])
    start = 0
    for source, total in zip(order, totals):
        rows = lax.div(total + (parts - 1), parts)
        pieces = []
        for part in range(parts):
            place = start + jnp.minimum(part * rows, total)
            shift = lax.rem(place, LANES)
            piece = arrived[source, pl.ds(part, values, stride=parts), :]
            pieces.append((place - shift, shift, pltpu.roll(piece, shift, 1)))
        for tile, shift, rolled in pieces:
            here = pl.ds(pl.multiple_of(tile, LANES), LANES)
            after = pl.ds(pl.multiple_of(tile + LANES, LANES), LANES)
            pltpu.store(row.at[:, here], rolled, mask=lane >= shift)
            row[:, after] = rolled
        start = start + total
    for level in range(levels):
        owned[level] = row[level * ntr : (level + 1) * ntr, :columns]


def place_owned(arrived, own, levels, ntr, columns):
    vmem = pl.BlockSpec(memory_space=pltpu.VMEM)
    smem = pl.BlockSpec(memory_space=pltpu.SMEM)
    values = levels * ntr
    return pl.pallas_call(
        place_kernel,
        out_shape=jax.ShapeDtypeStruct((levels, ntr, columns), jnp.float32),
        in_specs=[smem, vmem],
        out_specs=vmem,
        scratch_shapes=[pltpu.VMEM((values, columns + 2 * LANES), jnp.float32)],
        compiler_params=pltpu.CompilerParams(vmem_limit_bytes=16 * MIB),
        name="place_owned",
    )(own, arrived.reshape(arrived.shape[0], -1, LANES))


def ring(axis, distance):
    size = lax.axis_size(axis)
    return [(i, (i + distance) % size) for i in range(size)]


def body(tracers, offsets, weights, diffusion, send_index, send_count):
    ntr, levels, lats, lons = tracers.shape
    columns = lats * lons
    west_cells, east_cells = pack_halo(tracers)
    from_west = lax.ppermute(east_cells, "lon", ring("lon", 1))
    from_east = lax.ppermute(west_cells, "lon", ring("lon", -1))
    *fields, lists = advect_inside(tracers, offsets, weights, diffusion, send_index, send_count)
    sent = make_sent(from_west, from_east, fields, lists)
    arrived = lax.all_to_all(sent, ("lon", "lat"), split_axis=0, concat_axis=0, tiled=True)
    own = lax.axis_index(("lon", "lat")).astype(jnp.int32).reshape(1)
    owned = place_owned(arrived, own, levels, ntr, columns)
    return jnp.transpose(owned, (1, 0, 2))


def solution(mesh):
    return jax.shard_map(
        body,
        mesh=mesh,
        in_specs=(
            P(None, None, "lat", "lon"),
            P(None, "lat", "lon"),
            P(None, "lat", "lon"),
            P(None, "lat", "lon"),
            P(("lon", "lat"), None, None),
            P(("lon", "lat"), None),
        ),
        out_specs=P(None, None, ("lon", "lat")),
        check_vma=False,
    )
```

```python
import functools

import jax
import jax.numpy as jnp
from jax import lax
from jax.experimental import pallas as pl
from jax.experimental.pallas import tpu as pltpu
from jax.sharding import Mesh, PartitionSpec as P

HALO = 16
LON = ("half", "rest")
LANES = 128
SUB = 8
SLOT = 32
MIB = 1024 * 1024
LENGTH_BASE = 1000.0
BIG = 60 * MIB


def take_lanes(block, index):
    return jnp.take_along_axis(block, index, axis=1, mode="promise_in_bounds")


def lane_ids(rows):
    return lax.broadcasted_iota(jnp.int32, (rows, LANES), 1)


def pack_halo_kernel(tracers, west_cells, east_cells):
    ntr, levels, lats, _ = tracers.shape
    per_row = LANES // HALO
    group = lane_ids(SUB) // HALO

    def one_level(level, carry):
        for tracer in range(ntr):
            west = jnp.zeros((SUB, LANES), jnp.float32)
            east = jnp.zeros((SUB, LANES), jnp.float32)
            for part in range(lats // SUB):
                cells = tracers[tracer, level, part * SUB : (part + 1) * SUB, :]
                shift = part * HALO
                rolled_west = pltpu.roll(cells, shift, 1) if shift else cells
                shift = (part * HALO + HALO) % LANES
                rolled_east = pltpu.roll(cells, shift, 1) if shift else cells
                west = jnp.where(group == part, rolled_west, west)
                east = jnp.where(group == part, rolled_east, east)
            west_cells[level, tracer] = west
            east_cells[level, tracer] = east
        return carry

    assert lats == SUB * per_row
    lax.fori_loop(0, levels, one_level, 0)


def pack_halo(tracers):
    ntr, levels, _, _ = tracers.shape
    shape = jax.ShapeDtypeStruct((levels, ntr, SUB, LANES), jnp.float32)
    return pl.pallas_call(
        pack_halo_kernel,
        out_shape=(shape, shape),
        in_specs=[pl.BlockSpec(memory_space=pltpu.VMEM)],
        out_specs=[pl.BlockSpec(memory_space=pltpu.VMEM)] * 2,
        compiler_params=pltpu.CompilerParams(vmem_limit_bytes=16 * MIB),
        name="pack_halo",
    )(tracers)


def merge_halo(west, east, halo, count):
    lane = lane_ids(SUB)
    cell = lane % (2 * HALO)
    sources = [(half * 4 + lane // (2 * HALO)) * HALO + cell % HALO for half in range(2)]
    chunk = 5 if count % 5 == 0 else 1

    def some_values(step, carry):
        merged = []
        for item in range(chunk):
            value = step * chunk + item
            for half in range(2):
                both = take_lanes(west[value], sources[half]), take_lanes(east[value], sources[half])
                merged.append((value, half, jnp.where(cell < HALO, *both)))
        for value, half, cells in merged:
            halo[value, half] = cells
        return carry

    lax.fori_loop(0, count // chunk, some_values, 0)


def fetch(sources, targets, ready):
    copies = [
        pltpu.make_async_copy(source, target, ready.at[item])
        for item, (source, target) in enumerate(zip(sources, targets))
    ]
    for copy in copies:
        copy.start()
    return copies


def inside_kernel(
    tracers_in, offsets_in, weights_in, diffusion_in, index_in, count,
    inside, left_cell, west_edge, east_edge, lower, upper, lists,
    tracers, offsets, weights, diffusion, ready,
):
    ntr, levels, lats, _ = tracers.shape
    lane = lane_ids(SUB)
    owners = count.shape[1]
    copies = fetch(
        (diffusion_in, offsets_in, weights_in, tracers_in, index_in.at[0]),
        (diffusion, offsets, weights, tracers, lists.at[pl.ds(0, owners)]),
        ready,
    )
    lists[owners : owners + 1, :owners] = count[...]
    for copy in copies:
        copy.wait()

    def one_part(part, carry):
        rows = pl.ds(pl.multiple_of(part * SUB, SUB), SUB)
        coefs = [diffusion[level, rows, :] for level in range(levels - 1)]
        lowers, uppers, edges, results = [], [], [], []
        for level in range(levels):
            denom = 1.0
            if level > 0:
                denom = denom + coefs[level - 1]
            if level < levels - 1:
                denom = denom + coefs[level]
            if level > 0:
                denom = denom - coefs[level - 1] * uppers[level - 1]
            inverse = 1.0 / denom
            if level > 0:
                lowers.append(coefs[level - 1] * inverse)
            if level < levels - 1:
                uppers.append(coefs[level] * inverse)
            left = lane + offsets[level, rows, :]
            right = left + 1
            weight = weights[level, rows, :]
            west_weight = (1.0 - weight) * inverse
            east_weight = weight * inverse
            left_in = (left >= 0) & (left < LANES)
            right_in = (right >= 0) & (right < LANES)
            edges.append((left, jnp.where(left_in, 0.0, west_weight), jnp.where(right_in, 0.0, east_weight)))
            west_weight = jnp.where(left_in, west_weight, 0.0)
            east_weight = jnp.where(right_in, east_weight, 0.0)
            left = left & (LANES - 1)
            right = right & (LANES - 1)
            for tracer in range(ntr):
                cells = tracers[tracer, level, rows, :]
                results.append(west_weight * take_lanes(cells, left) + east_weight * take_lanes(cells, right))
        for value, result in enumerate(results):
            inside[value, rows, :] = result
        for level, (left, west_weight, east_weight) in enumerate(edges):
            left_cell[level, rows, :] = left
            west_edge[level, rows, :] = west_weight
            east_edge[level, rows, :] = east_weight
        for level in range(levels - 1):
            lower[level, rows, :] = lowers[level]
            upper[level, rows, :] = uppers[level]
        return carry

    lax.fori_loop(0, lats // SUB, one_part, 0)


def advect_inside(tracers, offsets, weights, diffusion, index, count):
    ntr, levels, lats, lons = tracers.shape
    lists, cap = index.shape[1:]
    vmem = pl.BlockSpec(memory_space=pltpu.VMEM)
    field = lambda count, kind=jnp.float32: jax.ShapeDtypeStruct((count, lats, lons), kind)
    outputs = (
        field(ntr * levels),
        field(levels, jnp.int32),
        field(levels),
        field(levels),
        field(levels - 1),
        field(levels - 1),
        jax.ShapeDtypeStruct((lists + SUB, cap), jnp.int32),
    )
    return pl.pallas_call(
        inside_kernel,
        out_shape=outputs,
        in_specs=[pl.BlockSpec(memory_space=pl.ANY)] * 5 + [vmem],
        out_specs=(vmem,) * len(outputs),
        scratch_shapes=[pltpu.VMEM(array.shape, array.dtype) for array in (tracers, offsets, weights, diffusion)]
        + [pltpu.SemaphoreType.DMA((5,))],
        compiler_params=pltpu.CompilerParams(vmem_limit_bytes=BIG),
        cost_estimate=pl.CostEstimate(flops=0, bytes_accessed=20 * MIB, transcendentals=0),
        name="advect_inside",
    )(tracers, offsets, weights, diffusion, index, count)


def add_edges_and_solve(inside, left_cell, west_edge, east_edge, lower, upper, halo, solved):
    levels, lats, _ = left_cell.shape
    ntr = inside.shape[0] // levels

    def one_part(part, carry):
        rows = pl.ds(pl.multiple_of(part * SUB, SUB), SUB)
        half = part // 4
        base = (part % 4) * (2 * HALO)
        reduced = [[] for _ in range(ntr)]
        for level in range(levels):
            left = left_cell[level, rows, :]
            right = base + ((left + (HALO + 1)) & (2 * HALO - 1))
            left = base + ((left + HALO) & (2 * HALO - 1))
            west_weight = west_edge[level, rows, :]
            east_weight = east_edge[level, rows, :]
            for tracer in range(ntr):
                value = level * ntr + tracer
                cells = halo[value, half]
                edges = west_weight * take_lanes(cells, left) + east_weight * take_lanes(cells, right)
                total = inside[value, rows, :] + edges
                if level > 0:
                    total = total + lower[level - 1, rows, :] * reduced[tracer][level - 1]
                reduced[tracer].append(total)
        results = []
        for tracer in range(ntr):
            x = reduced[tracer][levels - 1]
            for level in range(levels - 1, -1, -1):
                if level < levels - 1:
                    x = reduced[tracer][level] + upper[level, rows, :] * x
                results.append((level * ntr + tracer, x))
        target = solved.at[pl.ds(pl.multiple_of(part * (SUB * SLOT), SUB * SLOT), SUB * SLOT), :]
        for value, x in results:
            target[pl.ds(value, SUB, stride=SLOT), :] = x
        return carry

    lax.fori_loop(0, lats // SUB, one_part, 0)


def streams_of(rows, values, parts):
    lane = lane_ids(rows)
    width = values * parts
    item = sum((lane >= width * step).astype(jnp.int32) for step in range(1, 4 // parts))
    held = lane - item * width
    part = held & (parts - 1)
    return jnp.minimum(lax.shift_right_logical(held, parts.bit_length() - 1), values - 1), item * parts + part


def build_table(solved, table, values, parts):
    rows_per = LANES // SLOT
    spread = streams_of(LANES, values, parts)[0]
    together = 2

    def some_rows(step, carry):
        blocks = []
        for item in range(together):
            start = pl.multiple_of((step * together + item) * LANES, LANES)
            blocks.append(solved[pl.ds(start, LANES), :].T)
        for item, block in enumerate(blocks):
            for row in range(rows_per):
                start = pl.multiple_of(((step * together + item) * rows_per + row) * LANES, LANES)
                table[pl.ds(start, LANES), :] = take_lanes(block, spread + row * SLOT)
        return carry

    lax.fori_loop(0, solved.shape[0] // (LANES * together), some_rows, 0)


def owner_at(place, devices):
    return lax.rem(place, 2) * (devices // 2) + lax.div(place, 2)


def pick_rows(table, index, count, cap, values, packed, turned, sent, copied, wait_list):
    blocks, height, _ = sent.shape
    parts = cap // LANES
    lists = 4 // parts
    stream = streams_of(1, values, parts)[1]
    together = 2 if blocks % 2 == 0 else 1

    def copy_out(block):
        return pltpu.make_async_copy(turned.at[block], sent.at[block], copied.at[block])

    def pick_block(block, item):
        owners = [owner_at(block * lists + member, index.shape[0] // cap) for member in range(lists)]
        rows = [lax.div(count[owner] + (parts - 1), parts) for owner in owners]
        for owner in owners:
            wait_list(owner)
        longest = functools.reduce(jnp.maximum, rows)
        places = [owners[g // parts] * cap + (g % parts) * rows[g // parts] for g in range(4)]

        def pick_lines(start, lines):
            views = [index.at[pl.ds(place + start, lines)] for place in places]
            merged = []
            for line in range(lines):
                picked = [table[view[line]] for view in views]
                low = jnp.where(stream == 0, picked[0], picked[1])
                high = jnp.where(stream == 2, picked[2], picked[3])
                merged.append(jnp.where(stream < 2, low, high))
            target = packed.at[pl.ds(pl.multiple_of(item * LANES + start, SUB), lines), :]
            for line in range(lines):
                target[line : line + 1, :] = merged[line]

        def steps(begin, trips, lines):
            def one_step(step, carry):
                pick_lines(pl.multiple_of(begin + step * lines, SUB), lines)
                return carry

            lax.fori_loop(0, trips, one_step, 0)
            return begin + trips * lines

        eights = lax.div(longest + (SUB - 1), SUB)
        done = steps(0, lax.div(eights, 4), 4 * SUB)
        done = steps(done, lax.div(lax.rem(eights, 4), 2), 2 * SUB)
        steps(done, lax.rem(eights, 2), SUB)

    def some_blocks(step, carry):
        for item in range(together):
            pick_block(step * together + item, item)
        results = [packed[item * LANES : (item + 1) * LANES, :].T for item in range(together)]
        for item in range(together):
            block = step * together + item
            turned[block] = results[item][:height, :]
            for member in range(lists):
                total = count[owner_at(block * lists + member, index.shape[0] // cap)]
                row = turned.at[block, pl.ds((member * values + 1) * parts - 1, 1), :]
                note = jnp.full((1, LANES), LENGTH_BASE + total.astype(jnp.float32))
                pltpu.store(row, note, mask=(lane_ids(1) == LANES - 1) & (total < cap))
            copy_out(block).start()
        return carry

    def finish(block, carry):
        copy_out(block).wait()
        return carry

    lax.fori_loop(0, blocks // together, some_blocks, 0)
    lax.fori_loop(0, blocks, finish, 0)


def list_copies(lists_in, index, count, listed):
    owners = lists_in.shape[0] - SUB
    cap = lists_in.shape[1]
    lengths = pltpu.make_async_copy(lists_in.at[owners], count, listed.at[owners])

    def list_copy(item):
        place = pl.ds(pl.multiple_of(item * cap, LANES), cap)
        return pltpu.make_async_copy(lists_in.at[item], index.at[place], listed.at[item])

    def start_list(item, carry):
        list_copy(item).start()
        return carry

    lengths.start()
    lax.fori_loop(0, owners, start_list, 0)
    return lengths.wait, lambda item: list_copy(item).wait()


def solve_kernel(
    parts, west_in, east_in, inside_in, left_cell_in, west_edge_in, east_edge_in, lower_in, upper_in, lists_in,
    sent, west, east, inside, left_cell, west_edge, east_edge, lower, upper, ready,
    halo, solved, table, packed, turned, index, count, listed, copied,
):
    values, lats, _ = inside.shape
    sources = (west_in, east_in, left_cell_in, west_edge_in, east_edge_in, lower_in, upper_in, inside_in)
    copies = fetch(sources, (west, east, left_cell, west_edge, east_edge, lower, upper, inside), ready)
    wait_lengths, wait_list = list_copies(lists_in, index, count, listed)
    for value in range(values, SLOT):
        solved[pl.ds(value, lats, stride=SLOT), :] = jnp.zeros((lats, LANES), jnp.float32)
    for copy in copies[:2]:
        copy.wait()
    merge_halo(west, east, halo, values)
    for copy in copies[2:]:
        copy.wait()
    add_edges_and_solve(inside, left_cell, west_edge, east_edge, lower, upper, halo, solved)
    build_table(solved, table.reshape(table.shape[0], LANES), values, parts)
    wait_lengths()
    pick_rows(table, index, count, lists_in.shape[1], values, packed, turned, sent, copied, wait_list)


def make_sent(west, east, fields, lists_in):
    values, lats, lons = fields[0].shape
    lists, cap = lists_in.shape[0] - SUB, lists_in.shape[1]
    parts = cap // LANES
    blocks = lists * parts // 4
    inputs = (west.reshape(values, SUB, LANES), east.reshape(values, SUB, LANES), *fields)
    sent = pl.pallas_call(
        functools.partial(solve_kernel, parts),
        out_shape=jax.ShapeDtypeStruct((blocks, 4 * values, LANES), jnp.float32),
        in_specs=[pl.BlockSpec(memory_space=pl.ANY)] * (len(inputs) + 1),
        out_specs=pl.BlockSpec(memory_space=pl.ANY),
        scratch_shapes=[pltpu.VMEM(array.shape, array.dtype) for array in inputs]
        + [
            pltpu.SemaphoreType.DMA((len(inputs),)),
            pltpu.VMEM((values, 2, SUB, LANES), jnp.float32),
            pltpu.VMEM((lats * SLOT, LANES), jnp.float32),
            pltpu.VMEM((lats * lons, 1, LANES), jnp.float32),
            pltpu.VMEM((2 * LANES, LANES), jnp.float32),
            pltpu.VMEM((blocks, 4 * values, LANES), jnp.float32),
            pltpu.SMEM((lists * cap,), jnp.int32),
            pltpu.SMEM((cap,), jnp.int32),
            pltpu.SemaphoreType.DMA((lists + 1,)),
            pltpu.SemaphoreType.DMA((blocks,)),
        ],
        compiler_params=pltpu.CompilerParams(vmem_limit_bytes=BIG),
        cost_estimate=pl.CostEstimate(flops=0, bytes_accessed=40 * MIB, transcendentals=0),
        name="solve_pick",
    )(*inputs, lists_in)
    rows = values * parts
    tile = max(size for size in (1, 2, 4, 8) if rows % size == 0)
    return sent.reshape(lists, rows // tile, tile, LANES)


def place_kernel(own, arrived, owned, row):
    sources, height, _ = arrived.shape
    levels, ntr, columns = owned.shape
    values = levels * ntr
    parts = height // values
    lane = lax.broadcasted_iota(jnp.int32, (values, LANES), 1)
    order = [lax.rem(own[0] - turn + sources, sources) for turn in range(sources)]
    order = [2 * lax.rem(source, sources // 2) + lax.div(source, sources // 2) for source in order]
    totals = []
    for source in order:
        note = arrived[source, parts - 1 : parts, :]
        total = jnp.where(note > 0.5 * LENGTH_BASE, note - LENGTH_BASE, 1.0 * parts * LANES)
        totals.append(total.astype(jnp.int32)[0, LANES - 1])
    start = 0
    for source, total in zip(order, totals):
        rows = lax.div(total + (parts - 1), parts)
        pieces = []
        for part in range(parts):
            place = start + jnp.minimum(part * rows, total)
            shift = lax.rem(place, LANES)
            piece = arrived[source, pl.ds(part, values, stride=parts), :]
            pieces.append((place - shift, shift, pltpu.roll(piece, shift, 1)))
        for tile, shift, rolled in pieces:
            here = pl.ds(pl.multiple_of(tile, LANES), LANES)
            after = pl.ds(pl.multiple_of(tile + LANES, LANES), LANES)
            pltpu.store(row.at[:, here], rolled, mask=lane >= shift)
            row[:, after] = rolled
        start = start + total
    for level in range(levels):
        owned[level] = row[level * ntr : (level + 1) * ntr, :columns]


def place_owned(arrived, own, levels, ntr, columns):
    vmem = pl.BlockSpec(memory_space=pltpu.VMEM)
    smem = pl.BlockSpec(memory_space=pltpu.SMEM)
    values = levels * ntr
    return pl.pallas_call(
        place_kernel,
        out_shape=jax.ShapeDtypeStruct((levels, ntr, columns), jnp.float32),
        in_specs=[smem, vmem],
        out_specs=vmem,
        scratch_shapes=[pltpu.VMEM((values, columns + 2 * LANES), jnp.float32)],
        compiler_params=pltpu.CompilerParams(vmem_limit_bytes=16 * MIB),
        name="place_owned",
    )(own, arrived.reshape(arrived.shape[0], -1, LANES))


def ring(axis, distance):
    size = lax.axis_size(axis)
    return [(i, (i + distance) % size) for i in range(size)]


def body(tracers, offsets, weights, diffusion, send_index, send_count):
    ntr, levels, lats, lons = tracers.shape
    columns = lats * lons
    west_cells, east_cells = pack_halo(tracers)
    from_west = lax.ppermute(east_cells, LON, ring(LON, 1))
    from_east = lax.ppermute(west_cells, LON, ring(LON, -1))
    *fields, lists = advect_inside(tracers, offsets, weights, diffusion, send_index, send_count)
    sent = make_sent(from_west, from_east, fields, lists)
    arrived = lax.all_to_all(sent, ("rest", "lat", "half"), split_axis=0, concat_axis=0, tiled=True)
    own = lax.axis_index((*LON, "lat")).astype(jnp.int32).reshape(1)
    owned = place_owned(arrived, own, levels, ntr, columns)
    return jnp.transpose(owned, (1, 0, 2))


def solution(mesh):
    devices = mesh.devices.reshape(2, mesh.shape["lon"] // 2, mesh.shape["lat"])
    return jax.shard_map(
        body,
        mesh=Mesh(devices, (*LON, "lat")),
        in_specs=(
            P(None, None, "lat", LON),
            P(None, "lat", LON),
            P(None, "lat", LON),
            P(None, "lat", LON),
            P((*LON, "lat"), None, None),
            P((*LON, "lat"), None),
        ),
        out_specs=P(None, None, (*LON, "lat")),
        check_vma=False,
    )
```

```python
import functools

import jax
import jax.numpy as jnp
from jax import lax
from jax.experimental import pallas as pl
from jax.experimental.pallas import tpu as pltpu
from jax.sharding import PartitionSpec as P

HALO = 16
LANES = 128
SUB = 8
SLOT = 32
FIRST = 32
MIB = 1024 * 1024
LENGTH_BASE = 1000.0
BIG = 60 * MIB


def take_lanes(block, index):
    return jnp.take_along_axis(block, index, axis=1, mode="promise_in_bounds")


def lane_ids(rows):
    return lax.broadcasted_iota(jnp.int32, (rows, LANES), 1)


def fetch(sources, targets, ready):
    copies = [
        pltpu.make_async_copy(source, target, ready.at[item])
        for item, (source, target) in enumerate(zip(sources, targets))
    ]
    for copy in copies:
        copy.start()
    return copies


def pack_halo_kernel(tracers_in, west_cells, east_cells, tracers, ready):
    ntr, levels, lats, _ = tracers.shape
    per_row = LANES // HALO
    group = lane_ids(SUB) // HALO
    assert lats == SUB * per_row
    copies = fetch(
        [tracers_in.at[:, level] for level in range(levels)],
        [tracers.at[:, level] for level in range(levels)],
        ready,
    )
    for level in range(levels):
        copies[level].wait()
        for tracer in range(ntr):
            west = jnp.zeros((SUB, LANES), jnp.float32)
            east = jnp.zeros((SUB, LANES), jnp.float32)
            for part in range(lats // SUB):
                cells = tracers[tracer, level, part * SUB : (part + 1) * SUB, :]
                shift = part * HALO
                rolled_west = pltpu.roll(cells, shift, 1) if shift else cells
                shift = (part * HALO + HALO) % LANES
                rolled_east = pltpu.roll(cells, shift, 1) if shift else cells
                west = jnp.where(group == part, rolled_west, west)
                east = jnp.where(group == part, rolled_east, east)
            west_cells[level, tracer] = west
            east_cells[level, tracer] = east


def pack_halo(tracers):
    ntr, levels, _, _ = tracers.shape
    shape = jax.ShapeDtypeStruct((levels, ntr, SUB, LANES), jnp.float32)
    return pl.pallas_call(
        pack_halo_kernel,
        out_shape=(shape, shape),
        in_specs=[pl.BlockSpec(memory_space=pl.ANY)],
        out_specs=[pl.BlockSpec(memory_space=pltpu.VMEM)] * 2,
        scratch_shapes=[pltpu.VMEM(tracers.shape, jnp.float32), pltpu.SemaphoreType.DMA((levels,))],
        compiler_params=pltpu.CompilerParams(vmem_limit_bytes=BIG),
        name="pack_halo",
    )(tracers)


def merge_halo(west, east, halo, count):
    lane = lane_ids(SUB)
    cell = lane % (2 * HALO)
    sources = [(half * 4 + lane // (2 * HALO)) * HALO + cell % HALO for half in range(2)]
    chunk = 5 if count % 5 == 0 else 1

    def some_values(step, carry):
        merged = []
        for item in range(chunk):
            value = step * chunk + item
            for half in range(2):
                both = take_lanes(west[value], sources[half]), take_lanes(east[value], sources[half])
                merged.append((value, half, jnp.where(cell < HALO, *both)))
        for value, half, cells in merged:
            halo[value, half] = cells
        return carry

    lax.fori_loop(0, count // chunk, some_values, 0)


def inside_kernel(
    tracers_in, offsets_in, weights_in, diffusion_in, index_in, count,
    inside, left_cell, west_edge, east_edge, lower, upper, lists,
    tracers, offsets, weights, diffusion, ready,
):
    ntr, levels, lats, _ = tracers.shape
    lane = lane_ids(SUB)
    owners = count.shape[1]
    copies = fetch(
        (diffusion_in, offsets_in, weights_in, tracers_in, index_in.at[0]),
        (diffusion, offsets, weights, tracers, lists.at[pl.ds(0, owners)]),
        ready,
    )
    lists[owners : owners + 1, :owners] = count[...]
    for copy in copies:
        copy.wait()

    def one_part(part, carry):
        rows = pl.ds(pl.multiple_of(part * SUB, SUB), SUB)
        coefs = [diffusion[level, rows, :] for level in range(levels - 1)]
        lowers, uppers, edges, results = [], [], [], []
        for level in range(levels):
            denom = 1.0
            if level > 0:
                denom = denom + coefs[level - 1]
            if level < levels - 1:
                denom = denom + coefs[level]
            if level > 0:
                denom = denom - coefs[level - 1] * uppers[level - 1]
            inverse = 1.0 / denom
            if level > 0:
                lowers.append(coefs[level - 1] * inverse)
            if level < levels - 1:
                uppers.append(coefs[level] * inverse)
            left = lane + offsets[level, rows, :]
            right = left + 1
            weight = weights[level, rows, :]
            west_weight = (1.0 - weight) * inverse
            east_weight = weight * inverse
            left_in = (left >= 0) & (left < LANES)
            right_in = (right >= 0) & (right < LANES)
            edges.append((left, jnp.where(left_in, 0.0, west_weight), jnp.where(right_in, 0.0, east_weight)))
            west_weight = jnp.where(left_in, west_weight, 0.0)
            east_weight = jnp.where(right_in, east_weight, 0.0)
            left = left & (LANES - 1)
            right = right & (LANES - 1)
            for tracer in range(ntr):
                cells = tracers[tracer, level, rows, :]
                results.append(west_weight * take_lanes(cells, left) + east_weight * take_lanes(cells, right))
        for value, result in enumerate(results):
            inside[value, rows, :] = result
        for level, (left, west_weight, east_weight) in enumerate(edges):
            left_cell[level, rows, :] = left
            west_edge[level, rows, :] = west_weight
            east_edge[level, rows, :] = east_weight
        for level in range(levels - 1):
            lower[level, rows, :] = lowers[level]
            upper[level, rows, :] = uppers[level]
        return carry

    lax.fori_loop(0, lats // SUB, one_part, 0)


def advect_inside(tracers, offsets, weights, diffusion, index, count):
    ntr, levels, lats, lons = tracers.shape
    lists, cap = index.shape[1:]
    vmem = pl.BlockSpec(memory_space=pltpu.VMEM)
    field = lambda count, kind=jnp.float32: jax.ShapeDtypeStruct((count, lats, lons), kind)
    outputs = (
        field(ntr * levels),
        field(levels, jnp.int32),
        field(levels),
        field(levels),
        field(levels - 1),
        field(levels - 1),
        jax.ShapeDtypeStruct((lists + SUB, cap), jnp.int32),
    )
    return pl.pallas_call(
        inside_kernel,
        out_shape=outputs,
        in_specs=[pl.BlockSpec(memory_space=pl.ANY)] * 5 + [vmem],
        out_specs=(vmem,) * len(outputs),
        scratch_shapes=[pltpu.VMEM(array.shape, array.dtype) for array in (tracers, offsets, weights, diffusion)]
        + [pltpu.SemaphoreType.DMA((5,))],
        compiler_params=pltpu.CompilerParams(vmem_limit_bytes=BIG),
        cost_estimate=pl.CostEstimate(flops=0, bytes_accessed=20 * MIB, transcendentals=0),
        name="advect_inside",
    )(tracers, offsets, weights, diffusion, index, count)


def add_edges_and_solve(inside, left_cell, west_edge, east_edge, lower, upper, halo, solved):
    levels, lats, _ = left_cell.shape
    ntr = inside.shape[0] // levels
    together = 2

    def solve_part(part):
        rows = pl.ds(pl.multiple_of(part * SUB, SUB), SUB)
        half = part // 4
        base = (part % 4) * (2 * HALO)
        reduced = [[] for _ in range(ntr)]
        for level in range(levels):
            left = left_cell[level, rows, :]
            right = base + ((left + (HALO + 1)) & (2 * HALO - 1))
            left = base + ((left + HALO) & (2 * HALO - 1))
            west_weight = west_edge[level, rows, :]
            east_weight = east_edge[level, rows, :]
            for tracer in range(ntr):
                value = level * ntr + tracer
                cells = halo[value, half]
                edges = west_weight * take_lanes(cells, left) + east_weight * take_lanes(cells, right)
                total = inside[value, rows, :] + edges
                if level > 0:
                    total = total + lower[level - 1, rows, :] * reduced[tracer][level - 1]
                reduced[tracer].append(total)
        results = {}
        for level in range(levels - 1, -1, -1):
            for tracer in range(ntr):
                x = reduced[tracer][level]
                if level < levels - 1:
                    x = x + upper[level, rows, :] * results[(level + 1) * ntr + tracer]
                results[level * ntr + tracer] = x
        return results

    def some_parts(step, carry):
        solutions = [solve_part(step * together + item) for item in range(together)]
        for item, results in enumerate(solutions):
            first = pl.multiple_of((step * together + item) * (SUB * SLOT), SUB * SLOT)
            target = solved.at[pl.ds(first, SUB * SLOT), :]
            for value, x in results.items():
                target[pl.ds(value, SUB, stride=SLOT), :] = x
        return carry

    lax.fori_loop(0, lats // (SUB * together), some_parts, 0)


def streams_of(rows, values, parts):
    lane = lane_ids(rows)
    width = values * parts
    item = sum((lane >= width * step).astype(jnp.int32) for step in range(1, 4 // parts))
    held = lane - item * width
    part = held & (parts - 1)
    return jnp.minimum(lax.shift_right_logical(held, parts.bit_length() - 1), values - 1), item * parts + part


def build_table(solved, table, values, parts):
    rows_per = LANES // SLOT
    spread = streams_of(LANES, values, parts)[0]
    together = 4

    def some_rows(step, carry):
        blocks = []
        for item in range(together):
            start = pl.multiple_of((step * together + item) * LANES, LANES)
            blocks.append(solved[pl.ds(start, LANES), :].T)
        for item, block in enumerate(blocks):
            for row in range(rows_per):
                start = pl.multiple_of(((step * together + item) * rows_per + row) * LANES, LANES)
                table[pl.ds(start, LANES), :] = take_lanes(block, spread + row * SLOT)
        return carry

    lax.fori_loop(0, solved.shape[0] // (LANES * together), some_rows, 0)


def pick_rows(table, index, count, cap, values, packed, turned, sent, copied, wait_list):
    blocks, height, _ = sent.shape
    parts = cap // LANES
    lists = 4 // parts
    stream = streams_of(1, values, parts)[1]

    def copy_out(block):
        return pltpu.make_async_copy(turned.at[block + 1], sent.at[block], copied.at[block])

    def turn(block):
        half = pl.multiple_of(lax.rem(block + 2, 2) * LANES, LANES)
        return packed[pl.ds(half, LANES), :].T

    def send(block, result):
        turned[block + 1] = result[:height, :]
        for member in range(lists):
            total = count[jnp.maximum(block, 0) * lists + member]
            row = turned.at[block + 1, pl.ds((member * values + 1) * parts - 1, 1), :]
            note = jnp.full((1, LANES), LENGTH_BASE + total.astype(jnp.float32))
            pltpu.store(row, note, mask=(lane_ids(1) == LANES - 1) & (total < cap))

    def one_block(block, carry):
        owners = [block * lists + member for member in range(lists)]
        rows = [lax.div(count[owner] + (parts - 1), parts) for owner in owners]
        for owner in owners:
            wait_list(owner)
        longest = functools.reduce(jnp.maximum, rows)
        places = [owners[g // parts] * cap + (g % parts) * rows[g // parts] for g in range(4)]
        half = lax.rem(block, 2) * LANES

        def load_lines(start, lines):
            views = [index.at[pl.ds(place + start, lines)] for place in places]
            merged = []
            for line in range(lines):
                picked = [table[view[line]] for view in views]
                low = jnp.where(stream == 0, picked[0], picked[1])
                high = jnp.where(stream == 2, picked[2], picked[3])
                merged.append(jnp.where(stream < 2, low, high))
            return merged

        def store_lines(start, merged):
            target = packed.at[pl.ds(pl.multiple_of(half + start, SUB), len(merged)), :]
            for line, value in enumerate(merged):
                target[line : line + 1, :] = value

        def steps(begin, trips, lines):
            def one_step(step, inner):
                start = pl.multiple_of(begin + step * lines, SUB)
                store_lines(start, load_lines(start, lines))
                return inner

            lax.fori_loop(0, trips, one_step, 0)
            return begin + trips * lines

        before = turn(block - 1)
        merged = load_lines(0, FIRST)
        store_lines(0, merged)
        send(block - 1, before)

        @pl.when(block > 0)
        def _():
            copy_out(block - 1).start()

        eights = jnp.maximum(lax.div(longest + (SUB - 1), SUB) - FIRST // SUB, 0)
        done = steps(FIRST, lax.div(eights, 4), 4 * SUB)
        done = steps(done, lax.div(lax.rem(eights, 4), 2), 2 * SUB)
        steps(done, lax.rem(eights, 2), SUB)
        return carry

    def finish(block, carry):
        copy_out(block).wait()
        return carry

    lax.fori_loop(0, blocks, one_block, 0)
    send(blocks - 1, turn(blocks - 1))
    copy_out(blocks - 1).start()
    lax.fori_loop(0, blocks, finish, 0)


def list_copies(lists_in, index, count, listed):
    owners = lists_in.shape[0] - SUB
    cap = lists_in.shape[1]
    lengths = pltpu.make_async_copy(lists_in.at[owners], count, listed.at[owners])

    def list_copy(item):
        place = pl.ds(pl.multiple_of(item * cap, LANES), cap)
        return pltpu.make_async_copy(lists_in.at[item], index.at[place], listed.at[item])

    def start_list(item, carry):
        list_copy(item).start()
        return carry

    lengths.start()
    lax.fori_loop(0, owners, start_list, 0)
    return lengths.wait, lambda item: list_copy(item).wait()


def solve_kernel(
    parts, west_in, east_in, inside_in, left_cell_in, west_edge_in, east_edge_in, lower_in, upper_in, lists_in,
    sent, west, east, inside, left_cell, west_edge, east_edge, lower, upper, ready,
    halo, solved, table, packed, turned, index, count, listed, copied,
):
    values, lats, _ = inside.shape
    sources = (west_in, east_in, left_cell_in, west_edge_in, east_edge_in, lower_in, upper_in, inside_in)
    copies = fetch(sources, (west, east, left_cell, west_edge, east_edge, lower, upper, inside), ready)
    wait_lengths, wait_list = list_copies(lists_in, index, count, listed)
    for value in range(values, SLOT):
        solved[pl.ds(value, lats, stride=SLOT), :] = jnp.zeros((lats, LANES), jnp.float32)
    for copy in copies[:2]:
        copy.wait()
    merge_halo(west, east, halo, values)
    for copy in copies[2:]:
        copy.wait()
    add_edges_and_solve(inside, left_cell, west_edge, east_edge, lower, upper, halo, solved)
    build_table(solved, table.reshape(table.shape[0], LANES), values, parts)
    wait_lengths()
    pick_rows(table, index, count, lists_in.shape[1], values, packed, turned, sent, copied, wait_list)


def make_sent(west, east, fields, lists_in):
    values, lats, lons = fields[0].shape
    lists, cap = lists_in.shape[0] - SUB, lists_in.shape[1]
    parts = cap // LANES
    blocks = lists * parts // 4
    inputs = (west.reshape(values, SUB, LANES), east.reshape(values, SUB, LANES), *fields)
    sent = pl.pallas_call(
        functools.partial(solve_kernel, parts),
        out_shape=jax.ShapeDtypeStruct((blocks, 4 * values, LANES), jnp.float32),
        in_specs=[pl.BlockSpec(memory_space=pl.ANY)] * (len(inputs) + 1),
        out_specs=pl.BlockSpec(memory_space=pl.ANY),
        scratch_shapes=[pltpu.VMEM(array.shape, array.dtype) for array in inputs]
        + [
            pltpu.SemaphoreType.DMA((len(inputs),)),
            pltpu.VMEM((values, 2, SUB, LANES), jnp.float32),
            pltpu.VMEM((lats * SLOT, LANES), jnp.float32),
            pltpu.VMEM((lats * lons, 1, LANES), jnp.float32),
            pltpu.VMEM((2 * LANES, LANES), jnp.float32),
            pltpu.VMEM((blocks + 1, 4 * values, LANES), jnp.float32),
            pltpu.SMEM((lists * cap,), jnp.int32),
            pltpu.SMEM((cap,), jnp.int32),
            pltpu.SemaphoreType.DMA((lists + 1,)),
            pltpu.SemaphoreType.DMA((blocks,)),
        ],
        compiler_params=pltpu.CompilerParams(vmem_limit_bytes=BIG),
        cost_estimate=pl.CostEstimate(flops=0, bytes_accessed=40 * MIB, transcendentals=0),
        name="solve_pick",
    )(*inputs, lists_in)
    rows = values * parts
    tile = max(size for size in (1, 2, 4, 8) if rows % size == 0)
    return sent.reshape(lists, rows // tile, tile, LANES)


def place_kernel(own, arrived, owned, row):
    sources, height, _ = arrived.shape
    levels, ntr, columns = owned.shape
    values = levels * ntr
    parts = height // values
    lane = lax.broadcasted_iota(jnp.int32, (values, LANES), 1)
    order = [lax.rem(own[0] - turn + sources, sources) for turn in range(sources)]
    totals = []
    for source in order:
        note = arrived[source, parts - 1 : parts, :]
        total = jnp.where(note > 0.5 * LENGTH_BASE, note - LENGTH_BASE, 1.0 * parts * LANES)
        totals.append(total.astype(jnp.int32)[0, LANES - 1])
    start = 0
    for source, total in zip(order, totals):
        rows = lax.div(total + (parts - 1), parts)
        pieces = []
        for part in range(parts):
            place = start + jnp.minimum(part * rows, total)
            shift = lax.rem(place, LANES)
            piece = arrived[source, pl.ds(part, values, stride=parts), :]
            pieces.append((place - shift, shift, pltpu.roll(piece, shift, 1)))
        for tile, shift, rolled in pieces:
            here = pl.ds(pl.multiple_of(tile, LANES), LANES)
            after = pl.ds(pl.multiple_of(tile + LANES, LANES), LANES)
            pltpu.store(row.at[:, here], rolled, mask=lane >= shift)
            row[:, after] = rolled
        start = start + total
    for level in range(levels):
        owned[level] = row[level * ntr : (level + 1) * ntr, :columns]


def place_owned(arrived, own, levels, ntr, columns):
    vmem = pl.BlockSpec(memory_space=pltpu.VMEM)
    smem = pl.BlockSpec(memory_space=pltpu.SMEM)
    values = levels * ntr
    return pl.pallas_call(
        place_kernel,
        out_shape=jax.ShapeDtypeStruct((levels, ntr, columns), jnp.float32),
        in_specs=[smem, vmem],
        out_specs=vmem,
        scratch_shapes=[pltpu.VMEM((values, columns + 2 * LANES), jnp.float32)],
        compiler_params=pltpu.CompilerParams(vmem_limit_bytes=16 * MIB),
        name="place_owned",
    )(own, arrived.reshape(arrived.shape[0], -1, LANES))


def ring(axis, distance):
    size = lax.axis_size(axis)
    return [(i, (i + distance) % size) for i in range(size)]


def body(tracers, offsets, weights, diffusion, send_index, send_count):
    ntr, levels, lats, lons = tracers.shape
    columns = lats * lons
    west_cells, east_cells = pack_halo(tracers)
    from_west = lax.ppermute(east_cells, "lon", ring("lon", 1))
    from_east = lax.ppermute(west_cells, "lon", ring("lon", -1))
    *fields, lists = advect_inside(tracers, offsets, weights, diffusion, send_index, send_count)
    sent = make_sent(from_west, from_east, fields, lists)
    arrived = lax.all_to_all(sent, ("lon", "lat"), split_axis=0, concat_axis=0, tiled=True)
    own = lax.axis_index(("lon", "lat")).astype(jnp.int32).reshape(1)
    owned = place_owned(arrived, own, levels, ntr, columns)
    return jnp.transpose(owned, (1, 0, 2))


def solution(mesh):
    return jax.shard_map(
        body,
        mesh=mesh,
        in_specs=(
            P(None, None, "lat", "lon"),
            P(None, "lat", "lon"),
            P(None, "lat", "lon"),
            P(None, "lat", "lon"),
            P(("lon", "lat"), None, None),
            P(("lon", "lat"), None),
        ),
        out_specs=P(None, None, ("lon", "lat")),
        check_vma=False,
    )
```

```python
import functools

import jax
import jax.numpy as jnp
from jax import lax
from jax.experimental import pallas as pl
from jax.experimental.pallas import tpu as pltpu
from jax.sharding import PartitionSpec as P

HALO = 16
LANES = 128
SUB = 8
SLOT = 32
FIRST = 32
MIB = 1024 * 1024
LENGTH_BASE = 1000.0
BIG = 60 * MIB
SOLVE = 107 * MIB // 2
LIST_ROWS = 256


def take_lanes(block, index):
    return jnp.take_along_axis(block, index, axis=1, mode="promise_in_bounds")


def lane_ids(rows):
    return lax.broadcasted_iota(jnp.int32, (rows, LANES), 1)


def fetch(sources, targets, ready):
    copies = [
        pltpu.make_async_copy(source, target, ready.at[item])
        for item, (source, target) in enumerate(zip(sources, targets))
    ]
    for copy in copies:
        copy.start()
    return copies


def pack_halo_kernel(tracers, west_cells, east_cells):
    ntr, levels, lats, _ = tracers.shape
    per_row = LANES // HALO
    group = lane_ids(SUB) // HALO

    def one_level(level, carry):
        for tracer in range(ntr):
            west = jnp.zeros((SUB, LANES), jnp.float32)
            east = jnp.zeros((SUB, LANES), jnp.float32)
            for part in range(lats // SUB):
                cells = tracers[tracer, level, part * SUB : (part + 1) * SUB, :]
                shift = part * HALO
                rolled_west = pltpu.roll(cells, shift, 1) if shift else cells
                shift = (part * HALO + HALO) % LANES
                rolled_east = pltpu.roll(cells, shift, 1) if shift else cells
                west = jnp.where(group == part, rolled_west, west)
                east = jnp.where(group == part, rolled_east, east)
            west_cells[level, tracer] = west
            east_cells[level, tracer] = east
        return carry

    assert lats == SUB * per_row
    lax.fori_loop(0, levels, one_level, 0)


def pack_halo(tracers):
    ntr, levels, _, _ = tracers.shape
    shape = jax.ShapeDtypeStruct((levels, ntr, SUB, LANES), jnp.float32)
    return pl.pallas_call(
        pack_halo_kernel,
        out_shape=(shape, shape),
        in_specs=[pl.BlockSpec(memory_space=pltpu.VMEM)],
        out_specs=[pl.BlockSpec(memory_space=pltpu.VMEM)] * 2,
        compiler_params=pltpu.CompilerParams(vmem_limit_bytes=16 * MIB),
        name="pack_halo",
    )(tracers)


def merge_halo(west, east, halo, count):
    lane = lane_ids(SUB)
    cell = lane % (2 * HALO)
    sources = [(half * 4 + lane // (2 * HALO)) * HALO + cell % HALO for half in range(2)]
    chunk = 5 if count % 5 == 0 else 1

    def some_values(step, carry):
        merged = []
        for item in range(chunk):
            value = step * chunk + item
            for half in range(2):
                both = take_lanes(west[value], sources[half]), take_lanes(east[value], sources[half])
                merged.append((value, half, jnp.where(cell < HALO, *both)))
        for value, half, cells in merged:
            halo[value, half] = cells
        return carry

    lax.fori_loop(0, count // chunk, some_values, 0)


def inside_kernel(
    tracers_in, offsets_in, weights_in, diffusion_in, index_in, count,
    inside, left_cell, west_edge, east_edge, lower, upper, lists,
    tracers, offsets, weights, diffusion, ready,
):
    ntr, levels, lats, _ = tracers.shape
    lane = lane_ids(SUB)
    owners = count.shape[1]
    copies = fetch(
        (diffusion_in, offsets_in, weights_in, tracers_in, index_in.at[0]),
        (diffusion, offsets, weights, tracers, lists.at[pl.ds(0, owners)]),
        ready,
    )
    lists[owners : owners + 1, :owners] = count[...]
    for copy in copies:
        copy.wait()

    def one_part(part, carry):
        rows = pl.ds(pl.multiple_of(part * SUB, SUB), SUB)
        coefs = [diffusion[level, rows, :] for level in range(levels - 1)]
        lowers, uppers, edges, results = [], [], [], []
        for level in range(levels):
            denom = 1.0
            if level > 0:
                denom = denom + coefs[level - 1]
            if level < levels - 1:
                denom = denom + coefs[level]
            if level > 0:
                denom = denom - coefs[level - 1] * uppers[level - 1]
            inverse = 1.0 / denom
            if level > 0:
                lowers.append(coefs[level - 1] * inverse)
            if level < levels - 1:
                uppers.append(coefs[level] * inverse)
            left = lane + offsets[level, rows, :]
            right = left + 1
            weight = weights[level, rows, :]
            west_weight = (1.0 - weight) * inverse
            east_weight = weight * inverse
            left_in = (left >= 0) & (left < LANES)
            right_in = (right >= 0) & (right < LANES)
            edges.append((left, jnp.where(left_in, 0.0, west_weight), jnp.where(right_in, 0.0, east_weight)))
            west_weight = jnp.where(left_in, west_weight, 0.0)
            east_weight = jnp.where(right_in, east_weight, 0.0)
            left = left & (LANES - 1)
            right = right & (LANES - 1)
            for tracer in range(ntr):
                cells = tracers[tracer, level, rows, :]
                results.append(west_weight * take_lanes(cells, left) + east_weight * take_lanes(cells, right))
        for value, result in enumerate(results):
            inside[value, rows, :] = result
        for level, (left, west_weight, east_weight) in enumerate(edges):
            left_cell[level, rows, :] = left
            west_edge[level, rows, :] = west_weight
            east_edge[level, rows, :] = east_weight
        for level in range(levels - 1):
            lower[level, rows, :] = lowers[level]
            upper[level, rows, :] = uppers[level]
        return carry

    lax.fori_loop(0, lats // SUB, one_part, 0)


def advect_inside(tracers, offsets, weights, diffusion, index, count):
    ntr, levels, lats, lons = tracers.shape
    lists, cap = index.shape[1:]
    vmem = pl.BlockSpec(memory_space=pltpu.VMEM)
    field = lambda count, kind=jnp.float32: jax.ShapeDtypeStruct((count, lats, lons), kind)
    outputs = (
        field(ntr * levels),
        field(levels, jnp.int32),
        field(levels),
        field(levels),
        field(levels - 1),
        field(levels - 1),
        jax.ShapeDtypeStruct((max(lists + SUB, LIST_ROWS), cap), jnp.int32),
    )
    return pl.pallas_call(
        inside_kernel,
        out_shape=outputs,
        in_specs=[pl.BlockSpec(memory_space=pl.ANY)] * 5 + [vmem],
        out_specs=(vmem,) * len(outputs),
        scratch_shapes=[pltpu.VMEM(array.shape, array.dtype) for array in (tracers, offsets, weights, diffusion)]
        + [pltpu.SemaphoreType.DMA((5,))],
        compiler_params=pltpu.CompilerParams(vmem_limit_bytes=BIG),
        cost_estimate=pl.CostEstimate(flops=0, bytes_accessed=20 * MIB, transcendentals=0),
        name="advect_inside",
    )(tracers, offsets, weights, diffusion, index, count)


def add_edges_and_solve(inside, left_cell, west_edge, east_edge, lower, upper, halo, solved):
    levels, lats, _ = left_cell.shape
    ntr = inside.shape[0] // levels
    together = 2

    def solve_part(part):
        rows = pl.ds(pl.multiple_of(part * SUB, SUB), SUB)
        half = part // 4
        base = (part % 4) * (2 * HALO)
        reduced = [[] for _ in range(ntr)]
        for level in range(levels):
            left = left_cell[level, rows, :]
            right = base + ((left + (HALO + 1)) & (2 * HALO - 1))
            left = base + ((left + HALO) & (2 * HALO - 1))
            west_weight = west_edge[level, rows, :]
            east_weight = east_edge[level, rows, :]
            for tracer in range(ntr):
                value = level * ntr + tracer
                cells = halo[value, half]
                edges = west_weight * take_lanes(cells, left) + east_weight * take_lanes(cells, right)
                total = inside[value, rows, :] + edges
                if level > 0:
                    total = total + lower[level - 1, rows, :] * reduced[tracer][level - 1]
                reduced[tracer].append(total)
        results = {}
        for level in range(levels - 1, -1, -1):
            for tracer in range(ntr):
                x = reduced[tracer][level]
                if level < levels - 1:
                    x = x + upper[level, rows, :] * results[(level + 1) * ntr + tracer]
                results[level * ntr + tracer] = x
        return results

    def some_parts(step, carry):
        solutions = [solve_part(step * together + item) for item in range(together)]
        for item, results in enumerate(solutions):
            first = pl.multiple_of((step * together + item) * (SUB * SLOT), SUB * SLOT)
            target = solved.at[pl.ds(first, SUB * SLOT), :]
            for value, x in results.items():
                target[pl.ds(value, SUB, stride=SLOT), :] = x
        return carry

    lax.fori_loop(0, lats // (SUB * together), some_parts, 0)


def streams_of(rows, values, parts):
    lane = lane_ids(rows)
    width = values * parts
    item = sum((lane >= width * step).astype(jnp.int32) for step in range(1, 4 // parts))
    held = lane - item * width
    part = held & (parts - 1)
    return jnp.minimum(lax.shift_right_logical(held, parts.bit_length() - 1), values - 1), item * parts + part


def build_table(solved, table, values, parts):
    rows_per = LANES // SLOT
    spread = streams_of(LANES, values, parts)[0]
    together = 4

    def some_rows(step, carry):
        blocks = []
        for item in range(together):
            start = pl.multiple_of((step * together + item) * LANES, LANES)
            blocks.append(solved[pl.ds(start, LANES), :].T)
        for item, block in enumerate(blocks):
            for row in range(rows_per):
                start = pl.multiple_of(((step * together + item) * rows_per + row) * LANES, LANES)
                table[pl.ds(start, LANES), :] = take_lanes(block, spread + row * SLOT)
        return carry

    lax.fori_loop(0, solved.shape[0] // (LANES * together), some_rows, 0)


def pick_rows(table, index, count, cap, values, packed, turned, sent, copied, wait_list):
    blocks, height, _ = sent.shape
    parts = cap // LANES
    lists = 4 // parts
    stream = streams_of(1, values, parts)[1]

    def copy_out(block):
        return pltpu.make_async_copy(turned.at[block + 1], sent.at[block], copied.at[block])

    def turn(block):
        half = pl.multiple_of(lax.rem(block + 2, 2) * LANES, LANES)
        return packed[pl.ds(half, LANES), :].T

    def send(block, result):
        turned[block + 1] = result[:height, :]
        for member in range(lists):
            total = count[jnp.maximum(block, 0) * lists + member]
            row = turned.at[block + 1, pl.ds((member * values + 1) * parts - 1, 1), :]
            note = jnp.full((1, LANES), LENGTH_BASE + total.astype(jnp.float32))
            pltpu.store(row, note, mask=(lane_ids(1) == LANES - 1) & (total < cap))

    def one_block(block, carry):
        owners = [block * lists + member for member in range(lists)]
        rows = [lax.div(count[owner] + (parts - 1), parts) for owner in owners]
        for owner in owners:
            wait_list(owner)
        longest = functools.reduce(jnp.maximum, rows)
        places = [owners[g // parts] * cap + (g % parts) * rows[g // parts] for g in range(4)]
        half = lax.rem(block, 2) * LANES

        def load_lines(start, lines):
            views = [index.at[pl.ds(place + start, lines)] for place in places]
            merged = []
            for line in range(lines):
                picked = [table[view[line]] for view in views]
                low = jnp.where(stream == 0, picked[0], picked[1])
                high = jnp.where(stream == 2, picked[2], picked[3])
                merged.append(jnp.where(stream < 2, low, high))
            return merged

        def store_lines(start, merged):
            target = packed.at[pl.ds(pl.multiple_of(half + start, SUB), len(merged)), :]
            for line, value in enumerate(merged):
                target[line : line + 1, :] = value

        def steps(begin, trips, lines):
            def one_step(step, inner):
                start = pl.multiple_of(begin + step * lines, SUB)
                store_lines(start, load_lines(start, lines))
                return inner

            lax.fori_loop(0, trips, one_step, 0)
            return begin + trips * lines

        before = turn(block - 1)
        merged = load_lines(0, FIRST)
        store_lines(0, merged)
        send(block - 1, before)

        @pl.when(block > 0)
        def _():
            copy_out(block - 1).start()

        eights = jnp.maximum(lax.div(longest + (SUB - 1), SUB) - FIRST // SUB, 0)
        done = steps(FIRST, lax.div(eights, 4), 4 * SUB)
        done = steps(done, lax.div(lax.rem(eights, 4), 2), 2 * SUB)
        steps(done, lax.rem(eights, 2), SUB)
        return carry

    def finish(block, carry):
        copy_out(block).wait()
        return carry

    lax.fori_loop(0, blocks, one_block, 0)
    send(blocks - 1, turn(blocks - 1))
    copy_out(blocks - 1).start()
    lax.fori_loop(0, blocks, finish, 0)


def list_copies(lists_in, index, count, listed):
    cap = lists_in.shape[1]
    owners = index.shape[0] // cap
    lengths = pltpu.make_async_copy(lists_in.at[owners], count, listed.at[owners])

    def list_copy(item):
        place = pl.ds(pl.multiple_of(item * cap, LANES), cap)
        return pltpu.make_async_copy(lists_in.at[item], index.at[place], listed.at[item])

    def start_list(item, carry):
        list_copy(item).start()
        return carry

    lengths.start()
    lax.fori_loop(0, owners, start_list, 0)
    return lengths.wait, lambda item: list_copy(item).wait()


def solve_kernel(
    parts, west, east, inside_in, left_cell_in, west_edge_in, east_edge_in, lower_in, upper_in, lists_in,
    sent, inside, left_cell, west_edge, east_edge, lower, upper, ready,
    halo, solved, table, packed, turned, index, count, listed, copied,
):
    values, lats, _ = inside.shape
    sources = (left_cell_in, west_edge_in, east_edge_in, lower_in, upper_in, inside_in)
    copies = fetch(sources, (left_cell, west_edge, east_edge, lower, upper, inside), ready)
    wait_lengths, wait_list = list_copies(lists_in, index, count, listed)
    for value in range(values, SLOT):
        solved[pl.ds(value, lats, stride=SLOT), :] = jnp.zeros((lats, LANES), jnp.float32)
    merge_halo(west, east, halo, values)
    for copy in copies:
        copy.wait()
    add_edges_and_solve(inside, left_cell, west_edge, east_edge, lower, upper, halo, solved)
    build_table(solved, table.reshape(table.shape[0], LANES), values, parts)
    wait_lengths()
    pick_rows(table, index, count, lists_in.shape[1], values, packed, turned, sent, copied, wait_list)


def make_sent(west, east, fields, lists_in, lists):
    values, lats, lons = fields[0].shape
    cap = lists_in.shape[1]
    parts = cap // LANES
    blocks = lists * parts // 4
    halos = (west.reshape(values, SUB, LANES), east.reshape(values, SUB, LANES))
    sent = pl.pallas_call(
        functools.partial(solve_kernel, parts),
        out_shape=jax.ShapeDtypeStruct((blocks, 4 * values, LANES), jnp.float32),
        in_specs=[pl.BlockSpec(memory_space=pltpu.VMEM)] * 2 + [pl.BlockSpec(memory_space=pl.ANY)] * (len(fields) + 1),
        out_specs=pl.BlockSpec(memory_space=pl.ANY),
        scratch_shapes=[pltpu.VMEM(array.shape, array.dtype) for array in fields]
        + [
            pltpu.SemaphoreType.DMA((len(fields),)),
            pltpu.VMEM((values, 2, SUB, LANES), jnp.float32),
            pltpu.VMEM((lats * SLOT, LANES), jnp.float32),
            pltpu.VMEM((lats * lons, 1, LANES), jnp.float32),
            pltpu.VMEM((2 * LANES, LANES), jnp.float32),
            pltpu.VMEM((blocks + 1, 4 * values, LANES), jnp.float32),
            pltpu.SMEM((lists * cap,), jnp.int32),
            pltpu.SMEM((cap,), jnp.int32),
            pltpu.SemaphoreType.DMA((lists + 1,)),
            pltpu.SemaphoreType.DMA((blocks,)),
        ],
        compiler_params=pltpu.CompilerParams(vmem_limit_bytes=SOLVE),
        cost_estimate=pl.CostEstimate(flops=0, bytes_accessed=40 * MIB, transcendentals=0),
        name="solve_pick",
    )(*halos, *fields, lists_in)
    rows = values * parts
    tile = max(size for size in (1, 2, 4, 8) if rows % size == 0)
    return sent.reshape(lists, rows // tile, tile, LANES)


def place_kernel(own, arrived, owned, row):
    sources, height, _ = arrived.shape
    levels, ntr, columns = owned.shape
    values = levels * ntr
    parts = height // values
    lane = lax.broadcasted_iota(jnp.int32, (values, LANES), 1)
    order = [lax.rem(own[0] - turn + sources, sources) for turn in range(sources)]
    totals = []
    for source in order:
        note = arrived[source, parts - 1 : parts, :]
        total = jnp.where(note > 0.5 * LENGTH_BASE, note - LENGTH_BASE, 1.0 * parts * LANES)
        totals.append(total.astype(jnp.int32)[0, LANES - 1])
    start = 0
    for source, total in zip(order, totals):
        rows = lax.div(total + (parts - 1), parts)
        pieces = []
        for part in range(parts):
            place = start + jnp.minimum(part * rows, total)
            shift = lax.rem(place, LANES)
            piece = arrived[source, pl.ds(part, values, stride=parts), :]
            pieces.append((place - shift, shift, pltpu.roll(piece, shift, 1)))
        for tile, shift, rolled in pieces:
            here = pl.ds(pl.multiple_of(tile, LANES), LANES)
            after = pl.ds(pl.multiple_of(tile + LANES, LANES), LANES)
            pltpu.store(row.at[:, here], rolled, mask=lane >= shift)
            row[:, after] = rolled
        start = start + total
    for level in range(levels):
        owned[level] = row[level * ntr : (level + 1) * ntr, :columns]


def place_owned(arrived, own, levels, ntr, columns):
    vmem = pl.BlockSpec(memory_space=pltpu.VMEM)
    smem = pl.BlockSpec(memory_space=pltpu.SMEM)
    values = levels * ntr
    return pl.pallas_call(
        place_kernel,
        out_shape=jax.ShapeDtypeStruct((levels, ntr, columns), jnp.float32),
        in_specs=[smem, vmem],
        out_specs=vmem,
        scratch_shapes=[pltpu.VMEM((values, columns + 2 * LANES), jnp.float32)],
        compiler_params=pltpu.CompilerParams(vmem_limit_bytes=16 * MIB),
        name="place_owned",
    )(own, arrived.reshape(arrived.shape[0], -1, LANES))


def ring(axis, distance):
    size = lax.axis_size(axis)
    return [(i, (i + distance) % size) for i in range(size)]


def body(tracers, offsets, weights, diffusion, send_index, send_count):
    ntr, levels, lats, lons = tracers.shape
    columns = lats * lons
    west_cells, east_cells = pack_halo(tracers)
    from_west = lax.ppermute(east_cells, "lon", ring("lon", 1))
    from_east = lax.ppermute(west_cells, "lon", ring("lon", -1))
    *fields, lists = advect_inside(tracers, offsets, weights, diffusion, send_index, send_count)
    sent = make_sent(from_west, from_east, fields, lists, send_count.shape[1])
    arrived = lax.all_to_all(sent, ("lon", "lat"), split_axis=0, concat_axis=0, tiled=True)
    own = lax.axis_index(("lon", "lat")).astype(jnp.int32).reshape(1)
    owned = place_owned(arrived, own, levels, ntr, columns)
    return jnp.transpose(owned, (1, 0, 2))


def solution(mesh):
    return jax.shard_map(
        body,
        mesh=mesh,
        in_specs=(
            P(None, None, "lat", "lon"),
            P(None, "lat", "lon"),
            P(None, "lat", "lon"),
            P(None, "lat", "lon"),
            P(("lon", "lat"), None, None),
            P(("lon", "lat"), None),
        ),
        out_specs=P(None, None, ("lon", "lat")),
        check_vma=False,
    )
```

```python
import functools

import jax
import jax.numpy as jnp
from jax import lax
from jax.experimental import pallas as pl
from jax.experimental.pallas import tpu as pltpu
from jax.sharding import PartitionSpec as P

HALO = 16
LANES = 128
SUB = 8
SLOT = 32
FIRST = 32
MIB = 1024 * 1024
LENGTH_BASE = 1000.0
BIG = 60 * MIB
SOLVE = 107 * MIB // 2
LIST_ROWS = 256


def take_lanes(block, index):
    return jnp.take_along_axis(block, index, axis=1, mode="promise_in_bounds")


def lane_ids(rows):
    return lax.broadcasted_iota(jnp.int32, (rows, LANES), 1)


def fetch(sources, targets, ready):
    copies = [
        pltpu.make_async_copy(source, target, ready.at[item])
        for item, (source, target) in enumerate(zip(sources, targets))
    ]
    for copy in copies:
        copy.start()
    return copies


def pack_halo_kernel(tracers_in, west_cells, east_cells, tracers, ready):
    ntr, levels, lats, _ = tracers.shape
    per_row = LANES // HALO
    group = lane_ids(SUB) // HALO
    assert lats == SUB * per_row
    copies = fetch(
        [tracers_in.at[:, level] for level in range(levels)],
        [tracers.at[:, level] for level in range(levels)],
        ready,
    )
    for level in range(levels):
        copies[level].wait()
        for tracer in range(ntr):
            west = jnp.zeros((SUB, LANES), jnp.float32)
            east = jnp.zeros((SUB, LANES), jnp.float32)
            for part in range(lats // SUB):
                cells = tracers[tracer, level, part * SUB : (part + 1) * SUB, :]
                shift = part * HALO
                rolled_west = pltpu.roll(cells, shift, 1) if shift else cells
                shift = (part * HALO + HALO) % LANES
                rolled_east = pltpu.roll(cells, shift, 1) if shift else cells
                west = jnp.where(group == part, rolled_west, west)
                east = jnp.where(group == part, rolled_east, east)
            west_cells[level, tracer] = west
            east_cells[level, tracer] = east


def pack_halo(tracers):
    ntr, levels, _, _ = tracers.shape
    shape = jax.ShapeDtypeStruct((levels, ntr, SUB, LANES), jnp.float32)
    return pl.pallas_call(
        pack_halo_kernel,
        out_shape=(shape, shape),
        in_specs=[pl.BlockSpec(memory_space=pl.ANY)],
        out_specs=[pl.BlockSpec(memory_space=pltpu.VMEM)] * 2,
        scratch_shapes=[pltpu.VMEM(tracers.shape, jnp.float32), pltpu.SemaphoreType.DMA((levels,))],
        compiler_params=pltpu.CompilerParams(vmem_limit_bytes=SOLVE),
        name="pack_halo",
    )(tracers)


def merge_halo(west, east, halo, count):
    lane = lane_ids(SUB)
    cell = lane % (2 * HALO)
    sources = [(half * 4 + lane // (2 * HALO)) * HALO + cell % HALO for half in range(2)]
    chunk = 10 if count % 10 == 0 else 1

    def some_values(step, carry):
        merged = []
        for item in range(chunk):
            value = step * chunk + item
            for half in range(2):
                both = take_lanes(west[value], sources[half]), take_lanes(east[value], sources[half])
                merged.append((value, half, jnp.where(cell < HALO, *both)))
        for value, half, cells in merged:
            halo[value, half] = cells
        return carry

    lax.fori_loop(0, count // chunk, some_values, 0)


def inside_kernel(
    tracers_in, offsets_in, weights_in, diffusion_in, index_in, count,
    inside, left_cell, west_edge, east_edge, lower, upper, lists,
    tracers, offsets, weights, diffusion, ready,
):
    ntr, levels, lats, _ = tracers.shape
    lane = lane_ids(SUB)
    owners = count.shape[1]
    copies = fetch(
        (diffusion_in, offsets_in, weights_in, tracers_in, index_in.at[0]),
        (diffusion, offsets, weights, tracers, lists.at[pl.ds(0, owners)]),
        ready,
    )
    lists[owners : owners + 1, :owners] = count[...]
    for copy in copies:
        copy.wait()

    def one_part(part, carry):
        rows = pl.ds(pl.multiple_of(part * SUB, SUB), SUB)
        coefs = [diffusion[level, rows, :] for level in range(levels - 1)]
        lowers, uppers, edges, results = [], [], [], []
        for level in range(levels):
            denom = 1.0
            if level > 0:
                denom = denom + coefs[level - 1]
            if level < levels - 1:
                denom = denom + coefs[level]
            if level > 0:
                denom = denom - coefs[level - 1] * uppers[level - 1]
            inverse = 1.0 / denom
            if level > 0:
                lowers.append(coefs[level - 1] * inverse)
            if level < levels - 1:
                uppers.append(coefs[level] * inverse)
            left = lane + offsets[level, rows, :]
            right = left + 1
            weight = weights[level, rows, :]
            west_weight = (1.0 - weight) * inverse
            east_weight = weight * inverse
            left_in = (left >= 0) & (left < LANES)
            right_in = (right >= 0) & (right < LANES)
            edges.append((left, jnp.where(left_in, 0.0, west_weight), jnp.where(right_in, 0.0, east_weight)))
            west_weight = jnp.where(left_in, west_weight, 0.0)
            east_weight = jnp.where(right_in, east_weight, 0.0)
            left = left & (LANES - 1)
            right = right & (LANES - 1)
            for tracer in range(ntr):
                cells = tracers[tracer, level, rows, :]
                results.append(west_weight * take_lanes(cells, left) + east_weight * take_lanes(cells, right))
        for value, result in enumerate(results):
            inside[value, rows, :] = result
        for level, (left, west_weight, east_weight) in enumerate(edges):
            left_cell[level, rows, :] = left
            west_edge[level, rows, :] = west_weight
            east_edge[level, rows, :] = east_weight
        for level in range(levels - 1):
            lower[level, rows, :] = lowers[level]
            upper[level, rows, :] = uppers[level]
        return carry

    lax.fori_loop(0, lats // SUB, one_part, 0)


def advect_inside(tracers, offsets, weights, diffusion, index, count):
    ntr, levels, lats, lons = tracers.shape
    lists, cap = index.shape[1:]
    vmem = pl.BlockSpec(memory_space=pltpu.VMEM)
    field = lambda count, kind=jnp.float32: jax.ShapeDtypeStruct((count, lats, lons), kind)
    outputs = (
        field(ntr * levels),
        field(levels, jnp.int32),
        field(levels),
        field(levels),
        field(levels - 1),
        field(levels - 1),
        jax.ShapeDtypeStruct((max(lists + SUB, LIST_ROWS), cap), jnp.int32),
    )
    return pl.pallas_call(
        inside_kernel,
        out_shape=outputs,
        in_specs=[pl.BlockSpec(memory_space=pl.ANY)] * 5 + [vmem],
        out_specs=(vmem,) * len(outputs),
        scratch_shapes=[pltpu.VMEM(array.shape, array.dtype) for array in (tracers, offsets, weights, diffusion)]
        + [pltpu.SemaphoreType.DMA((5,))],
        compiler_params=pltpu.CompilerParams(vmem_limit_bytes=BIG),
        cost_estimate=pl.CostEstimate(flops=0, bytes_accessed=20 * MIB, transcendentals=0),
        name="advect_inside",
    )(tracers, offsets, weights, diffusion, index, count)


def add_edges_and_solve(inside, left_cell, west_edge, east_edge, lower, upper, halo, solved):
    levels, lats, _ = left_cell.shape
    ntr = inside.shape[0] // levels
    together = 2

    def solve_part(part):
        rows = pl.ds(pl.multiple_of(part * SUB, SUB), SUB)
        half = part // 4
        base = (part % 4) * (2 * HALO)
        reduced = [[] for _ in range(ntr)]
        for level in range(levels):
            left = left_cell[level, rows, :]
            right = base + ((left + (HALO + 1)) & (2 * HALO - 1))
            left = base + ((left + HALO) & (2 * HALO - 1))
            west_weight = west_edge[level, rows, :]
            east_weight = east_edge[level, rows, :]
            for tracer in range(ntr):
                value = level * ntr + tracer
                cells = halo[value, half]
                edges = west_weight * take_lanes(cells, left) + east_weight * take_lanes(cells, right)
                total = inside[value, rows, :] + edges
                if level > 0:
                    total = total + lower[level - 1, rows, :] * reduced[tracer][level - 1]
                reduced[tracer].append(total)
        results = {}
        for level in range(levels - 1, -1, -1):
            for tracer in range(ntr):
                x = reduced[tracer][level]
                if level < levels - 1:
                    x = x + upper[level, rows, :] * results[(level + 1) * ntr + tracer]
                results[level * ntr + tracer] = x
        return results

    def some_parts(step, carry):
        solutions = [solve_part(step * together + item) for item in range(together)]
        for item, results in enumerate(solutions):
            first = pl.multiple_of((step * together + item) * (SUB * SLOT), SUB * SLOT)
            target = solved.at[pl.ds(first, SUB * SLOT), :]
            for value, x in results.items():
                target[pl.ds(value, SUB, stride=SLOT), :] = x
        return carry

    lax.fori_loop(0, lats // (SUB * together), some_parts, 0)


def streams_of(rows, values, parts):
    lane = lane_ids(rows)
    width = values * parts
    item = sum((lane >= width * step).astype(jnp.int32) for step in range(1, 4 // parts))
    held = lane - item * width
    part = held & (parts - 1)
    return jnp.minimum(lax.shift_right_logical(held, parts.bit_length() - 1), values - 1), item * parts + part


def build_table(solved, table, values, parts):
    rows_per = LANES // SLOT
    spread = streams_of(LANES, values, parts)[0]
    together = 4

    def some_rows(step, carry):
        blocks = []
        for item in range(together):
            start = pl.multiple_of((step * together + item) * LANES, LANES)
            blocks.append(solved[pl.ds(start, LANES), :].T)
        for item, block in enumerate(blocks):
            for row in range(rows_per):
                start = pl.multiple_of(((step * together + item) * rows_per + row) * LANES, LANES)
                table[pl.ds(start, LANES), :] = take_lanes(block, spread + row * SLOT)
        return carry

    lax.fori_loop(0, solved.shape[0] // (LANES * together), some_rows, 0)


def pick_rows(table, index, count, cap, values, packed, turned, sent, copied, wait_list):
    blocks, height, _ = sent.shape
    parts = cap // LANES
    lists = 4 // parts
    stream = streams_of(1, values, parts)[1]

    def copy_out(block):
        return pltpu.make_async_copy(turned.at[block + 1], sent.at[block], copied.at[block])

    def turn(block):
        half = pl.multiple_of(lax.rem(block + 2, 2) * LANES, LANES)
        return packed[pl.ds(half, LANES), :].T

    def send(block, result):
        turned[block + 1] = result[:height, :]
        for member in range(lists):
            total = count[jnp.maximum(block, 0) * lists + member]
            row = turned.at[block + 1, pl.ds((member * values + 1) * parts - 1, 1), :]
            note = jnp.full((1, LANES), LENGTH_BASE + total.astype(jnp.float32))
            pltpu.store(row, note, mask=(lane_ids(1) == LANES - 1) & (total < cap))

    def one_block(block, carry):
        owners = [block * lists + member for member in range(lists)]
        rows = [lax.div(count[owner] + (parts - 1), parts) for owner in owners]
        for owner in owners:
            wait_list(owner)
        longest = functools.reduce(jnp.maximum, rows)
        places = [owners[g // parts] * cap + (g % parts) * rows[g // parts] for g in range(4)]
        half = lax.rem(block, 2) * LANES

        def load_lines(start, lines):
            views = [index.at[pl.ds(place + start, lines)] for place in places]
            merged = []
            for line in range(lines):
                picked = [table[view[line]] for view in views]
                low = jnp.where(stream == 0, picked[0], picked[1])
                high = jnp.where(stream == 2, picked[2], picked[3])
                merged.append(jnp.where(stream < 2, low, high))
            return merged

        def store_lines(start, merged):
            target = packed.at[pl.ds(pl.multiple_of(half + start, SUB), len(merged)), :]
            for line, value in enumerate(merged):
                target[line : line + 1, :] = value

        def steps(begin, trips, lines):
            def one_step(step, inner):
                start = pl.multiple_of(begin + step * lines, SUB)
                store_lines(start, load_lines(start, lines))
                return inner

            lax.fori_loop(0, trips, one_step, 0)
            return begin + trips * lines

        before = turn(block - 1)
        merged = load_lines(0, FIRST)
        store_lines(0, merged)
        send(block - 1, before)

        @pl.when(block > 0)
        def _():
            copy_out(block - 1).start()

        eights = jnp.maximum(lax.div(longest + (SUB - 1), SUB) - FIRST // SUB, 0)
        done = steps(FIRST, lax.div(eights, 4), 4 * SUB)
        done = steps(done, lax.div(lax.rem(eights, 4), 2), 2 * SUB)
        steps(done, lax.rem(eights, 2), SUB)
        return carry

    def finish(block, carry):
        copy_out(block).wait()
        return carry

    lax.fori_loop(0, blocks, one_block, 0)
    send(blocks - 1, turn(blocks - 1))
    copy_out(blocks - 1).start()
    lax.fori_loop(0, blocks, finish, 0)


def list_copies(lists_in, index, count, listed):
    cap = lists_in.shape[1]
    owners = index.shape[0] // cap
    lengths = pltpu.make_async_copy(lists_in.at[owners], count, listed.at[owners])

    def list_copy(item):
        place = pl.ds(pl.multiple_of(item * cap, LANES), cap)
        return pltpu.make_async_copy(lists_in.at[item], index.at[place], listed.at[item])

    def start_list(item, carry):
        list_copy(item).start()
        return carry

    lengths.start()
    lax.fori_loop(0, owners, start_list, 0)
    return lengths.wait, lambda item: list_copy(item).wait()


def solve_kernel(
    parts, west, east, inside_in, left_cell_in, west_edge_in, east_edge_in, lower_in, upper_in, lists_in,
    sent, inside, left_cell, west_edge, east_edge, lower, upper, ready,
    halo, solved, table, packed, turned, index, count, listed, copied,
):
    values, lats, _ = inside.shape
    sources = (left_cell_in, west_edge_in, east_edge_in, lower_in, upper_in, inside_in)
    copies = fetch(sources, (left_cell, west_edge, east_edge, lower, upper, inside), ready)
    wait_lengths, wait_list = list_copies(lists_in, index, count, listed)
    for value in range(values, SLOT):
        solved[pl.ds(value, lats, stride=SLOT), :] = jnp.zeros((lats, LANES), jnp.float32)
    merge_halo(west, east, halo, values)
    for copy in copies:
        copy.wait()
    add_edges_and_solve(inside, left_cell, west_edge, east_edge, lower, upper, halo, solved)
    build_table(solved, table.reshape(table.shape[0], LANES), values, parts)
    wait_lengths()
    pick_rows(table, index, count, lists_in.shape[1], values, packed, turned, sent, copied, wait_list)


def make_sent(west, east, fields, lists_in, lists):
    values, lats, lons = fields[0].shape
    cap = lists_in.shape[1]
    parts = cap // LANES
    blocks = lists * parts // 4
    halos = (west.reshape(values, SUB, LANES), east.reshape(values, SUB, LANES))
    sent = pl.pallas_call(
        functools.partial(solve_kernel, parts),
        out_shape=jax.ShapeDtypeStruct((blocks, 4 * values, LANES), jnp.float32),
        in_specs=[pl.BlockSpec(memory_space=pltpu.VMEM)] * 2 + [pl.BlockSpec(memory_space=pl.ANY)] * (len(fields) + 1),
        out_specs=pl.BlockSpec(memory_space=pl.ANY),
        scratch_shapes=[pltpu.VMEM(array.shape, array.dtype) for array in fields]
        + [
            pltpu.SemaphoreType.DMA((len(fields),)),
            pltpu.VMEM((values, 2, SUB, LANES), jnp.float32),
            pltpu.VMEM((lats * SLOT, LANES), jnp.float32),
            pltpu.VMEM((lats * lons, 1, LANES), jnp.float32),
            pltpu.VMEM((2 * LANES, LANES), jnp.float32),
            pltpu.VMEM((blocks + 1, 4 * values, LANES), jnp.float32),
            pltpu.SMEM((lists * cap,), jnp.int32),
            pltpu.SMEM((cap,), jnp.int32),
            pltpu.SemaphoreType.DMA((lists + 1,)),
            pltpu.SemaphoreType.DMA((blocks,)),
        ],
        compiler_params=pltpu.CompilerParams(vmem_limit_bytes=SOLVE),
        cost_estimate=pl.CostEstimate(flops=0, bytes_accessed=40 * MIB, transcendentals=0),
        name="solve_pick",
    )(*halos, *fields, lists_in)
    rows = values * parts
    tile = max(size for size in (1, 2, 4, 8) if rows % size == 0)
    return sent.reshape(lists, rows // tile, tile, LANES)


def place_kernel(own, arrived, owned_out, row, owned, written):
    sources, height, _ = arrived.shape
    levels, ntr, columns = owned.shape
    values = levels * ntr
    parts = height // values
    lane = lax.broadcasted_iota(jnp.int32, (values, LANES), 1)
    order = [lax.rem(own[0] - turn + sources, sources) for turn in range(sources)]
    totals = []
    for source in order:
        note = arrived[source, parts - 1 : parts, :]
        total = jnp.where(note > 0.5 * LENGTH_BASE, note - LENGTH_BASE, 1.0 * parts * LANES)
        totals.append(total.astype(jnp.int32)[0, LANES - 1])
    start = 0
    for source, total in zip(order, totals):
        rows = lax.div(total + (parts - 1), parts)
        pieces = []
        for part in range(parts):
            place = start + jnp.minimum(part * rows, total)
            shift = lax.rem(place, LANES)
            piece = arrived[source, pl.ds(part, values, stride=parts), :]
            pieces.append((place - shift, shift, pltpu.roll(piece, shift, 1)))
        for tile, shift, rolled in pieces:
            here = pl.ds(pl.multiple_of(tile, LANES), LANES)
            after = pl.ds(pl.multiple_of(tile + LANES, LANES), LANES)
            pltpu.store(row.at[:, here], rolled, mask=lane >= shift)
            row[:, after] = rolled
        start = start + total
    copies = []
    for level in range(levels):
        owned[level] = row[level * ntr : (level + 1) * ntr, :columns]
        copies.append(pltpu.make_async_copy(owned.at[level], owned_out.at[level], written.at[level]))
        copies[level].start()
    for copy in copies:
        copy.wait()


def place_owned(arrived, own, levels, ntr, columns):
    vmem = pl.BlockSpec(memory_space=pltpu.VMEM)
    smem = pl.BlockSpec(memory_space=pltpu.SMEM)
    values = levels * ntr
    return pl.pallas_call(
        place_kernel,
        out_shape=jax.ShapeDtypeStruct((levels, ntr, columns), jnp.float32),
        in_specs=[smem, vmem],
        out_specs=pl.BlockSpec(memory_space=pl.ANY),
        scratch_shapes=[
            pltpu.VMEM((values, columns + 2 * LANES), jnp.float32),
            pltpu.VMEM((levels, ntr, columns), jnp.float32),
            pltpu.SemaphoreType.DMA((levels,)),
        ],
        compiler_params=pltpu.CompilerParams(vmem_limit_bytes=16 * MIB),
        name="place_owned",
    )(own, arrived.reshape(arrived.shape[0], -1, LANES))


def ring(axis, distance):
    size = lax.axis_size(axis)
    return [(i, (i + distance) % size) for i in range(size)]


def body(tracers, offsets, weights, diffusion, send_index, send_count):
    ntr, levels, lats, lons = tracers.shape
    columns = lats * lons
    west_cells, east_cells = pack_halo(tracers)
    from_west = lax.ppermute(east_cells, "lon", ring("lon", 1))
    from_east = lax.ppermute(west_cells, "lon", ring("lon", -1))
    *fields, lists = advect_inside(tracers, offsets, weights, diffusion, send_index, send_count)
    sent = make_sent(from_west, from_east, fields, lists, send_count.shape[1])
    arrived = lax.all_to_all(sent, ("lon", "lat"), split_axis=0, concat_axis=0, tiled=True)
    own = lax.axis_index(("lon", "lat")).astype(jnp.int32).reshape(1)
    owned = place_owned(arrived, own, levels, ntr, columns)
    return jnp.transpose(owned, (1, 0, 2))


def solution(mesh):
    return jax.shard_map(
        body,
        mesh=mesh,
        in_specs=(
            P(None, None, "lat", "lon"),
            P(None, "lat", "lon"),
            P(None, "lat", "lon"),
            P(None, "lat", "lon"),
            P(("lon", "lat"), None, None),
            P(("lon", "lat"), None),
        ),
        out_specs=P(None, None, ("lon", "lat")),
        check_vma=False,
    )
```

```python
import functools

import jax
import jax.numpy as jnp
from jax import lax
from jax.experimental import pallas as pl
from jax.experimental.pallas import tpu as pltpu
from jax.sharding import PartitionSpec as P

HALO = 16
LANES = 128
SUB = 8
SLOT = 32
FIRST = 32
PAIR = 65536
MIB = 1024 * 1024
LENGTH_BASE = 1000.0
BIG = 60 * MIB
SOLVE = 107 * MIB // 2
LIST_ROWS = 256


def take_lanes(block, index):
    return jnp.take_along_axis(block, index, axis=1, mode="promise_in_bounds")


def lane_ids(rows):
    return lax.broadcasted_iota(jnp.int32, (rows, LANES), 1)


def fetch(sources, targets, ready):
    copies = [
        pltpu.make_async_copy(source, target, ready.at[item])
        for item, (source, target) in enumerate(zip(sources, targets))
    ]
    for copy in copies:
        copy.start()
    return copies


def pack_halo_kernel(tracers_in, west_cells, east_cells, tracers, ready):
    ntr, levels, lats, _ = tracers.shape
    per_row = LANES // HALO
    group = lane_ids(SUB) // HALO
    assert lats == SUB * per_row
    copies = fetch(
        [tracers_in.at[:, level] for level in range(levels)],
        [tracers.at[:, level] for level in range(levels)],
        ready,
    )
    for level in range(levels):
        copies[level].wait()
        for tracer in range(ntr):
            west = jnp.zeros((SUB, LANES), jnp.float32)
            east = jnp.zeros((SUB, LANES), jnp.float32)
            for part in range(lats // SUB):
                cells = tracers[tracer, level, part * SUB : (part + 1) * SUB, :]
                shift = part * HALO
                rolled_west = pltpu.roll(cells, shift, 1) if shift else cells
                shift = (part * HALO + HALO) % LANES
                rolled_east = pltpu.roll(cells, shift, 1) if shift else cells
                west = jnp.where(group == part, rolled_west, west)
                east = jnp.where(group == part, rolled_east, east)
            west_cells[level, tracer] = west
            east_cells[level, tracer] = east


def pack_halo(tracers):
    ntr, levels, _, _ = tracers.shape
    shape = jax.ShapeDtypeStruct((levels, ntr, SUB, LANES), jnp.float32)
    return pl.pallas_call(
        pack_halo_kernel,
        out_shape=(shape, shape),
        in_specs=[pl.BlockSpec(memory_space=pl.ANY)],
        out_specs=[pl.BlockSpec(memory_space=pltpu.VMEM)] * 2,
        scratch_shapes=[pltpu.VMEM(tracers.shape, jnp.float32), pltpu.SemaphoreType.DMA((levels,))],
        compiler_params=pltpu.CompilerParams(vmem_limit_bytes=SOLVE),
        name="pack_halo",
    )(tracers)


def merge_halo(west, east, halo, count):
    lane = lane_ids(SUB)
    cell = lane % (2 * HALO)
    sources = [(half * 4 + lane // (2 * HALO)) * HALO + cell % HALO for half in range(2)]
    chunk = 10 if count % 10 == 0 else 1

    def some_values(step, carry):
        merged = []
        for item in range(chunk):
            value = step * chunk + item
            for half in range(2):
                both = take_lanes(west[value], sources[half]), take_lanes(east[value], sources[half])
                merged.append((value, half, jnp.where(cell < HALO, *both)))
        for value, half, cells in merged:
            halo[value, half] = cells
        return carry

    lax.fori_loop(0, count // chunk, some_values, 0)


def inside_kernel(
    tracers_in, offsets_in, weights_in, diffusion_in, index_in, count,
    inside, left_cell, west_edge, east_edge, lower, upper, lists,
    tracers, offsets, weights, diffusion, index, ready,
):
    ntr, levels, lats, _ = tracers.shape
    lane = lane_ids(SUB)
    owners = count.shape[1]
    copies = fetch(
        (diffusion_in, offsets_in, weights_in, tracers_in, index_in.at[0]),
        (diffusion, offsets, weights, tracers, index),
        ready,
    )
    lists[owners : owners + 1, :owners] = count[...]
    for copy in copies:
        copy.wait()
    following = pltpu.roll(index[...], index.shape[1] - 1, 1)
    lists[:owners, :] = index[...] + following * PAIR

    def one_part(part, carry):
        rows = pl.ds(pl.multiple_of(part * SUB, SUB), SUB)
        coefs = [diffusion[level, rows, :] for level in range(levels - 1)]
        lowers, uppers, edges, results = [], [], [], []
        for level in range(levels):
            denom = 1.0
            if level > 0:
                denom = denom + coefs[level - 1]
            if level < levels - 1:
                denom = denom + coefs[level]
            if level > 0:
                denom = denom - coefs[level - 1] * uppers[level - 1]
            inverse = 1.0 / denom
            if level > 0:
                lowers.append(coefs[level - 1] * inverse)
            if level < levels - 1:
                uppers.append(coefs[level] * inverse)
            left = lane + offsets[level, rows, :]
            right = left + 1
            weight = weights[level, rows, :]
            west_weight = (1.0 - weight) * inverse
            east_weight = weight * inverse
            left_in = (left >= 0) & (left < LANES)
            right_in = (right >= 0) & (right < LANES)
            edges.append((left, jnp.where(left_in, 0.0, west_weight), jnp.where(right_in, 0.0, east_weight)))
            west_weight = jnp.where(left_in, west_weight, 0.0)
            east_weight = jnp.where(right_in, east_weight, 0.0)
            left = left & (LANES - 1)
            right = right & (LANES - 1)
            for tracer in range(ntr):
                cells = tracers[tracer, level, rows, :]
                results.append(west_weight * take_lanes(cells, left) + east_weight * take_lanes(cells, right))
        for value, result in enumerate(results):
            inside[value, rows, :] = result
        for level, (left, west_weight, east_weight) in enumerate(edges):
            left_cell[level, rows, :] = left
            west_edge[level, rows, :] = west_weight
            east_edge[level, rows, :] = east_weight
        for level in range(levels - 1):
            lower[level, rows, :] = lowers[level]
            upper[level, rows, :] = uppers[level]
        return carry

    lax.fori_loop(0, lats // SUB, one_part, 0)


def advect_inside(tracers, offsets, weights, diffusion, index, count):
    ntr, levels, lats, lons = tracers.shape
    lists, cap = index.shape[1:]
    vmem = pl.BlockSpec(memory_space=pltpu.VMEM)
    field = lambda count, kind=jnp.float32: jax.ShapeDtypeStruct((count, lats, lons), kind)
    outputs = (
        field(ntr * levels),
        field(levels, jnp.int32),
        field(levels),
        field(levels),
        field(levels - 1),
        field(levels - 1),
        jax.ShapeDtypeStruct((max(lists + SUB, LIST_ROWS), cap), jnp.int32),
    )
    return pl.pallas_call(
        inside_kernel,
        out_shape=outputs,
        in_specs=[pl.BlockSpec(memory_space=pl.ANY)] * 5 + [vmem],
        out_specs=(vmem,) * len(outputs),
        scratch_shapes=[pltpu.VMEM(array.shape, array.dtype) for array in (tracers, offsets, weights, diffusion)]
        + [pltpu.VMEM((lists, cap), jnp.int32), pltpu.SemaphoreType.DMA((5,))],
        compiler_params=pltpu.CompilerParams(vmem_limit_bytes=BIG),
        cost_estimate=pl.CostEstimate(flops=0, bytes_accessed=20 * MIB, transcendentals=0),
        name="advect_inside",
    )(tracers, offsets, weights, diffusion, index, count)


def add_edges_and_solve(inside, left_cell, west_edge, east_edge, lower, upper, halo, solved):
    levels, lats, _ = left_cell.shape
    ntr = inside.shape[0] // levels
    together = 2

    def solve_part(part):
        rows = pl.ds(pl.multiple_of(part * SUB, SUB), SUB)
        half = part // 4
        base = (part % 4) * (2 * HALO)
        reduced = [[] for _ in range(ntr)]
        for level in range(levels):
            left = left_cell[level, rows, :]
            right = base + ((left + (HALO + 1)) & (2 * HALO - 1))
            left = base + ((left + HALO) & (2 * HALO - 1))
            west_weight = west_edge[level, rows, :]
            east_weight = east_edge[level, rows, :]
            for tracer in range(ntr):
                value = level * ntr + tracer
                cells = halo[value, half]
                edges = west_weight * take_lanes(cells, left) + east_weight * take_lanes(cells, right)
                total = inside[value, rows, :] + edges
                if level > 0:
                    total = total + lower[level - 1, rows, :] * reduced[tracer][level - 1]
                reduced[tracer].append(total)
        results = {}
        for level in range(levels - 1, -1, -1):
            for tracer in range(ntr):
                x = reduced[tracer][level]
                if level < levels - 1:
                    x = x + upper[level, rows, :] * results[(level + 1) * ntr + tracer]
                results[level * ntr + tracer] = x
        return results

    def some_parts(step, carry):
        solutions = [solve_part(step * together + item) for item in range(together)]
        for item, results in enumerate(solutions):
            first = pl.multiple_of((step * together + item) * (SUB * SLOT), SUB * SLOT)
            target = solved.at[pl.ds(first, SUB * SLOT), :]
            for value, x in results.items():
                target[pl.ds(value, SUB, stride=SLOT), :] = x
        return carry

    lax.fori_loop(0, lats // (SUB * together), some_parts, 0)


def streams_of(rows, values, parts):
    lane = lane_ids(rows)
    width = values * parts
    item = sum((lane >= width * step).astype(jnp.int32) for step in range(1, 4 // parts))
    held = lane - item * width
    part = held & (parts - 1)
    return jnp.minimum(lax.shift_right_logical(held, parts.bit_length() - 1), values - 1), item * parts + part


def build_table(solved, table, values, parts):
    rows_per = LANES // SLOT
    spread = streams_of(LANES, values, parts)[0]
    together = 4

    def some_rows(step, carry):
        blocks = []
        for item in range(together):
            start = pl.multiple_of((step * together + item) * LANES, LANES)
            blocks.append(solved[pl.ds(start, LANES), :].T)
        for item, block in enumerate(blocks):
            for row in range(rows_per):
                start = pl.multiple_of(((step * together + item) * rows_per + row) * LANES, LANES)
                table[pl.ds(start, LANES), :] = take_lanes(block, spread + row * SLOT)
        return carry

    lax.fori_loop(0, solved.shape[0] // (LANES * together), some_rows, 0)


def pick_rows(table, index, count, cap, values, packed, turned, sent, copied, wait_list):
    blocks, height, _ = sent.shape
    parts = cap // LANES
    lists = 4 // parts
    stream = streams_of(1, values, parts)[1]

    def copy_out(block):
        return pltpu.make_async_copy(turned.at[block + 1], sent.at[block], copied.at[block])

    def turn(block):
        half = pl.multiple_of(lax.rem(block + 2, 2) * LANES, LANES)
        return packed[pl.ds(half, LANES), :].T

    def send(block, result):
        turned[block + 1] = result[:height, :]
        for member in range(lists):
            total = count[jnp.maximum(block, 0) * lists + member]
            row = turned.at[block + 1, pl.ds((member * values + 1) * parts - 1, 1), :]
            note = jnp.full((1, LANES), LENGTH_BASE + total.astype(jnp.float32))
            pltpu.store(row, note, mask=(lane_ids(1) == LANES - 1) & (total < cap))

    def one_block(block, carry):
        owners = [block * lists + member for member in range(lists)]
        rows = [lax.div(count[owner] + (parts - 1), parts) for owner in owners]
        for owner in owners:
            wait_list(owner)
        longest = functools.reduce(jnp.maximum, rows)
        places = [owners[g // parts] * cap + (g % parts) * rows[g // parts] for g in range(4)]
        half = lax.rem(block, 2) * LANES

        def load_lines(start, lines):
            views = [index.at[pl.ds(place + start, lines)] for place in places]
            merged = []
            for line in range(0, lines, 2):
                pairs = [view[line] for view in views]
                for columns in (
                    [pair & (PAIR - 1) for pair in pairs],
                    [lax.shift_right_logical(pair, 16) for pair in pairs],
                ):
                    picked = [table[column] for column in columns]
                    low = jnp.where(stream == 0, picked[0], picked[1])
                    high = jnp.where(stream == 2, picked[2], picked[3])
                    merged.append(jnp.where(stream < 2, low, high))
            return merged

        def store_lines(start, merged):
            target = packed.at[pl.ds(pl.multiple_of(half + start, SUB), len(merged)), :]
            for line, value in enumerate(merged):
                target[line : line + 1, :] = value

        def steps(begin, trips, lines):
            def one_step(step, inner):
                start = pl.multiple_of(begin + step * lines, SUB)
                store_lines(start, load_lines(start, lines))
                return inner

            lax.fori_loop(0, trips, one_step, 0)
            return begin + trips * lines

        before = turn(block - 1)
        merged = load_lines(0, FIRST)
        store_lines(0, merged)
        send(block - 1, before)

        @pl.when(block > 0)
        def _():
            copy_out(block - 1).start()

        eights = jnp.maximum(lax.div(longest + (SUB - 1), SUB) - FIRST // SUB, 0)
        done = steps(FIRST, lax.div(eights, 4), 4 * SUB)
        done = steps(done, lax.div(lax.rem(eights, 4), 2), 2 * SUB)
        steps(done, lax.rem(eights, 2), SUB)
        return carry

    def finish(block, carry):
        copy_out(block).wait()
        return carry

    lax.fori_loop(0, blocks, one_block, 0)
    send(blocks - 1, turn(blocks - 1))
    copy_out(blocks - 1).start()
    lax.fori_loop(0, blocks, finish, 0)


def list_copies(lists_in, index, count, listed):
    cap = lists_in.shape[1]
    owners = index.shape[0] // cap
    lengths = pltpu.make_async_copy(lists_in.at[owners], count, listed.at[owners])

    def list_copy(item):
        place = pl.ds(pl.multiple_of(item * cap, LANES), cap)
        return pltpu.make_async_copy(lists_in.at[item], index.at[place], listed.at[item])

    def start_list(item, carry):
        list_copy(item).start()
        return carry

    lengths.start()
    lax.fori_loop(0, owners, start_list, 0)
    return lengths.wait, lambda item: list_copy(item).wait()


def solve_kernel(
    parts, west, east, inside_in, left_cell_in, west_edge_in, east_edge_in, lower_in, upper_in, lists_in,
    sent, inside, left_cell, west_edge, east_edge, lower, upper, ready,
    halo, solved, table, packed, turned, index, count, listed, copied,
):
    values, lats, _ = inside.shape
    sources = (left_cell_in, west_edge_in, east_edge_in, lower_in, upper_in, inside_in)
    copies = fetch(sources, (left_cell, west_edge, east_edge, lower, upper, inside), ready)
    wait_lengths, wait_list = list_copies(lists_in, index, count, listed)
    for value in range(values, SLOT):
        solved[pl.ds(value, lats, stride=SLOT), :] = jnp.zeros((lats, LANES), jnp.float32)
    merge_halo(west, east, halo, values)
    for copy in copies:
        copy.wait()
    add_edges_and_solve(inside, left_cell, west_edge, east_edge, lower, upper, halo, solved)
    build_table(solved, table.reshape(table.shape[0], LANES), values, parts)
    wait_lengths()
    pick_rows(table, index, count, lists_in.shape[1], values, packed, turned, sent, copied, wait_list)


def make_sent(west, east, fields, lists_in, lists):
    values, lats, lons = fields[0].shape
    cap = lists_in.shape[1]
    parts = cap // LANES
    blocks = lists * parts // 4
    halos = (west.reshape(values, SUB, LANES), east.reshape(values, SUB, LANES))
    sent = pl.pallas_call(
        functools.partial(solve_kernel, parts),
        out_shape=jax.ShapeDtypeStruct((blocks, 4 * values, LANES), jnp.float32),
        in_specs=[pl.BlockSpec(memory_space=pltpu.VMEM)] * 2 + [pl.BlockSpec(memory_space=pl.ANY)] * (len(fields) + 1),
        out_specs=pl.BlockSpec(memory_space=pl.ANY),
        scratch_shapes=[pltpu.VMEM(array.shape, array.dtype) for array in fields]
        + [
            pltpu.SemaphoreType.DMA((len(fields),)),
            pltpu.VMEM((values, 2, SUB, LANES), jnp.float32),
            pltpu.VMEM((lats * SLOT, LANES), jnp.float32),
            pltpu.VMEM((lats * lons, 1, LANES), jnp.float32),
            pltpu.VMEM((2 * LANES, LANES), jnp.float32),
            pltpu.VMEM((blocks + 1, 4 * values, LANES), jnp.float32),
            pltpu.SMEM((lists * cap,), jnp.int32),
            pltpu.SMEM((cap,), jnp.int32),
            pltpu.SemaphoreType.DMA((lists + 1,)),
            pltpu.SemaphoreType.DMA((blocks,)),
        ],
        compiler_params=pltpu.CompilerParams(vmem_limit_bytes=SOLVE),
        cost_estimate=pl.CostEstimate(flops=0, bytes_accessed=40 * MIB, transcendentals=0),
        name="solve_pick",
    )(*halos, *fields, lists_in)
    rows = values * parts
    tile = max(size for size in (1, 2, 4, 8) if rows % size == 0)
    return sent.reshape(lists, rows // tile, tile, LANES)


def place_kernel(own, arrived, owned_out, row, owned, written):
    sources, height, _ = arrived.shape
    levels, ntr, columns = owned.shape
    values = levels * ntr
    parts = height // values
    lane = lax.broadcasted_iota(jnp.int32, (values, LANES), 1)
    order = [lax.rem(own[0] - turn + sources, sources) for turn in range(sources)]
    totals = []
    for source in order:
        note = arrived[source, parts - 1 : parts, :]
        total = jnp.where(note > 0.5 * LENGTH_BASE, note - LENGTH_BASE, 1.0 * parts * LANES)
        totals.append(total.astype(jnp.int32)[0, LANES - 1])
    start = 0
    for source, total in zip(order, totals):
        rows = lax.div(total + (parts - 1), parts)
        pieces = []
        for part in range(parts):
            place = start + jnp.minimum(part * rows, total)
            shift = lax.rem(place, LANES)
            piece = arrived[source, pl.ds(part, values, stride=parts), :]
            pieces.append((place - shift, shift, pltpu.roll(piece, shift, 1)))
        for tile, shift, rolled in pieces:
            here = pl.ds(pl.multiple_of(tile, LANES), LANES)
            after = pl.ds(pl.multiple_of(tile + LANES, LANES), LANES)
            pltpu.store(row.at[:, here], rolled, mask=lane >= shift)
            row[:, after] = rolled
        start = start + total
    copies = []
    for level in range(levels):
        owned[level] = row[level * ntr : (level + 1) * ntr, :columns]
        copies.append(pltpu.make_async_copy(owned.at[level], owned_out.at[level], written.at[level]))
        copies[level].start()
    for copy in copies:
        copy.wait()


def place_owned(arrived, own, levels, ntr, columns):
    vmem = pl.BlockSpec(memory_space=pltpu.VMEM)
    smem = pl.BlockSpec(memory_space=pltpu.SMEM)
    values = levels * ntr
    return pl.pallas_call(
        place_kernel,
        out_shape=jax.ShapeDtypeStruct((levels, ntr, columns), jnp.float32),
        in_specs=[smem, vmem],
        out_specs=pl.BlockSpec(memory_space=pl.ANY),
        scratch_shapes=[
            pltpu.VMEM((values, columns + 2 * LANES), jnp.float32),
            pltpu.VMEM((levels, ntr, columns), jnp.float32),
            pltpu.SemaphoreType.DMA((levels,)),
        ],
        compiler_params=pltpu.CompilerParams(vmem_limit_bytes=16 * MIB),
        name="place_owned",
    )(own, arrived.reshape(arrived.shape[0], -1, LANES))


def ring(axis, distance):
    size = lax.axis_size(axis)
    return [(i, (i + distance) % size) for i in range(size)]


def body(tracers, offsets, weights, diffusion, send_index, send_count):
    ntr, levels, lats, lons = tracers.shape
    columns = lats * lons
    west_cells, east_cells = pack_halo(tracers)
    from_west = lax.ppermute(east_cells, "lon", ring("lon", 1))
    from_east = lax.ppermute(west_cells, "lon", ring("lon", -1))
    *fields, lists = advect_inside(tracers, offsets, weights, diffusion, send_index, send_count)
    sent = make_sent(from_west, from_east, fields, lists, send_count.shape[1])
    arrived = lax.all_to_all(sent, ("lon", "lat"), split_axis=0, concat_axis=0, tiled=True)
    own = lax.axis_index(("lon", "lat")).astype(jnp.int32).reshape(1)
    owned = place_owned(arrived, own, levels, ntr, columns)
    return jnp.transpose(owned, (1, 0, 2))


def solution(mesh):
    return jax.shard_map(
        body,
        mesh=mesh,
        in_specs=(
            P(None, None, "lat", "lon"),
            P(None, "lat", "lon"),
            P(None, "lat", "lon"),
            P(None, "lat", "lon"),
            P(("lon", "lat"), None, None),
            P(("lon", "lat"), None),
        ),
        out_specs=P(None, None, ("lon", "lat")),
        check_vma=False,
    )
```

```python
import functools

import jax
import jax.numpy as jnp
from jax import lax
from jax.experimental import pallas as pl
from jax.experimental.pallas import tpu as pltpu
from jax.sharding import PartitionSpec as P

HALO = 16
LANES = 128
SUB = 8
SLOT = 32
FIRST = 32
MIB = 1024 * 1024
LENGTH_BASE = 1000.0
BIG = 60 * MIB
SOLVE = 107 * MIB // 2
LIST_ROWS = 256


def take_lanes(block, index):
    return jnp.take_along_axis(block, index, axis=1, mode="promise_in_bounds")


def lane_ids(rows):
    return lax.broadcasted_iota(jnp.int32, (rows, LANES), 1)


def fetch(sources, targets, ready):
    copies = [
        pltpu.make_async_copy(source, target, ready.at[item])
        for item, (source, target) in enumerate(zip(sources, targets))
    ]
    for copy in copies:
        copy.start()
    return copies


def pack_halo_kernel(tracers_in, west_cells, east_cells, tracers, ready):
    ntr, levels, lats, _ = tracers.shape
    per_row = LANES // HALO
    group = lane_ids(SUB) // HALO
    assert lats == SUB * per_row
    copies = fetch(
        [tracers_in.at[:, level] for level in range(levels)],
        [tracers.at[:, level] for level in range(levels)],
        ready,
    )
    for level in range(levels):
        copies[level].wait()
        for tracer in range(ntr):
            west = jnp.zeros((SUB, LANES), jnp.float32)
            east = jnp.zeros((SUB, LANES), jnp.float32)
            for part in range(lats // SUB):
                cells = tracers[tracer, level, part * SUB : (part + 1) * SUB, :]
                shift = part * HALO
                rolled_west = pltpu.roll(cells, shift, 1) if shift else cells
                shift = (part * HALO + HALO) % LANES
                rolled_east = pltpu.roll(cells, shift, 1) if shift else cells
                west = jnp.where(group == part, rolled_west, west)
                east = jnp.where(group == part, rolled_east, east)
            west_cells[level, tracer] = west
            east_cells[level, tracer] = east


def pack_halo(tracers):
    ntr, levels, _, _ = tracers.shape
    shape = jax.ShapeDtypeStruct((levels, ntr, SUB, LANES), jnp.float32)
    return pl.pallas_call(
        pack_halo_kernel,
        out_shape=(shape, shape),
        in_specs=[pl.BlockSpec(memory_space=pl.ANY)],
        out_specs=[pl.BlockSpec(memory_space=pltpu.VMEM)] * 2,
        scratch_shapes=[pltpu.VMEM(tracers.shape, jnp.float32), pltpu.SemaphoreType.DMA((levels,))],
        compiler_params=pltpu.CompilerParams(vmem_limit_bytes=SOLVE),
        name="pack_halo",
    )(tracers)


def merge_halo(west, east, halo, count):
    lane = lane_ids(SUB)
    cell = lane % (2 * HALO)
    sources = [(half * 4 + lane // (2 * HALO)) * HALO + cell % HALO for half in range(2)]
    chunk = 10 if count % 10 == 0 else 1

    def some_values(step, carry):
        merged = []
        for item in range(chunk):
            value = step * chunk + item
            for half in range(2):
                both = take_lanes(west[value], sources[half]), take_lanes(east[value], sources[half])
                merged.append((value, half, jnp.where(cell < HALO, *both)))
        for value, half, cells in merged:
            halo[value, half] = cells
        return carry

    lax.fori_loop(0, count // chunk, some_values, 0)


def inside_kernel(
    tracers_in, offsets_in, weights_in, diffusion_in, index_in, count,
    inside, left_cell, west_edge, east_edge, lower, upper, lists,
    tracers, offsets, weights, diffusion, ready,
):
    ntr, levels, lats, _ = tracers.shape
    lane = lane_ids(SUB)
    owners = count.shape[1]
    copies = fetch(
        (diffusion_in, offsets_in, weights_in, tracers_in, index_in.at[0]),
        (diffusion, offsets, weights, tracers, lists.at[pl.ds(0, owners)]),
        ready,
    )
    lists[owners : owners + 1, :owners] = count[...]
    for copy in copies:
        copy.wait()

    def one_part(part, carry):
        rows = pl.ds(pl.multiple_of(part * SUB, SUB), SUB)
        coefs = [diffusion[level, rows, :] for level in range(levels - 1)]
        lowers, uppers, edges, results = [], [], [], []
        for level in range(levels):
            denom = 1.0
            if level > 0:
                denom = denom + coefs[level - 1]
            if level < levels - 1:
                denom = denom + coefs[level]
            if level > 0:
                denom = denom - coefs[level - 1] * uppers[level - 1]
            inverse = 1.0 / denom
            if level > 0:
                lowers.append(coefs[level - 1] * inverse)
            if level < levels - 1:
                uppers.append(coefs[level] * inverse)
            left = lane + offsets[level, rows, :]
            right = left + 1
            weight = weights[level, rows, :]
            west_weight = (1.0 - weight) * inverse
            east_weight = weight * inverse
            left_in = (left >= 0) & (left < LANES)
            right_in = (right >= 0) & (right < LANES)
            edges.append((left, jnp.where(left_in, 0.0, west_weight), jnp.where(right_in, 0.0, east_weight)))
            west_weight = jnp.where(left_in, west_weight, 0.0)
            east_weight = jnp.where(right_in, east_weight, 0.0)
            left = left & (LANES - 1)
            right = right & (LANES - 1)
            for tracer in range(ntr):
                cells = tracers[tracer, level, rows, :]
                results.append(west_weight * take_lanes(cells, left) + east_weight * take_lanes(cells, right))
        for value, result in enumerate(results):
            inside[value, rows, :] = result
        for level, (left, west_weight, east_weight) in enumerate(edges):
            left_cell[level, rows, :] = left
            west_edge[level, rows, :] = west_weight
            east_edge[level, rows, :] = east_weight
        for level in range(levels - 1):
            lower[level, rows, :] = lowers[level]
            upper[level, rows, :] = uppers[level]
        return carry

    lax.fori_loop(0, lats // SUB, one_part, 0)


def advect_inside(tracers, offsets, weights, diffusion, index, count):
    ntr, levels, lats, lons = tracers.shape
    lists, cap = index.shape[1:]
    vmem = pl.BlockSpec(memory_space=pltpu.VMEM)
    field = lambda count, kind=jnp.float32: jax.ShapeDtypeStruct((count, lats, lons), kind)
    outputs = (
        field(ntr * levels),
        field(levels, jnp.int32),
        field(levels),
        field(levels),
        field(levels - 1),
        field(levels - 1),
        jax.ShapeDtypeStruct((max(lists + SUB, LIST_ROWS), cap), jnp.int32),
    )
    return pl.pallas_call(
        inside_kernel,
        out_shape=outputs,
        in_specs=[pl.BlockSpec(memory_space=pl.ANY)] * 5 + [vmem],
        out_specs=(vmem,) * len(outputs),
        scratch_shapes=[pltpu.VMEM(array.shape, array.dtype) for array in (tracers, offsets, weights, diffusion)]
        + [pltpu.SemaphoreType.DMA((5,))],
        compiler_params=pltpu.CompilerParams(vmem_limit_bytes=BIG),
        cost_estimate=pl.CostEstimate(flops=0, bytes_accessed=20 * MIB, transcendentals=0),
        name="advect_inside",
    )(tracers, offsets, weights, diffusion, index, count)


def add_edges_and_solve(inside, left_cell, west_edge, east_edge, lower, upper, halo, solved):
    levels, lats, _ = left_cell.shape
    ntr = inside.shape[0] // levels
    together = 2

    def solve_part(part):
        rows = pl.ds(pl.multiple_of(part * SUB, SUB), SUB)
        half = shift_down(part, 4)
        base = (part & 3) * (2 * HALO)
        reduced = [[] for _ in range(ntr)]
        for level in range(levels):
            left = left_cell[level, rows, :]
            right = base + ((left + (HALO + 1)) & (2 * HALO - 1))
            left = base + ((left + HALO) & (2 * HALO - 1))
            west_weight = west_edge[level, rows, :]
            east_weight = east_edge[level, rows, :]
            for tracer in range(ntr):
                value = level * ntr + tracer
                cells = halo[value, half]
                edges = west_weight * take_lanes(cells, left) + east_weight * take_lanes(cells, right)
                total = inside[value, rows, :] + edges
                if level > 0:
                    total = total + lower[level - 1, rows, :] * reduced[tracer][level - 1]
                reduced[tracer].append(total)
        results = {}
        for level in range(levels - 1, -1, -1):
            for tracer in range(ntr):
                x = reduced[tracer][level]
                if level < levels - 1:
                    x = x + upper[level, rows, :] * results[(level + 1) * ntr + tracer]
                results[level * ntr + tracer] = x
        return results

    def some_parts(step, carry):
        solutions = [solve_part(step * together + item) for item in range(together)]
        for item, results in enumerate(solutions):
            first = pl.multiple_of((step * together + item) * (SUB * SLOT), SUB * SLOT)
            target = solved.at[pl.ds(first, SUB * SLOT), :]
            for value, x in results.items():
                target[pl.ds(value, SUB, stride=SLOT), :] = x
        return carry

    lax.fori_loop(0, lats // (SUB * together), some_parts, 0)


def streams_of(rows, values, parts):
    lane = lane_ids(rows)
    width = values * parts
    item = sum((lane >= width * step).astype(jnp.int32) for step in range(1, 4 // parts))
    held = lane - item * width
    part = held & (parts - 1)
    return jnp.minimum(lax.shift_right_logical(held, parts.bit_length() - 1), values - 1), item * parts + part


def build_table(solved, table, values, parts):
    rows_per = LANES // SLOT
    spread = streams_of(LANES, values, parts)[0]
    together = 4

    def some_rows(step, carry):
        blocks = []
        for item in range(together):
            start = pl.multiple_of((step * together + item) * LANES, LANES)
            blocks.append(solved[pl.ds(start, LANES), :].T)
        for item, block in enumerate(blocks):
            for row in range(rows_per):
                start = pl.multiple_of(((step * together + item) * rows_per + row) * LANES, LANES)
                table[pl.ds(start, LANES), :] = take_lanes(block, spread + row * SLOT)
        return carry

    lax.fori_loop(0, solved.shape[0] // (LANES * together), some_rows, 0)


def shift_down(number, power):
    return lax.shift_right_logical(number, power.bit_length() - 1)


def pick_rows(table, index, count, cap, values, packed, turned, sent, copied, wait_list):
    blocks, height, _ = sent.shape
    parts = cap // LANES
    lists = 4 // parts
    stream = streams_of(1, values, parts)[1]

    def copy_out(block):
        return pltpu.make_async_copy(turned.at[block + 1], sent.at[block], copied.at[block])

    def turn(block):
        half = pl.multiple_of((block & 1) * LANES, LANES)
        return packed[pl.ds(half, LANES), :].T

    def send(block, result):
        turned[block + 1] = result[:height, :]
        for member in range(lists):
            total = count[jnp.maximum(block, 0) * lists + member]
            row = turned.at[block + 1, pl.ds((member * values + 1) * parts - 1, 1), :]
            note = jnp.full((1, LANES), LENGTH_BASE + total.astype(jnp.float32))
            pltpu.store(row, note, mask=(lane_ids(1) == LANES - 1) & (total < cap))

    def one_block(block, carry):
        owners = [block * lists + member for member in range(lists)]
        rows = [shift_down(count[owner] + (parts - 1), parts) for owner in owners]
        for owner in owners:
            wait_list(owner)
        longest = functools.reduce(jnp.maximum, rows)
        places = [owners[g // parts] * cap + (g % parts) * rows[g // parts] for g in range(4)]
        half = (block & 1) * LANES

        def load_lines(start, lines):
            views = [index.at[pl.ds(place + start, lines)] for place in places]
            merged = []
            for line in range(lines):
                picked = [table[view[line]] for view in views]
                low = jnp.where(stream == 0, picked[0], picked[1])
                high = jnp.where(stream == 2, picked[2], picked[3])
                merged.append(jnp.where(stream < 2, low, high))
            return merged

        def store_lines(start, merged):
            target = packed.at[pl.ds(pl.multiple_of(half + start, SUB), len(merged)), :]
            for line, value in enumerate(merged):
                target[line : line + 1, :] = value

        def steps(begin, trips, lines):
            def one_step(step, inner):
                start = pl.multiple_of(begin + step * lines, SUB)
                store_lines(start, load_lines(start, lines))
                return inner

            lax.fori_loop(0, trips, one_step, 0)
            return begin + trips * lines

        before = turn(block - 1)
        merged = load_lines(0, FIRST)
        store_lines(0, merged)
        send(block - 1, before)

        @pl.when(block > 0)
        def _():
            copy_out(block - 1).start()

        eights = jnp.maximum(shift_down(longest + (SUB - 1), SUB) - FIRST // SUB, 0)
        done = steps(FIRST, shift_down(eights, 4), 4 * SUB)
        done = steps(done, shift_down(eights & 3, 2), 2 * SUB)
        steps(done, eights & 1, SUB)
        return carry

    def finish(block, carry):
        copy_out(block).wait()
        return carry

    lax.fori_loop(0, blocks, one_block, 0)
    send(blocks - 1, turn(blocks - 1))
    copy_out(blocks - 1).start()
    lax.fori_loop(0, blocks, finish, 0)


def list_copies(lists_in, index, count, listed):
    cap = lists_in.shape[1]
    owners = index.shape[0] // cap
    lengths = pltpu.make_async_copy(lists_in.at[owners], count, listed.at[owners])

    def list_copy(item):
        place = pl.ds(pl.multiple_of(item * cap, LANES), cap)
        return pltpu.make_async_copy(lists_in.at[item], index.at[place], listed.at[item])

    def start_list(item, carry):
        list_copy(item).start()
        return carry

    lengths.start()
    lax.fori_loop(0, owners, start_list, 0)
    return lengths.wait, lambda item: list_copy(item).wait()


def solve_kernel(
    parts, west, east, inside_in, left_cell_in, west_edge_in, east_edge_in, lower_in, upper_in, lists_in,
    sent, inside, left_cell, west_edge, east_edge, lower, upper, ready,
    halo, solved, table, packed, turned, index, count, listed, copied,
):
    values, lats, _ = inside.shape
    sources = (left_cell_in, west_edge_in, east_edge_in, lower_in, upper_in, inside_in)
    copies = fetch(sources, (left_cell, west_edge, east_edge, lower, upper, inside), ready)
    wait_lengths, wait_list = list_copies(lists_in, index, count, listed)
    for value in range(values, SLOT):
        solved[pl.ds(value, lats, stride=SLOT), :] = jnp.zeros((lats, LANES), jnp.float32)
    merge_halo(west, east, halo, values)
    for copy in copies:
        copy.wait()
    add_edges_and_solve(inside, left_cell, west_edge, east_edge, lower, upper, halo, solved)
    build_table(solved, table.reshape(table.shape[0], LANES), values, parts)
    wait_lengths()
    pick_rows(table, index, count, lists_in.shape[1], values, packed, turned, sent, copied, wait_list)


def make_sent(west, east, fields, lists_in, lists):
    values, lats, lons = fields[0].shape
    cap = lists_in.shape[1]
    parts = cap // LANES
    blocks = lists * parts // 4
    halos = (west.reshape(values, SUB, LANES), east.reshape(values, SUB, LANES))
    sent = pl.pallas_call(
        functools.partial(solve_kernel, parts),
        out_shape=jax.ShapeDtypeStruct((blocks, 4 * values, LANES), jnp.float32),
        in_specs=[pl.BlockSpec(memory_space=pltpu.VMEM)] * 2 + [pl.BlockSpec(memory_space=pl.ANY)] * (len(fields) + 1),
        out_specs=pl.BlockSpec(memory_space=pl.ANY),
        scratch_shapes=[pltpu.VMEM(array.shape, array.dtype) for array in fields]
        + [
            pltpu.SemaphoreType.DMA((len(fields),)),
            pltpu.VMEM((values, 2, SUB, LANES), jnp.float32),
            pltpu.VMEM((lats * SLOT, LANES), jnp.float32),
            pltpu.VMEM((lats * lons, 1, LANES), jnp.float32),
            pltpu.VMEM((2 * LANES, LANES), jnp.float32),
            pltpu.VMEM((blocks + 1, 4 * values, LANES), jnp.float32),
            pltpu.SMEM((lists * cap,), jnp.int32),
            pltpu.SMEM((cap,), jnp.int32),
            pltpu.SemaphoreType.DMA((lists + 1,)),
            pltpu.SemaphoreType.DMA((blocks,)),
        ],
        compiler_params=pltpu.CompilerParams(vmem_limit_bytes=SOLVE),
        cost_estimate=pl.CostEstimate(flops=0, bytes_accessed=40 * MIB, transcendentals=0),
        name="solve_pick",
    )(*halos, *fields, lists_in)
    rows = values * parts
    tile = max(size for size in (1, 2, 4, 8) if rows % size == 0)
    return sent.reshape(lists, rows // tile, tile, LANES)


def place_kernel(own, arrived, owned_out, row, owned, written):
    sources, height, _ = arrived.shape
    levels, ntr, columns = owned.shape
    values = levels * ntr
    parts = height // values
    lane = lax.broadcasted_iota(jnp.int32, (values, LANES), 1)
    order = [own[0] - turn for turn in range(sources)]
    order = [jnp.where(source < 0, source + sources, source) for source in order]
    totals = []
    for source in order:
        note = arrived[source, parts - 1 : parts, :]
        total = jnp.where(note > 0.5 * LENGTH_BASE, note - LENGTH_BASE, 1.0 * parts * LANES)
        totals.append(total.astype(jnp.int32)[0, LANES - 1])
    start = 0
    for source, total in zip(order, totals):
        rows = shift_down(total + (parts - 1), parts)
        pieces = []
        for part in range(parts):
            place = start + jnp.minimum(part * rows, total)
            shift = place & (LANES - 1)
            piece = arrived[source, pl.ds(part, values, stride=parts), :]
            pieces.append((place - shift, shift, pltpu.roll(piece, shift, 1)))
        for tile, shift, rolled in pieces:
            here = pl.ds(pl.multiple_of(tile, LANES), LANES)
            after = pl.ds(pl.multiple_of(tile + LANES, LANES), LANES)
            pltpu.store(row.at[:, here], rolled, mask=lane >= shift)
            row[:, after] = rolled
        start = start + total
    copies = []
    for level in range(levels):
        owned[level] = row[level * ntr : (level + 1) * ntr, :columns]
        copies.append(pltpu.make_async_copy(owned.at[level], owned_out.at[level], written.at[level]))
        copies[level].start()
    for copy in copies:
        copy.wait()


def place_owned(arrived, own, levels, ntr, columns):
    vmem = pl.BlockSpec(memory_space=pltpu.VMEM)
    smem = pl.BlockSpec(memory_space=pltpu.SMEM)
    values = levels * ntr
    return pl.pallas_call(
        place_kernel,
        out_shape=jax.ShapeDtypeStruct((levels, ntr, columns), jnp.float32),
        in_specs=[smem, vmem],
        out_specs=pl.BlockSpec(memory_space=pl.ANY),
        scratch_shapes=[
            pltpu.VMEM((values, columns + 2 * LANES), jnp.float32),
            pltpu.VMEM((levels, ntr, columns), jnp.float32),
            pltpu.SemaphoreType.DMA((levels,)),
        ],
        compiler_params=pltpu.CompilerParams(vmem_limit_bytes=16 * MIB),
        name="place_owned",
    )(own, arrived.reshape(arrived.shape[0], -1, LANES))


def ring(axis, distance):
    size = lax.axis_size(axis)
    return [(i, (i + distance) % size) for i in range(size)]


def body(tracers, offsets, weights, diffusion, send_index, send_count):
    ntr, levels, lats, lons = tracers.shape
    columns = lats * lons
    west_cells, east_cells = pack_halo(tracers)
    from_west = lax.ppermute(east_cells, "lon", ring("lon", 1))
    from_east = lax.ppermute(west_cells, "lon", ring("lon", -1))
    *fields, lists = advect_inside(tracers, offsets, weights, diffusion, send_index, send_count)
    sent = make_sent(from_west, from_east, fields, lists, send_count.shape[1])
    arrived = lax.all_to_all(sent, ("lon", "lat"), split_axis=0, concat_axis=0, tiled=True)
    own = lax.axis_index(("lon", "lat")).astype(jnp.int32).reshape(1)
    owned = place_owned(arrived, own, levels, ntr, columns)
    return jnp.transpose(owned, (1, 0, 2))


def solution(mesh):
    return jax.shard_map(
        body,
        mesh=mesh,
        in_specs=(
            P(None, None, "lat", "lon"),
            P(None, "lat", "lon"),
            P(None, "lat", "lon"),
            P(None, "lat", "lon"),
            P(("lon", "lat"), None, None),
            P(("lon", "lat"), None),
        ),
        out_specs=P(None, None, ("lon", "lat")),
        check_vma=False,
    )
```

```python
import functools

import jax
import jax.numpy as jnp
from jax import lax
from jax.experimental import pallas as pl
from jax.experimental.pallas import tpu as pltpu
from jax.sharding import PartitionSpec as P

HALO = 16
LANES = 128
SUB = 8
SLOT = 32
FIRST = 32
MIB = 1024 * 1024
LENGTH_BASE = 1000.0
BIG = 60 * MIB
SOLVE = 107 * MIB // 2
LIST_ROWS = 256


def take_lanes(block, index):
    return jnp.take_along_axis(block, index, axis=1, mode="promise_in_bounds")


def shift_down(number, power):
    return lax.shift_right_logical(number, power.bit_length() - 1)


def lane_ids(rows):
    return lax.broadcasted_iota(jnp.int32, (rows, LANES), 1)


def fetch(sources, targets, ready):
    copies = [
        pltpu.make_async_copy(source, target, ready.at[item])
        for item, (source, target) in enumerate(zip(sources, targets))
    ]
    for copy in copies:
        copy.start()
    return copies


def pack_halo_kernel(tracers_in, west_cells, east_cells, tracers, ready):
    ntr, levels, lats, _ = tracers.shape
    per_row = LANES // HALO
    group = lane_ids(SUB) // HALO
    assert lats == SUB * per_row
    copies = fetch(
        [tracers_in.at[:, level] for level in range(levels)],
        [tracers.at[:, level] for level in range(levels)],
        ready,
    )
    for level in range(levels):
        copies[level].wait()
        for tracer in range(ntr):
            west = jnp.zeros((SUB, LANES), jnp.float32)
            east = jnp.zeros((SUB, LANES), jnp.float32)
            for part in range(lats // SUB):
                cells = tracers[tracer, level, part * SUB : (part + 1) * SUB, :]
                shift = part * HALO
                rolled_west = pltpu.roll(cells, shift, 1) if shift else cells
                shift = (part * HALO + HALO) % LANES
                rolled_east = pltpu.roll(cells, shift, 1) if shift else cells
                west = jnp.where(group == part, rolled_west, west)
                east = jnp.where(group == part, rolled_east, east)
            west_cells[level, tracer] = west
            east_cells[level, tracer] = east


def pack_halo(tracers):
    ntr, levels, _, _ = tracers.shape
    shape = jax.ShapeDtypeStruct((levels, ntr, SUB, LANES), jnp.float32)
    return pl.pallas_call(
        pack_halo_kernel,
        out_shape=(shape, shape),
        in_specs=[pl.BlockSpec(memory_space=pl.ANY)],
        out_specs=[pl.BlockSpec(memory_space=pltpu.VMEM)] * 2,
        scratch_shapes=[pltpu.VMEM(tracers.shape, jnp.float32), pltpu.SemaphoreType.DMA((levels,))],
        compiler_params=pltpu.CompilerParams(vmem_limit_bytes=SOLVE),
        name="pack_halo",
    )(tracers)


def merge_halo(west, east, halo, count):
    lane = lane_ids(SUB)
    cell = lane % (2 * HALO)
    sources = [(half * 4 + lane // (2 * HALO)) * HALO + cell % HALO for half in range(2)]
    chunk = 10 if count % 10 == 0 else 1

    def some_values(step, carry):
        merged = []
        for item in range(chunk):
            value = step * chunk + item
            for half in range(2):
                both = take_lanes(west[value], sources[half]), take_lanes(east[value], sources[half])
                merged.append((value, half, jnp.where(cell < HALO, *both)))
        for value, half, cells in merged:
            halo[value, half] = cells
        return carry

    lax.fori_loop(0, count // chunk, some_values, 0)


def edge_place(part):
    quarter = part & 3
    group = shift_down(lane_ids(SUB), 2 * HALO) == quarter
    return shift_down(part, 4), group, (quarter * (2 * HALO) + HALO) & (LANES - 1)


def edge_tile(kind, level, half, levels, lats):
    tile = (kind * levels + level) * 2 + half
    per_plane = lats // SUB
    row = pl.multiple_of((tile & (per_plane - 1)) * SUB, SUB)
    return shift_down(tile, per_plane), pl.ds(row, SUB)


def inside_kernel(
    tracers_in, offsets_in, weights_in, diffusion_in, index_in, count,
    inside, lower, upper, lists,
    tracers, offsets, weights, diffusion, ready,
):
    ntr, levels, lats, _ = tracers.shape
    lane = lane_ids(SUB)
    owners = count.shape[1]
    copies = fetch(
        (diffusion_in, offsets_in, weights_in, tracers_in, index_in.at[0]),
        (diffusion, offsets, weights, tracers, lists.at[pl.ds(0, owners)]),
        ready,
    )
    lists[owners : owners + 1, :owners] = count[...]
    for copy in copies:
        copy.wait()

    def one_part(part, carry):
        rows = pl.ds(pl.multiple_of(part * SUB, SUB), SUB)
        coefs = [diffusion[level, rows, :] for level in range(levels - 1)]
        lowers, uppers, edges, results = [], [], [], []
        for level in range(levels):
            denom = 1.0
            if level > 0:
                denom = denom + coefs[level - 1]
            if level < levels - 1:
                denom = denom + coefs[level]
            if level > 0:
                denom = denom - coefs[level - 1] * uppers[level - 1]
            inverse = 1.0 / denom
            if level > 0:
                lowers.append(coefs[level - 1] * inverse)
            if level < levels - 1:
                uppers.append(coefs[level] * inverse)
            left = lane + offsets[level, rows, :]
            right = left + 1
            weight = weights[level, rows, :]
            west_weight = (1.0 - weight) * inverse
            east_weight = weight * inverse
            left_in = (left >= 0) & (left < LANES)
            right_in = (right >= 0) & (right < LANES)
            edges.append((left.astype(jnp.float32), jnp.where(left_in, 0.0, west_weight), jnp.where(right_in, 0.0, east_weight)))
            west_weight = jnp.where(left_in, west_weight, 0.0)
            east_weight = jnp.where(right_in, east_weight, 0.0)
            left = left & (LANES - 1)
            right = right & (LANES - 1)
            for tracer in range(ntr):
                cells = tracers[tracer, level, rows, :]
                results.append(west_weight * take_lanes(cells, left) + east_weight * take_lanes(cells, right))
        for value, result in enumerate(results):
            inside[value, rows, :] = result
        half, group, shift = edge_place(part)
        packed = [[pltpu.roll(field, shift, 1) for field in fields] for fields in edges]
        for level, fields in enumerate(packed):
            for kind, field in enumerate(fields):
                plane, band = edge_tile(kind, level, half, levels, lats)
                pltpu.store(inside.at[ntr * levels + plane, band, :], field, mask=group)
        for level in range(levels - 1):
            lower[level, rows, :] = lowers[level]
            upper[level, rows, :] = uppers[level]
        return carry

    lax.fori_loop(0, lats // SUB, one_part, 0)


def advect_inside(tracers, offsets, weights, diffusion, index, count):
    ntr, levels, lats, lons = tracers.shape
    lists, cap = index.shape[1:]
    vmem = pl.BlockSpec(memory_space=pltpu.VMEM)
    field = lambda count: jax.ShapeDtypeStruct((count, lats, lons), jnp.float32)
    edge_planes = -(-3 * levels * 2 * SUB // lats)
    outputs = (
        field(ntr * levels + edge_planes),
        field(levels - 1),
        field(levels - 1),
        jax.ShapeDtypeStruct((max(lists + SUB, LIST_ROWS), cap), jnp.int32),
    )
    return pl.pallas_call(
        inside_kernel,
        out_shape=outputs,
        in_specs=[pl.BlockSpec(memory_space=pl.ANY)] * 5 + [vmem],
        out_specs=(vmem,) * len(outputs),
        scratch_shapes=[pltpu.VMEM(array.shape, array.dtype) for array in (tracers, offsets, weights, diffusion)]
        + [pltpu.SemaphoreType.DMA((5,))],
        compiler_params=pltpu.CompilerParams(vmem_limit_bytes=BIG),
        cost_estimate=pl.CostEstimate(flops=0, bytes_accessed=20 * MIB, transcendentals=0),
        name="advect_inside",
    )(tracers, offsets, weights, diffusion, index, count)


def make_edges(fields, halo, edges, levels):
    ntr = edges.shape[0] // levels
    lats = fields.shape[1]
    group = lane_ids(SUB) & (LANES - 2 * HALO)

    def one_level(level, carry):
        results = []
        for half in range(2):
            left, west_weight, east_weight = [
                fields[plane, band, :]
                for plane, band in [edge_tile(kind, level, half, levels, lats) for kind in range(3)]
            ]
            left = left.astype(jnp.int32) + HALO
            right = group + ((left + 1) & (2 * HALO - 1))
            left = group + (left & (2 * HALO - 1))
            for tracer in range(ntr):
                value = level * ntr + tracer
                cells = halo[value, half]
                share = west_weight * take_lanes(cells, left)
                results.append((value, half, share + east_weight * take_lanes(cells, right)))
        for value, half, share in results:
            edges[value, half] = share
        return carry

    lax.fori_loop(0, levels, one_level, 0)


def add_edges_and_solve(inside, lower, upper, edges, solved, together, wait_rows):
    values, lats, _ = inside.shape
    levels = upper.shape[0] + 1
    ntr = values // levels
    lane = lane_ids(SUB)
    at_edge = (lane < HALO) | (lane >= LANES - HALO)

    def solve_part(part):
        rows = pl.ds(pl.multiple_of(part * SUB, SUB), SUB)
        half, _, shift = edge_place(part)
        back = (LANES - shift) & (LANES - 1)
        reduced = [[] for _ in range(ntr)]
        for level in range(levels):
            for tracer in range(ntr):
                value = level * ntr + tracer
                share = jnp.where(at_edge, pltpu.roll(edges[value, half], back, 1), 0.0)
                total = inside[value, rows, :] + share
                if level > 0:
                    total = total + lower[level - 1, rows, :] * reduced[tracer][level - 1]
                reduced[tracer].append(total)
        results = {}
        for level in range(levels - 1, -1, -1):
            for tracer in range(ntr):
                x = reduced[tracer][level]
                if level < levels - 1:
                    x = x + upper[level, rows, :] * results[(level + 1) * ntr + tracer]
                results[level * ntr + tracer] = x
        return results

    def some_parts(step, carry):
        wait_rows(step)
        solutions = [solve_part(step * together + item) for item in range(together)]
        for item, results in enumerate(solutions):
            first = pl.multiple_of((step * together + item) * (SUB * SLOT), SUB * SLOT)
            target = solved.at[pl.ds(first, SUB * SLOT), :]
            for value, x in results.items():
                target[pl.ds(value, SUB, stride=SLOT), :] = x
        return carry

    lax.fori_loop(0, lats // (SUB * together), some_parts, 0)


def streams_of(rows, values, parts):
    lane = lane_ids(rows)
    width = values * parts
    item = sum((lane >= width * step).astype(jnp.int32) for step in range(1, 4 // parts))
    held = lane - item * width
    part = held & (parts - 1)
    return jnp.minimum(lax.shift_right_logical(held, parts.bit_length() - 1), values - 1), item * parts + part


def build_table(solved, table, values, parts):
    rows_per = LANES // SLOT
    spread = streams_of(LANES, values, parts)[0]
    together = 4

    def some_rows(step, carry):
        blocks = []
        for item in range(together):
            start = pl.multiple_of((step * together + item) * LANES, LANES)
            blocks.append(solved[pl.ds(start, LANES), :].T)
        for item, block in enumerate(blocks):
            for row in range(rows_per):
                start = pl.multiple_of(((step * together + item) * rows_per + row) * LANES, LANES)
                table[pl.ds(start, LANES), :] = take_lanes(block, spread + row * SLOT)
        return carry

    lax.fori_loop(0, solved.shape[0] // (LANES * together), some_rows, 0)


def pick_rows(table, index, count, cap, values, packed, turned, sent, copied, wait_list):
    blocks, height, _ = sent.shape
    parts = cap // LANES
    lists = 4 // parts
    stream = streams_of(1, values, parts)[1]

    def copy_out(block):
        return pltpu.make_async_copy(turned.at[block + 1], sent.at[block], copied.at[block])

    def turn(block):
        half = pl.multiple_of((block & 1) * LANES, LANES)
        return packed[pl.ds(half, LANES), :].T

    def send(block, result):
        turned[block + 1] = result[:height, :]
        for member in range(lists):
            total = count[jnp.maximum(block, 0) * lists + member]
            row = turned.at[block + 1, pl.ds((member * values + 1) * parts - 1, 1), :]
            note = jnp.full((1, LANES), LENGTH_BASE + total.astype(jnp.float32))
            pltpu.store(row, note, mask=(lane_ids(1) == LANES - 1) & (total < cap))

    def one_block(block, carry):
        owners = [block * lists + member for member in range(lists)]
        rows = [shift_down(count[owner] + (parts - 1), parts) for owner in owners]
        for owner in owners:
            wait_list(owner)
        longest = functools.reduce(jnp.maximum, rows)
        places = [owners[g // parts] * cap + (g % parts) * rows[g // parts] for g in range(4)]
        half = (block & 1) * LANES

        def load_lines(start, lines):
            views = [index.at[pl.ds(place + start, lines)] for place in places]
            merged = []
            for line in range(lines):
                picked = [table[view[line]] for view in views]
                low = jnp.where(stream == 0, picked[0], picked[1])
                high = jnp.where(stream == 2, picked[2], picked[3])
                merged.append(jnp.where(stream < 2, low, high))
            return merged

        def store_lines(start, merged):
            target = packed.at[pl.ds(pl.multiple_of(half + start, SUB), len(merged)), :]
            for line, value in enumerate(merged):
                target[line : line + 1, :] = value

        def steps(begin, trips, lines):
            def one_step(step, inner):
                start = pl.multiple_of(begin + step * lines, SUB)
                store_lines(start, load_lines(start, lines))
                return inner

            lax.fori_loop(0, trips, one_step, 0)
            return begin + trips * lines

        before = turn(block - 1)
        merged = load_lines(0, FIRST)
        store_lines(0, merged)
        send(block - 1, before)

        @pl.when(block > 0)
        def _():
            copy_out(block - 1).start()

        eights = jnp.maximum(shift_down(longest + (SUB - 1), SUB) - FIRST // SUB, 0)
        done = steps(FIRST, shift_down(eights, 4), 4 * SUB)
        done = steps(done, shift_down(eights & 3, 2), 2 * SUB)
        steps(done, eights & 1, SUB)
        return carry

    def finish(block, carry):
        copy_out(block).wait()
        return carry

    lax.fori_loop(0, blocks, one_block, 0)
    send(blocks - 1, turn(blocks - 1))
    copy_out(blocks - 1).start()
    lax.fori_loop(0, blocks, finish, 0)


def list_copies(lists_in, index, count, listed):
    cap = lists_in.shape[1]
    owners = index.shape[0] // cap
    lengths = pltpu.make_async_copy(lists_in.at[owners], count, listed.at[owners])

    def list_copy(item):
        place = pl.ds(pl.multiple_of(item * cap, LANES), cap)
        return pltpu.make_async_copy(lists_in.at[item], index.at[place], listed.at[item])

    def start_list(item, carry):
        list_copy(item).start()
        return carry

    lengths.start()
    lax.fori_loop(0, owners, start_list, 0)
    return lengths.wait, lambda item: list_copy(item).wait()


def solve_kernel(
    parts, west, east, inside_in, lower_in, upper_in, lists_in, sent, inside, lower, upper, edge_fields, ready, arrived,
    halo, edges, solved, table, packed, turned, index, count, listed, copied,
):
    values, lats, _ = inside.shape
    together = 2
    band = SUB * together

    def row_copies(step):
        rows = pl.ds(pl.multiple_of(step * band, band), band)
        return [
            pltpu.make_async_copy(source.at[: target.shape[0], rows], target.at[:, rows], arrived.at[step, item])
            for item, (source, target) in enumerate(
                ((inside_in, inside), (lower_in, lower), (upper_in, upper))
            )
        ]

    def wait_rows(step):
        for copy in row_copies(step):
            copy.wait()

    copies = fetch([inside_in.at[values:]], [edge_fields], ready)
    for step in range(lats // band):
        for copy in row_copies(step):
            copy.start()
    wait_lengths, wait_list = list_copies(lists_in, index, count, listed)
    for value in range(values, SLOT):
        solved[pl.ds(value, lats, stride=SLOT), :] = jnp.zeros((lats, LANES), jnp.float32)
    merge_halo(west, east, halo, values)
    for copy in copies:
        copy.wait()
    make_edges(edge_fields, halo, edges, upper.shape[0] + 1)
    add_edges_and_solve(inside, lower, upper, edges, solved, together, wait_rows)
    build_table(solved, table.reshape(table.shape[0], LANES), values, parts)
    wait_lengths()
    pick_rows(table, index, count, lists_in.shape[1], values, packed, turned, sent, copied, wait_list)


def make_sent(west, east, fields, lists_in, lists):
    _, lats, lons = fields[0].shape
    values = west.shape[0] * west.shape[1]
    edge_planes = fields[0].shape[0] - values
    cap = lists_in.shape[1]
    parts = cap // LANES
    blocks = lists * parts // 4
    halos = (west.reshape(values, SUB, LANES), east.reshape(values, SUB, LANES))
    sent = pl.pallas_call(
        functools.partial(solve_kernel, parts),
        out_shape=jax.ShapeDtypeStruct((blocks, 4 * values, LANES), jnp.float32),
        in_specs=[pl.BlockSpec(memory_space=pltpu.VMEM)] * 2 + [pl.BlockSpec(memory_space=pl.ANY)] * (len(fields) + 1),
        out_specs=pl.BlockSpec(memory_space=pl.ANY),
        scratch_shapes=[
            pltpu.VMEM((values, lats, lons), jnp.float32),
            pltpu.VMEM(fields[1].shape, jnp.float32),
            pltpu.VMEM(fields[2].shape, jnp.float32),
            pltpu.VMEM((edge_planes, lats, lons), jnp.float32),
            pltpu.SemaphoreType.DMA((1,)),
            pltpu.SemaphoreType.DMA((lats // (2 * SUB), 3)),
            pltpu.VMEM((values, 2, SUB, LANES), jnp.float32),
            pltpu.VMEM((values, 2, SUB, LANES), jnp.float32),
            pltpu.VMEM((lats * SLOT, LANES), jnp.float32),
            pltpu.VMEM((lats * lons, 1, LANES), jnp.float32),
            pltpu.VMEM((2 * LANES, LANES), jnp.float32),
            pltpu.VMEM((blocks + 1, 4 * values, LANES), jnp.float32),
            pltpu.SMEM((lists * cap,), jnp.int32),
            pltpu.SMEM((cap,), jnp.int32),
            pltpu.SemaphoreType.DMA((lists + 1,)),
            pltpu.SemaphoreType.DMA((blocks,)),
        ],
        compiler_params=pltpu.CompilerParams(vmem_limit_bytes=SOLVE),
        cost_estimate=pl.CostEstimate(flops=0, bytes_accessed=40 * MIB, transcendentals=0),
        name="solve_pick",
    )(*halos, *fields, lists_in)
    rows = values * parts
    tile = max(size for size in (1, 2, 4, 8) if rows % size == 0)
    return sent.reshape(lists, rows // tile, tile, LANES)


def place_kernel(own, arrived, owned_out, row, owned, written):
    sources, height, _ = arrived.shape
    levels, ntr, columns = owned.shape
    values = levels * ntr
    parts = height // values
    lane = lax.broadcasted_iota(jnp.int32, (values, LANES), 1)
    order = [own[0] - turn for turn in range(sources)]
    order = [jnp.where(source < 0, source + sources, source) for source in order]
    totals = []
    for source in order:
        note = arrived[source, parts - 1 : parts, :]
        total = jnp.where(note > 0.5 * LENGTH_BASE, note - LENGTH_BASE, 1.0 * parts * LANES)
        totals.append(total.astype(jnp.int32)[0, LANES - 1])
    start = 0
    for source, total in zip(order, totals):
        rows = shift_down(total + (parts - 1), parts)
        pieces = []
        for part in range(parts):
            place = start + jnp.minimum(part * rows, total)
            shift = place & (LANES - 1)
            piece = arrived[source, pl.ds(part, values, stride=parts), :]
            pieces.append((place - shift, shift, pltpu.roll(piece, shift, 1)))
        for tile, shift, rolled in pieces:
            here = pl.ds(pl.multiple_of(tile, LANES), LANES)
            after = pl.ds(pl.multiple_of(tile + LANES, LANES), LANES)
            pltpu.store(row.at[:, here], rolled, mask=lane >= shift)
            row[:, after] = rolled
        start = start + total
    copies = []
    for level in range(levels):
        owned[level] = row[level * ntr : (level + 1) * ntr, :columns]
        copies.append(pltpu.make_async_copy(owned.at[level], owned_out.at[level], written.at[level]))
        copies[level].start()
    for copy in copies:
        copy.wait()


def place_owned(arrived, own, levels, ntr, columns):
    vmem = pl.BlockSpec(memory_space=pltpu.VMEM)
    smem = pl.BlockSpec(memory_space=pltpu.SMEM)
    values = levels * ntr
    return pl.pallas_call(
        place_kernel,
        out_shape=jax.ShapeDtypeStruct((levels, ntr, columns), jnp.float32),
        in_specs=[smem, vmem],
        out_specs=pl.BlockSpec(memory_space=pl.ANY),
        scratch_shapes=[
            pltpu.VMEM((values, columns + 2 * LANES), jnp.float32),
            pltpu.VMEM((levels, ntr, columns), jnp.float32),
            pltpu.SemaphoreType.DMA((levels,)),
        ],
        compiler_params=pltpu.CompilerParams(vmem_limit_bytes=16 * MIB),
        name="place_owned",
    )(own, arrived.reshape(arrived.shape[0], -1, LANES))


def ring(axis, distance):
    size = lax.axis_size(axis)
    return [(i, (i + distance) % size) for i in range(size)]


def body(tracers, offsets, weights, diffusion, send_index, send_count):
    ntr, levels, lats, lons = tracers.shape
    columns = lats * lons
    west_cells, east_cells = pack_halo(tracers)
    from_west = lax.ppermute(east_cells, "lon", ring("lon", 1))
    from_east = lax.ppermute(west_cells, "lon", ring("lon", -1))
    *fields, lists = advect_inside(tracers, offsets, weights, diffusion, send_index, send_count)
    sent = make_sent(from_west, from_east, fields, lists, send_count.shape[1])
    arrived = lax.all_to_all(sent, ("lon", "lat"), split_axis=0, concat_axis=0, tiled=True)
    own = lax.axis_index(("lon", "lat")).astype(jnp.int32).reshape(1)
    owned = place_owned(arrived, own, levels, ntr, columns)
    return jnp.transpose(owned, (1, 0, 2))


def solution(mesh):
    return jax.shard_map(
        body,
        mesh=mesh,
        in_specs=(
            P(None, None, "lat", "lon"),
            P(None, "lat", "lon"),
            P(None, "lat", "lon"),
            P(None, "lat", "lon"),
            P(("lon", "lat"), None, None),
            P(("lon", "lat"), None),
        ),
        out_specs=P(None, None, ("lon", "lat")),
        check_vma=False,
    )
```

```python
import functools

import jax
import jax.numpy as jnp
from jax import lax
from jax.experimental import pallas as pl
from jax.experimental.pallas import tpu as pltpu
from jax.sharding import PartitionSpec as P

HALO = 16
LANES = 128
SUB = 8
SLOT = 32
FIRST = 32
MIB = 1024 * 1024
LENGTH_BASE = 1000.0
BIG = 60 * MIB
SOLVE = 107 * MIB // 2
LIST_ROWS = 256


def take_lanes(block, index):
    return jnp.take_along_axis(block, index, axis=1, mode="promise_in_bounds")


def lane_ids(rows):
    return lax.broadcasted_iota(jnp.int32, (rows, LANES), 1)


def fetch(sources, targets, ready):
    copies = [
        pltpu.make_async_copy(source, target, ready.at[item])
        for item, (source, target) in enumerate(zip(sources, targets))
    ]
    for copy in copies:
        copy.start()
    return copies


def pack_halo_kernel(tracers_in, west_cells, east_cells, tracers, ready):
    ntr, levels, lats, _ = tracers.shape
    per_row = LANES // HALO
    group = lane_ids(SUB) // HALO
    assert lats == SUB * per_row
    copies = fetch(
        [tracers_in.at[:, level] for level in range(levels)],
        [tracers.at[:, level] for level in range(levels)],
        ready,
    )
    for level in range(levels):
        copies[level].wait()
        for tracer in range(ntr):
            west = jnp.zeros((SUB, LANES), jnp.float32)
            east = jnp.zeros((SUB, LANES), jnp.float32)
            for part in range(lats // SUB):
                cells = tracers[tracer, level, part * SUB : (part + 1) * SUB, :]
                shift = part * HALO
                rolled_west = pltpu.roll(cells, shift, 1) if shift else cells
                shift = (part * HALO + HALO) % LANES
                rolled_east = pltpu.roll(cells, shift, 1) if shift else cells
                west = jnp.where(group == part, rolled_west, west)
                east = jnp.where(group == part, rolled_east, east)
            west_cells[level, tracer] = west
            east_cells[level, tracer] = east


def pack_halo(tracers):
    ntr, levels, _, _ = tracers.shape
    shape = jax.ShapeDtypeStruct((levels, ntr, SUB, LANES), jnp.float32)
    return pl.pallas_call(
        pack_halo_kernel,
        out_shape=(shape, shape),
        in_specs=[pl.BlockSpec(memory_space=pl.ANY)],
        out_specs=[pl.BlockSpec(memory_space=pltpu.VMEM)] * 2,
        scratch_shapes=[pltpu.VMEM(tracers.shape, jnp.float32), pltpu.SemaphoreType.DMA((levels,))],
        compiler_params=pltpu.CompilerParams(vmem_limit_bytes=SOLVE),
        name="pack_halo",
    )(tracers)


def merge_halo(west, east, halo, count):
    lane = lane_ids(SUB)
    cell = lane % (2 * HALO)
    sources = [(half * 4 + lane // (2 * HALO)) * HALO + cell % HALO for half in range(2)]
    chunk = 10 if count % 10 == 0 else 1

    def some_values(step, carry):
        merged = []
        for item in range(chunk):
            value = step * chunk + item
            for half in range(2):
                both = take_lanes(west[value], sources[half]), take_lanes(east[value], sources[half])
                merged.append((value, half, jnp.where(cell < HALO, *both)))
        for value, half, cells in merged:
            halo[value, half] = cells
        return carry

    lax.fori_loop(0, count // chunk, some_values, 0)


def inside_kernel(
    tracers_in, offsets_in, weights_in, diffusion_in, index_in, count,
    inside, left_cell, west_edge, east_edge, lower, upper, lists,
    tracers, offsets, weights, diffusion, ready,
):
    ntr, levels, lats, _ = tracers.shape
    lane = lane_ids(SUB)
    owners = count.shape[1]
    copies = fetch(
        (diffusion_in, offsets_in, weights_in, tracers_in, index_in.at[0]),
        (diffusion, offsets, weights, tracers, lists.at[pl.ds(0, owners)]),
        ready,
    )
    lists[owners : owners + 1, :owners] = count[...]
    for copy in copies:
        copy.wait()

    def one_part(part, carry):
        rows = pl.ds(pl.multiple_of(part * SUB, SUB), SUB)
        coefs = [diffusion[level, rows, :] for level in range(levels - 1)]
        lowers, uppers, edges, results = [], [], [], []
        for level in range(levels):
            denom = 1.0
            if level > 0:
                denom = denom + coefs[level - 1]
            if level < levels - 1:
                denom = denom + coefs[level]
            if level > 0:
                denom = denom - coefs[level - 1] * uppers[level - 1]
            inverse = 1.0 / denom
            if level > 0:
                lowers.append(coefs[level - 1] * inverse)
            if level < levels - 1:
                uppers.append(coefs[level] * inverse)
            left = lane + offsets[level, rows, :]
            right = left + 1
            weight = weights[level, rows, :]
            west_weight = (1.0 - weight) * inverse
            east_weight = weight * inverse
            left_in = (left >= 0) & (left < LANES)
            right_in = (right >= 0) & (right < LANES)
            edges.append((left, jnp.where(left_in, 0.0, west_weight), jnp.where(right_in, 0.0, east_weight)))
            west_weight = jnp.where(left_in, west_weight, 0.0)
            east_weight = jnp.where(right_in, east_weight, 0.0)
            left = left & (LANES - 1)
            right = right & (LANES - 1)
            for tracer in range(ntr):
                cells = tracers[tracer, level, rows, :]
                results.append(west_weight * take_lanes(cells, left) + east_weight * take_lanes(cells, right))
        for value, result in enumerate(results):
            inside[value, rows, :] = result
        for level, (left, west_weight, east_weight) in enumerate(edges):
            left_cell[level, rows, :] = left
            west_edge[level, rows, :] = west_weight
            east_edge[level, rows, :] = east_weight
        for level in range(levels - 1):
            lower[level, rows, :] = lowers[level]
            upper[level, rows, :] = uppers[level]
        return carry

    lax.fori_loop(0, lats // SUB, one_part, 0)


def advect_inside(tracers, offsets, weights, diffusion, index, count):
    ntr, levels, lats, lons = tracers.shape
    lists, cap = index.shape[1:]
    vmem = pl.BlockSpec(memory_space=pltpu.VMEM)
    field = lambda count, kind=jnp.float32: jax.ShapeDtypeStruct((count, lats, lons), kind)
    outputs = (
        field(ntr * levels),
        field(levels, jnp.int32),
        field(levels),
        field(levels),
        field(levels - 1),
        field(levels - 1),
        jax.ShapeDtypeStruct((max(lists + SUB, LIST_ROWS), cap), jnp.int32),
    )
    return pl.pallas_call(
        inside_kernel,
        out_shape=outputs,
        in_specs=[pl.BlockSpec(memory_space=pl.ANY)] * 5 + [vmem],
        out_specs=(vmem,) * len(outputs),
        scratch_shapes=[pltpu.VMEM(array.shape, array.dtype) for array in (tracers, offsets, weights, diffusion)]
        + [pltpu.SemaphoreType.DMA((5,))],
        compiler_params=pltpu.CompilerParams(vmem_limit_bytes=BIG),
        cost_estimate=pl.CostEstimate(flops=0, bytes_accessed=20 * MIB, transcendentals=0),
        name="advect_inside",
    )(tracers, offsets, weights, diffusion, index, count)


def add_edges_and_solve(inside, left_cell, west_edge, east_edge, lower, upper, halo, solved):
    levels, lats, _ = left_cell.shape
    ntr = inside.shape[0] // levels
    together = 2

    def solve_part(part):
        rows = pl.ds(pl.multiple_of(part * SUB, SUB), SUB)
        half = shift_down(part, 4)
        base = (part & 3) * (2 * HALO)
        reduced = [[] for _ in range(ntr)]
        for level in range(levels):
            left = left_cell[level, rows, :]
            right = base + ((left + (HALO + 1)) & (2 * HALO - 1))
            left = base + ((left + HALO) & (2 * HALO - 1))
            west_weight = west_edge[level, rows, :]
            east_weight = east_edge[level, rows, :]
            for tracer in range(ntr):
                value = level * ntr + tracer
                cells = halo[value, half]
                edges = west_weight * take_lanes(cells, left) + east_weight * take_lanes(cells, right)
                total = inside[value, rows, :] + edges
                if level > 0:
                    total = total + lower[level - 1, rows, :] * reduced[tracer][level - 1]
                reduced[tracer].append(total)
        results = {}
        for level in range(levels - 1, -1, -1):
            for tracer in range(ntr):
                x = reduced[tracer][level]
                if level < levels - 1:
                    x = x + upper[level, rows, :] * results[(level + 1) * ntr + tracer]
                results[level * ntr + tracer] = x
        return results

    def some_parts(step, carry):
        solutions = [solve_part(step * together + item) for item in range(together)]
        for item, results in enumerate(solutions):
            first = pl.multiple_of((step * together + item) * (SUB * SLOT), SUB * SLOT)
            target = solved.at[pl.ds(first, SUB * SLOT), :]
            for value, x in results.items():
                target[pl.ds(value, SUB, stride=SLOT), :] = x
        return carry

    lax.fori_loop(0, lats // (SUB * together), some_parts, 0)


def streams_of(rows, values, parts):
    lane = lane_ids(rows)
    width = values * parts
    item = sum((lane >= width * step).astype(jnp.int32) for step in range(1, 4 // parts))
    held = lane - item * width
    part = held & (parts - 1)
    return jnp.minimum(lax.shift_right_logical(held, parts.bit_length() - 1), values - 1), item * parts + part


def build_table(solved, table, values, parts):
    rows_per = LANES // SLOT
    spread = streams_of(LANES, values, parts)[0]
    together = 8

    def some_rows(step, carry):
        blocks = []
        for item in range(together):
            start = pl.multiple_of((step * together + item) * LANES, LANES)
            blocks.append(solved[pl.ds(start, LANES), :].T)
        for item, block in enumerate(blocks):
            for row in range(rows_per):
                start = pl.multiple_of(((step * together + item) * rows_per + row) * LANES, LANES)
                table[pl.ds(start, LANES), :] = take_lanes(block, spread + row * SLOT)
        return carry

    lax.fori_loop(0, solved.shape[0] // (LANES * together), some_rows, 0)


def shift_down(number, power):
    return lax.shift_right_logical(number, power.bit_length() - 1)


def pick_rows(table, index, count, cap, values, packed, turned, sent, copied, wait_list):
    blocks, height, _ = sent.shape
    parts = cap // LANES
    lists = 4 // parts
    stream = streams_of(1, values, parts)[1]

    def copy_out(block):
        return pltpu.make_async_copy(turned.at[block + 1], sent.at[block], copied.at[block])

    def turn(block):
        half = pl.multiple_of((block & 1) * LANES, LANES)
        return packed[pl.ds(half, LANES), :].T

    def send(block, result):
        turned[block + 1] = result[:height, :]
        for member in range(lists):
            total = count[jnp.maximum(block, 0) * lists + member]
            row = turned.at[block + 1, pl.ds((member * values + 1) * parts - 1, 1), :]
            note = jnp.full((1, LANES), LENGTH_BASE + total.astype(jnp.float32))
            pltpu.store(row, note, mask=(lane_ids(1) == LANES - 1) & (total < cap))

    def one_block(block, carry):
        owners = [block * lists + member for member in range(lists)]
        rows = [shift_down(count[owner] + (parts - 1), parts) for owner in owners]
        for owner in owners:
            wait_list(owner)
        longest = functools.reduce(jnp.maximum, rows)
        places = [owners[g // parts] * cap + (g % parts) * rows[g // parts] for g in range(4)]
        half = (block & 1) * LANES

        def load_lines(start, lines):
            views = [index.at[pl.ds(place + start, lines)] for place in places]
            merged = []
            for line in range(lines):
                picked = [table[view[line]] for view in views]
                low = jnp.where(stream == 0, picked[0], picked[1])
                high = jnp.where(stream == 2, picked[2], picked[3])
                merged.append(jnp.where(stream < 2, low, high))
            return merged

        def store_lines(start, merged):
            target = packed.at[pl.ds(pl.multiple_of(half + start, SUB), len(merged)), :]
            for line, value in enumerate(merged):
                target[line : line + 1, :] = value

        def steps(begin, trips, lines):
            def one_step(step, inner):
                start = pl.multiple_of(begin + step * lines, SUB)
                store_lines(start, load_lines(start, lines))
                return inner

            lax.fori_loop(0, trips, one_step, 0)

        before = turn(block - 1)
        merged = load_lines(0, FIRST)
        store_lines(0, merged)
        send(block - 1, before)

        @pl.when(block > 0)
        def _():
            copy_out(block - 1).start()

        eights = jnp.maximum(shift_down(longest + (SUB - 1), SUB) - FIRST // SUB, 0)
        steps(FIRST, shift_down(eights, 4), 4 * SUB)

        @pl.when((eights & 2) != 0)
        def _():
            start = pl.multiple_of(FIRST + shift_down(eights, 4) * (4 * SUB), SUB)
            store_lines(start, load_lines(start, 2 * SUB))

        @pl.when((eights & 1) != 0)
        def _():
            start = pl.multiple_of(FIRST + (eights - 1) * SUB, SUB)
            store_lines(start, load_lines(start, SUB))

        return carry

    def finish(block, carry):
        copy_out(block).wait()
        return carry

    lax.fori_loop(0, blocks, one_block, 0)
    send(blocks - 1, turn(blocks - 1))
    copy_out(blocks - 1).start()
    lax.fori_loop(0, blocks, finish, 0)


def list_copies(lists_in, index, count, listed):
    cap = lists_in.shape[1]
    owners = index.shape[0] // cap
    lengths = pltpu.make_async_copy(lists_in.at[owners], count, listed.at[owners])

    def list_copy(item):
        place = pl.ds(pl.multiple_of(item * cap, LANES), cap)
        return pltpu.make_async_copy(lists_in.at[item], index.at[place], listed.at[item])

    def start_list(item, carry):
        list_copy(item).start()
        return carry

    lengths.start()
    lax.fori_loop(0, owners, start_list, 0)
    return lengths.wait, lambda item: list_copy(item).wait()


def solve_kernel(
    parts, west, east, inside_in, left_cell_in, west_edge_in, east_edge_in, lower_in, upper_in, lists_in,
    sent, inside, left_cell, west_edge, east_edge, lower, upper, ready,
    halo, solved, table, packed, turned, index, count, listed, copied,
):
    values, lats, _ = inside.shape
    sources = (left_cell_in, west_edge_in, east_edge_in, lower_in, upper_in, inside_in)
    copies = fetch(sources, (left_cell, west_edge, east_edge, lower, upper, inside), ready)
    wait_lengths, wait_list = list_copies(lists_in, index, count, listed)
    for value in range(values, SLOT):
        solved[pl.ds(value, lats, stride=SLOT), :] = jnp.zeros((lats, LANES), jnp.float32)
    merge_halo(west, east, halo, values)
    for copy in copies:
        copy.wait()
    add_edges_and_solve(inside, left_cell, west_edge, east_edge, lower, upper, halo, solved)
    build_table(solved, table.reshape(table.shape[0], LANES), values, parts)
    wait_lengths()
    pick_rows(table, index, count, lists_in.shape[1], values, packed, turned, sent, copied, wait_list)


def make_sent(west, east, fields, lists_in, lists):
    values, lats, lons = fields[0].shape
    cap = lists_in.shape[1]
    parts = cap // LANES
    blocks = lists * parts // 4
    halos = (west.reshape(values, SUB, LANES), east.reshape(values, SUB, LANES))
    sent = pl.pallas_call(
        functools.partial(solve_kernel, parts),
        out_shape=jax.ShapeDtypeStruct((blocks, 4 * values, LANES), jnp.float32),
        in_specs=[pl.BlockSpec(memory_space=pltpu.VMEM)] * 2 + [pl.BlockSpec(memory_space=pl.ANY)] * (len(fields) + 1),
        out_specs=pl.BlockSpec(memory_space=pl.ANY),
        scratch_shapes=[pltpu.VMEM(array.shape, array.dtype) for array in fields]
        + [
            pltpu.SemaphoreType.DMA((len(fields),)),
            pltpu.VMEM((values, 2, SUB, LANES), jnp.float32),
            pltpu.VMEM((lats * SLOT, LANES), jnp.float32),
            pltpu.VMEM((lats * lons, 1, LANES), jnp.float32),
            pltpu.VMEM((2 * LANES, LANES), jnp.float32),
            pltpu.VMEM((blocks + 1, 4 * values, LANES), jnp.float32),
            pltpu.SMEM((lists * cap,), jnp.int32),
            pltpu.SMEM((cap,), jnp.int32),
            pltpu.SemaphoreType.DMA((lists + 1,)),
            pltpu.SemaphoreType.DMA((blocks,)),
        ],
        compiler_params=pltpu.CompilerParams(vmem_limit_bytes=SOLVE),
        cost_estimate=pl.CostEstimate(flops=0, bytes_accessed=40 * MIB, transcendentals=0),
        name="solve_pick",
    )(*halos, *fields, lists_in)
    rows = values * parts
    tile = max(size for size in (1, 2, 4, 8) if rows % size == 0)
    return sent.reshape(lists, rows // tile, tile, LANES)


def place_kernel(own, arrived, owned_out, row, owned, written):
    sources, height, _ = arrived.shape
    levels, ntr, columns = owned.shape
    values = levels * ntr
    parts = height // values
    lane = lax.broadcasted_iota(jnp.int32, (values, LANES), 1)
    order = [own[0] - turn for turn in range(sources)]
    order = [jnp.where(source < 0, source + sources, source) for source in order]
    totals = []
    for source in order:
        note = arrived[source, parts - 1 : parts, :]
        total = jnp.where(note > 0.5 * LENGTH_BASE, note - LENGTH_BASE, 1.0 * parts * LANES)
        totals.append(total.astype(jnp.int32)[0, LANES - 1])
    start = 0
    for source, total in zip(order, totals):
        rows = shift_down(total + (parts - 1), parts)
        pieces = []
        for part in range(parts):
            place = start + jnp.minimum(part * rows, total)
            shift = place & (LANES - 1)
            piece = arrived[source, pl.ds(part, values, stride=parts), :]
            pieces.append((place - shift, shift, pltpu.roll(piece, shift, 1)))
        for tile, shift, rolled in pieces:
            here = pl.ds(pl.multiple_of(tile, LANES), LANES)
            after = pl.ds(pl.multiple_of(tile + LANES, LANES), LANES)
            pltpu.store(row.at[:, here], rolled, mask=lane >= shift)
            row[:, after] = rolled
        start = start + total
    copies = []
    for level in range(levels):
        owned[level] = row[level * ntr : (level + 1) * ntr, :columns]
        copies.append(pltpu.make_async_copy(owned.at[level], owned_out.at[level], written.at[level]))
        copies[level].start()
    for copy in copies:
        copy.wait()


def place_owned(arrived, own, levels, ntr, columns):
    vmem = pl.BlockSpec(memory_space=pltpu.VMEM)
    smem = pl.BlockSpec(memory_space=pltpu.SMEM)
    values = levels * ntr
    return pl.pallas_call(
        place_kernel,
        out_shape=jax.ShapeDtypeStruct((levels, ntr, columns), jnp.float32),
        in_specs=[smem, vmem],
        out_specs=pl.BlockSpec(memory_space=pl.ANY),
        scratch_shapes=[
            pltpu.VMEM((values, columns + 2 * LANES), jnp.float32),
            pltpu.VMEM((levels, ntr, columns), jnp.float32),
            pltpu.SemaphoreType.DMA((levels,)),
        ],
        compiler_params=pltpu.CompilerParams(vmem_limit_bytes=16 * MIB),
        name="place_owned",
    )(own, arrived.reshape(arrived.shape[0], -1, LANES))


def ring(axis, distance):
    size = lax.axis_size(axis)
    return [(i, (i + distance) % size) for i in range(size)]


def body(tracers, offsets, weights, diffusion, send_index, send_count):
    ntr, levels, lats, lons = tracers.shape
    columns = lats * lons
    west_cells, east_cells = pack_halo(tracers)
    from_west = lax.ppermute(east_cells, "lon", ring("lon", 1))
    from_east = lax.ppermute(west_cells, "lon", ring("lon", -1))
    *fields, lists = advect_inside(tracers, offsets, weights, diffusion, send_index, send_count)
    sent = make_sent(from_west, from_east, fields, lists, send_count.shape[1])
    arrived = lax.all_to_all(sent, ("lon", "lat"), split_axis=0, concat_axis=0, tiled=True)
    own = lax.axis_index(("lon", "lat")).astype(jnp.int32).reshape(1)
    owned = place_owned(arrived, own, levels, ntr, columns)
    return jnp.transpose(owned, (1, 0, 2))


def solution(mesh):
    return jax.shard_map(
        body,
        mesh=mesh,
        in_specs=(
            P(None, None, "lat", "lon"),
            P(None, "lat", "lon"),
            P(None, "lat", "lon"),
            P(None, "lat", "lon"),
            P(("lon", "lat"), None, None),
            P(("lon", "lat"), None),
        ),
        out_specs=P(None, None, ("lon", "lat")),
        check_vma=False,
    )
```

```python
import functools

import jax
import jax.numpy as jnp
from jax import lax
from jax.experimental import pallas as pl
from jax.experimental.pallas import tpu as pltpu
from jax.sharding import PartitionSpec as P

HALO = 16
LANES = 128
SUB = 8
SLOT = 32
FIRST = 32
MIB = 1024 * 1024
LENGTH_BASE = 1000.0
BIG = 60 * MIB
SOLVE = 107 * MIB // 2
LIST_ROWS = 256


def take_lanes(block, index):
    return jnp.take_along_axis(block, index, axis=1, mode="promise_in_bounds")


def lane_ids(rows):
    return lax.broadcasted_iota(jnp.int32, (rows, LANES), 1)


def fetch(sources, targets, ready):
    copies = [
        pltpu.make_async_copy(source, target, ready.at[item])
        for item, (source, target) in enumerate(zip(sources, targets))
    ]
    for copy in copies:
        copy.start()
    return copies


def pack_halo_kernel(tracers_in, west_cells, east_cells, tracers, ready):
    ntr, levels, lats, _ = tracers.shape
    per_row = LANES // HALO
    group = lane_ids(SUB) // HALO
    assert lats == SUB * per_row
    copies = fetch(
        [tracers_in.at[:, level] for level in range(levels)],
        [tracers.at[:, level] for level in range(levels)],
        ready,
    )
    for level in range(levels):
        copies[level].wait()
        for tracer in range(ntr):
            west = jnp.zeros((SUB, LANES), jnp.float32)
            east = jnp.zeros((SUB, LANES), jnp.float32)
            for part in range(lats // SUB):
                cells = tracers[tracer, level, part * SUB : (part + 1) * SUB, :]
                shift = part * HALO
                rolled_west = pltpu.roll(cells, shift, 1) if shift else cells
                shift = (part * HALO + HALO) % LANES
                rolled_east = pltpu.roll(cells, shift, 1) if shift else cells
                west = jnp.where(group == part, rolled_west, west)
                east = jnp.where(group == part, rolled_east, east)
            west_cells[level, tracer] = west
            east_cells[level, tracer] = east


def pack_halo(tracers):
    ntr, levels, _, _ = tracers.shape
    shape = jax.ShapeDtypeStruct((levels, ntr, SUB, LANES), jnp.float32)
    return pl.pallas_call(
        pack_halo_kernel,
        out_shape=(shape, shape),
        in_specs=[pl.BlockSpec(memory_space=pl.ANY)],
        out_specs=[pl.BlockSpec(memory_space=pltpu.VMEM)] * 2,
        scratch_shapes=[pltpu.VMEM(tracers.shape, jnp.float32), pltpu.SemaphoreType.DMA((levels,))],
        compiler_params=pltpu.CompilerParams(vmem_limit_bytes=SOLVE),
        name="pack_halo",
    )(tracers)


def merge_halo(west, east, halo, count):
    lane = lane_ids(SUB)
    cell = lane % (2 * HALO)
    sources = [(half * 4 + lane // (2 * HALO)) * HALO + cell % HALO for half in range(2)]
    chunk = 10 if count % 10 == 0 else 1

    def some_values(step, carry):
        merged = []
        for item in range(chunk):
            value = step * chunk + item
            for half in range(2):
                both = take_lanes(west[value], sources[half]), take_lanes(east[value], sources[half])
                merged.append((value, half, jnp.where(cell < HALO, *both)))
        for value, half, cells in merged:
            halo[value, half] = cells
        return carry

    lax.fori_loop(0, count // chunk, some_values, 0)


def inside_kernel(
    tracers_in, offsets_in, weights_in, diffusion_in, index_in, count,
    inside, left_cell, west_edge, east_edge, lower, upper, lists,
    tracers, offsets, weights, diffusion, ready,
):
    ntr, levels, lats, _ = tracers.shape
    lane = lane_ids(SUB)
    owners = count.shape[1]
    copies = fetch(
        (diffusion_in, offsets_in, weights_in, tracers_in, index_in.at[0]),
        (diffusion, offsets, weights, tracers, lists.at[pl.ds(0, owners)]),
        ready,
    )
    lists[owners : owners + 1, :owners] = count[...]
    for copy in copies:
        copy.wait()

    def one_part(part, carry):
        rows = pl.ds(pl.multiple_of(part * SUB, SUB), SUB)
        coefs = [diffusion[level, rows, :] for level in range(levels - 1)]
        lowers, uppers, edges, results = [], [], [], []
        for level in range(levels):
            denom = 1.0
            if level > 0:
                denom = denom + coefs[level - 1]
            if level < levels - 1:
                denom = denom + coefs[level]
            if level > 0:
                denom = denom - coefs[level - 1] * uppers[level - 1]
            inverse = 1.0 / denom
            if level > 0:
                lowers.append(coefs[level - 1] * inverse)
            if level < levels - 1:
                uppers.append(coefs[level] * inverse)
            left = lane + offsets[level, rows, :]
            right = left + 1
            weight = weights[level, rows, :]
            west_weight = (1.0 - weight) * inverse
            east_weight = weight * inverse
            left_in = (left >= 0) & (left < LANES)
            right_in = (right >= 0) & (right < LANES)
            edges.append((left, jnp.where(left_in, 0.0, west_weight), jnp.where(right_in, 0.0, east_weight)))
            west_weight = jnp.where(left_in, west_weight, 0.0)
            east_weight = jnp.where(right_in, east_weight, 0.0)
            left = left & (LANES - 1)
            right = right & (LANES - 1)
            for tracer in range(ntr):
                cells = tracers[tracer, level, rows, :]
                results.append(west_weight * take_lanes(cells, left) + east_weight * take_lanes(cells, right))
        for value, result in enumerate(results):
            inside[value, rows, :] = result
        for level, (left, west_weight, east_weight) in enumerate(edges):
            left_cell[level, rows, :] = left
            west_edge[level, rows, :] = west_weight
            east_edge[level, rows, :] = east_weight
        for level in range(levels - 1):
            lower[level, rows, :] = lowers[level]
            upper[level, rows, :] = uppers[level]
        return carry

    lax.fori_loop(0, lats // SUB, one_part, 0)


def advect_inside(tracers, offsets, weights, diffusion, index, count):
    ntr, levels, lats, lons = tracers.shape
    lists, cap = index.shape[1:]
    vmem = pl.BlockSpec(memory_space=pltpu.VMEM)
    field = lambda count, kind=jnp.float32: jax.ShapeDtypeStruct((count, lats, lons), kind)
    outputs = (
        field(ntr * levels),
        field(levels, jnp.int32),
        field(levels),
        field(levels),
        field(levels - 1),
        field(levels - 1),
        jax.ShapeDtypeStruct((max(lists + SUB, LIST_ROWS), cap), jnp.int32),
    )
    return pl.pallas_call(
        inside_kernel,
        out_shape=outputs,
        in_specs=[pl.BlockSpec(memory_space=pl.ANY)] * 5 + [vmem],
        out_specs=(vmem,) * len(outputs),
        scratch_shapes=[pltpu.VMEM(array.shape, array.dtype) for array in (tracers, offsets, weights, diffusion)]
        + [pltpu.SemaphoreType.DMA((5,))],
        compiler_params=pltpu.CompilerParams(vmem_limit_bytes=BIG),
        cost_estimate=pl.CostEstimate(flops=0, bytes_accessed=20 * MIB, transcendentals=0),
        name="advect_inside",
    )(tracers, offsets, weights, diffusion, index, count)


def add_edges_and_solve(inside, left_cell, west_edge, east_edge, lower, upper, halo, solved):
    levels, lats, _ = left_cell.shape
    ntr = inside.shape[0] // levels
    together = 2

    def solve_part(part):
        rows = pl.ds(pl.multiple_of(part * SUB, SUB), SUB)
        half = shift_down(part, 4)
        base = (part & 3) * (2 * HALO)
        reduced = [[] for _ in range(ntr)]
        for level in range(levels):
            left = left_cell[level, rows, :]
            right = base + ((left + (HALO + 1)) & (2 * HALO - 1))
            left = base + ((left + HALO) & (2 * HALO - 1))
            west_weight = west_edge[level, rows, :]
            east_weight = east_edge[level, rows, :]
            for tracer in range(ntr):
                value = level * ntr + tracer
                cells = halo[value, half]
                edges = west_weight * take_lanes(cells, left) + east_weight * take_lanes(cells, right)
                total = inside[value, rows, :] + edges
                if level > 0:
                    total = total + lower[level - 1, rows, :] * reduced[tracer][level - 1]
                reduced[tracer].append(total)
        results = {}
        for level in range(levels - 1, -1, -1):
            for tracer in range(ntr):
                x = reduced[tracer][level]
                if level < levels - 1:
                    x = x + upper[level, rows, :] * results[(level + 1) * ntr + tracer]
                results[level * ntr + tracer] = x
        return results

    def some_parts(step, carry):
        solutions = [solve_part(step * together + item) for item in range(together)]
        for item, results in enumerate(solutions):
            first = pl.multiple_of((step * together + item) * (SUB * SLOT), SUB * SLOT)
            target = solved.at[pl.ds(first, SUB * SLOT), :]
            for value, x in results.items():
                target[pl.ds(value, SUB, stride=SLOT), :] = x
        return carry

    lax.fori_loop(0, lats // (SUB * together), some_parts, 0)


def streams_of(rows, values, parts):
    lane = lane_ids(rows)
    width = values * parts
    item = sum((lane >= width * step).astype(jnp.int32) for step in range(1, 4 // parts))
    held = lane - item * width
    part = held & (parts - 1)
    return jnp.minimum(lax.shift_right_logical(held, parts.bit_length() - 1), values - 1), item * parts + part


def build_table(solved, table, values, parts):
    rows_per = LANES // SLOT
    spread = streams_of(LANES, values, parts)[0]
    together = 8

    def some_rows(step, carry):
        blocks = []
        for item in range(together):
            start = pl.multiple_of((step * together + item) * LANES, LANES)
            blocks.append(solved[pl.ds(start, LANES), :].T)
        for item, block in enumerate(blocks):
            for row in range(rows_per):
                start = pl.multiple_of(((step * together + item) * rows_per + row) * LANES, LANES)
                table[pl.ds(start, LANES), :] = take_lanes(block, spread + row * SLOT)
        return carry

    lax.fori_loop(0, solved.shape[0] // (LANES * together), some_rows, 0)


def shift_down(number, power):
    return lax.shift_right_logical(number, power.bit_length() - 1)


def pick_rows(table, index, count, cap, values, packed, turned, sent, copied, wait_list):
    blocks, height, _ = sent.shape
    parts = cap // LANES
    lists = 4 // parts
    stream = streams_of(1, values, parts)[1]

    together = 2 if blocks % 2 == 0 else 1

    def copy_out(block):
        return pltpu.make_async_copy(turned.at[block + together], sent.at[block], copied.at[block])

    def buffer_of(block):
        return pl.multiple_of((block & (2 * together - 1)) * LANES, LANES)

    def turn(block):
        return packed[pl.ds(buffer_of(block), LANES), :].T

    def send(block, result):
        turned[block + together] = result[:height, :]
        for member in range(lists):
            total = count[jnp.maximum(block, 0) * lists + member]
            row = turned.at[block + together, pl.ds((member * values + 1) * parts - 1, 1), :]
            note = jnp.full((1, LANES), LENGTH_BASE + total.astype(jnp.float32))
            pltpu.store(row, note, mask=(lane_ids(1) == LANES - 1) & (total < cap))

    def plan(block):
        owners = [block * lists + member for member in range(lists)]
        rows = [shift_down(count[owner] + (parts - 1), parts) for owner in owners]
        for owner in owners:
            wait_list(owner)
        longest = functools.reduce(jnp.maximum, rows)
        eights = jnp.maximum(shift_down(longest + (SUB - 1), SUB) - FIRST // SUB, 0)
        return eights, [owners[g // parts] * cap + (g % parts) * rows[g // parts] for g in range(4)]

    def load_lines(places, start, lines):
        views = [index.at[pl.ds(place + start, lines)] for place in places]
        merged = []
        for line in range(lines):
            picked = [table[view[line]] for view in views]
            low = jnp.where(stream == 0, picked[0], picked[1])
            high = jnp.where(stream == 2, picked[2], picked[3])
            merged.append(jnp.where(stream < 2, low, high))
        return merged

    def store_lines(block, start, merged):
        target = packed.at[pl.ds(pl.multiple_of(buffer_of(block) + start, SUB), len(merged)), :]
        for line, value in enumerate(merged):
            target[line : line + 1, :] = value

    def finish_block(block, eights, places):
        def one_step(step, inner):
            start = pl.multiple_of(FIRST + step * (4 * SUB), SUB)
            store_lines(block, start, load_lines(places, start, 4 * SUB))
            return inner

        lax.fori_loop(0, shift_down(eights, 4), one_step, 0)

        @pl.when((eights & 2) != 0)
        def _():
            start = pl.multiple_of(FIRST + shift_down(eights, 4) * (4 * SUB), SUB)
            store_lines(block, start, load_lines(places, start, 2 * SUB))

        @pl.when((eights & 1) != 0)
        def _():
            start = pl.multiple_of(FIRST + (eights - 1) * SUB, SUB)
            store_lines(block, start, load_lines(places, start, SUB))

    def some_blocks(step, carry):
        group = [step * together + item for item in range(together)]
        plans = [plan(block) for block in group]
        before = [turn(block - together) for block in group]
        merged = [load_lines(places, 0, FIRST) for _, places in plans]
        for block, lines in zip(group, merged):
            store_lines(block, 0, lines)
        for block, result in zip(group, before):
            send(block - together, result)

        @pl.when(step > 0)
        def _():
            for block in group:
                copy_out(block - together).start()

        for block, (eights, places) in zip(group, plans):
            finish_block(block, eights, places)
        return carry

    def finish(block, carry):
        copy_out(block).wait()
        return carry

    lax.fori_loop(0, blocks // together, some_blocks, 0)
    last = range(blocks - together, blocks)
    for block, result in zip(last, [turn(block) for block in last]):
        send(block, result)
        copy_out(block).start()
    lax.fori_loop(0, blocks, finish, 0)


def list_copies(lists_in, index, count, listed):
    cap = lists_in.shape[1]
    owners = index.shape[0] // cap
    lengths = pltpu.make_async_copy(lists_in.at[owners], count, listed.at[owners])

    def list_copy(item):
        place = pl.ds(pl.multiple_of(item * cap, LANES), cap)
        return pltpu.make_async_copy(lists_in.at[item], index.at[place], listed.at[item])

    def start_list(item, carry):
        list_copy(item).start()
        return carry

    lengths.start()
    lax.fori_loop(0, owners, start_list, 0)
    return lengths.wait, lambda item: list_copy(item).wait()


def solve_kernel(
    parts, west, east, inside_in, left_cell_in, west_edge_in, east_edge_in, lower_in, upper_in, lists_in,
    sent, inside, left_cell, west_edge, east_edge, lower, upper, ready,
    halo, solved, table, packed, turned, index, count, listed, copied,
):
    values, lats, _ = inside.shape
    sources = (left_cell_in, west_edge_in, east_edge_in, lower_in, upper_in, inside_in)
    copies = fetch(sources, (left_cell, west_edge, east_edge, lower, upper, inside), ready)
    wait_lengths, wait_list = list_copies(lists_in, index, count, listed)
    for value in range(values, SLOT):
        solved[pl.ds(value, lats, stride=SLOT), :] = jnp.zeros((lats, LANES), jnp.float32)
    merge_halo(west, east, halo, values)
    for copy in copies:
        copy.wait()
    add_edges_and_solve(inside, left_cell, west_edge, east_edge, lower, upper, halo, solved)
    build_table(solved, table.reshape(table.shape[0], LANES), values, parts)
    wait_lengths()
    pick_rows(table, index, count, lists_in.shape[1], values, packed, turned, sent, copied, wait_list)


def make_sent(west, east, fields, lists_in, lists):
    values, lats, lons = fields[0].shape
    cap = lists_in.shape[1]
    parts = cap // LANES
    blocks = lists * parts // 4
    halos = (west.reshape(values, SUB, LANES), east.reshape(values, SUB, LANES))
    sent = pl.pallas_call(
        functools.partial(solve_kernel, parts),
        out_shape=jax.ShapeDtypeStruct((blocks, 4 * values, LANES), jnp.float32),
        in_specs=[pl.BlockSpec(memory_space=pltpu.VMEM)] * 2 + [pl.BlockSpec(memory_space=pl.ANY)] * (len(fields) + 1),
        out_specs=pl.BlockSpec(memory_space=pl.ANY),
        scratch_shapes=[pltpu.VMEM(array.shape, array.dtype) for array in fields]
        + [
            pltpu.SemaphoreType.DMA((len(fields),)),
            pltpu.VMEM((values, 2, SUB, LANES), jnp.float32),
            pltpu.VMEM((lats * SLOT, LANES), jnp.float32),
            pltpu.VMEM((lats * lons, 1, LANES), jnp.float32),
            pltpu.VMEM((4 * LANES, LANES), jnp.float32),
            pltpu.VMEM((blocks + 2, 4 * values, LANES), jnp.float32),
            pltpu.SMEM((lists * cap,), jnp.int32),
            pltpu.SMEM((cap,), jnp.int32),
            pltpu.SemaphoreType.DMA((lists + 1,)),
            pltpu.SemaphoreType.DMA((blocks,)),
        ],
        compiler_params=pltpu.CompilerParams(vmem_limit_bytes=SOLVE),
        cost_estimate=pl.CostEstimate(flops=0, bytes_accessed=40 * MIB, transcendentals=0),
        name="solve_pick",
    )(*halos, *fields, lists_in)
    rows = values * parts
    tile = max(size for size in (1, 2, 4, 8) if rows % size == 0)
    return sent.reshape(lists, rows // tile, tile, LANES)


def place_kernel(own, arrived, owned_out, row, owned, written):
    sources, height, _ = arrived.shape
    levels, ntr, columns = owned.shape
    values = levels * ntr
    parts = height // values
    lane = lax.broadcasted_iota(jnp.int32, (values, LANES), 1)
    order = [own[0] - turn for turn in range(sources)]
    order = [jnp.where(source < 0, source + sources, source) for source in order]
    totals = []
    for source in order:
        note = arrived[source, parts - 1 : parts, :]
        total = jnp.where(note > 0.5 * LENGTH_BASE, note - LENGTH_BASE, 1.0 * parts * LANES)
        totals.append(total.astype(jnp.int32)[0, LANES - 1])
    start = 0
    for source, total in zip(order, totals):
        rows = shift_down(total + (parts - 1), parts)
        pieces = []
        for part in range(parts):
            place = start + jnp.minimum(part * rows, total)
            shift = place & (LANES - 1)
            piece = arrived[source, pl.ds(part, values, stride=parts), :]
            pieces.append((place - shift, shift, pltpu.roll(piece, shift, 1)))
        for tile, shift, rolled in pieces:
            here = pl.ds(pl.multiple_of(tile, LANES), LANES)
            after = pl.ds(pl.multiple_of(tile + LANES, LANES), LANES)
            pltpu.store(row.at[:, here], rolled, mask=lane >= shift)
            row[:, after] = rolled
        start = start + total
    copies = []
    for level in range(levels):
        owned[level] = row[level * ntr : (level + 1) * ntr, :columns]
        copies.append(pltpu.make_async_copy(owned.at[level], owned_out.at[level], written.at[level]))
        copies[level].start()
    for copy in copies:
        copy.wait()


def place_owned(arrived, own, levels, ntr, columns):
    vmem = pl.BlockSpec(memory_space=pltpu.VMEM)
    smem = pl.BlockSpec(memory_space=pltpu.SMEM)
    values = levels * ntr
    return pl.pallas_call(
        place_kernel,
        out_shape=jax.ShapeDtypeStruct((levels, ntr, columns), jnp.float32),
        in_specs=[smem, vmem],
        out_specs=pl.BlockSpec(memory_space=pl.ANY),
        scratch_shapes=[
            pltpu.VMEM((values, columns + 2 * LANES), jnp.float32),
            pltpu.VMEM((levels, ntr, columns), jnp.float32),
            pltpu.SemaphoreType.DMA((levels,)),
        ],
        compiler_params=pltpu.CompilerParams(vmem_limit_bytes=16 * MIB),
        name="place_owned",
    )(own, arrived.reshape(arrived.shape[0], -1, LANES))


def ring(axis, distance):
    size = lax.axis_size(axis)
    return [(i, (i + distance) % size) for i in range(size)]


def body(tracers, offsets, weights, diffusion, send_index, send_count):
    ntr, levels, lats, lons = tracers.shape
    columns = lats * lons
    west_cells, east_cells = pack_halo(tracers)
    from_west = lax.ppermute(east_cells, "lon", ring("lon", 1))
    from_east = lax.ppermute(west_cells, "lon", ring("lon", -1))
    *fields, lists = advect_inside(tracers, offsets, weights, diffusion, send_index, send_count)
    sent = make_sent(from_west, from_east, fields, lists, send_count.shape[1])
    arrived = lax.all_to_all(sent, ("lon", "lat"), split_axis=0, concat_axis=0, tiled=True)
    own = lax.axis_index(("lon", "lat")).astype(jnp.int32).reshape(1)
    owned = place_owned(arrived, own, levels, ntr, columns)
    return jnp.transpose(owned, (1, 0, 2))


def solution(mesh):
    return jax.shard_map(
        body,
        mesh=mesh,
        in_specs=(
            P(None, None, "lat", "lon"),
            P(None, "lat", "lon"),
            P(None, "lat", "lon"),
            P(None, "lat", "lon"),
            P(("lon", "lat"), None, None),
            P(("lon", "lat"), None),
        ),
        out_specs=P(None, None, ("lon", "lat")),
        check_vma=False,
    )
```

```python
import functools

import jax
import jax.numpy as jnp
from jax import lax
from jax.experimental import pallas as pl
from jax.experimental.pallas import tpu as pltpu
from jax.sharding import PartitionSpec as P

HALO = 16
LANES = 128
SUB = 8
SLOT = 32
FIRST = 24
MIB = 1024 * 1024
LENGTH_BASE = 1000.0
BIG = 60 * MIB
SOLVE = 107 * MIB // 2
LIST_ROWS = 256


def take_lanes(block, index):
    return jnp.take_along_axis(block, index, axis=1, mode="promise_in_bounds")


def lane_ids(rows):
    return lax.broadcasted_iota(jnp.int32, (rows, LANES), 1)


def fetch(sources, targets, ready):
    copies = [
        pltpu.make_async_copy(source, target, ready.at[item])
        for item, (source, target) in enumerate(zip(sources, targets))
    ]
    for copy in copies:
        copy.start()
    return copies


def pack_halo_kernel(tracers_in, west_cells, east_cells, tracers, ready):
    ntr, levels, lats, _ = tracers.shape
    per_row = LANES // HALO
    group = lane_ids(SUB) // HALO
    assert lats == SUB * per_row
    copies = fetch(
        [tracers_in.at[:, level] for level in range(levels)],
        [tracers.at[:, level] for level in range(levels)],
        ready,
    )
    for level in range(levels):
        copies[level].wait()
        for tracer in range(ntr):
            west = jnp.zeros((SUB, LANES), jnp.float32)
            east = jnp.zeros((SUB, LANES), jnp.float32)
            for part in range(lats // SUB):
                cells = tracers[tracer, level, part * SUB : (part + 1) * SUB, :]
                shift = part * HALO
                rolled_west = pltpu.roll(cells, shift, 1) if shift else cells
                shift = (part * HALO + HALO) % LANES
                rolled_east = pltpu.roll(cells, shift, 1) if shift else cells
                west = jnp.where(group == part, rolled_west, west)
                east = jnp.where(group == part, rolled_east, east)
            west_cells[level, tracer] = west
            east_cells[level, tracer] = east


def pack_halo(tracers):
    ntr, levels, _, _ = tracers.shape
    shape = jax.ShapeDtypeStruct((levels, ntr, SUB, LANES), jnp.float32)
    return pl.pallas_call(
        pack_halo_kernel,
        out_shape=(shape, shape),
        in_specs=[pl.BlockSpec(memory_space=pl.ANY)],
        out_specs=[pl.BlockSpec(memory_space=pltpu.VMEM)] * 2,
        scratch_shapes=[pltpu.VMEM(tracers.shape, jnp.float32), pltpu.SemaphoreType.DMA((levels,))],
        compiler_params=pltpu.CompilerParams(vmem_limit_bytes=SOLVE),
        name="pack_halo",
    )(tracers)


def merge_halo(west, east, halo, count):
    lane = lane_ids(SUB)
    cell = lane % (2 * HALO)
    sources = [(half * 4 + lane // (2 * HALO)) * HALO + cell % HALO for half in range(2)]
    chunk = 10 if count % 10 == 0 else 1

    def some_values(step, carry):
        merged = []
        for item in range(chunk):
            value = step * chunk + item
            for half in range(2):
                both = take_lanes(west[value], sources[half]), take_lanes(east[value], sources[half])
                merged.append((value, half, jnp.where(cell < HALO, *both)))
        for value, half, cells in merged:
            halo[value, half] = cells
        return carry

    lax.fori_loop(0, count // chunk, some_values, 0)


def inside_kernel(
    tracers_in, offsets_in, weights_in, diffusion_in, index_in, count,
    inside, left_cell, west_edge, east_edge, lower, upper, lists,
    tracers, offsets, weights, diffusion, ready,
):
    ntr, levels, lats, _ = tracers.shape
    lane = lane_ids(SUB)
    owners = count.shape[1]
    copies = fetch(
        (diffusion_in, offsets_in, weights_in, tracers_in, index_in.at[0]),
        (diffusion, offsets, weights, tracers, lists.at[pl.ds(0, owners)]),
        ready,
    )
    lists[owners : owners + 1, :owners] = count[...]
    for copy in copies:
        copy.wait()

    def one_part(part, carry):
        rows = pl.ds(pl.multiple_of(part * SUB, SUB), SUB)
        coefs = [diffusion[level, rows, :] for level in range(levels - 1)]
        lowers, uppers, edges, results = [], [], [], []
        for level in range(levels):
            denom = 1.0
            if level > 0:
                denom = denom + coefs[level - 1]
            if level < levels - 1:
                denom = denom + coefs[level]
            if level > 0:
                denom = denom - coefs[level - 1] * uppers[level - 1]
            inverse = 1.0 / denom
            if level > 0:
                lowers.append(coefs[level - 1] * inverse)
            if level < levels - 1:
                uppers.append(coefs[level] * inverse)
            left = lane + offsets[level, rows, :]
            right = left + 1
            weight = weights[level, rows, :]
            west_weight = (1.0 - weight) * inverse
            east_weight = weight * inverse
            left_in = (left >= 0) & (left < LANES)
            right_in = (right >= 0) & (right < LANES)
            edges.append((left, jnp.where(left_in, 0.0, west_weight), jnp.where(right_in, 0.0, east_weight)))
            west_weight = jnp.where(left_in, west_weight, 0.0)
            east_weight = jnp.where(right_in, east_weight, 0.0)
            left = left & (LANES - 1)
            right = right & (LANES - 1)
            for tracer in range(ntr):
                cells = tracers[tracer, level, rows, :]
                results.append(west_weight * take_lanes(cells, left) + east_weight * take_lanes(cells, right))
        for value, result in enumerate(results):
            inside[value, rows, :] = result
        for level, (left, west_weight, east_weight) in enumerate(edges):
            left_cell[level, rows, :] = left
            west_edge[level, rows, :] = west_weight
            east_edge[level, rows, :] = east_weight
        for level in range(levels - 1):
            lower[level, rows, :] = lowers[level]
            upper[level, rows, :] = uppers[level]
        return carry

    lax.fori_loop(0, lats // SUB, one_part, 0)


def advect_inside(tracers, offsets, weights, diffusion, index, count):
    ntr, levels, lats, lons = tracers.shape
    lists, cap = index.shape[1:]
    vmem = pl.BlockSpec(memory_space=pltpu.VMEM)
    field = lambda count, kind=jnp.float32: jax.ShapeDtypeStruct((count, lats, lons), kind)
    outputs = (
        field(ntr * levels),
        field(levels, jnp.int32),
        field(levels),
        field(levels),
        field(levels - 1),
        field(levels - 1),
        jax.ShapeDtypeStruct((max(lists + SUB, LIST_ROWS), cap), jnp.int32),
    )
    return pl.pallas_call(
        inside_kernel,
        out_shape=outputs,
        in_specs=[pl.BlockSpec(memory_space=pl.ANY)] * 5 + [vmem],
        out_specs=(vmem,) * len(outputs),
        scratch_shapes=[pltpu.VMEM(array.shape, array.dtype) for array in (tracers, offsets, weights, diffusion)]
        + [pltpu.SemaphoreType.DMA((5,))],
        compiler_params=pltpu.CompilerParams(vmem_limit_bytes=BIG),
        cost_estimate=pl.CostEstimate(flops=0, bytes_accessed=20 * MIB, transcendentals=0),
        name="advect_inside",
    )(tracers, offsets, weights, diffusion, index, count)


def add_edges_and_solve(inside, left_cell, west_edge, east_edge, lower, upper, halo, solved):
    levels, lats, _ = left_cell.shape
    ntr = inside.shape[0] // levels
    together = 2

    def solve_part(part):
        rows = pl.ds(pl.multiple_of(part * SUB, SUB), SUB)
        half = shift_down(part, 4)
        base = (part & 3) * (2 * HALO)
        reduced = [[] for _ in range(ntr)]
        for level in range(levels):
            left = left_cell[level, rows, :]
            right = base + ((left + (HALO + 1)) & (2 * HALO - 1))
            left = base + ((left + HALO) & (2 * HALO - 1))
            west_weight = west_edge[level, rows, :]
            east_weight = east_edge[level, rows, :]
            for tracer in range(ntr):
                value = level * ntr + tracer
                cells = halo[value, half]
                edges = west_weight * take_lanes(cells, left) + east_weight * take_lanes(cells, right)
                total = inside[value, rows, :] + edges
                if level > 0:
                    total = total + lower[level - 1, rows, :] * reduced[tracer][level - 1]
                reduced[tracer].append(total)
        results = {}
        for level in range(levels - 1, -1, -1):
            for tracer in range(ntr):
                x = reduced[tracer][level]
                if level < levels - 1:
                    x = x + upper[level, rows, :] * results[(level + 1) * ntr + tracer]
                results[level * ntr + tracer] = x
        return results

    def some_parts(step, carry):
        solutions = [solve_part(step * together + item) for item in range(together)]
        for item, results in enumerate(solutions):
            first = pl.multiple_of((step * together + item) * (SUB * SLOT), SUB * SLOT)
            target = solved.at[pl.ds(first, SUB * SLOT), :]
            for value, x in results.items():
                target[pl.ds(value, SUB, stride=SLOT), :] = x
        return carry

    lax.fori_loop(0, lats // (SUB * together), some_parts, 0)


def streams_of(rows, values, parts):
    lane = lane_ids(rows)
    width = values * parts
    item = sum((lane >= width * step).astype(jnp.int32) for step in range(1, 4 // parts))
    held = lane - item * width
    part = held & (parts - 1)
    return jnp.minimum(lax.shift_right_logical(held, parts.bit_length() - 1), values - 1), item * parts + part


def build_table(solved, table, values, parts):
    rows_per = LANES // SLOT
    spread = streams_of(LANES, values, parts)[0]
    together = 8

    def some_rows(step, carry):
        blocks = []
        for item in range(together):
            start = pl.multiple_of((step * together + item) * LANES, LANES)
            blocks.append(solved[pl.ds(start, LANES), :].T)
        for item, block in enumerate(blocks):
            for row in range(rows_per):
                start = pl.multiple_of(((step * together + item) * rows_per + row) * LANES, LANES)
                table[pl.ds(start, LANES), :] = take_lanes(block, spread + row * SLOT)
        return carry

    lax.fori_loop(0, solved.shape[0] // (LANES * together), some_rows, 0)


def shift_down(number, power):
    return lax.shift_right_logical(number, power.bit_length() - 1)


def pick_rows(table, index, count, cap, values, packed, turned, sent, copied, wait_list):
    blocks, height, _ = sent.shape
    parts = cap // LANES
    lists = 4 // parts
    stream = streams_of(1, values, parts)[1]

    def copy_out(block):
        return pltpu.make_async_copy(turned.at[block + 1], sent.at[block], copied.at[block])

    def turn(block):
        half = pl.multiple_of((block & 1) * LANES, LANES)
        return packed[pl.ds(half, LANES), :].T

    def send(block, result):
        turned[block + 1] = result[:height, :]
        for member in range(lists):
            total = count[jnp.maximum(block, 0) * lists + member]
            row = turned.at[block + 1, pl.ds((member * values + 1) * parts - 1, 1), :]
            note = jnp.full((1, LANES), LENGTH_BASE + total.astype(jnp.float32))
            pltpu.store(row, note, mask=(lane_ids(1) == LANES - 1) & (total < cap))

    def one_block(block, carry):
        owners = [block * lists + member for member in range(lists)]
        rows = [shift_down(count[owner] + (parts - 1), parts) for owner in owners]
        for owner in owners:
            wait_list(owner)
        longest = functools.reduce(jnp.maximum, rows)
        places = [owners[g // parts] * cap + (g % parts) * rows[g // parts] for g in range(4)]
        half = (block & 1) * LANES

        def load_lines(start, lines):
            views = [index.at[pl.ds(place + start, lines)] for place in places]
            merged = []
            for line in range(lines):
                picked = [table[view[line]] for view in views]
                low = jnp.where(stream == 0, picked[0], picked[1])
                high = jnp.where(stream == 2, picked[2], picked[3])
                merged.append(jnp.where(stream < 2, low, high))
            return merged

        def store_lines(start, merged):
            target = packed.at[pl.ds(pl.multiple_of(half + start, SUB), len(merged)), :]
            for line, value in enumerate(merged):
                target[line : line + 1, :] = value

        def steps(begin, trips, lines):
            def one_step(step, inner):
                start = pl.multiple_of(begin + step * lines, SUB)
                store_lines(start, load_lines(start, lines))
                return inner

            lax.fori_loop(0, trips, one_step, 0)

        before = turn(block - 1)
        merged = load_lines(0, FIRST)
        store_lines(0, merged)
        send(block - 1, before)

        @pl.when(block > 0)
        def _():
            copy_out(block - 1).start()

        eights = jnp.maximum(shift_down(longest + (SUB - 1), SUB) - FIRST // SUB, 0)
        steps(FIRST, shift_down(eights, 4), 4 * SUB)

        @pl.when((eights & 2) != 0)
        def _():
            start = pl.multiple_of(FIRST + shift_down(eights, 4) * (4 * SUB), SUB)
            store_lines(start, load_lines(start, 2 * SUB))

        @pl.when((eights & 1) != 0)
        def _():
            start = pl.multiple_of(FIRST + (eights - 1) * SUB, SUB)
            store_lines(start, load_lines(start, SUB))

        return carry

    def finish(block, carry):
        copy_out(block).wait()
        return carry

    lax.fori_loop(0, blocks, one_block, 0)
    send(blocks - 1, turn(blocks - 1))
    copy_out(blocks - 1).start()
    lax.fori_loop(0, blocks, finish, 0)


def list_copies(lists_in, index, count, listed):
    cap = lists_in.shape[1]
    owners = index.shape[0] // cap
    lengths = pltpu.make_async_copy(lists_in.at[owners], count, listed.at[owners])

    def list_copy(item):
        place = pl.ds(pl.multiple_of(item * cap, LANES), cap)
        return pltpu.make_async_copy(lists_in.at[item], index.at[place], listed.at[item])

    def start_list(item, carry):
        list_copy(item).start()
        return carry

    lengths.start()
    lax.fori_loop(0, owners, start_list, 0)
    return lengths.wait, lambda item: list_copy(item).wait()


def solve_kernel(
    parts, west, east, inside_in, left_cell_in, west_edge_in, east_edge_in, lower_in, upper_in, lists_in,
    sent, inside, left_cell, west_edge, east_edge, lower, upper, ready,
    halo, solved, table, packed, turned, index, count, listed, copied,
):
    values, lats, _ = inside.shape
    sources = (left_cell_in, west_edge_in, east_edge_in, lower_in, upper_in, inside_in)
    copies = fetch(sources, (left_cell, west_edge, east_edge, lower, upper, inside), ready)
    wait_lengths, wait_list = list_copies(lists_in, index, count, listed)
    for value in range(values, SLOT):
        solved[pl.ds(value, lats, stride=SLOT), :] = jnp.zeros((lats, LANES), jnp.float32)
    merge_halo(west, east, halo, values)
    for copy in copies:
        copy.wait()
    add_edges_and_solve(inside, left_cell, west_edge, east_edge, lower, upper, halo, solved)
    build_table(solved, table.reshape(table.shape[0], LANES), values, parts)
    wait_lengths()
    pick_rows(table, index, count, lists_in.shape[1], values, packed, turned, sent, copied, wait_list)


def make_sent(west, east, fields, lists_in, lists):
    values, lats, lons = fields[0].shape
    cap = lists_in.shape[1]
    parts = cap // LANES
    blocks = lists * parts // 4
    halos = (west.reshape(values, SUB, LANES), east.reshape(values, SUB, LANES))
    sent = pl.pallas_call(
        functools.partial(solve_kernel, parts),
        out_shape=jax.ShapeDtypeStruct((blocks, 4 * values, LANES), jnp.float32),
        in_specs=[pl.BlockSpec(memory_space=pltpu.VMEM)] * 2 + [pl.BlockSpec(memory_space=pl.ANY)] * (len(fields) + 1),
        out_specs=pl.BlockSpec(memory_space=pl.ANY),
        scratch_shapes=[pltpu.VMEM(array.shape, array.dtype) for array in fields]
        + [
            pltpu.SemaphoreType.DMA((len(fields),)),
            pltpu.VMEM((values, 2, SUB, LANES), jnp.float32),
            pltpu.VMEM((lats * SLOT, LANES), jnp.float32),
            pltpu.VMEM((lats * lons, 1, LANES), jnp.float32),
            pltpu.VMEM((2 * LANES, LANES), jnp.float32),
            pltpu.VMEM((blocks + 1, 4 * values, LANES), jnp.float32),
            pltpu.SMEM((lists * cap,), jnp.int32),
            pltpu.SMEM((cap,), jnp.int32),
            pltpu.SemaphoreType.DMA((lists + 1,)),
            pltpu.SemaphoreType.DMA((blocks,)),
        ],
        compiler_params=pltpu.CompilerParams(vmem_limit_bytes=SOLVE),
        cost_estimate=pl.CostEstimate(flops=0, bytes_accessed=40 * MIB, transcendentals=0),
        name="solve_pick",
    )(*halos, *fields, lists_in)
    rows = values * parts
    tile = max(size for size in (1, 2, 4, 8) if rows % size == 0)
    return sent.reshape(lists, rows // tile, tile, LANES)


def place_kernel(own, arrived, owned_out, row, owned, written):
    sources, height, _ = arrived.shape
    levels, ntr, columns = owned.shape
    values = levels * ntr
    parts = height // values
    lane = lax.broadcasted_iota(jnp.int32, (values, LANES), 1)
    order = [own[0] - turn for turn in range(sources)]
    order = [jnp.where(source < 0, source + sources, source) for source in order]
    totals = []
    for source in order:
        note = arrived[source, parts - 1 : parts, :]
        total = jnp.where(note > 0.5 * LENGTH_BASE, note - LENGTH_BASE, 1.0 * parts * LANES)
        totals.append(total.astype(jnp.int32)[0, LANES - 1])
    start = 0
    for source, total in zip(order, totals):
        rows = shift_down(total + (parts - 1), parts)
        pieces = []
        for part in range(parts):
            place = start + jnp.minimum(part * rows, total)
            shift = place & (LANES - 1)
            piece = arrived[source, pl.ds(part, values, stride=parts), :]
            pieces.append((place - shift, shift, pltpu.roll(piece, shift, 1)))
        for tile, shift, rolled in pieces:
            here = pl.ds(pl.multiple_of(tile, LANES), LANES)
            after = pl.ds(pl.multiple_of(tile + LANES, LANES), LANES)
            pltpu.store(row.at[:, here], rolled, mask=lane >= shift)
            row[:, after] = rolled
        start = start + total
    copies = []
    for level in range(levels):
        owned[level] = row[level * ntr : (level + 1) * ntr, :columns]
        copies.append(pltpu.make_async_copy(owned.at[level], owned_out.at[level], written.at[level]))
        copies[level].start()
    for copy in copies:
        copy.wait()


def place_owned(arrived, own, levels, ntr, columns):
    vmem = pl.BlockSpec(memory_space=pltpu.VMEM)
    smem = pl.BlockSpec(memory_space=pltpu.SMEM)
    values = levels * ntr
    return pl.pallas_call(
        place_kernel,
        out_shape=jax.ShapeDtypeStruct((levels, ntr, columns), jnp.float32),
        in_specs=[smem, vmem],
        out_specs=pl.BlockSpec(memory_space=pl.ANY),
        scratch_shapes=[
            pltpu.VMEM((values, columns + 2 * LANES), jnp.float32),
            pltpu.VMEM((levels, ntr, columns), jnp.float32),
            pltpu.SemaphoreType.DMA((levels,)),
        ],
        compiler_params=pltpu.CompilerParams(vmem_limit_bytes=16 * MIB),
        name="place_owned",
    )(own, arrived.reshape(arrived.shape[0], -1, LANES))


def ring(axis, distance):
    size = lax.axis_size(axis)
    return [(i, (i + distance) % size) for i in range(size)]


def body(tracers, offsets, weights, diffusion, send_index, send_count):
    ntr, levels, lats, lons = tracers.shape
    columns = lats * lons
    west_cells, east_cells = pack_halo(tracers)
    from_west = lax.ppermute(east_cells, "lon", ring("lon", 1))
    from_east = lax.ppermute(west_cells, "lon", ring("lon", -1))
    *fields, lists = advect_inside(tracers, offsets, weights, diffusion, send_index, send_count)
    sent = make_sent(from_west, from_east, fields, lists, send_count.shape[1])
    arrived = lax.all_to_all(sent, ("lon", "lat"), split_axis=0, concat_axis=0, tiled=True)
    own = lax.axis_index(("lon", "lat")).astype(jnp.int32).reshape(1)
    owned = place_owned(arrived, own, levels, ntr, columns)
    return jnp.transpose(owned, (1, 0, 2))


def solution(mesh):
    return jax.shard_map(
        body,
        mesh=mesh,
        in_specs=(
            P(None, None, "lat", "lon"),
            P(None, "lat", "lon"),
            P(None, "lat", "lon"),
            P(None, "lat", "lon"),
            P(("lon", "lat"), None, None),
            P(("lon", "lat"), None),
        ),
        out_specs=P(None, None, ("lon", "lat")),
        check_vma=False,
    )
```

```python
import functools

import jax
import jax.numpy as jnp
from jax import lax
from jax.experimental import pallas as pl
from jax.experimental.pallas import tpu as pltpu
from jax.sharding import PartitionSpec as P

HALO = 16
LANES = 128
SUB = 8
SLOT = 32
FIRST = 40
MIB = 1024 * 1024
LENGTH_BASE = 1000.0
BIG = 60 * MIB
SOLVE = 107 * MIB // 2
LIST_ROWS = 256


def take_lanes(block, index):
    return jnp.take_along_axis(block, index, axis=1, mode="promise_in_bounds")


def lane_ids(rows):
    return lax.broadcasted_iota(jnp.int32, (rows, LANES), 1)


def fetch(sources, targets, ready):
    copies = [
        pltpu.make_async_copy(source, target, ready.at[item])
        for item, (source, target) in enumerate(zip(sources, targets))
    ]
    for copy in copies:
        copy.start()
    return copies


def pack_halo_kernel(tracers_in, west_cells, east_cells, tracers, ready):
    ntr, levels, lats, _ = tracers.shape
    per_row = LANES // HALO
    group = lane_ids(SUB) // HALO
    assert lats == SUB * per_row
    copies = fetch(
        [tracers_in.at[:, level] for level in range(levels)],
        [tracers.at[:, level] for level in range(levels)],
        ready,
    )
    for level in range(levels):
        copies[level].wait()
        for tracer in range(ntr):
            west = jnp.zeros((SUB, LANES), jnp.float32)
            east = jnp.zeros((SUB, LANES), jnp.float32)
            for part in range(lats // SUB):
                cells = tracers[tracer, level, part * SUB : (part + 1) * SUB, :]
                shift = part * HALO
                rolled_west = pltpu.roll(cells, shift, 1) if shift else cells
                shift = (part * HALO + HALO) % LANES
                rolled_east = pltpu.roll(cells, shift, 1) if shift else cells
                west = jnp.where(group == part, rolled_west, west)
                east = jnp.where(group == part, rolled_east, east)
            west_cells[level, tracer] = west
            east_cells[level, tracer] = east


def pack_halo(tracers):
    ntr, levels, _, _ = tracers.shape
    shape = jax.ShapeDtypeStruct((levels, ntr, SUB, LANES), jnp.float32)
    return pl.pallas_call(
        pack_halo_kernel,
        out_shape=(shape, shape),
        in_specs=[pl.BlockSpec(memory_space=pl.ANY)],
        out_specs=[pl.BlockSpec(memory_space=pltpu.VMEM)] * 2,
        scratch_shapes=[pltpu.VMEM(tracers.shape, jnp.float32), pltpu.SemaphoreType.DMA((levels,))],
        compiler_params=pltpu.CompilerParams(vmem_limit_bytes=SOLVE),
        name="pack_halo",
    )(tracers)


def merge_halo(west, east, halo, count):
    lane = lane_ids(SUB)
    cell = lane % (2 * HALO)
    sources = [(half * 4 + lane // (2 * HALO)) * HALO + cell % HALO for half in range(2)]
    chunk = 10 if count % 10 == 0 else 1

    def some_values(step, carry):
        merged = []
        for item in range(chunk):
            value = step * chunk + item
            for half in range(2):
                both = take_lanes(west[value], sources[half]), take_lanes(east[value], sources[half])
                merged.append((value, half, jnp.where(cell < HALO, *both)))
        for value, half, cells in merged:
            halo[value, half] = cells
        return carry

    lax.fori_loop(0, count // chunk, some_values, 0)


def inside_kernel(
    tracers_in, offsets_in, weights_in, diffusion_in, index_in, count,
    inside, left_cell, west_edge, east_edge, lower, upper, lists,
    tracers, offsets, weights, diffusion, ready,
):
    ntr, levels, lats, _ = tracers.shape
    lane = lane_ids(SUB)
    owners = count.shape[1]
    copies = fetch(
        (diffusion_in, offsets_in, weights_in, tracers_in, index_in.at[0]),
        (diffusion, offsets, weights, tracers, lists.at[pl.ds(0, owners)]),
        ready,
    )
    lists[owners : owners + 1, :owners] = count[...]
    for copy in copies:
        copy.wait()

    def one_part(part, carry):
        rows = pl.ds(pl.multiple_of(part * SUB, SUB), SUB)
        coefs = [diffusion[level, rows, :] for level in range(levels - 1)]
        lowers, uppers, edges, results = [], [], [], []
        for level in range(levels):
            denom = 1.0
            if level > 0:
                denom = denom + coefs[level - 1]
            if level < levels - 1:
                denom = denom + coefs[level]
            if level > 0:
                denom = denom - coefs[level - 1] * uppers[level - 1]
            inverse = 1.0 / denom
            if level > 0:
                lowers.append(coefs[level - 1] * inverse)
            if level < levels - 1:
                uppers.append(coefs[level] * inverse)
            left = lane + offsets[level, rows, :]
            right = left + 1
            weight = weights[level, rows, :]
            west_weight = (1.0 - weight) * inverse
            east_weight = weight * inverse
            left_in = (left >= 0) & (left < LANES)
            right_in = (right >= 0) & (right < LANES)
            edges.append((left, jnp.where(left_in, 0.0, west_weight), jnp.where(right_in, 0.0, east_weight)))
            west_weight = jnp.where(left_in, west_weight, 0.0)
            east_weight = jnp.where(right_in, east_weight, 0.0)
            left = left & (LANES - 1)
            right = right & (LANES - 1)
            for tracer in range(ntr):
                cells = tracers[tracer, level, rows, :]
                results.append(west_weight * take_lanes(cells, left) + east_weight * take_lanes(cells, right))
        for value, result in enumerate(results):
            inside[value, rows, :] = result
        for level, (left, west_weight, east_weight) in enumerate(edges):
            left_cell[level, rows, :] = left
            west_edge[level, rows, :] = west_weight
            east_edge[level, rows, :] = east_weight
        for level in range(levels - 1):
            lower[level, rows, :] = lowers[level]
            upper[level, rows, :] = uppers[level]
        return carry

    lax.fori_loop(0, lats // SUB, one_part, 0)


def advect_inside(tracers, offsets, weights, diffusion, index, count):
    ntr, levels, lats, lons = tracers.shape
    lists, cap = index.shape[1:]
    vmem = pl.BlockSpec(memory_space=pltpu.VMEM)
    field = lambda count, kind=jnp.float32: jax.ShapeDtypeStruct((count, lats, lons), kind)
    outputs = (
        field(ntr * levels),
        field(levels, jnp.int32),
        field(levels),
        field(levels),
        field(levels - 1),
        field(levels - 1),
        jax.ShapeDtypeStruct((max(lists + SUB, LIST_ROWS), cap), jnp.int32),
    )
    return pl.pallas_call(
        inside_kernel,
        out_shape=outputs,
        in_specs=[pl.BlockSpec(memory_space=pl.ANY)] * 5 + [vmem],
        out_specs=(vmem,) * len(outputs),
        scratch_shapes=[pltpu.VMEM(array.shape, array.dtype) for array in (tracers, offsets, weights, diffusion)]
        + [pltpu.SemaphoreType.DMA((5,))],
        compiler_params=pltpu.CompilerParams(vmem_limit_bytes=BIG),
        cost_estimate=pl.CostEstimate(flops=0, bytes_accessed=20 * MIB, transcendentals=0),
        name="advect_inside",
    )(tracers, offsets, weights, diffusion, index, count)


def add_edges_and_solve(inside, left_cell, west_edge, east_edge, lower, upper, halo, solved):
    levels, lats, _ = left_cell.shape
    ntr = inside.shape[0] // levels
    together = 2

    def solve_part(part):
        rows = pl.ds(pl.multiple_of(part * SUB, SUB), SUB)
        half = shift_down(part, 4)
        base = (part & 3) * (2 * HALO)
        reduced = [[] for _ in range(ntr)]
        for level in range(levels):
            left = left_cell[level, rows, :]
            right = base + ((left + (HALO + 1)) & (2 * HALO - 1))
            left = base + ((left + HALO) & (2 * HALO - 1))
            west_weight = west_edge[level, rows, :]
            east_weight = east_edge[level, rows, :]
            for tracer in range(ntr):
                value = level * ntr + tracer
                cells = halo[value, half]
                edges = west_weight * take_lanes(cells, left) + east_weight * take_lanes(cells, right)
                total = inside[value, rows, :] + edges
                if level > 0:
                    total = total + lower[level - 1, rows, :] * reduced[tracer][level - 1]
                reduced[tracer].append(total)
        results = {}
        for level in range(levels - 1, -1, -1):
            for tracer in range(ntr):
                x = reduced[tracer][level]
                if level < levels - 1:
                    x = x + upper[level, rows, :] * results[(level + 1) * ntr + tracer]
                results[level * ntr + tracer] = x
        return results

    def some_parts(step, carry):
        solutions = [solve_part(step * together + item) for item in range(together)]
        for item, results in enumerate(solutions):
            first = pl.multiple_of((step * together + item) * (SUB * SLOT), SUB * SLOT)
            target = solved.at[pl.ds(first, SUB * SLOT), :]
            for value, x in results.items():
                target[pl.ds(value, SUB, stride=SLOT), :] = x
        return carry

    lax.fori_loop(0, lats // (SUB * together), some_parts, 0)


def streams_of(rows, values, parts):
    lane = lane_ids(rows)
    width = values * parts
    item = sum((lane >= width * step).astype(jnp.int32) for step in range(1, 4 // parts))
    held = lane - item * width
    part = held & (parts - 1)
    return jnp.minimum(lax.shift_right_logical(held, parts.bit_length() - 1), values - 1), item * parts + part


def build_table(solved, table, values, parts):
    rows_per = LANES // SLOT
    spread = streams_of(LANES, values, parts)[0]
    together = 8

    def some_rows(step, carry):
        blocks = []
        for item in range(together):
            start = pl.multiple_of((step * together + item) * LANES, LANES)
            blocks.append(solved[pl.ds(start, LANES), :].T)
        for item, block in enumerate(blocks):
            for row in range(rows_per):
                start = pl.multiple_of(((step * together + item) * rows_per + row) * LANES, LANES)
                table[pl.ds(start, LANES), :] = take_lanes(block, spread + row * SLOT)
        return carry

    lax.fori_loop(0, solved.shape[0] // (LANES * together), some_rows, 0)


def shift_down(number, power):
    return lax.shift_right_logical(number, power.bit_length() - 1)


def pick_rows(table, index, count, cap, values, packed, turned, sent, copied, wait_list):
    blocks, height, _ = sent.shape
    parts = cap // LANES
    lists = 4 // parts
    stream = streams_of(1, values, parts)[1]

    def copy_out(block):
        return pltpu.make_async_copy(turned.at[block + 1], sent.at[block], copied.at[block])

    def turn(block):
        half = pl.multiple_of((block & 1) * LANES, LANES)
        return packed[pl.ds(half, LANES), :].T

    def send(block, result):
        turned[block + 1] = result[:height, :]
        for member in range(lists):
            total = count[jnp.maximum(block, 0) * lists + member]
            row = turned.at[block + 1, pl.ds((member * values + 1) * parts - 1, 1), :]
            note = jnp.full((1, LANES), LENGTH_BASE + total.astype(jnp.float32))
            pltpu.store(row, note, mask=(lane_ids(1) == LANES - 1) & (total < cap))

    def one_block(block, carry):
        owners = [block * lists + member for member in range(lists)]
        rows = [shift_down(count[owner] + (parts - 1), parts) for owner in owners]
        for owner in owners:
            wait_list(owner)
        longest = functools.reduce(jnp.maximum, rows)
        places = [owners[g // parts] * cap + (g % parts) * rows[g // parts] for g in range(4)]
        half = (block & 1) * LANES

        def load_lines(start, lines):
            views = [index.at[pl.ds(place + start, lines)] for place in places]
            merged = []
            for line in range(lines):
                picked = [table[view[line]] for view in views]
                low = jnp.where(stream == 0, picked[0], picked[1])
                high = jnp.where(stream == 2, picked[2], picked[3])
                merged.append(jnp.where(stream < 2, low, high))
            return merged

        def store_lines(start, merged):
            target = packed.at[pl.ds(pl.multiple_of(half + start, SUB), len(merged)), :]
            for line, value in enumerate(merged):
                target[line : line + 1, :] = value

        def steps(begin, trips, lines):
            def one_step(step, inner):
                start = pl.multiple_of(begin + step * lines, SUB)
                store_lines(start, load_lines(start, lines))
                return inner

            lax.fori_loop(0, trips, one_step, 0)

        before = turn(block - 1)
        merged = load_lines(0, FIRST)
        store_lines(0, merged)
        send(block - 1, before)

        @pl.when(block > 0)
        def _():
            copy_out(block - 1).start()

        eights = jnp.maximum(shift_down(longest + (SUB - 1), SUB) - FIRST // SUB, 0)
        steps(FIRST, shift_down(eights, 4), 4 * SUB)

        @pl.when((eights & 2) != 0)
        def _():
            start = pl.multiple_of(FIRST + shift_down(eights, 4) * (4 * SUB), SUB)
            store_lines(start, load_lines(start, 2 * SUB))

        @pl.when((eights & 1) != 0)
        def _():
            start = pl.multiple_of(FIRST + (eights - 1) * SUB, SUB)
            store_lines(start, load_lines(start, SUB))

        return carry

    def finish(block, carry):
        copy_out(block).wait()
        return carry

    lax.fori_loop(0, blocks, one_block, 0)
    send(blocks - 1, turn(blocks - 1))
    copy_out(blocks - 1).start()
    lax.fori_loop(0, blocks, finish, 0)


def list_copies(lists_in, index, count, listed):
    cap = lists_in.shape[1]
    owners = index.shape[0] // cap
    lengths = pltpu.make_async_copy(lists_in.at[owners], count, listed.at[owners])

    def list_copy(item):
        place = pl.ds(pl.multiple_of(item * cap, LANES), cap)
        return pltpu.make_async_copy(lists_in.at[item], index.at[place], listed.at[item])

    def start_list(item, carry):
        list_copy(item).start()
        return carry

    lengths.start()
    lax.fori_loop(0, owners, start_list, 0)
    return lengths.wait, lambda item: list_copy(item).wait()


def solve_kernel(
    parts, west, east, inside_in, left_cell_in, west_edge_in, east_edge_in, lower_in, upper_in, lists_in,
    sent, inside, left_cell, west_edge, east_edge, lower, upper, ready,
    halo, solved, table, packed, turned, index, count, listed, copied,
):
    values, lats, _ = inside.shape
    sources = (left_cell_in, west_edge_in, east_edge_in, lower_in, upper_in, inside_in)
    copies = fetch(sources, (left_cell, west_edge, east_edge, lower, upper, inside), ready)
    wait_lengths, wait_list = list_copies(lists_in, index, count, listed)
    for value in range(values, SLOT):
        solved[pl.ds(value, lats, stride=SLOT), :] = jnp.zeros((lats, LANES), jnp.float32)
    merge_halo(west, east, halo, values)
    for copy in copies:
        copy.wait()
    add_edges_and_solve(inside, left_cell, west_edge, east_edge, lower, upper, halo, solved)
    build_table(solved, table.reshape(table.shape[0], LANES), values, parts)
    wait_lengths()
    pick_rows(table, index, count, lists_in.shape[1], values, packed, turned, sent, copied, wait_list)


def make_sent(west, east, fields, lists_in, lists):
    values, lats, lons = fields[0].shape
    cap = lists_in.shape[1]
    parts = cap // LANES
    blocks = lists * parts // 4
    halos = (west.reshape(values, SUB, LANES), east.reshape(values, SUB, LANES))
    sent = pl.pallas_call(
        functools.partial(solve_kernel, parts),
        out_shape=jax.ShapeDtypeStruct((blocks, 4 * values, LANES), jnp.float32),
        in_specs=[pl.BlockSpec(memory_space=pltpu.VMEM)] * 2 + [pl.BlockSpec(memory_space=pl.ANY)] * (len(fields) + 1),
        out_specs=pl.BlockSpec(memory_space=pl.ANY),
        scratch_shapes=[pltpu.VMEM(array.shape, array.dtype) for array in fields]
        + [
            pltpu.SemaphoreType.DMA((len(fields),)),
            pltpu.VMEM((values, 2, SUB, LANES), jnp.float32),
            pltpu.VMEM((lats * SLOT, LANES), jnp.float32),
            pltpu.VMEM((lats * lons, 1, LANES), jnp.float32),
            pltpu.VMEM((2 * LANES, LANES), jnp.float32),
            pltpu.VMEM((blocks + 1, 4 * values, LANES), jnp.float32),
            pltpu.SMEM((lists * cap,), jnp.int32),
            pltpu.SMEM((cap,), jnp.int32),
            pltpu.SemaphoreType.DMA((lists + 1,)),
            pltpu.SemaphoreType.DMA((blocks,)),
        ],
        compiler_params=pltpu.CompilerParams(vmem_limit_bytes=SOLVE),
        cost_estimate=pl.CostEstimate(flops=0, bytes_accessed=40 * MIB, transcendentals=0),
        name="solve_pick",
    )(*halos, *fields, lists_in)
    rows = values * parts
    tile = max(size for size in (1, 2, 4, 8) if rows % size == 0)
    return sent.reshape(lists, rows // tile, tile, LANES)


def place_kernel(own, arrived, owned_out, row, owned, written):
    sources, height, _ = arrived.shape
    levels, ntr, columns = owned.shape
    values = levels * ntr
    parts = height // values
    lane = lax.broadcasted_iota(jnp.int32, (values, LANES), 1)
    order = [own[0] - turn for turn in range(sources)]
    order = [jnp.where(source < 0, source + sources, source) for source in order]
    totals = []
    for source in order:
        note = arrived[source, parts - 1 : parts, :]
        total = jnp.where(note > 0.5 * LENGTH_BASE, note - LENGTH_BASE, 1.0 * parts * LANES)
        totals.append(total.astype(jnp.int32)[0, LANES - 1])
    start = 0
    for source, total in zip(order, totals):
        rows = shift_down(total + (parts - 1), parts)
        pieces = []
        for part in range(parts):
            place = start + jnp.minimum(part * rows, total)
            shift = place & (LANES - 1)
            piece = arrived[source, pl.ds(part, values, stride=parts), :]
            pieces.append((place - shift, shift, pltpu.roll(piece, shift, 1)))
        for tile, shift, rolled in pieces:
            here = pl.ds(pl.multiple_of(tile, LANES), LANES)
            after = pl.ds(pl.multiple_of(tile + LANES, LANES), LANES)
            pltpu.store(row.at[:, here], rolled, mask=lane >= shift)
            row[:, after] = rolled
        start = start + total
    copies = []
    for level in range(levels):
        owned[level] = row[level * ntr : (level + 1) * ntr, :columns]
        copies.append(pltpu.make_async_copy(owned.at[level], owned_out.at[level], written.at[level]))
        copies[level].start()
    for copy in copies:
        copy.wait()


def place_owned(arrived, own, levels, ntr, columns):
    vmem = pl.BlockSpec(memory_space=pltpu.VMEM)
    smem = pl.BlockSpec(memory_space=pltpu.SMEM)
    values = levels * ntr
    return pl.pallas_call(
        place_kernel,
        out_shape=jax.ShapeDtypeStruct((levels, ntr, columns), jnp.float32),
        in_specs=[smem, vmem],
        out_specs=pl.BlockSpec(memory_space=pl.ANY),
        scratch_shapes=[
            pltpu.VMEM((values, columns + 2 * LANES), jnp.float32),
            pltpu.VMEM((levels, ntr, columns), jnp.float32),
            pltpu.SemaphoreType.DMA((levels,)),
        ],
        compiler_params=pltpu.CompilerParams(vmem_limit_bytes=16 * MIB),
        name="place_owned",
    )(own, arrived.reshape(arrived.shape[0], -1, LANES))


def ring(axis, distance):
    size = lax.axis_size(axis)
    return [(i, (i + distance) % size) for i in range(size)]


def body(tracers, offsets, weights, diffusion, send_index, send_count):
    ntr, levels, lats, lons = tracers.shape
    columns = lats * lons
    west_cells, east_cells = pack_halo(tracers)
    from_west = lax.ppermute(east_cells, "lon", ring("lon", 1))
    from_east = lax.ppermute(west_cells, "lon", ring("lon", -1))
    *fields, lists = advect_inside(tracers, offsets, weights, diffusion, send_index, send_count)
    sent = make_sent(from_west, from_east, fields, lists, send_count.shape[1])
    arrived = lax.all_to_all(sent, ("lon", "lat"), split_axis=0, concat_axis=0, tiled=True)
    own = lax.axis_index(("lon", "lat")).astype(jnp.int32).reshape(1)
    owned = place_owned(arrived, own, levels, ntr, columns)
    return jnp.transpose(owned, (1, 0, 2))


def solution(mesh):
    return jax.shard_map(
        body,
        mesh=mesh,
        in_specs=(
            P(None, None, "lat", "lon"),
            P(None, "lat", "lon"),
            P(None, "lat", "lon"),
            P(None, "lat", "lon"),
            P(("lon", "lat"), None, None),
            P(("lon", "lat"), None),
        ),
        out_specs=P(None, None, ("lon", "lat")),
        check_vma=False,
    )
```

```python
import functools

import jax
import jax.numpy as jnp
from jax import lax
from jax.experimental import pallas as pl
from jax.experimental.pallas import tpu as pltpu
from jax.sharding import PartitionSpec as P

HALO = 16
LANES = 128
SUB = 8
SLOT = 32
FIRST = 48
MIB = 1024 * 1024
LENGTH_BASE = 1000.0
BIG = 60 * MIB
SOLVE = 107 * MIB // 2
LIST_ROWS = 256


def take_lanes(block, index):
    return jnp.take_along_axis(block, index, axis=1, mode="promise_in_bounds")


def lane_ids(rows):
    return lax.broadcasted_iota(jnp.int32, (rows, LANES), 1)


def fetch(sources, targets, ready):
    copies = [
        pltpu.make_async_copy(source, target, ready.at[item])
        for item, (source, target) in enumerate(zip(sources, targets))
    ]
    for copy in copies:
        copy.start()
    return copies


def pack_halo_kernel(tracers_in, west_cells, east_cells, tracers, ready):
    ntr, levels, lats, _ = tracers.shape
    per_row = LANES // HALO
    group = lane_ids(SUB) // HALO
    assert lats == SUB * per_row
    copies = fetch(
        [tracers_in.at[:, level] for level in range(levels)],
        [tracers.at[:, level] for level in range(levels)],
        ready,
    )
    for level in range(levels):
        copies[level].wait()
        for tracer in range(ntr):
            west = jnp.zeros((SUB, LANES), jnp.float32)
            east = jnp.zeros((SUB, LANES), jnp.float32)
            for part in range(lats // SUB):
                cells = tracers[tracer, level, part * SUB : (part + 1) * SUB, :]
                shift = part * HALO
                rolled_west = pltpu.roll(cells, shift, 1) if shift else cells
                shift = (part * HALO + HALO) % LANES
                rolled_east = pltpu.roll(cells, shift, 1) if shift else cells
                west = jnp.where(group == part, rolled_west, west)
                east = jnp.where(group == part, rolled_east, east)
            west_cells[level, tracer] = west
            east_cells[level, tracer] = east


def pack_halo(tracers):
    ntr, levels, _, _ = tracers.shape
    shape = jax.ShapeDtypeStruct((levels, ntr, SUB, LANES), jnp.float32)
    return pl.pallas_call(
        pack_halo_kernel,
        out_shape=(shape, shape),
        in_specs=[pl.BlockSpec(memory_space=pl.ANY)],
        out_specs=[pl.BlockSpec(memory_space=pltpu.VMEM)] * 2,
        scratch_shapes=[pltpu.VMEM(tracers.shape, jnp.float32), pltpu.SemaphoreType.DMA((levels,))],
        compiler_params=pltpu.CompilerParams(vmem_limit_bytes=SOLVE),
        name="pack_halo",
    )(tracers)


def merge_halo(west, east, halo, count):
    lane = lane_ids(SUB)
    cell = lane % (2 * HALO)
    sources = [(half * 4 + lane // (2 * HALO)) * HALO + cell % HALO for half in range(2)]
    chunk = 10 if count % 10 == 0 else 1

    def some_values(step, carry):
        merged = []
        for item in range(chunk):
            value = step * chunk + item
            for half in range(2):
                both = take_lanes(west[value], sources[half]), take_lanes(east[value], sources[half])
                merged.append((value, half, jnp.where(cell < HALO, *both)))
        for value, half, cells in merged:
            halo[value, half] = cells
        return carry

    lax.fori_loop(0, count // chunk, some_values, 0)


def inside_kernel(
    tracers_in, offsets_in, weights_in, diffusion_in, index_in, count,
    inside, left_cell, west_edge, east_edge, lower, upper, lists,
    tracers, offsets, weights, diffusion, ready,
):
    ntr, levels, lats, _ = tracers.shape
    lane = lane_ids(SUB)
    owners = count.shape[1]
    copies = fetch(
        (diffusion_in, offsets_in, weights_in, tracers_in, index_in.at[0]),
        (diffusion, offsets, weights, tracers, lists.at[pl.ds(0, owners)]),
        ready,
    )
    lists[owners : owners + 1, :owners] = count[...]
    for copy in copies:
        copy.wait()

    def one_part(part, carry):
        rows = pl.ds(pl.multiple_of(part * SUB, SUB), SUB)
        coefs = [diffusion[level, rows, :] for level in range(levels - 1)]
        lowers, uppers, edges, results = [], [], [], []
        for level in range(levels):
            denom = 1.0
            if level > 0:
                denom = denom + coefs[level - 1]
            if level < levels - 1:
                denom = denom + coefs[level]
            if level > 0:
                denom = denom - coefs[level - 1] * uppers[level - 1]
            inverse = 1.0 / denom
            if level > 0:
                lowers.append(coefs[level - 1] * inverse)
            if level < levels - 1:
                uppers.append(coefs[level] * inverse)
            left = lane + offsets[level, rows, :]
            right = left + 1
            weight = weights[level, rows, :]
            west_weight = (1.0 - weight) * inverse
            east_weight = weight * inverse
            left_in = (left >= 0) & (left < LANES)
            right_in = (right >= 0) & (right < LANES)
            edges.append((left, jnp.where(left_in, 0.0, west_weight), jnp.where(right_in, 0.0, east_weight)))
            west_weight = jnp.where(left_in, west_weight, 0.0)
            east_weight = jnp.where(right_in, east_weight, 0.0)
            left = left & (LANES - 1)
            right = right & (LANES - 1)
            for tracer in range(ntr):
                cells = tracers[tracer, level, rows, :]
                results.append(west_weight * take_lanes(cells, left) + east_weight * take_lanes(cells, right))
        for value, result in enumerate(results):
            inside[value, rows, :] = result
        for level, (left, west_weight, east_weight) in enumerate(edges):
            left_cell[level, rows, :] = left
            west_edge[level, rows, :] = west_weight
            east_edge[level, rows, :] = east_weight
        for level in range(levels - 1):
            lower[level, rows, :] = lowers[level]
            upper[level, rows, :] = uppers[level]
        return carry

    lax.fori_loop(0, lats // SUB, one_part, 0)


def advect_inside(tracers, offsets, weights, diffusion, index, count):
    ntr, levels, lats, lons = tracers.shape
    lists, cap = index.shape[1:]
    vmem = pl.BlockSpec(memory_space=pltpu.VMEM)
    field = lambda count, kind=jnp.float32: jax.ShapeDtypeStruct((count, lats, lons), kind)
    outputs = (
        field(ntr * levels),
        field(levels, jnp.int32),
        field(levels),
        field(levels),
        field(levels - 1),
        field(levels - 1),
        jax.ShapeDtypeStruct((max(lists + SUB, LIST_ROWS), cap), jnp.int32),
    )
    return pl.pallas_call(
        inside_kernel,
        out_shape=outputs,
        in_specs=[pl.BlockSpec(memory_space=pl.ANY)] * 5 + [vmem],
        out_specs=(vmem,) * len(outputs),
        scratch_shapes=[pltpu.VMEM(array.shape, array.dtype) for array in (tracers, offsets, weights, diffusion)]
        + [pltpu.SemaphoreType.DMA((5,))],
        compiler_params=pltpu.CompilerParams(vmem_limit_bytes=BIG),
        cost_estimate=pl.CostEstimate(flops=0, bytes_accessed=20 * MIB, transcendentals=0),
        name="advect_inside",
    )(tracers, offsets, weights, diffusion, index, count)


def add_edges_and_solve(inside, left_cell, west_edge, east_edge, lower, upper, halo, solved):
    levels, lats, _ = left_cell.shape
    ntr = inside.shape[0] // levels
    together = 2

    def solve_part(part):
        rows = pl.ds(pl.multiple_of(part * SUB, SUB), SUB)
        half = shift_down(part, 4)
        base = (part & 3) * (2 * HALO)
        reduced = [[] for _ in range(ntr)]
        for level in range(levels):
            left = left_cell[level, rows, :]
            right = base + ((left + (HALO + 1)) & (2 * HALO - 1))
            left = base + ((left + HALO) & (2 * HALO - 1))
            west_weight = west_edge[level, rows, :]
            east_weight = east_edge[level, rows, :]
            for tracer in range(ntr):
                value = level * ntr + tracer
                cells = halo[value, half]
                edges = west_weight * take_lanes(cells, left) + east_weight * take_lanes(cells, right)
                total = inside[value, rows, :] + edges
                if level > 0:
                    total = total + lower[level - 1, rows, :] * reduced[tracer][level - 1]
                reduced[tracer].append(total)
        results = {}
        for level in range(levels - 1, -1, -1):
            for tracer in range(ntr):
                x = reduced[tracer][level]
                if level < levels - 1:
                    x = x + upper[level, rows, :] * results[(level + 1) * ntr + tracer]
                results[level * ntr + tracer] = x
        return results

    def some_parts(step, carry):
        solutions = [solve_part(step * together + item) for item in range(together)]
        for item, results in enumerate(solutions):
            first = pl.multiple_of((step * together + item) * (SUB * SLOT), SUB * SLOT)
            target = solved.at[pl.ds(first, SUB * SLOT), :]
            for value, x in results.items():
                target[pl.ds(value, SUB, stride=SLOT), :] = x
        return carry

    lax.fori_loop(0, lats // (SUB * together), some_parts, 0)


def streams_of(rows, values, parts):
    lane = lane_ids(rows)
    width = values * parts
    item = sum((lane >= width * step).astype(jnp.int32) for step in range(1, 4 // parts))
    held = lane - item * width
    part = held & (parts - 1)
    return jnp.minimum(lax.shift_right_logical(held, parts.bit_length() - 1), values - 1), item * parts + part


def build_table(solved, table, values, parts):
    rows_per = LANES // SLOT
    spread = streams_of(LANES, values, parts)[0]
    together = 8

    def some_rows(step, carry):
        blocks = []
        for item in range(together):
            start = pl.multiple_of((step * together + item) * LANES, LANES)
            blocks.append(solved[pl.ds(start, LANES), :].T)
        for item, block in enumerate(blocks):
            for row in range(rows_per):
                start = pl.multiple_of(((step * together + item) * rows_per + row) * LANES, LANES)
                table[pl.ds(start, LANES), :] = take_lanes(block, spread + row * SLOT)
        return carry

    lax.fori_loop(0, solved.shape[0] // (LANES * together), some_rows, 0)


def shift_down(number, power):
    return lax.shift_right_logical(number, power.bit_length() - 1)


def pick_rows(table, index, count, cap, values, packed, turned, sent, copied, wait_list):
    blocks, height, _ = sent.shape
    parts = cap // LANES
    lists = 4 // parts
    stream = streams_of(1, values, parts)[1]

    def copy_out(block):
        return pltpu.make_async_copy(turned.at[block + 1], sent.at[block], copied.at[block])

    def turn(block):
        half = pl.multiple_of((block & 1) * LANES, LANES)
        return packed[pl.ds(half, LANES), :].T

    def send(block, result):
        turned[block + 1] = result[:height, :]
        for member in range(lists):
            total = count[jnp.maximum(block, 0) * lists + member]
            row = turned.at[block + 1, pl.ds((member * values + 1) * parts - 1, 1), :]
            note = jnp.full((1, LANES), LENGTH_BASE + total.astype(jnp.float32))
            pltpu.store(row, note, mask=(lane_ids(1) == LANES - 1) & (total < cap))

    def one_block(block, carry):
        owners = [block * lists + member for member in range(lists)]
        rows = [shift_down(count[owner] + (parts - 1), parts) for owner in owners]
        for owner in owners:
            wait_list(owner)
        longest = functools.reduce(jnp.maximum, rows)
        places = [owners[g // parts] * cap + (g % parts) * rows[g // parts] for g in range(4)]
        half = (block & 1) * LANES

        def load_lines(start, lines):
            views = [index.at[pl.ds(place + start, lines)] for place in places]
            merged = []
            for line in range(lines):
                picked = [table[view[line]] for view in views]
                low = jnp.where(stream == 0, picked[0], picked[1])
                high = jnp.where(stream == 2, picked[2], picked[3])
                merged.append(jnp.where(stream < 2, low, high))
            return merged

        def store_lines(start, merged):
            target = packed.at[pl.ds(pl.multiple_of(half + start, SUB), len(merged)), :]
            for line, value in enumerate(merged):
                target[line : line + 1, :] = value

        def steps(begin, trips, lines):
            def one_step(step, inner):
                start = pl.multiple_of(begin + step * lines, SUB)
                store_lines(start, load_lines(start, lines))
                return inner

            lax.fori_loop(0, trips, one_step, 0)

        before = turn(block - 1)
        merged = load_lines(0, FIRST)
        store_lines(0, merged)
        send(block - 1, before)

        @pl.when(block > 0)
        def _():
            copy_out(block - 1).start()

        eights = jnp.maximum(shift_down(longest + (SUB - 1), SUB) - FIRST // SUB, 0)
        steps(FIRST, shift_down(eights, 4), 4 * SUB)

        @pl.when((eights & 2) != 0)
        def _():
            start = pl.multiple_of(FIRST + shift_down(eights, 4) * (4 * SUB), SUB)
            store_lines(start, load_lines(start, 2 * SUB))

        @pl.when((eights & 1) != 0)
        def _():
            start = pl.multiple_of(FIRST + (eights - 1) * SUB, SUB)
            store_lines(start, load_lines(start, SUB))

        return carry

    def finish(block, carry):
        copy_out(block).wait()
        return carry

    lax.fori_loop(0, blocks, one_block, 0)
    send(blocks - 1, turn(blocks - 1))
    copy_out(blocks - 1).start()
    lax.fori_loop(0, blocks, finish, 0)


def list_copies(lists_in, index, count, listed):
    cap = lists_in.shape[1]
    owners = index.shape[0] // cap
    lengths = pltpu.make_async_copy(lists_in.at[owners], count, listed.at[owners])

    def list_copy(item):
        place = pl.ds(pl.multiple_of(item * cap, LANES), cap)
        return pltpu.make_async_copy(lists_in.at[item], index.at[place], listed.at[item])

    def start_list(item, carry):
        list_copy(item).start()
        return carry

    lengths.start()
    lax.fori_loop(0, owners, start_list, 0)
    return lengths.wait, lambda item: list_copy(item).wait()


def solve_kernel(
    parts, west, east, inside_in, left_cell_in, west_edge_in, east_edge_in, lower_in, upper_in, lists_in,
    sent, inside, left_cell, west_edge, east_edge, lower, upper, ready,
    halo, solved, table, packed, turned, index, count, listed, copied,
):
    values, lats, _ = inside.shape
    sources = (left_cell_in, west_edge_in, east_edge_in, lower_in, upper_in, inside_in)
    copies = fetch(sources, (left_cell, west_edge, east_edge, lower, upper, inside), ready)
    wait_lengths, wait_list = list_copies(lists_in, index, count, listed)
    for value in range(values, SLOT):
        solved[pl.ds(value, lats, stride=SLOT), :] = jnp.zeros((lats, LANES), jnp.float32)
    merge_halo(west, east, halo, values)
    for copy in copies:
        copy.wait()
    add_edges_and_solve(inside, left_cell, west_edge, east_edge, lower, upper, halo, solved)
    build_table(solved, table.reshape(table.shape[0], LANES), values, parts)
    wait_lengths()
    pick_rows(table, index, count, lists_in.shape[1], values, packed, turned, sent, copied, wait_list)


def make_sent(west, east, fields, lists_in, lists):
    values, lats, lons = fields[0].shape
    cap = lists_in.shape[1]
    parts = cap // LANES
    blocks = lists * parts // 4
    halos = (west.reshape(values, SUB, LANES), east.reshape(values, SUB, LANES))
    sent = pl.pallas_call(
        functools.partial(solve_kernel, parts),
        out_shape=jax.ShapeDtypeStruct((blocks, 4 * values, LANES), jnp.float32),
        in_specs=[pl.BlockSpec(memory_space=pltpu.VMEM)] * 2 + [pl.BlockSpec(memory_space=pl.ANY)] * (len(fields) + 1),
        out_specs=pl.BlockSpec(memory_space=pl.ANY),
        scratch_shapes=[pltpu.VMEM(array.shape, array.dtype) for array in fields]
        + [
            pltpu.SemaphoreType.DMA((len(fields),)),
            pltpu.VMEM((values, 2, SUB, LANES), jnp.float32),
            pltpu.VMEM((lats * SLOT, LANES), jnp.float32),
            pltpu.VMEM((lats * lons, 1, LANES), jnp.float32),
            pltpu.VMEM((2 * LANES, LANES), jnp.float32),
            pltpu.VMEM((blocks + 1, 4 * values, LANES), jnp.float32),
            pltpu.SMEM((lists * cap,), jnp.int32),
            pltpu.SMEM((cap,), jnp.int32),
            pltpu.SemaphoreType.DMA((lists + 1,)),
            pltpu.SemaphoreType.DMA((blocks,)),
        ],
        compiler_params=pltpu.CompilerParams(vmem_limit_bytes=SOLVE),
        cost_estimate=pl.CostEstimate(flops=0, bytes_accessed=40 * MIB, transcendentals=0),
        name="solve_pick",
    )(*halos, *fields, lists_in)
    rows = values * parts
    tile = max(size for size in (1, 2, 4, 8) if rows % size == 0)
    return sent.reshape(lists, rows // tile, tile, LANES)


def place_kernel(own, arrived, owned_out, row, owned, written):
    sources, height, _ = arrived.shape
    levels, ntr, columns = owned.shape
    values = levels * ntr
    parts = height // values
    lane = lax.broadcasted_iota(jnp.int32, (values, LANES), 1)
    order = [own[0] - turn for turn in range(sources)]
    order = [jnp.where(source < 0, source + sources, source) for source in order]
    totals = []
    for source in order:
        note = arrived[source, parts - 1 : parts, :]
        total = jnp.where(note > 0.5 * LENGTH_BASE, note - LENGTH_BASE, 1.0 * parts * LANES)
        totals.append(total.astype(jnp.int32)[0, LANES - 1])
    start = 0
    for source, total in zip(order, totals):
        rows = shift_down(total + (parts - 1), parts)
        pieces = []
        for part in range(parts):
            place = start + jnp.minimum(part * rows, total)
            shift = place & (LANES - 1)
            piece = arrived[source, pl.ds(part, values, stride=parts), :]
            pieces.append((place - shift, shift, pltpu.roll(piece, shift, 1)))
        for tile, shift, rolled in pieces:
            here = pl.ds(pl.multiple_of(tile, LANES), LANES)
            after = pl.ds(pl.multiple_of(tile + LANES, LANES), LANES)
            pltpu.store(row.at[:, here], rolled, mask=lane >= shift)
            row[:, after] = rolled
        start = start + total
    copies = []
    for level in range(levels):
        owned[level] = row[level * ntr : (level + 1) * ntr, :columns]
        copies.append(pltpu.make_async_copy(owned.at[level], owned_out.at[level], written.at[level]))
        copies[level].start()
    for copy in copies:
        copy.wait()


def place_owned(arrived, own, levels, ntr, columns):
    vmem = pl.BlockSpec(memory_space=pltpu.VMEM)
    smem = pl.BlockSpec(memory_space=pltpu.SMEM)
    values = levels * ntr
    return pl.pallas_call(
        place_kernel,
        out_shape=jax.ShapeDtypeStruct((levels, ntr, columns), jnp.float32),
        in_specs=[smem, vmem],
        out_specs=pl.BlockSpec(memory_space=pl.ANY),
        scratch_shapes=[
            pltpu.VMEM((values, columns + 2 * LANES), jnp.float32),
            pltpu.VMEM((levels, ntr, columns), jnp.float32),
            pltpu.SemaphoreType.DMA((levels,)),
        ],
        compiler_params=pltpu.CompilerParams(vmem_limit_bytes=16 * MIB),
        name="place_owned",
    )(own, arrived.reshape(arrived.shape[0], -1, LANES))


def ring(axis, distance):
    size = lax.axis_size(axis)
    return [(i, (i + distance) % size) for i in range(size)]


def body(tracers, offsets, weights, diffusion, send_index, send_count):
    ntr, levels, lats, lons = tracers.shape
    columns = lats * lons
    west_cells, east_cells = pack_halo(tracers)
    from_west = lax.ppermute(east_cells, "lon", ring("lon", 1))
    from_east = lax.ppermute(west_cells, "lon", ring("lon", -1))
    *fields, lists = advect_inside(tracers, offsets, weights, diffusion, send_index, send_count)
    sent = make_sent(from_west, from_east, fields, lists, send_count.shape[1])
    arrived = lax.all_to_all(sent, ("lon", "lat"), split_axis=0, concat_axis=0, tiled=True)
    own = lax.axis_index(("lon", "lat")).astype(jnp.int32).reshape(1)
    owned = place_owned(arrived, own, levels, ntr, columns)
    return jnp.transpose(owned, (1, 0, 2))


def solution(mesh):
    return jax.shard_map(
        body,
        mesh=mesh,
        in_specs=(
            P(None, None, "lat", "lon"),
            P(None, "lat", "lon"),
            P(None, "lat", "lon"),
            P(None, "lat", "lon"),
            P(("lon", "lat"), None, None),
            P(("lon", "lat"), None),
        ),
        out_specs=P(None, None, ("lon", "lat")),
        check_vma=False,
    )
```

```python
import functools

import jax
import jax.numpy as jnp
from jax import lax
from jax.experimental import pallas as pl
from jax.experimental.pallas import tpu as pltpu
from jax.sharding import PartitionSpec as P

HALO = 16
LANES = 128
SUB = 8
SLOT = 32
FIRST = 40
MIB = 1024 * 1024
LENGTH_BASE = 1000.0
BIG = 60 * MIB
SOLVE = 107 * MIB // 2
LIST_ROWS = 256


def take_lanes(block, index):
    return jnp.take_along_axis(block, index, axis=1, mode="promise_in_bounds")


def lane_ids(rows):
    return lax.broadcasted_iota(jnp.int32, (rows, LANES), 1)


def fetch(sources, targets, ready):
    copies = [
        pltpu.make_async_copy(source, target, ready.at[item])
        for item, (source, target) in enumerate(zip(sources, targets))
    ]
    for copy in copies:
        copy.start()
    return copies


def pack_halo_kernel(tracers_in, west_cells, east_cells, tracers, ready):
    ntr, levels, lats, _ = tracers.shape
    per_row = LANES // HALO
    group = lane_ids(SUB) // HALO
    assert lats == SUB * per_row
    copies = fetch(
        [tracers_in.at[:, level] for level in range(levels)],
        [tracers.at[:, level] for level in range(levels)],
        ready,
    )
    for level in range(levels):
        copies[level].wait()
        for tracer in range(ntr):
            west = jnp.zeros((SUB, LANES), jnp.float32)
            east = jnp.zeros((SUB, LANES), jnp.float32)
            for part in range(lats // SUB):
                cells = tracers[tracer, level, part * SUB : (part + 1) * SUB, :]
                shift = part * HALO
                rolled_west = pltpu.roll(cells, shift, 1) if shift else cells
                shift = (part * HALO + HALO) % LANES
                rolled_east = pltpu.roll(cells, shift, 1) if shift else cells
                west = jnp.where(group == part, rolled_west, west)
                east = jnp.where(group == part, rolled_east, east)
            west_cells[level, tracer] = west
            east_cells[level, tracer] = east


def pack_halo(tracers):
    ntr, levels, _, _ = tracers.shape
    shape = jax.ShapeDtypeStruct((levels, ntr, SUB, LANES), jnp.float32)
    return pl.pallas_call(
        pack_halo_kernel,
        out_shape=(shape, shape),
        in_specs=[pl.BlockSpec(memory_space=pl.ANY)],
        out_specs=[pl.BlockSpec(memory_space=pltpu.VMEM)] * 2,
        scratch_shapes=[pltpu.VMEM(tracers.shape, jnp.float32), pltpu.SemaphoreType.DMA((levels,))],
        compiler_params=pltpu.CompilerParams(vmem_limit_bytes=SOLVE),
        name="pack_halo",
    )(tracers)


def merge_halo(west, east, halo, count):
    lane = lane_ids(SUB)
    cell = lane % (2 * HALO)
    sources = [(half * 4 + lane // (2 * HALO)) * HALO + cell % HALO for half in range(2)]
    chunk = 10 if count % 10 == 0 else 1

    def some_values(step, carry):
        merged = []
        for item in range(chunk):
            value = step * chunk + item
            for half in range(2):
                both = take_lanes(west[value], sources[half]), take_lanes(east[value], sources[half])
                merged.append((value, half, jnp.where(cell < HALO, *both)))
        for value, half, cells in merged:
            halo[value, half] = cells
        return carry

    lax.fori_loop(0, count // chunk, some_values, 0)


def inside_kernel(
    tracers_in, offsets_in, weights_in, diffusion_in, index_in, count,
    inside, left_cell, west_edge, east_edge, lower, upper, lists,
    tracers, offsets, weights, diffusion, ready,
):
    ntr, levels, lats, _ = tracers.shape
    lane = lane_ids(SUB)
    owners = count.shape[1]
    copies = fetch(
        (diffusion_in, offsets_in, weights_in, tracers_in, index_in.at[0]),
        (diffusion, offsets, weights, tracers, lists.at[pl.ds(0, owners)]),
        ready,
    )
    lists[owners : owners + 1, :owners] = count[...]
    for copy in copies:
        copy.wait()

    def one_part(part, carry):
        rows = pl.ds(pl.multiple_of(part * SUB, SUB), SUB)
        coefs = [diffusion[level, rows, :] for level in range(levels - 1)]
        lowers, uppers, edges, results = [], [], [], []
        for level in range(levels):
            denom = 1.0
            if level > 0:
                denom = denom + coefs[level - 1]
            if level < levels - 1:
                denom = denom + coefs[level]
            if level > 0:
                denom = denom - coefs[level - 1] * uppers[level - 1]
            inverse = 1.0 / denom
            if level > 0:
                lowers.append(coefs[level - 1] * inverse)
            if level < levels - 1:
                uppers.append(coefs[level] * inverse)
            left = lane + offsets[level, rows, :]
            right = left + 1
            weight = weights[level, rows, :]
            west_weight = (1.0 - weight) * inverse
            east_weight = weight * inverse
            left_in = (left >= 0) & (left < LANES)
            right_in = (right >= 0) & (right < LANES)
            edges.append((left, jnp.where(left_in, 0.0, west_weight), jnp.where(right_in, 0.0, east_weight)))
            west_weight = jnp.where(left_in, west_weight, 0.0)
            east_weight = jnp.where(right_in, east_weight, 0.0)
            left = left & (LANES - 1)
            right = right & (LANES - 1)
            for tracer in range(ntr):
                cells = tracers[tracer, level, rows, :]
                results.append(west_weight * take_lanes(cells, left) + east_weight * take_lanes(cells, right))
        for value, result in enumerate(results):
            inside[value, rows, :] = result
        for level, (left, west_weight, east_weight) in enumerate(edges):
            left_cell[level, rows, :] = left
            west_edge[level, rows, :] = west_weight
            east_edge[level, rows, :] = east_weight
        for level in range(levels - 1):
            lower[level, rows, :] = lowers[level]
            upper[level, rows, :] = uppers[level]
        return carry

    lax.fori_loop(0, lats // SUB, one_part, 0)


def advect_inside(tracers, offsets, weights, diffusion, index, count):
    ntr, levels, lats, lons = tracers.shape
    lists, cap = index.shape[1:]
    vmem = pl.BlockSpec(memory_space=pltpu.VMEM)
    field = lambda count, kind=jnp.float32: jax.ShapeDtypeStruct((count, lats, lons), kind)
    outputs = (
        field(ntr * levels),
        field(levels, jnp.int32),
        field(levels),
        field(levels),
        field(levels - 1),
        field(levels - 1),
        jax.ShapeDtypeStruct((max(lists + SUB, LIST_ROWS), cap), jnp.int32),
    )
    return pl.pallas_call(
        inside_kernel,
        out_shape=outputs,
        in_specs=[pl.BlockSpec(memory_space=pl.ANY)] * 5 + [vmem],
        out_specs=(vmem,) * len(outputs),
        scratch_shapes=[pltpu.VMEM(array.shape, array.dtype) for array in (tracers, offsets, weights, diffusion)]
        + [pltpu.SemaphoreType.DMA((5,))],
        compiler_params=pltpu.CompilerParams(vmem_limit_bytes=BIG),
        cost_estimate=pl.CostEstimate(flops=0, bytes_accessed=20 * MIB, transcendentals=0),
        name="advect_inside",
    )(tracers, offsets, weights, diffusion, index, count)


def add_edges_and_solve(inside, left_cell, west_edge, east_edge, lower, upper, halo, solved):
    levels, lats, _ = left_cell.shape
    ntr = inside.shape[0] // levels
    together = 4

    def solve_part(part):
        rows = pl.ds(pl.multiple_of(part * SUB, SUB), SUB)
        half = shift_down(part, 4)
        base = (part & 3) * (2 * HALO)
        reduced = [[] for _ in range(ntr)]
        for level in range(levels):
            left = left_cell[level, rows, :]
            right = base + ((left + (HALO + 1)) & (2 * HALO - 1))
            left = base + ((left + HALO) & (2 * HALO - 1))
            west_weight = west_edge[level, rows, :]
            east_weight = east_edge[level, rows, :]
            for tracer in range(ntr):
                value = level * ntr + tracer
                cells = halo[value, half]
                edges = west_weight * take_lanes(cells, left) + east_weight * take_lanes(cells, right)
                total = inside[value, rows, :] + edges
                if level > 0:
                    total = total + lower[level - 1, rows, :] * reduced[tracer][level - 1]
                reduced[tracer].append(total)
        results = {}
        for level in range(levels - 1, -1, -1):
            for tracer in range(ntr):
                x = reduced[tracer][level]
                if level < levels - 1:
                    x = x + upper[level, rows, :] * results[(level + 1) * ntr + tracer]
                results[level * ntr + tracer] = x
        return results

    def some_parts(step, carry):
        solutions = [solve_part(step * together + item) for item in range(together)]
        for item, results in enumerate(solutions):
            first = pl.multiple_of((step * together + item) * (SUB * SLOT), SUB * SLOT)
            target = solved.at[pl.ds(first, SUB * SLOT), :]
            for value, x in results.items():
                target[pl.ds(value, SUB, stride=SLOT), :] = x
        return carry

    lax.fori_loop(0, lats // (SUB * together), some_parts, 0)


def streams_of(rows, values, parts):
    lane = lane_ids(rows)
    width = values * parts
    item = sum((lane >= width * step).astype(jnp.int32) for step in range(1, 4 // parts))
    held = lane - item * width
    part = held & (parts - 1)
    return jnp.minimum(lax.shift_right_logical(held, parts.bit_length() - 1), values - 1), item * parts + part


def build_table(solved, table, values, parts):
    rows_per = LANES // SLOT
    spread = streams_of(LANES, values, parts)[0]
    together = 8

    def some_rows(step, carry):
        blocks = []
        for item in range(together):
            start = pl.multiple_of((step * together + item) * LANES, LANES)
            blocks.append(solved[pl.ds(start, LANES), :].T)
        for item, block in enumerate(blocks):
            for row in range(rows_per):
                start = pl.multiple_of(((step * together + item) * rows_per + row) * LANES, LANES)
                table[pl.ds(start, LANES), :] = take_lanes(block, spread + row * SLOT)
        return carry

    lax.fori_loop(0, solved.shape[0] // (LANES * together), some_rows, 0)


def shift_down(number, power):
    return lax.shift_right_logical(number, power.bit_length() - 1)


def pick_rows(table, index, count, cap, values, packed, turned, sent, copied, wait_list):
    blocks, height, _ = sent.shape
    parts = cap // LANES
    lists = 4 // parts
    stream = streams_of(1, values, parts)[1]

    def copy_out(block):
        return pltpu.make_async_copy(turned.at[block + 1], sent.at[block], copied.at[block])

    def turn(block):
        half = pl.multiple_of((block & 1) * LANES, LANES)
        return packed[pl.ds(half, LANES), :].T

    def send(block, result):
        turned[block + 1] = result[:height, :]
        for member in range(lists):
            total = count[jnp.maximum(block, 0) * lists + member]
            row = turned.at[block + 1, pl.ds((member * values + 1) * parts - 1, 1), :]
            note = jnp.full((1, LANES), LENGTH_BASE + total.astype(jnp.float32))
            pltpu.store(row, note, mask=(lane_ids(1) == LANES - 1) & (total < cap))

    def one_block(block, carry):
        owners = [block * lists + member for member in range(lists)]
        rows = [shift_down(count[owner] + (parts - 1), parts) for owner in owners]
        for owner in owners:
            wait_list(owner)
        longest = functools.reduce(jnp.maximum, rows)
        places = [owners[g // parts] * cap + (g % parts) * rows[g // parts] for g in range(4)]
        half = (block & 1) * LANES

        def load_lines(start, lines):
            views = [index.at[pl.ds(place + start, lines)] for place in places]
            merged = []
            for line in range(lines):
                picked = [table[view[line]] for view in views]
                low = jnp.where(stream == 0, picked[0], picked[1])
                high = jnp.where(stream == 2, picked[2], picked[3])
                merged.append(jnp.where(stream < 2, low, high))
            return merged

        def store_lines(start, merged):
            target = packed.at[pl.ds(pl.multiple_of(half + start, SUB), len(merged)), :]
            for line, value in enumerate(merged):
                target[line : line + 1, :] = value

        def steps(begin, trips, lines):
            def one_step(step, inner):
                start = pl.multiple_of(begin + step * lines, SUB)
                store_lines(start, load_lines(start, lines))
                return inner

            lax.fori_loop(0, trips, one_step, 0)

        before = turn(block - 1)
        merged = load_lines(0, FIRST)
        store_lines(0, merged)
        send(block - 1, before)

        @pl.when(block > 0)
        def _():
            copy_out(block - 1).start()

        eights = jnp.maximum(shift_down(longest + (SUB - 1), SUB) - FIRST // SUB, 0)
        steps(FIRST, shift_down(eights, 4), 4 * SUB)

        @pl.when((eights & 2) != 0)
        def _():
            start = pl.multiple_of(FIRST + shift_down(eights, 4) * (4 * SUB), SUB)
            store_lines(start, load_lines(start, 2 * SUB))

        @pl.when((eights & 1) != 0)
        def _():
            start = pl.multiple_of(FIRST + (eights - 1) * SUB, SUB)
            store_lines(start, load_lines(start, SUB))

        return carry

    def finish(block, carry):
        copy_out(block).wait()
        return carry

    lax.fori_loop(0, blocks, one_block, 0)
    send(blocks - 1, turn(blocks - 1))
    copy_out(blocks - 1).start()
    lax.fori_loop(0, blocks, finish, 0)


def list_copies(lists_in, index, count, listed):
    cap = lists_in.shape[1]
    owners = index.shape[0] // cap
    lengths = pltpu.make_async_copy(lists_in.at[owners], count, listed.at[owners])

    def list_copy(item):
        place = pl.ds(pl.multiple_of(item * cap, LANES), cap)
        return pltpu.make_async_copy(lists_in.at[item], index.at[place], listed.at[item])

    def start_list(item, carry):
        list_copy(item).start()
        return carry

    lengths.start()
    lax.fori_loop(0, owners, start_list, 0)
    return lengths.wait, lambda item: list_copy(item).wait()


def solve_kernel(
    parts, west, east, inside_in, left_cell_in, west_edge_in, east_edge_in, lower_in, upper_in, lists_in,
    sent, inside, left_cell, west_edge, east_edge, lower, upper, ready,
    halo, solved, table, packed, turned, index, count, listed, copied,
):
    values, lats, _ = inside.shape
    sources = (left_cell_in, west_edge_in, east_edge_in, lower_in, upper_in, inside_in)
    copies = fetch(sources, (left_cell, west_edge, east_edge, lower, upper, inside), ready)
    wait_lengths, wait_list = list_copies(lists_in, index, count, listed)
    for value in range(values, SLOT):
        solved[pl.ds(value, lats, stride=SLOT), :] = jnp.zeros((lats, LANES), jnp.float32)
    merge_halo(west, east, halo, values)
    for copy in copies:
        copy.wait()
    add_edges_and_solve(inside, left_cell, west_edge, east_edge, lower, upper, halo, solved)
    build_table(solved, table.reshape(table.shape[0], LANES), values, parts)
    wait_lengths()
    pick_rows(table, index, count, lists_in.shape[1], values, packed, turned, sent, copied, wait_list)


def make_sent(west, east, fields, lists_in, lists):
    values, lats, lons = fields[0].shape
    cap = lists_in.shape[1]
    parts = cap // LANES
    blocks = lists * parts // 4
    halos = (west.reshape(values, SUB, LANES), east.reshape(values, SUB, LANES))
    sent = pl.pallas_call(
        functools.partial(solve_kernel, parts),
        out_shape=jax.ShapeDtypeStruct((blocks, 4 * values, LANES), jnp.float32),
        in_specs=[pl.BlockSpec(memory_space=pltpu.VMEM)] * 2 + [pl.BlockSpec(memory_space=pl.ANY)] * (len(fields) + 1),
        out_specs=pl.BlockSpec(memory_space=pl.ANY),
        scratch_shapes=[pltpu.VMEM(array.shape, array.dtype) for array in fields]
        + [
            pltpu.SemaphoreType.DMA((len(fields),)),
            pltpu.VMEM((values, 2, SUB, LANES), jnp.float32),
            pltpu.VMEM((lats * SLOT, LANES), jnp.float32),
            pltpu.VMEM((lats * lons, 1, LANES), jnp.float32),
            pltpu.VMEM((2 * LANES, LANES), jnp.float32),
            pltpu.VMEM((blocks + 1, 4 * values, LANES), jnp.float32),
            pltpu.SMEM((lists * cap,), jnp.int32),
            pltpu.SMEM((cap,), jnp.int32),
            pltpu.SemaphoreType.DMA((lists + 1,)),
            pltpu.SemaphoreType.DMA((blocks,)),
        ],
        compiler_params=pltpu.CompilerParams(vmem_limit_bytes=SOLVE),
        cost_estimate=pl.CostEstimate(flops=0, bytes_accessed=40 * MIB, transcendentals=0),
        name="solve_pick",
    )(*halos, *fields, lists_in)
    rows = values * parts
    tile = max(size for size in (1, 2, 4, 8) if rows % size == 0)
    return sent.reshape(lists, rows // tile, tile, LANES)


def place_kernel(own, arrived, owned_out, row, owned, written):
    sources, height, _ = arrived.shape
    levels, ntr, columns = owned.shape
    values = levels * ntr
    parts = height // values
    lane = lax.broadcasted_iota(jnp.int32, (values, LANES), 1)
    order = [own[0] - turn for turn in range(sources)]
    order = [jnp.where(source < 0, source + sources, source) for source in order]
    totals = []
    for source in order:
        note = arrived[source, parts - 1 : parts, :]
        total = jnp.where(note > 0.5 * LENGTH_BASE, note - LENGTH_BASE, 1.0 * parts * LANES)
        totals.append(total.astype(jnp.int32)[0, LANES - 1])
    start = 0
    for source, total in zip(order, totals):
        rows = shift_down(total + (parts - 1), parts)
        pieces = []
        for part in range(parts):
            place = start + jnp.minimum(part * rows, total)
            shift = place & (LANES - 1)
            piece = arrived[source, pl.ds(part, values, stride=parts), :]
            pieces.append((place - shift, shift, pltpu.roll(piece, shift, 1)))
        for tile, shift, rolled in pieces:
            here = pl.ds(pl.multiple_of(tile, LANES), LANES)
            after = pl.ds(pl.multiple_of(tile + LANES, LANES), LANES)
            pltpu.store(row.at[:, here], rolled, mask=lane >= shift)
            row[:, after] = rolled
        start = start + total
    copies = []
    for level in range(levels):
        owned[level] = row[level * ntr : (level + 1) * ntr, :columns]
        copies.append(pltpu.make_async_copy(owned.at[level], owned_out.at[level], written.at[level]))
        copies[level].start()
    for copy in copies:
        copy.wait()


def place_owned(arrived, own, levels, ntr, columns):
    vmem = pl.BlockSpec(memory_space=pltpu.VMEM)
    smem = pl.BlockSpec(memory_space=pltpu.SMEM)
    values = levels * ntr
    return pl.pallas_call(
        place_kernel,
        out_shape=jax.ShapeDtypeStruct((levels, ntr, columns), jnp.float32),
        in_specs=[smem, vmem],
        out_specs=pl.BlockSpec(memory_space=pl.ANY),
        scratch_shapes=[
            pltpu.VMEM((values, columns + 2 * LANES), jnp.float32),
            pltpu.VMEM((levels, ntr, columns), jnp.float32),
            pltpu.SemaphoreType.DMA((levels,)),
        ],
        compiler_params=pltpu.CompilerParams(vmem_limit_bytes=16 * MIB),
        name="place_owned",
    )(own, arrived.reshape(arrived.shape[0], -1, LANES))


def ring(axis, distance):
    size = lax.axis_size(axis)
    return [(i, (i + distance) % size) for i in range(size)]


def body(tracers, offsets, weights, diffusion, send_index, send_count):
    ntr, levels, lats, lons = tracers.shape
    columns = lats * lons
    west_cells, east_cells = pack_halo(tracers)
    from_west = lax.ppermute(east_cells, "lon", ring("lon", 1))
    from_east = lax.ppermute(west_cells, "lon", ring("lon", -1))
    *fields, lists = advect_inside(tracers, offsets, weights, diffusion, send_index, send_count)
    sent = make_sent(from_west, from_east, fields, lists, send_count.shape[1])
    arrived = lax.all_to_all(sent, ("lon", "lat"), split_axis=0, concat_axis=0, tiled=True)
    own = lax.axis_index(("lon", "lat")).astype(jnp.int32).reshape(1)
    owned = place_owned(arrived, own, levels, ntr, columns)
    return jnp.transpose(owned, (1, 0, 2))


def solution(mesh):
    return jax.shard_map(
        body,
        mesh=mesh,
        in_specs=(
            P(None, None, "lat", "lon"),
            P(None, "lat", "lon"),
            P(None, "lat", "lon"),
            P(None, "lat", "lon"),
            P(("lon", "lat"), None, None),
            P(("lon", "lat"), None),
        ),
        out_specs=P(None, None, ("lon", "lat")),
        check_vma=False,
    )
```
